32 devices in a mesh: ctx: 4 (over y, x), exp: 4 (over z), fsdp: 2 (over core).
Axes of the slice: x: 2, y: 2, z: 4, core: 2. Of those that a mesh axis runs over, the one named last changes fastest.
Arguments:
- hidden_in: bfloat16 [16, 2, 128, 768], P(('exp', 'fsdp'), None, 'ctx'), may hold values from -6 to 6
- seq_lengths: int32 [16], P(('exp', 'fsdp')), may hold values from 64 to 256, as said below
- expert_ids: int32 [16, 2, 128, 2], P(('exp', 'fsdp'), None, 'ctx'), may hold values from 0 to 15, all different within a row
- route_rank: int32 [8, 4, 128], P(('exp', 'fsdp'), 'ctx'), may hold values from 0 to 127, each once within a row
- gain_attn: bfloat16 [768], P(('ctx', 'exp', 'fsdp')), may hold values from 0.5 to 1.5
- w_qkv: bfloat16 [768, 2304], P(('ctx', 'exp', 'fsdp')), may hold values from -0.21875 to 0.21875
- w_out: bfloat16 [768, 768], P(('ctx', 'exp', 'fsdp')), may hold values from -3.5 to 3.5
- w_router: bfloat16 [768, 16], P(('ctx', 'exp', 'fsdp')), may hold values from -0.125 to 0.125
- gain_ffn: bfloat16 [768], P(('ctx', 'exp', 'fsdp')), may hold values from 0.5 to 1.5
- w_gate_up: bfloat16 [768, 4096], P(('ctx', 'exp', 'fsdp')), may hold values from -0.21875 to 0.21875
- w_shared_down: bfloat16 [2048, 768], P(('ctx', 'exp', 'fsdp')), may hold values from -0.125 to 0.125
- w_experts_in: bfloat16 [16, 768, 4096], P('exp', ('ctx', 'fsdp')), may hold values from -0.21875 to 0.21875
- w_experts_out: bfloat16 [16, 2048, 768], P('exp', ('ctx', 'fsdp')), may hold values from -0.125 to 0.125
- grad_output: bfloat16 [16, 2, 128, 768], P(('exp', 'fsdp'), None, 'ctx'), may hold values from -6 to 6
Outputs:
- layer_out: bfloat16 [16, 2, 128, 768], P(('exp', 'fsdp'), None, 'ctx')
- grad_input: float32 [16, 2, 128, 768], P(('exp', 'fsdp'), None, 'ctx')
- grad_gain_attn: float32 [768], P(('ctx', 'exp', 'fsdp'))
- grad_w_qkv: float32 [768, 2304], P(('ctx', 'exp', 'fsdp'))
- grad_w_out: float32 [768, 768], P(('ctx', 'exp', 'fsdp'))
- grad_w_router: float32 [768, 16], P(('ctx', 'exp', 'fsdp'))
- grad_gain_ffn: float32 [768], P(('ctx', 'exp', 'fsdp'))
- grad_w_gate_up: float32 [768, 4096], P(('ctx', 'exp', 'fsdp'))
- grad_w_shared_down: float32 [2048, 768], P(('ctx', 'exp', 'fsdp'))
- grad_w_experts_in: float32 [16, 768, 4096], P('exp', ('ctx', 'fsdp'))
- grad_w_experts_out: float32 [16, 2048, 768], P('exp', ('ctx', 'fsdp'))
The draws below stay inside these ranges and needn't reach their ends.
Inputs may be any that keep to these rules, and one draw needn't show every extreme that they name: `seq_lengths`: of each 2 consecutive sequences, one has length exactly 256. `expert_ids`: the 2 experts of a slot differ. `route_rank`: each row of 128 entries holds every rank once.
All inputs are finite; a program needn't handle non-finite values.
Results may differ from the reference program's by a relative error of at most 0.015.
Values may be sent and summed in bfloat16 or wider, within the bound.
A program may use at most 256 MiB of HBM per device.

```python
import jax
import jax.numpy as jnp
from jax import lax

D = 768
H = 12
HS = 64
E = 16
TOP = 2
FE = 2048
FS = 2048
CT = 64
SEQS_GRP = 2
TOK_DEV = 128
SEQ = 256
B = 16
CAP = 18
N_CTX = 4
N_EXP = 4
N_FSDP = 2


def draw_seq_lengths(key, part):
    key = jax.random.fold_in(key, 7)
    first_key, second_key = jax.random.split(key)
    groups = B // SEQS_GRP
    ragged = jax.random.randint(first_key, (groups, SEQS_GRP), SEQ // 4, SEQ + 1)
    longest = jax.random.randint(second_key, (groups, 1), 0, SEQS_GRP)
    whole = jnp.arange(SEQS_GRP)[None, :] == longest
    return jnp.where(whole, SEQ, ragged).reshape(B).astype(jnp.int32)


def steps_of(own_key, dims, shards, smallest, largest):
    factor_of, own = 1.0, jax.random.fold_in(own_key, 6)
    for dim, blocks in shards:
        steps = jnp.exp(jax.random.uniform(jax.random.fold_in(own, dim), (blocks,), jnp.float32, smallest / len(shards), largest / len(shards)))
        factor_of = factor_of * jnp.repeat(steps, dims[dim] // blocks).reshape([-1 if axis == dim else 1 for axis in range(len(dims))])
    return factor_of


def distinct(own_key, rows, count, top, lift):
    sequence = jax.random.permutation(jax.random.fold_in(own_key, 1), count)
    pull = sequence
    for power in range(3):
        pull = pull * pull // count
    pull = pull * lift // count
    chance = jax.random.randint(jax.random.fold_in(own_key, 2), (rows, count), 0, 4096) + pull
    fixed_rows = jax.random.permutation(jax.random.fold_in(own_key, 3), rows)[jnp.arange(count) % rows]
    chance = jnp.where(jnp.arange(rows)[:, None] == fixed_rows[None, :], 1 << 14, chance)
    priority = chance * count + jnp.arange(count)
    return lax.top_k(priority.astype(jnp.int32), top)[1].astype(jnp.int32)


def noise(own_key, shape, deviation, reach, shards=(), held_as=jnp.bfloat16):
    result = jax.random.normal(own_key, shape, jnp.float32) * deviation
    if len(shards) > 0:
        result = steps_of(own_key, shape, shards, -0.22, 0.18) * result
    return jnp.clip(result, min=-reach, max=reach).astype(held_as)


def setup_inputs(seed: int = 0) -> dict:
    seeds = jax.random.split(jax.random.key(seed), 15)
    return {
        "hidden_in": noise(seeds[0], (B, 2, SEQ // 2, D), 1.0, 6.0, ((0, 8), (2, 4))),
        "seq_lengths": draw_seq_lengths(jax.random.fold_in(seeds[14], 71), 0),
        "expert_ids": distinct(seeds[2], B * 2 * (SEQ // 2), E, TOP, 2048).reshape((B, 2, SEQ // 2, TOP)),
        "route_rank": jax.vmap(lambda own: jax.random.permutation(own, TOK_DEV))(jax.random.split(seeds[3], (N_EXP * N_FSDP) * N_CTX)).reshape((N_EXP * N_FSDP, N_CTX, TOK_DEV)).astype(jnp.int32),
        "gain_attn": jnp.clip(1.0 + 0.1 * jax.random.normal(seeds[4], (D,), jnp.float32), 0.5, 1.5).astype(jnp.bfloat16),
        "w_qkv": noise(seeds[5], (D, 3 * D), D ** -0.5, 0.21875, ((0, 32),)),
        "w_out": noise(seeds[6], (D, D), (max(D // 256, 1)) ** -0.5, 3.5, ((0, 32),)),
        "w_router": noise(seeds[7], (D, E), (3 * D) ** -0.5, 0.125, ((0, 32),)),
        "gain_ffn": jnp.clip(1.0 + 0.1 * jax.random.normal(seeds[8], (D,), jnp.float32), 0.5, 1.5).astype(jnp.bfloat16),
        "w_gate_up": noise(seeds[9], (D, 2 * FS), D ** -0.5, 0.21875, ((0, 32),)),
        "w_shared_down": noise(seeds[10], (FS, D), FS ** -0.5, 0.125, ((0, 32),)),
        "w_experts_in": noise(seeds[11], (E, D, 2 * FE), D ** -0.5, 0.21875, ((0, 4), (1, 8))),
        "w_experts_out": noise(seeds[12], (E, FE, D), FE ** -0.5, 0.125, ((0, 4), (1, 8))),
        "grad_output": noise(seeds[13], (B, 2, SEQ // 2, D), 1.0, 6.0, ((0, 8), (2, 4))),
    }


epsilon = 1e-06
masked_out = -1e+30
highest = lax.Precision.HIGHEST

@jax.custom_vjp
def low(v):
    return lax.optimization_barrier(v.astype(jnp.bfloat16)).astype(jnp.float32)

@jax.custom_vjp
def low_back(v):
    return v

def low_keep(v):
    return (low(v), None)

def low_pass(kept, grad):
    return (grad,)

def back_keep(v):
    return (v, None)

def back_low(kept, grad):
    return (low(grad),)
low.defvjp(low_keep, low_pass)
low_back.defvjp(back_keep, back_low)

def product(left_side, right_side):
    return jnp.dot(left_side, right_side, precision=highest, preferred_element_type=jnp.float32)

def rms_norm(values_in, gain_row):
    return values_in * lax.rsqrt(lax.optimization_barrier(jnp.mean(values_in * values_in, axis=-1, keepdims=True)) + epsilon) * gain_row

def to_sequence(array_in):
    return jnp.concatenate([array_in[:, 0], jnp.flip(array_in[:, 1], axis=1)], axis=1)

def to_folded(array_in):
    half_len = array_in.shape[1] // 2
    return jnp.stack([array_in[:, :half_len], jnp.flip(array_in[:, half_len:], axis=1)], axis=1)

def rope_tables(places):
    half_size = HS // 2
    frequency = 10000.0 ** (-jnp.arange(half_size, dtype=jnp.float32) * 2.0 / HS)
    angles = places.astype(jnp.float32)[:, None] * frequency[None, :]
    return (jnp.cos(angles), jnp.sin(angles))

def rotate(values_in, cosines, sine_rows):
    half_size = values_in.shape[-1] // 2
    leading = values_in[..., :half_size]
    trailing = values_in[..., half_size:]
    cos_rows = cosines[:, None, :]
    sin_rows = sine_rows[:, None, :]
    return jnp.concatenate([leading * cos_rows - trailing * sin_rows, leading * sin_rows + trailing * cos_rows], axis=-1)

def one_sequence(stacked):
    queries, keys_in, values_in, seq_len = stacked
    count = queries.shape[0]
    scores = jnp.einsum('qhd,khd->hqk', queries, keys_in, precision=highest) * HS ** (-0.5)
    scores = low_back(scores)
    places = jnp.arange(count, dtype=jnp.int32)
    allowed = (places[None, :] <= places[:, None]) & (places[None, :] < seq_len)
    scores = jnp.where(allowed[None], scores, masked_out)
    weights = low(jax.nn.softmax(scores, axis=-1))
    return jnp.einsum('hqk,khd->qhd', weights, values_in, precision=highest)

def expert_rows(stacked):
    rows_in, gate_up, down_proj = stacked
    merged_rows = low_back(product(rows_in, gate_up))
    gate_part, up_part = jnp.split(merged_rows, 2, axis=-1)
    hidden_rows = low(jax.nn.silu(gate_part) * up_part)
    return low_back(low(product(hidden_rows, down_proj)))

def slot_positions(stacked):
    expert_load, rank_rows = stacked
    earlier = (rank_rows[None, :] < rank_rows[:, None]).astype(jnp.int32)
    return jnp.dot(earlier, expert_load)

def to_blocks(array_in, groups):
    trailing_shape = array_in.shape[3:]
    half_ct = CT // 2
    array_in = array_in.reshape((groups, SEQS_GRP, 2, N_CTX, half_ct) + trailing_shape)
    array_in = jnp.moveaxis(array_in, 3, 1)
    return array_in.reshape((groups * N_CTX, SEQS_GRP * CT) + trailing_shape)

def from_blocks(array_in, groups):
    trailing_shape = array_in.shape[2:]
    half_ct = CT // 2
    array_in = array_in.reshape((groups, N_CTX, SEQS_GRP, 2, half_ct) + trailing_shape)
    array_in = jnp.moveaxis(array_in, 1, 3)
    return array_in.reshape((groups * SEQS_GRP, 2, N_CTX * half_ct) + trailing_shape)

def forward(hidden_in, seq_lengths, expert_ids, route_rank, gain_attn, w_qkv, w_out, w_router, gain_ffn, w_gate_up, w_shared_down, w_experts_in, w_experts_out):
    num_batch, seq_len, model_width = hidden_in.shape
    groups = num_batch // SEQS_GRP
    places = jnp.arange(seq_len, dtype=jnp.int32)
    live_int = (places[None, :] < seq_lengths[:, None]).astype(jnp.int32)
    live_mask = live_int.astype(jnp.float32)
    normed = low(rms_norm(hidden_in, gain_attn))
    qkv_merged = low_back(product(normed, w_qkv)).reshape(num_batch, seq_len, 3, H, HS)
    cosines, sine_rows = rope_tables(places)
    queries = low(rotate(qkv_merged[:, :, 0], cosines, sine_rows))
    keys_all = low(rotate(qkv_merged[:, :, 1], cosines, sine_rows))
    values_all = low(qkv_merged[:, :, 2])
    context = lax.map(jax.checkpoint(one_sequence), (queries, keys_all, values_all, seq_lengths))
    context = low_back(low(context.reshape(num_batch, seq_len, model_width)))
    attended = hidden_in + low_back(product(context, w_out))
    normed_two = low(rms_norm(attended, gain_ffn))
    logits = product(normed_two, w_router)
    expert_range = jnp.arange(E, dtype=jnp.int32)
    ids_seq = to_sequence(expert_ids)
    pick_hot = (ids_seq[..., None] == expert_range).astype(jnp.float32)
    chosen = lax.optimization_barrier(jnp.sum(pick_hot * logits[:, :, None, :], axis=-1))
    gate_probs = jax.nn.softmax(chosen, axis=-1)
    num_blocks = groups * N_CTX
    ids_blocks = to_blocks(expert_ids, groups)
    live_blocks = to_blocks(to_folded(live_int), groups)
    pick_int = (ids_blocks[..., None] == expert_range).astype(jnp.int32)
    expert_load = lax.optimization_barrier(jnp.sum(pick_int, axis=2)) * live_blocks[..., None]
    rank_rows = route_rank.reshape(num_blocks, SEQS_GRP * CT)
    position = lax.map(slot_positions, (expert_load, rank_rows))
    chosen_pos = lax.optimization_barrier(jnp.sum(pick_int * position[:, :, None, :], axis=-1))
    kept_mask = jnp.logical_and(chosen_pos < CAP, live_blocks[..., None] > 0)
    slot_ids = jnp.where(kept_mask, ids_blocks * CAP + chosen_pos, E * CAP)
    block_ids = jnp.arange(num_blocks, dtype=jnp.int32)[:, None, None]
    normed_blocks = to_blocks(to_folded(normed_two), groups)
    spread_rows = jnp.broadcast_to(normed_blocks[:, :, None, :], slot_ids.shape + (model_width,))
    buffers = jnp.zeros((num_blocks, E * CAP + 1, model_width), jnp.float32).at[block_ids, slot_ids].add(spread_rows)
    buffers = low_back(buffers[:, :E * CAP].reshape(num_blocks, E, CAP, model_width))
    per_expert = jnp.moveaxis(buffers, 1, 0).reshape(E, num_blocks * CAP, model_width)
    outputs = lax.map(jax.checkpoint(expert_rows), (per_expert, w_experts_in, w_experts_out))
    outputs = jnp.moveaxis(outputs.reshape(E, num_blocks, CAP, model_width), 0, 1).reshape(num_blocks, E * CAP, model_width)
    outputs = jnp.concatenate([outputs, jnp.zeros((num_blocks, 1, model_width), jnp.float32)], axis=1)
    routed = outputs[block_ids, slot_ids]
    gate_blocks = to_blocks(to_folded(gate_probs), groups)
    mixture = to_sequence(from_blocks(lax.optimization_barrier(jnp.sum(gate_blocks[..., None] * routed, axis=2)), groups))
    mixture = low_back(mixture)
    shared_merged = low_back(product(normed_two, w_gate_up))
    gate_part, up_part = jnp.split(shared_merged, 2, axis=-1)
    shared_hidden = low(jax.nn.silu(gate_part) * up_part)
    shared_out = low_back(product(shared_hidden, w_shared_down))
    return live_mask[..., None] * (attended + mixture + shared_out)

def reference(hidden_in, seq_lengths, expert_ids, route_rank, gain_attn, w_qkv, w_out, w_router, gain_ffn, w_gate_up, w_shared_down, w_experts_in, w_experts_out, grad_output):
    weights = tuple((array_in.astype(jnp.float32) for array_in in (gain_attn, w_qkv, w_out, w_router, gain_ffn, w_gate_up, w_shared_down, w_experts_in, w_experts_out)))

    def layer_fn(inputs_f, *params):
        return forward(inputs_f, seq_lengths, expert_ids, route_rank, *params)
    inputs_seq = to_sequence(hidden_in.astype(jnp.float32))
    cotangent = to_sequence(grad_output.astype(jnp.float32))
    layer_out, pull_back = jax.vjp(layer_fn, inputs_seq, *weights)
    gradients = pull_back(cotangent)
    return (to_folded(layer_out).astype(jnp.bfloat16), to_folded(gradients[0]), gradients[1], gradients[2], gradients[3], gradients[4], gradients[5], gradients[6], gradients[7], gradients[8], gradients[9])
```

```python
import functools

import jax
import jax.numpy as jnp
from jax import lax
from jax.experimental import pallas as pl
from jax.experimental.pallas import tpu as pltpu
from jax.sharding import PartitionSpec as P

HS = 64
CAP = 18


epsilon = 1e-06
masked_out = -1e30
highest = lax.Precision.HIGHEST


def rms_norm(values_in, gain_row):
    return (
        values_in
        * lax.rsqrt(jnp.mean(values_in * values_in, axis=-1, keepdims=True) + epsilon)
        * gain_row
    )


def rope_tables(places):
    half_size = HS // 2
    frequency = 10000.0 ** (-jnp.arange(half_size, dtype=jnp.float32) * 2.0 / HS)
    angles = places.astype(jnp.float32)[:, None] * frequency[None, :]
    return (jnp.cos(angles), jnp.sin(angles))


def rotate(values_in, cosines, sine_rows):
    half_size = values_in.shape[-1] // 2
    leading = values_in[..., :half_size]
    trailing = values_in[..., half_size:]
    cos_rows = cosines[:, None, :]
    sin_rows = sine_rows[:, None, :]
    return jnp.concatenate(
        [leading * cos_rows - trailing * sin_rows, leading * sin_rows + trailing * cos_rows],
        axis=-1,
    )


def swiglu(merged_rows):
    gate_part, up_part = jnp.split(merged_rows, 2, axis=-1)
    return jax.nn.silu(gate_part) * up_part


def first_t(left_side, right_side, precision=None):
    return lax.dot_general(
        left_side,
        right_side,
        (((0,), (0,)), ((), ())),
        precision=precision,
        preferred_element_type=jnp.float32,
    )


def second_t(left_side, right_side, precision=None):
    return lax.dot_general(
        left_side,
        right_side,
        (((1,), (1,)), ((), ())),
        precision=precision,
        preferred_element_type=jnp.float32,
    )


def per_device(
    hidden_in,
    seq_lengths,
    expert_ids,
    route_rank,
    gain_attn,
    w_qkv,
    w_out,
    w_router,
    gain_ffn,
    w_gate_up,
    w_shared_down,
    w_experts_in,
    w_experts_out,
    grad_output,
):
    num_seqs, two_ends, half_len, model_width = hidden_in.shape
    shard_len = 2 * half_len
    tok_count = num_seqs * shard_len
    num_heads = model_width // HS
    score_scale = HS ** (-0.5)
    ctx_size = lax.axis_size("ctx")
    full_len = shard_len * ctx_size
    whole_half = half_len * ctx_size
    gain_one, wqkv_all, wout_all, router_all, gain_two, shared_in, shared_down = (
        lax.all_gather(gain_attn, ("ctx", "exp", "fsdp"), axis=0, tiled=True),
        lax.all_gather(w_qkv, ("ctx", "exp", "fsdp"), axis=0, tiled=True),
        lax.all_gather(w_out, ("ctx", "exp", "fsdp"), axis=0, tiled=True),
        lax.all_gather(w_router, ("ctx", "exp", "fsdp"), axis=0, tiled=True),
        lax.all_gather(gain_ffn, ("ctx", "exp", "fsdp"), axis=0, tiled=True),
        lax.all_gather(w_gate_up, ("ctx", "exp", "fsdp"), axis=0, tiled=True),
        lax.all_gather(w_shared_down, ("ctx", "exp", "fsdp"), axis=0, tiled=True),
    )
    experts_in, experts_out = (
        lax.all_gather(w_experts_in, ("ctx", "fsdp"), axis=1, tiled=True),
        lax.all_gather(w_experts_out, ("ctx", "fsdp"), axis=1, tiled=True),
    )
    lower_places = lax.axis_index("ctx") * half_len + jnp.arange(half_len, dtype=jnp.int32)
    places = jnp.concatenate([lower_places, full_len - 1 - lower_places])
    whole_range = jnp.arange(whole_half, dtype=jnp.int32)
    full_places = jnp.concatenate([whole_range, full_len - 1 - whole_range])
    live_mask = (places[None, :] < seq_lengths[:, None]).astype(jnp.float32)
    live_rows = live_mask.reshape(tok_count, 1)
    inputs_f = hidden_in.astype(jnp.float32).reshape(tok_count, model_width)
    gain_attn_f = gain_one.astype(jnp.float32)
    normed_b = rms_norm(inputs_f, gain_attn_f).astype(jnp.bfloat16)
    qkv_merged = jnp.dot(normed_b, wqkv_all, preferred_element_type=jnp.float32).reshape(
        num_seqs, shard_len, 3, num_heads, HS
    )
    cosines, sine_rows = rope_tables(places)
    queries = rotate(qkv_merged[:, :, 0], cosines, sine_rows).astype(jnp.bfloat16)
    keys_local = rotate(qkv_merged[:, :, 1], cosines, sine_rows).astype(jnp.bfloat16)
    values_local = qkv_merged[:, :, 2].astype(jnp.bfloat16)
    end_shape = (num_seqs, 2, half_len, model_width)
    keys_full, values_full = (
        lax.all_gather(keys_local.reshape(end_shape), "ctx", axis=2, tiled=True),
        lax.all_gather(values_local.reshape(end_shape), "ctx", axis=2, tiled=True),
    )
    keys_full = keys_full.reshape(num_seqs, full_len, num_heads, HS)
    values_full = values_full.reshape(num_seqs, full_len, num_heads, HS)
    stat_shape = (num_seqs, num_heads, shard_len)
    block_range = jnp.arange(ctx_size, dtype=jnp.int32)

    def block_scores(query_rows, query_places, key_rows, key_places):
        scores = (
            jnp.einsum("bqhd,bkhd->bhqk", query_rows, key_rows, preferred_element_type=jnp.float32)
            * score_scale
        )
        allowed = (key_places[None, None, :] <= query_places[None, :, None]) & (
            key_places[None, None, :] < seq_lengths[:, None, None]
        )
        return jnp.where(allowed[:, None], scores, masked_out)

    def key_block(block_idx):
        offset = block_idx * shard_len
        return (
            lax.dynamic_slice_in_dim(keys_full, offset, shard_len, 1),
            lax.dynamic_slice_in_dim(values_full, offset, shard_len, 1),
            lax.dynamic_slice_in_dim(full_places, offset, shard_len, 0),
        )

    def lse_step(state_in, block_idx):
        run_max, run_sum = state_in
        key_rows, value_rows, key_places = key_block(block_idx)
        scores = block_scores(queries, places, key_rows, key_places)
        new_max = jnp.maximum(run_max, jnp.max(scores, axis=-1))
        run_sum = run_sum * jnp.exp(run_max - new_max) + jnp.sum(
            jnp.exp(scores - new_max[..., None]), axis=-1
        )
        return ((new_max, run_sum), None)

    (row_max, row_sum), unused = lax.scan(
        lse_step,
        (jnp.full(stat_shape, masked_out, jnp.float32), jnp.zeros(stat_shape, jnp.float32)),
        block_range,
    )
    log_total = row_max + jnp.log(row_sum)

    def context_step(running, block_idx):
        key_rows, value_rows, key_places = key_block(block_idx)
        prob_rows = jnp.exp(
            block_scores(queries, places, key_rows, key_places) - log_total[..., None]
        ).astype(jnp.bfloat16)
        return (
            running
            + jnp.einsum(
                "bhqk,bkhd->bqhd", prob_rows, value_rows, preferred_element_type=jnp.float32
            ),
            None,
        )

    context, unused = lax.scan(
        context_step, jnp.zeros((num_seqs, shard_len, num_heads, HS), jnp.float32), block_range
    )
    context_b = context.reshape(tok_count, model_width).astype(jnp.bfloat16)
    attended = inputs_f + jnp.dot(context_b, wout_all, preferred_element_type=jnp.float32)
    gain_ffn_f = gain_two.astype(jnp.float32)
    normed_two = rms_norm(attended, gain_ffn_f).astype(jnp.bfloat16)
    logits = jnp.dot(normed_two, router_all, preferred_element_type=jnp.float32)
    num_experts = router_all.shape[1]
    expert_range = jnp.arange(num_experts, dtype=jnp.int32)
    picked_ids = expert_ids.reshape(tok_count, 2)
    pick_hot = (picked_ids[:, :, None] == expert_range).astype(jnp.float32)
    chosen = jnp.sum(pick_hot * logits[:, None, :], axis=-1)
    gate_probs = jax.nn.softmax(chosen, axis=-1)
    expert_load = (jnp.sum(pick_hot, axis=1) * live_rows).astype(jnp.bfloat16)
    rank_rows = route_rank.reshape(tok_count)
    earlier = (rank_rows[None, :] < rank_rows[:, None]).astype(jnp.bfloat16)
    position = jnp.dot(earlier, expert_load, preferred_element_type=jnp.float32)
    chosen_pos = jnp.sum(pick_hot * position[:, None, :], axis=-1)
    kept_mask = live_rows * (chosen_pos < CAP).astype(jnp.float32)
    slot_hot = (chosen_pos[:, :, None] == jnp.arange(CAP, dtype=jnp.float32)).astype(jnp.float32)
    dispatch = (
        (pick_hot[:, :, :, None] * slot_hot[:, :, None, :] * kept_mask[:, :, None, None])
        .reshape(tok_count, 2, num_experts * CAP)
        .astype(jnp.bfloat16)
    )
    dispatch_any = dispatch[:, 0] + dispatch[:, 1]
    exp_size = lax.axis_size("exp")
    per_owner = num_experts // exp_size
    send_rows = (
        first_t(dispatch_any, normed_two)
        .astype(jnp.bfloat16)
        .reshape(exp_size, per_owner, CAP, model_width)
    )
    arrived = lax.all_to_all(send_rows, "exp", split_axis=0, concat_axis=0, tiled=True)
    expert_merged = jnp.einsum(
        "secd,edf->secf", arrived, experts_in, preferred_element_type=jnp.float32
    )
    expert_hidden = swiglu(expert_merged).astype(jnp.bfloat16)
    expert_result = jnp.einsum(
        "secf,efd->secd", expert_hidden, experts_out, preferred_element_type=jnp.float32
    ).astype(jnp.bfloat16)
    returned = lax.all_to_all(
        expert_result, "exp", split_axis=0, concat_axis=0, tiled=True
    ).reshape(num_experts * CAP, model_width)
    routed = jnp.einsum("tks,sd->tkd", dispatch, returned, preferred_element_type=jnp.float32)
    mixture = jnp.sum(gate_probs[:, :, None] * routed, axis=1)
    shared_merged = jnp.dot(normed_two, shared_in, preferred_element_type=jnp.float32)
    shared_hidden = swiglu(shared_merged).astype(jnp.bfloat16)
    shared_result = jnp.dot(shared_hidden, shared_down, preferred_element_type=jnp.float32)
    layer_out = (
        (live_rows * (attended + mixture + shared_result)).reshape(end_shape).astype(jnp.bfloat16)
    )
    upstream = grad_output.astype(jnp.float32).reshape(tok_count, model_width) * live_rows
    upstream_b = upstream.astype(jnp.bfloat16)
    upstream_f = upstream_b.astype(jnp.float32)
    d_shared_down = first_t(shared_hidden, upstream_b)
    d_shared_hidden = second_t(upstream_b, shared_down)
    unused, swiglu_pull = jax.vjp(swiglu, shared_merged)
    d_shared_merged = swiglu_pull(d_shared_hidden)[0].astype(jnp.bfloat16)
    d_shared_in = first_t(normed_two, d_shared_merged)
    d_normed_two = second_t(d_shared_merged, shared_in)
    gate_grads = jnp.sum(routed * upstream_f[:, None, :], axis=-1)
    weighted = (gate_probs[:, :, None] * upstream_f[:, None, :]).astype(jnp.bfloat16)
    d_returned = (
        jnp.einsum("tks,tkd->sd", dispatch, weighted, preferred_element_type=jnp.float32)
        .astype(jnp.bfloat16)
        .reshape(exp_size, per_owner, CAP, model_width)
    )
    d_result = lax.all_to_all(d_returned, "exp", split_axis=0, concat_axis=0, tiled=True)
    d_experts_out = jnp.einsum(
        "secf,secd->efd", expert_hidden, d_result, preferred_element_type=jnp.float32
    )
    d_expert_hidden = jnp.einsum(
        "secd,efd->secf", d_result, experts_out, preferred_element_type=jnp.float32
    )
    unused, expert_pull = jax.vjp(swiglu, expert_merged)
    d_expert_merged = expert_pull(d_expert_hidden)[0].astype(jnp.bfloat16)
    d_experts_in = jnp.einsum(
        "secd,secf->edf", arrived, d_expert_merged, preferred_element_type=jnp.float32
    )
    d_arrived = jnp.einsum(
        "secf,edf->secd", d_expert_merged, experts_in, preferred_element_type=jnp.float32
    ).astype(jnp.bfloat16)
    d_sent = lax.all_to_all(d_arrived, "exp", split_axis=0, concat_axis=0, tiled=True).reshape(
        num_experts * CAP, model_width
    )
    d_normed_two = d_normed_two + jnp.dot(dispatch_any, d_sent, preferred_element_type=jnp.float32)
    unused, gate_pull = jax.vjp(lambda chosen_in: jax.nn.softmax(chosen_in, axis=-1), chosen)
    d_chosen = gate_pull(gate_grads)[0]
    d_logits = jnp.sum(pick_hot * d_chosen[:, :, None], axis=1)
    d_router = first_t(normed_two.astype(jnp.float32), d_logits, highest)
    d_normed_two = d_normed_two + second_t(d_logits, router_all.astype(jnp.float32), highest)
    unused, second_pull = jax.vjp(rms_norm, attended, gain_ffn_f)
    d_attended, d_gain_ffn = second_pull(d_normed_two)
    d_attended = d_attended + upstream
    d_attended_b = d_attended.astype(jnp.bfloat16)
    d_out_proj = first_t(context_b, d_attended_b)
    d_context = (
        second_t(d_attended_b, wout_all)
        .astype(jnp.bfloat16)
        .reshape(num_seqs, shard_len, num_heads, HS)
    )

    def score_grads(
        query_rows, query_places, key_rows, value_rows, key_places, d_rows, lse_rows, delta_rows
    ):
        prob_rows = jnp.exp(
            block_scores(query_rows, query_places, key_rows, key_places) - lse_rows[..., None]
        )
        d_probs = jnp.einsum(
            "bqhd,bkhd->bhqk", d_rows, value_rows, preferred_element_type=jnp.float32
        )
        d_scores = (prob_rows * (d_probs - delta_rows[..., None])).astype(jnp.bfloat16)
        return (prob_rows.astype(jnp.bfloat16), d_scores)

    def delta_step(running, block_idx):
        key_rows, value_rows, key_places = key_block(block_idx)
        prob_rows = jnp.exp(
            block_scores(queries, places, key_rows, key_places) - log_total[..., None]
        )
        d_probs = jnp.einsum(
            "bqhd,bkhd->bhqk", d_context, value_rows, preferred_element_type=jnp.float32
        )
        return (running + jnp.sum(prob_rows * d_probs, axis=-1), None)

    row_delta, unused = lax.scan(delta_step, jnp.zeros(stat_shape, jnp.float32), block_range)
    head_shape = (num_seqs, shard_len, num_heads, HS)

    def query_step(d_query, block_idx):
        key_rows, value_rows, key_places = key_block(block_idx)
        prob_b, d_scores = score_grads(
            queries, places, key_rows, value_rows, key_places, d_context, log_total, row_delta
        )
        return (
            d_query
            + jnp.einsum("bhqk,bkhd->bqhd", d_scores, key_rows, preferred_element_type=jnp.float32)
            * score_scale,
            None,
        )

    d_query, unused = lax.scan(query_step, jnp.zeros(head_shape, jnp.float32), block_range)
    query_all, d_context_all = (
        lax.all_gather(queries.reshape(end_shape), "ctx", axis=2, tiled=True),
        lax.all_gather(d_context.reshape(end_shape), "ctx", axis=2, tiled=True),
    )
    stat_ends = (num_seqs, num_heads, 2, half_len)
    lse_all, delta_all = (
        lax.all_gather(log_total.reshape(stat_ends), "ctx", axis=3, tiled=True),
        lax.all_gather(row_delta.reshape(stat_ends), "ctx", axis=3, tiled=True),
    )
    query_all = query_all.reshape(num_seqs, full_len, num_heads, HS)
    d_context_all = d_context_all.reshape(num_seqs, full_len, num_heads, HS)
    lse_all = lse_all.reshape(num_seqs, num_heads, full_len)
    delta_all = delta_all.reshape(num_seqs, num_heads, full_len)

    def owner_step(state_in, block_idx):
        d_keys, d_values = state_in
        offset = block_idx * shard_len
        query_rows = lax.dynamic_slice_in_dim(query_all, offset, shard_len, 1)
        d_rows = lax.dynamic_slice_in_dim(d_context_all, offset, shard_len, 1)
        lse_rows = lax.dynamic_slice_in_dim(lse_all, offset, shard_len, 2)
        delta_rows = lax.dynamic_slice_in_dim(delta_all, offset, shard_len, 2)
        query_places = lax.dynamic_slice_in_dim(full_places, offset, shard_len, 0)
        prob_b, d_scores = score_grads(
            query_rows, query_places, keys_local, values_local, places, d_rows, lse_rows, delta_rows
        )
        d_keys = (
            d_keys
            + jnp.einsum(
                "bhqk,bqhd->bkhd", d_scores, query_rows, preferred_element_type=jnp.float32
            )
            * score_scale
        )
        d_values = d_values + jnp.einsum(
            "bhqk,bqhd->bkhd", prob_b, d_rows, preferred_element_type=jnp.float32
        )
        return ((d_keys, d_values), None)

    (d_keys_local, d_values_local), unused = lax.scan(
        owner_step,
        (jnp.zeros(head_shape, jnp.float32), jnp.zeros(head_shape, jnp.float32)),
        block_range,
    )
    unused, rope_pull = jax.vjp(
        lambda rows_in: rotate(rows_in, cosines, sine_rows), qkv_merged[:, :, 0]
    )
    d_query_pre = rope_pull(d_query)[0]
    d_key_pre = rope_pull(d_keys_local)[0]
    d_qkv_merged = (
        jnp.stack([d_query_pre, d_key_pre, d_values_local], axis=2)
        .reshape(tok_count, 3 * model_width)
        .astype(jnp.bfloat16)
    )
    d_qkv = first_t(normed_b, d_qkv_merged)
    d_normed = second_t(d_qkv_merged, wqkv_all)
    unused, first_pull = jax.vjp(rms_norm, inputs_f, gain_attn_f)
    d_inputs, d_gain_attn = first_pull(d_normed)
    grad_input = (d_attended + d_inputs).reshape(end_shape)
    dense_sums = (
        lax.psum_scatter(d_gain_attn, ("ctx", "exp", "fsdp"), scatter_dimension=0, tiled=True),
        lax.psum_scatter(d_qkv, ("ctx", "exp", "fsdp"), scatter_dimension=0, tiled=True),
        lax.psum_scatter(d_out_proj, ("ctx", "exp", "fsdp"), scatter_dimension=0, tiled=True),
        lax.psum_scatter(d_router, ("ctx", "exp", "fsdp"), scatter_dimension=0, tiled=True),
        lax.psum_scatter(d_gain_ffn, ("ctx", "exp", "fsdp"), scatter_dimension=0, tiled=True),
        lax.psum_scatter(d_shared_in, ("ctx", "exp", "fsdp"), scatter_dimension=0, tiled=True),
        lax.psum_scatter(d_shared_down, ("ctx", "exp", "fsdp"), scatter_dimension=0, tiled=True),
    )
    expert_sums = (
        lax.psum_scatter(
            d_experts_in.astype(jnp.bfloat16), ("ctx", "fsdp"), scatter_dimension=1, tiled=True
        ).astype(jnp.float32),
        lax.psum_scatter(
            d_experts_out.astype(jnp.bfloat16), ("ctx", "fsdp"), scatter_dimension=1, tiled=True
        ).astype(jnp.float32),
    )
    return (
        layer_out,
        grad_input,
        dense_sums[0],
        dense_sums[1],
        dense_sums[2],
        dense_sums[3],
        dense_sums[4],
        dense_sums[5],
        dense_sums[6],
        expert_sums[0],
        expert_sums[1],
    )


F32 = jnp.float32
BF = jnp.bfloat16
MESH = pl.DeviceIdType.MESH
ROWS = 24
VMEM_BYTES = 60 * 1024 * 1024


def place():
    return lax.axis_index("ctx"), lax.axis_index("exp"), lax.axis_index("fsdp")


def wrap(value, size):
    return lax.rem(value, size)


def mm(left, right):
    return lax.dot_general(
        left, right, (((1,), (0,)), ((), ())), preferred_element_type=F32
    )


def mm_nt(left, right):
    return lax.dot_general(
        left, right, (((1,), (1,)), ((), ())), preferred_element_type=F32
    )


def mm_tn(left, right):
    return lax.dot_general(
        left, right, (((0,), (0,)), ((), ())), preferred_element_type=F32
    )


def greet(peers):
    barrier = pltpu.get_barrier_semaphore()
    for peer in peers:
        pl.semaphore_signal(barrier, inc=1, device_id=peer, device_id_type=MESH)
    pl.semaphore_wait(barrier, len(peers))


class Courier:
    def __init__(self, send, recv):
        self.send, self.recv, self.count, self.sent = send, recv, 0, []

    def push(self, src, dst, device):
        index = self.count
        self.count += 1
        copy = pltpu.make_async_remote_copy(
            src_ref=src,
            dst_ref=dst,
            send_sem=self.send.at[index],
            recv_sem=self.recv.at[index],
            device_id=device,
            device_id_type=MESH,
        )
        copy.start()
        self.sent.append(copy)
        return copy

    def finish(self):
        for copy in self.sent:
            copy.wait_send()


def swap_halves(rows):
    width = rows.shape[1]
    lane = lax.broadcasted_iota(jnp.int32, rows.shape, 1)
    ahead = pltpu.roll(rows, width - HS // 2, 1)
    behind = pltpu.roll(rows, HS // 2, 1)
    return jnp.where((lane & (HS - 1)) < HS // 2, -ahead, behind)


def wide(table, times):
    return jnp.concatenate([table] * times, axis=1)


def position_of(index, half_len, full_len):
    block = index // (2 * half_len)
    inside = index & (2 * half_len - 1)
    low = block * half_len + (inside & (half_len - 1))
    return jnp.where(inside >= half_len, full_len - 1 - low, low)


def allowed_keys(length, half_len, full_len):
    shape = (full_len, full_len)
    query_at = position_of(lax.broadcasted_iota(jnp.int32, shape, 0), half_len, full_len)
    key_at = position_of(lax.broadcasted_iota(jnp.int32, shape, 1), half_len, full_len)
    return (key_at <= query_at) & (key_at < length)


def head_probs(query, key, allowed):
    scores = jnp.where(allowed, mm_nt(query, key) * (HS**-0.5), masked_out)
    weights = jnp.exp(scores - jnp.max(scores, axis=1, keepdims=True))
    return weights * (1.0 / jnp.sum(weights, axis=1, keepdims=True))


def column_row(tail, lane):
    pick = (lax.broadcasted_iota(jnp.int32, (8, 128), 1) == lane).astype(BF)
    return mm_nt(pick, tail)[0:1]


def local_copy(src, dst, sem):
    return pltpu.make_async_copy(src, dst, sem)


def plane_peers(c, z, f, nc):
    return [(wrap(c + s, nc), z, f) for s in range(1, nc)]


def column_peers(c, z, f, nz):
    return [(c, wrap(z + s, nz), f) for s in range(1, nz)]


def attention_forward(
    nc, nz, len_ref, hid_ref, wq_ref, gu_ref, wo_ref, sd_ref, win_ref, wout_ref, cos_ref, sin_ref,
    att_ref, normed_ref, qkv_ref, ctx_ref, w_ref, wo_all, gu_all, sd_all, wie_ref, woe_ref,
    hid_all, wq_st, wq_buf, gu_st, gu_buf, wo_buf, part, part_own, rs_in,
    send, recv, esend, erecv, lsem,
):
    c, z, f = place()
    in_plane = plane_peers(c, z, f, nc)
    in_column = column_peers(c, z, f, nz)
    sibling = (c, z, 1 - f)
    across = [(wrap(c + s, nc), z, 1 - f) for s in range(1, nc)]
    greet(in_plane + in_column + [sibling] + across)
    mail = Courier(send, recv)
    num_seqs, shard_len, width = hid_ref.shape
    full_len = nc * shard_len
    half_len = shard_len // 2
    down_rows = sd_ref.shape[0]

    staged_wq = [
        mail.push(wq_ref.at[wrap(c + s, nc)], wq_st.at[c], in_plane[s - 1]) for s in range(1, nc)
    ]
    arriving = [
        [mail.push(hid_ref.at[q], hid_all.at[q, c], peer) for peer in in_plane]
        for q in range(num_seqs)
    ]
    staged_gu = [
        mail.push(gu_ref.at[wrap(c + s, nc)], gu_st.at[c], in_plane[s - 1]) for s in range(1, nc)
    ]
    wq_st[c] = wq_ref[c]
    gu_st[c] = gu_ref[c]
    wo_buf[z, f] = wo_ref[...]
    own_down = pl.ds(pl.multiple_of((z * 2 + f) * down_rows, down_rows), down_rows)
    sd_all[own_down] = sd_ref[...]
    for q in range(num_seqs):
        hid_all[q, c] = hid_ref[q]

    for copy in staged_wq:
        copy.wait_recv()
    column_wq = [mail.push(wq_st, wq_buf.at[:, z, f], peer) for peer in in_column]
    column_wo = [mail.push(wo_ref, wo_buf.at[z, f], peer) for peer in in_column]
    sibling_wq = [mail.push(wq_st, wq_buf.at[:, z, f], sibling)]
    sibling_wo = [mail.push(wo_ref, wo_buf.at[z, f], sibling)]
    for i in range(nc):
        wq_buf[i, z, f] = wq_st[i]

    for copy in staged_gu:
        copy.wait_recv()
    column_gu = [mail.push(gu_st, gu_buf.at[:, z, f], peer) for peer in in_column]
    column_sd = [mail.push(sd_ref, sd_all.at[own_down], peer) for peer in in_column]
    sibling_late = [
        mail.push(gu_st, gu_buf.at[:, z, f], sibling),
        mail.push(sd_ref, sd_all.at[own_down], sibling),
    ]
    for i in range(nc):
        gu_buf[i, z, f] = gu_st[i]

    block = 2 * c + f
    shard_rows, units = win_ref.shape[1], win_ref.shape[2] // 2
    half_units = units // 2
    lands = pl.ds(pl.multiple_of(block * shard_rows, shard_rows), shard_rows)
    expert_in = []
    own_in = []
    for s in range(nc):
        owner = wrap(c + s, nc)
        for g in range(2):
            core = f if g == 0 else 1 - f
            for side in range(2):
                from_lane = pl.multiple_of(side * units + core * half_units, half_units)
                src = win_ref.at[owner, :, pl.ds(from_lane, half_units)]
                dst = wie_ref.at[lands, pl.ds(side * half_units, half_units)]
                if s == 0 and g == 0:
                    own_in.append(local_copy(src, dst, lsem.at[side]))
                    own_in[-1].start()
                else:
                    expert_in.append(mail.push(src, dst, (owner, z, core)))
    out_rows = wout_ref.shape[1]
    to_core = block // nc
    slot = wrap(block, nc)
    out_lands = pl.ds(pl.multiple_of(slot * out_rows, out_rows), out_rows)

    def out_copy(s, device, to_slot, lands_at):
        return pltpu.make_async_remote_copy(
            src_ref=wout_ref.at[wrap(c + s, nc)],
            dst_ref=woe_ref.at[lands_at],
            send_sem=esend.at[s],
            recv_sem=erecv.at[to_slot],
            device_id=device,
            device_id_type=MESH,
        )

    for s in range(1, nc):
        out_copy(s, (wrap(c + s, nc), z, to_core), slot, out_lands).start()
    own_out = local_copy(wout_ref.at[c], woe_ref.at[out_lands], lsem.at[2])

    @pl.when(to_core == f)
    def _():
        own_out.start()

    @pl.when(to_core != f)
    def _():
        out_copy(0, sibling, slot, out_lands).start()

    for s in range(1, nz):
        origin = wrap(z + nz - s, nz)
        column_wq[s - 1].wait_recv()
        sibling_wq.append(mail.push(wq_buf.at[:, origin, f], wq_buf.at[:, origin, f], sibling))
    for s in range(1, nz):
        origin = wrap(z + nz - s, nz)
        column_wo[s - 1].wait_recv()
        sibling_wo.append(mail.push(wo_buf.at[origin, f], wo_buf.at[origin, f], sibling))
    for copy in sibling_wq:
        copy.wait_recv()
    for i in range(nc):
        rows = nz * 2 * wq_ref.shape[1]
        w_ref[i * rows : (i + 1) * rows, :] = (
            wq_buf[i].astype(F32).reshape(rows, wq_ref.shape[2]).astype(BF)
        )
    for copy in sibling_wo:
        copy.wait_recv()
    wo_all[...] = wo_buf[...].astype(F32).reshape(wo_all.shape).astype(BF)

    head_width = wo_all.shape[0]
    cosines = wide(cos_ref[...], 2 * head_width // 128)
    sines = wide(sin_ref[...], 2 * head_width // 128)
    gain_row = column_row(w_ref[:, 512:640], 80)
    parting = []
    for q in range(num_seqs):
        for copy in arriving[q]:
            copy.wait_recv()
        rows = hid_all[q].reshape(full_len, width).astype(F32)
        normed = (
            rows * lax.rsqrt(jnp.mean(rows * rows, axis=1, keepdims=True) + epsilon) * gain_row
        ).astype(BF)
        normed_ref[q] = normed
        merged = mm(normed, w_ref[:, : 3 * head_width])
        both = merged[:, : 2 * head_width]
        both = (both * cosines + swap_halves(both) * sines).astype(BF)
        values = merged[:, 2 * head_width :].astype(BF)
        qkv_ref[q, :, : 2 * head_width] = both
        qkv_ref[q, :, 2 * head_width :] = values
        allowed = allowed_keys(len_ref[q], half_len, full_len)
        heads = []
        for h in range(head_width // HS):
            probs = head_probs(
                both[:, h * HS : (h + 1) * HS],
                both[:, head_width + h * HS : head_width + (h + 1) * HS],
                allowed,
            ).astype(BF)
            heads.append(mm(probs, values[:, h * HS : (h + 1) * HS]))
        context = jnp.concatenate(heads, axis=1).astype(BF)
        ctx_ref[q] = context
        product = mm(context, wo_all[...]).reshape(nc, shard_len, width)
        part_own[q] = product
        part[q] = product.astype(BF)
        parting.append(
            [
                mail.push(part.at[q, wrap(c + s, nc)], rs_in.at[s - 1, q], in_plane[s - 1])
                for s in range(1, nc)
            ]
        )
    for s in range(1, nz):
        origin = wrap(z + nz - s, nz)
        column_gu[s - 1].wait_recv()
        column_sd[s - 1].wait_recv()
        from_rows = pl.ds(pl.multiple_of((origin * 2 + f) * down_rows, down_rows), down_rows)
        sibling_late.append(mail.push(gu_buf.at[:, origin, f], gu_buf.at[:, origin, f], sibling))
        sibling_late.append(mail.push(sd_all.at[from_rows], sd_all.at[from_rows], sibling))
    for q in range(num_seqs):
        total = hid_ref[q].astype(F32) + part_own[q, c]
        for s in range(1, nc):
            parting[q][s - 1].wait_recv()
            total = total + rs_in[s - 1, q].astype(F32)
        att_ref[q] = total
    for copy in sibling_late:
        copy.wait_recv()
    for i in range(nc):
        rows = nz * 2 * gu_ref.shape[1]
        gu_all[i * rows : (i + 1) * rows, :] = (
            gu_buf[i].astype(F32).reshape(rows, gu_ref.shape[2]).astype(BF)
        )
    for copy in own_in:
        copy.wait()
    for copy in expert_in:
        copy.wait_recv()
    for at in range(nc):
        origin_block = f * nc + at

        @pl.when(origin_block != block)
        def _(at=at):
            out_copy(0, sibling, at, pl.ds(at * out_rows, out_rows)).wait_recv()

    @pl.when(to_core == f)
    def _():
        own_out.wait()

    @pl.when(to_core != f)
    def _():
        out_copy(0, sibling, slot, out_lands).wait_send()

    for s in range(1, nc):
        out_copy(s, (wrap(c + s, nc), z, to_core), slot, out_lands).wait_send()
    mail.finish()


def ffn_pass(rows_ref, grads_ref, in_ref, out_ref, hidden_ref, dm_ref, result, back, units, step):
    result[...] = jnp.zeros_like(result)
    back[...] = jnp.zeros_like(back)

    def body(j, carry):
        low = pl.multiple_of(j * step, step)
        gate_at, up_at = pl.ds(low, step), pl.ds(pl.multiple_of(units + low, step), step)
        rows, grads = rows_ref[...], grads_ref[...]
        gate, up = mm(rows, in_ref[:, gate_at]), mm(rows, in_ref[:, up_at])
        down = out_ref[gate_at, :]
        d_hidden = mm_nt(grads, down)
        share = 1.0 / (1.0 + jnp.exp(-gate))
        lit = gate * share
        hidden = (lit * up).astype(BF)
        d_gate = (d_hidden * up * (share * (1.0 + gate * (1.0 - share)))).astype(BF)
        d_up = (d_hidden * lit).astype(BF)
        hidden_ref[:, gate_at] = hidden
        dm_ref[:, gate_at] = d_gate
        dm_ref[:, up_at] = d_up
        result[...] += mm(hidden, down)
        back[...] += mm_nt(d_gate, in_ref[:, gate_at]) + mm_nt(d_up, in_ref[:, up_at])
        return carry

    lax.fori_loop(0, units // step, body, 0)


def split_dot(dot, left, right, left_wide=True):
    whole = left if left_wide else right
    high = whole.astype(BF)
    low = (whole - high.astype(F32)).astype(BF)
    if left_wide:
        return dot(high, right) + dot(low, right)
    return dot(left, high) + dot(left, low)


def middle(
    nc, nz, att_ref, go_ref, rt_ref, w_ref, gu_ref, sd_ref, wie_ref, woe_ref,
    out_ref, datt_ref, ggu_ref, gsd_ref, gex_ref, gwi_ref, gwo_ref,
    up_own, up_all, nt_all, sb, ar, xs, ds, rs_shared, sh_hidden, sh_dm, sh_out, sh_back, sh_send,
    ex_hidden, ex_dm, ex_out, ex_back, pr, pin, fb, rb, send, recv,
):
    c, z, f = place()
    in_plane = plane_peers(c, z, f, nc)
    sibling = (c, z, 1 - f)
    ring = [(dz, dc) for dz in range(nz) for dc in range(nc) if dz or dc]

    def peer(dz, dc):
        return (wrap(c + dc, nc), wrap(z + dz, nz), f)

    greet([peer(*step) for step in ring] + [sibling])
    mail = Courier(send, recv)
    tok, width = att_ref.shape

    table = rt_ref[...]
    live = table[:, 4:5]
    upstream = go_ref[...].astype(F32) * live
    up_b = upstream.astype(BF)
    up_f = up_b.astype(F32)
    up_own[...] = up_b
    up_all[c] = up_b
    up_copies = [mail.push(up_own, up_all.at[c], p) for p in in_plane]
    tail = w_ref[:, 512:640]
    gain_row = column_row(tail, 81)
    attended = att_ref[...]
    inverse = lax.rsqrt(jnp.mean(attended * attended, axis=1, keepdims=True) + epsilon)
    normed = (attended * inverse * gain_row).astype(BF)
    nt_all[c] = normed

    lane = lax.broadcasted_iota(jnp.int32, (tok, 128), 1).astype(F32)
    logits = mm(normed, tail)
    hots = [(lane == 64.0 + table[:, 2 + k : 3 + k]).astype(F32) for k in range(2)]
    chosen = [jnp.sum(hot * logits, axis=1, keepdims=True) for hot in hots]
    top = jnp.maximum(chosen[0], chosen[1])
    raised = [jnp.exp(value - top) for value in chosen]
    total = raised[0] + raised[1]
    gates = [value / total for value in raised]
    num_slots = nz * nc * ROWS
    slot_lane = lax.broadcasted_iota(jnp.int32, (tok, num_slots), 1).astype(F32)
    dispatch = [(slot_lane == table[:, k : k + 1]).astype(BF) for k in range(2)]
    anyone = dispatch[0] + dispatch[1]
    weighted = [(gates[k] * up_f).astype(BF) for k in range(2)]
    rows_out = mm_tn(anyone, normed).astype(BF)
    grads_out = (mm_tn(dispatch[0], weighted[0]) + mm_tn(dispatch[1], weighted[1])).astype(BF)
    num_experts = nz * nc
    sb[:, 0] = rows_out.astype(F32).reshape(num_experts, ROWS, width).astype(BF)
    sb[:, 1] = grads_out.astype(F32).reshape(num_experts, ROWS, width).astype(BF)
    row_copies = []
    for dz, dc in ring:
        to = peer(dz, dc)
        row_copies.append(mail.push(sb.at[to[1] * nc + to[0]], ar.at[f, z, c], to))
    nt_copies = [mail.push(nt_all.at[c], nt_all.at[c], p) for p in in_plane]
    ar[f, z, c] = sb[z * nc + c]
    forwards = [mail.push(sb.at[z * nc + c], ar.at[f, z, c], sibling)]
    for copy, (dz, dc) in zip(row_copies, ring):
        copy.wait_recv()
        oz, oc = wrap(z + nz - dz, nz), wrap(c + nc - dc, nc)
        forwards.append(mail.push(ar.at[f, oz, oc], ar.at[f, oz, oc], sibling))

    for copy in up_copies + nt_copies:
        copy.wait_recv()
    rows_ref = nt_all.reshape(nc * tok, width)
    grads_ref = up_all.reshape(nc * tok, width)
    units = sd_ref.shape[0]
    ffn_pass(rows_ref, grads_ref, gu_ref, sd_ref, sh_hidden, sh_dm, sh_out, sh_back, units, 256)
    sh_send[0] = sh_out[...].astype(BF).reshape(nc, tok, width)
    sh_send[1] = sh_back[...].astype(BF).reshape(nc, tok, width)
    shared_copies = [
        mail.push(sh_send.at[:, wrap(c + s, nc)], rs_shared.at[s - 1], in_plane[s - 1])
        for s in range(1, nc)
    ]

    for copy in forwards:
        copy.wait_recv()
    half = nz * nc * ROWS
    for core in range(2):
        xs[core * half : (core + 1) * half] = (
            ar[core, :, :, 0].astype(F32).reshape(half, width).astype(BF)
        )
        ds[core * half : (core + 1) * half] = (
            ar[core, :, :, 1].astype(F32).reshape(half, width).astype(BF)
        )
    half_units = woe_ref.shape[0]
    ffn_pass(xs, ds, wie_ref, woe_ref, ex_hidden, ex_dm, ex_out, ex_back, half_units, 256)
    theirs = pl.ds(pl.multiple_of((1 - f) * half, half), half)
    ours = pl.ds(pl.multiple_of(f * half, half), half)
    pr[:, 0] = ex_out[theirs].reshape(num_experts, ROWS, width).astype(BF)
    pr[:, 1] = ex_back[theirs].reshape(num_experts, ROWS, width).astype(BF)
    swap = mail.push(pr, pin, sibling)
    swap.wait_recv()
    fb[:, 0] = (
        ex_out[ours].reshape(num_experts, ROWS, width) + pin[:, 0].astype(F32)
    ).astype(BF)
    fb[:, 1] = (
        ex_back[ours].reshape(num_experts, ROWS, width) + pin[:, 1].astype(F32)
    ).astype(BF)
    returns = []
    for dz, dc in ring:
        to = peer(dz, dc)
        returns.append(mail.push(fb.at[to[1] * nc + to[0]], rb.at[z * nc + c], to))
    rb[z * nc + c] = fb[z * nc + c]

    def shared_grads(j, carry):
        at = pl.ds(pl.multiple_of(j * 256, 256), 256)
        piece = mm_tn(rows_ref[...], sh_dm[:, at])
        ggu_ref[:, :, :, :, at] = piece.reshape(ggu_ref.shape[:4] + (256,)).astype(BF)
        return carry

    lax.fori_loop(0, 2 * units // 256, shared_grads, 0)
    gsd_ref[...] = mm_tn(sh_hidden[...], grads_ref[...]).reshape(gsd_ref.shape).astype(BF)

    def expert_grads(j, carry):
        at = pl.ds(pl.multiple_of(j * 256, 256), 256)
        gwi_ref[:, at] = mm_tn(xs[...], ex_dm[:, at]).astype(BF)
        return carry

    lax.fori_loop(0, 2 * half_units // 256, expert_grads, 0)

    def down_grads(j, carry):
        at = pl.ds(pl.multiple_of(j * 256, 256), 256)
        gwo_ref[at, :] = mm_tn(ex_hidden[:, at], ds[...]).astype(BF)
        return carry

    lax.fori_loop(0, half_units // 256, down_grads, 0)

    mine = pl.ds(pl.multiple_of(c * tok, tok), tok)
    shared = sh_out[mine]
    d_normed = sh_back[mine]
    for s in range(1, nc):
        shared_copies[s - 1].wait_recv()
        shared = shared + rs_shared[s - 1, 0].astype(F32)
        d_normed = d_normed + rs_shared[s - 1, 1].astype(F32)
    for copy in returns:
        copy.wait_recv()
    results = rb[:, 0].astype(F32).reshape(num_slots, width).astype(BF)
    d_rows = rb[:, 1].astype(F32).reshape(num_slots, width).astype(BF)
    routed = [mm(dispatch[k], results) for k in range(2)]
    mixture = gates[0] * routed[0] + gates[1] * routed[1]
    out_ref[...] = (live * (attended + mixture + shared)).astype(BF)
    d_gates = [jnp.sum(routed[k] * up_f, axis=1, keepdims=True) for k in range(2)]
    mean_gate = gates[0] * d_gates[0] + gates[1] * d_gates[1]
    d_logits = hots[0] * (gates[0] * (d_gates[0] - mean_gate)) + hots[1] * (
        gates[1] * (d_gates[1] - mean_gate)
    )
    d_normed = d_normed + mm(anyone, d_rows) + split_dot(mm_nt, d_logits, tail)
    d_router = split_dot(mm_tn, normed, d_logits, left_wide=False)
    scaled = d_normed * gain_row
    d_attended = (
        upstream
        + inverse * scaled
        - attended * (inverse * inverse * inverse)
        * jnp.mean(attended * scaled, axis=1, keepdims=True)
    )
    datt_ref[...] = d_attended
    d_gain = jnp.sum(d_normed * attended * inverse, axis=0, keepdims=True)
    turned = jnp.transpose(jnp.broadcast_to(d_gain, (128, width)), (1, 0))
    extra_lane = lax.broadcasted_iota(jnp.int32, (width, 128), 1)
    gex_ref[...] = jnp.where(extra_lane == 80, turned, d_router).reshape(gex_ref.shape)
    mail.finish()


def attention_backward(
    nc, nz, len_ref, datt_ref, hid_ref, normed_ref, qkv_ref, w_ref, wo_ref, ctx_ref, cos_ref,
    sin_ref, gex_ref, ggu_ref, gsd_ref, gwi_ref, gwo_ref,
    gin_ref, fq_ref, fgu_ref, fsd_ref, fwo_ref, fex_ref, ein_ref, eout_ref,
    da_own, da_all, part, part_own, rs_in, gq, gwo_at,
    sib_gu, zb_gu, zi_gu, pb_gu, sib_q, zb_q, zi_q, pb_q, sib_ex, zb_ex, zi_ex, pb_ex, in_ex,
    sib_sd, zb_sd, zi_sd, sib_wo, zb_wo, zi_wo,
    send, recv, esend, erecv, lsem,
):
    c, z, f = place()
    in_plane = plane_peers(c, z, f, nc)
    in_column = column_peers(c, z, f, nz)
    sibling = (c, z, 1 - f)
    across = [(wrap(c + s, nc), z, 1 - f) for s in range(1, nc)]
    greet(in_plane + in_column + [sibling] + across)
    mail = Courier(send, recv)
    num_seqs, shard_len, width = datt_ref.shape
    full_len = nc * shard_len
    half_len = shard_len // 2
    head_width = wo_ref.shape[0]

    da_own[...] = datt_ref[...].astype(BF)
    arriving = []
    for q in range(num_seqs):
        arriving.append([mail.push(da_own.at[q], da_all.at[q, c], p) for p in in_plane])
        da_all[q, c] = da_own[q]
    sibling_gu = mail.push(ggu_ref.at[:, :, 1 - f], sib_gu, sibling)
    sibling_ex = mail.push(gex_ref.at[:, :, 1 - f], sib_ex, sibling)
    sibling_sd = mail.push(gsd_ref.at[:, 1 - f], sib_sd, sibling)

    block = 2 * c + f
    shard_rows, units = ein_ref.shape[1], ein_ref.shape[2] // 2
    half_units = units // 2
    expert_in, own_in = [], []
    for s in range(nc):
        owner = wrap(c + s, nc)
        for g in range(2):
            core = f if g == 0 else 1 - f
            from_rows = pl.ds(
                pl.multiple_of((2 * owner + core) * shard_rows, shard_rows), shard_rows
            )
            for side in range(2):
                to_lane = pl.multiple_of(side * units + f * half_units, half_units)
                src = gwi_ref.at[from_rows, pl.ds(side * half_units, half_units)]
                dst = ein_ref.at[c, :, pl.ds(to_lane, half_units)]
                if s == 0 and g == 0:
                    own_in.append(local_copy(src, dst, lsem.at[side]))
                    own_in[-1].start()
                else:
                    expert_in.append(mail.push(src, dst, (owner, z, core)))
    out_rows = eout_ref.shape[1]
    from_core = block // nc

    def out_copy(j, arrives):
        to_block = f * nc + j
        return pltpu.make_async_remote_copy(
            src_ref=gwo_ref.at[pl.ds(j * out_rows, out_rows)],
            dst_ref=eout_ref.at[arrives],
            send_sem=esend.at[j],
            recv_sem=erecv.at[arrives],
            device_id=(to_block // 2, z, wrap(to_block, 2)),
            device_id_type=MESH,
        )

    def own_out(j):
        return local_copy(
            gwo_ref.at[pl.ds(j * out_rows, out_rows)], eout_ref.at[c], lsem.at[2]
        )

    for j in range(nc):

        @pl.when(f * nc + j == block)
        def _(j=j):
            own_out(j).start()

        @pl.when(f * nc + j != block)
        def _(j=j):
            out_copy(j, c).start()

    sibling_gu.wait_recv()
    for i in range(nc):
        zb_gu[i] = (ggu_ref[i, :, f].astype(F32) + sib_gu[i].astype(F32)).astype(BF)
    gu_copies = [
        mail.push(zb_gu.at[:, wrap(z + s, nz)], zi_gu.at[s - 1], in_column[s - 1])
        for s in range(1, nz)
    ]
    sibling_ex.wait_recv()
    for i in range(nc):
        zb_ex[i] = gex_ref[i, :, f] + sib_ex[i]
    ex_copies = [
        mail.push(zb_ex.at[:, wrap(z + s, nz)], zi_ex.at[s - 1], in_column[s - 1])
        for s in range(1, nz)
    ]
    sibling_sd.wait_recv()
    zb_sd[...] = (gsd_ref[:, f].astype(F32) + sib_sd[...].astype(F32)).astype(BF)
    sd_copies = [
        mail.push(zb_sd.at[wrap(z + s, nz)], zi_sd.at[s - 1], in_column[s - 1])
        for s in range(1, nz)
    ]

    cosines = wide(cos_ref[...], 2 * head_width // 128)
    sines = wide(sin_ref[...], 2 * head_width // 128)
    grad_qkv = jnp.zeros((width, 3 * head_width), F32)
    grad_out = jnp.zeros((head_width, width), F32)
    parting = []
    for q in range(num_seqs):
        for copy in arriving[q]:
            copy.wait_recv()
        d_rows = da_all[q].reshape(full_len, width)
        d_context = mm_nt(d_rows, wo_ref[...]).astype(BF)
        grad_out = grad_out + mm_tn(ctx_ref[q], d_rows)
        allowed = allowed_keys(len_ref[q], half_len, full_len)
        merged = qkv_ref[q]
        d_query, d_key, d_value = [], [], []
        for h in range(head_width // HS):
            query = merged[:, h * HS : (h + 1) * HS]
            key = merged[:, head_width + h * HS : head_width + (h + 1) * HS]
            value = merged[:, 2 * head_width + h * HS : 2 * head_width + (h + 1) * HS]
            d_head = d_context[:, h * HS : (h + 1) * HS]
            probs = head_probs(query, key, allowed)
            d_probs = mm_nt(d_head, value)
            delta = jnp.sum(probs * d_probs, axis=1, keepdims=True)
            d_scores = (probs * (d_probs - delta)).astype(BF)
            d_query.append(mm(d_scores, key) * (HS**-0.5))
            d_key.append(mm_tn(d_scores, query) * (HS**-0.5))
            d_value.append(mm_tn(probs.astype(BF), d_head))
        both = jnp.concatenate(d_query + d_key, axis=1)
        both = both * cosines - swap_halves(both) * sines
        d_merged = jnp.concatenate([both] + d_value, axis=1).astype(BF)
        product = mm_nt(d_merged, w_ref[:, : 3 * head_width]).reshape(nc, shard_len, width)
        part_own[q] = product
        part[q] = product.astype(BF)
        parting.append(
            [
                mail.push(part.at[q, wrap(c + s, nc)], rs_in.at[s - 1, q], in_plane[s - 1])
                for s in range(1, nc)
            ]
        )
        grad_qkv = grad_qkv + mm_tn(normed_ref[q], d_merged)
    gq[...] = grad_qkv.reshape(gq.shape).astype(BF)
    sibling_q = mail.push(gq.at[:, :, 1 - f], sib_q, sibling)
    gwo_at[...] = grad_out.reshape(gwo_at.shape).astype(BF)
    sibling_wo = mail.push(gwo_at.at[:, 1 - f], sib_wo, sibling)

    sibling_q.wait_recv()
    for i in range(nc):
        zb_q[i] = (gq[i, :, f].astype(F32) + sib_q[i].astype(F32)).astype(BF)
    q_copies = [
        mail.push(zb_q.at[:, wrap(z + s, nz)], zi_q.at[s - 1], in_column[s - 1])
        for s in range(1, nz)
    ]
    sibling_wo.wait_recv()
    zb_wo[...] = (gwo_at[:, f].astype(F32) + sib_wo[...].astype(F32)).astype(BF)
    wo_copies = [
        mail.push(zb_wo.at[wrap(z + s, nz)], zi_wo.at[s - 1], in_column[s - 1])
        for s in range(1, nz)
    ]

    def column_sum(own, copies, inbox):
        total = own.astype(F32)
        for s in range(1, nz):
            copies[s - 1].wait_recv()
            total = total + inbox[s - 1].astype(F32)
        return total

    def hand_out(box, final):
        final[c] = box[c]
        return [
            mail.push(box.at[wrap(c + s, nc)], final.at[c], in_plane[s - 1])
            for s in range(1, nc)
        ]

    pb_gu[...] = column_sum(zb_gu[:, z], gu_copies, zi_gu).astype(BF)
    final_gu = hand_out(pb_gu, fgu_ref)
    pb_ex[...] = column_sum(zb_ex[:, z], ex_copies, zi_ex)
    final_ex = hand_out(pb_ex, in_ex)
    fsd_ref[...] = column_sum(zb_sd[z], sd_copies, zi_sd)
    for q in range(num_seqs):
        d_normed = part_own[q, c]
        for s in range(1, nc):
            parting[q][s - 1].wait_recv()
            d_normed = d_normed + rs_in[s - 1, q].astype(F32)
        gain_row = column_row(w_ref[:, 512:640], 80)
        rows = hid_ref[q].astype(F32)
        inverse = lax.rsqrt(jnp.mean(rows * rows, axis=1, keepdims=True) + epsilon)
        scaled = d_normed * gain_row
        gin_ref[q] = (
            datt_ref[q]
            + inverse * scaled
            - rows * (inverse * inverse * inverse)
            * jnp.mean(rows * scaled, axis=1, keepdims=True)
        )
    fwo_ref[...] = column_sum(zb_wo[z], wo_copies, zi_wo)
    pb_q[...] = column_sum(zb_q[:, z], q_copies, zi_q).astype(BF)
    final_q = hand_out(pb_q, fq_ref)
    for copy in final_ex:
        copy.wait_recv()
    fex_ref[...] = jnp.sum(in_ex[...], axis=0)
    for copy in final_gu + final_q:
        copy.wait_recv()

    for copy in own_in:
        copy.wait()
    for copy in expert_in:
        copy.wait_recv()
    for arrives in range(nc):

        @pl.when((arrives != c) | (from_core != f))
        def _(arrives=arrives):
            out_copy(0, arrives).wait_recv()

    for j in range(nc):

        @pl.when(f * nc + j == block)
        def _(j=j):
            own_out(j).wait()

        @pl.when(f * nc + j != block)
        def _(j=j):
            out_copy(j, c).wait_send()

    mail.finish()


def vmem(*shape, dtype=jnp.bfloat16):
    return pltpu.VMEM(shape, dtype)


def run(kernel, args, outs, scratch, copies, collective, spaces_in, spaces_out, flops, name):
    dma = pltpu.SemaphoreType.DMA
    return pl.pallas_call(
        kernel,
        out_shape=[jax.ShapeDtypeStruct(shape, dtype) for shape, dtype in outs],
        in_specs=[pl.BlockSpec(memory_space=space) for space in spaces_in],
        out_specs=[pl.BlockSpec(memory_space=space) for space in spaces_out],
        scratch_shapes=list(scratch) + copies,
        compiler_params=pltpu.CompilerParams(
            collective_id=collective, has_side_effects=True, vmem_limit_bytes=VMEM_BYTES
        ),
        cost_estimate=pl.CostEstimate(flops=flops, bytes_accessed=20_000_000, transcendentals=0),
        name=name,
    )(*args)


def fast_device(
    hidden_in, seq_lengths, expert_ids, route_rank, gain_attn, w_qkv, w_out, w_router, gain_ffn,
    w_gate_up, w_shared_down, w_experts_in, w_experts_out, grad_output,
):
    nc, nz = lax.axis_size("ctx"), lax.axis_size("exp")
    num_seqs, two_ends, half_len, width = hidden_in.shape
    shard_len = 2 * half_len
    full_len = nc * shard_len
    tok = num_seqs * shard_len
    rows_w = w_qkv.shape[0]
    head_width = w_qkv.shape[1] // 3 // nc
    num_experts = w_router.shape[1]
    down_rows = w_shared_down.shape[0]
    units = w_gate_up.shape[1] // 2
    own_units = units // nc
    half_units = w_experts_in.shape[2] // 4
    in_rows, out_rows = w_experts_in.shape[1], w_experts_out.shape[1]
    hbm, vm, sm = pl.ANY, pltpu.VMEM, pltpu.SMEM
    dma = pltpu.SemaphoreType.DMA

    wq = w_qkv.reshape(rows_w, 3, nc, head_width).transpose(2, 0, 1, 3)
    wq = wq.reshape(nc, rows_w, 3 * head_width)
    small = jnp.concatenate([w_router, gain_attn[:, None], gain_ffn[:, None]], axis=1)
    small = jnp.pad(small, ((0, 0), (0, 640 - 3 * head_width - small.shape[1])))
    wq = jnp.concatenate([wq, jnp.broadcast_to(small, (nc,) + small.shape)], axis=2)
    gu = w_gate_up.reshape(rows_w, 2, nc, own_units).transpose(2, 0, 1, 3)
    gu = gu.reshape(nc, rows_w, 2 * own_units)

    every = jnp.arange(full_len, dtype=jnp.int32)
    inside = every % shard_len
    low = every // shard_len * half_len + inside % half_len
    cosines, sines = rope_tables(jnp.where(inside >= half_len, full_len - 1 - low, low))
    cosines = jnp.tile(cosines, (1, 4))
    sines = jnp.tile(sines, (1, 4))

    mine = lax.axis_index("ctx") * half_len + jnp.arange(half_len, dtype=jnp.int32)
    places = jnp.concatenate([mine, full_len - 1 - mine])
    live = (places[None, :] < seq_lengths[:, None]).astype(F32).reshape(tok, 1)
    picked = expert_ids.reshape(tok, 2)
    hot = (picked[:, :, None] == jnp.arange(num_experts, dtype=jnp.int32)).astype(F32)
    load = (jnp.sum(hot, axis=1) * live).astype(BF)
    rank = route_rank.reshape(tok)
    earlier = (rank[None, :] < rank[:, None]).astype(BF)
    position = jnp.dot(earlier, load, preferred_element_type=F32)
    at = jnp.sum(hot * position[:, None, :], axis=-1)
    kept = (live > 0) & (at < CAP)
    slots = jnp.where(kept, picked.astype(F32) * ROWS + at, -1.0)
    table = jnp.concatenate([slots, picked.astype(F32), live], axis=1)
    table = jnp.pad(table, ((0, 0), (0, 128 - table.shape[1])))

    hidden = hidden_in.reshape(num_seqs, shard_len, width)
    grads = grad_output.reshape(tok, width)
    blocks = (nc, nz, 2, rows_w)
    wqkv_width = wq.shape[2]
    att, normed, qkv, context, w_all, wo_all, gu_all, sd_all, wie, woe = run(
        functools.partial(attention_forward, nc, nz),
        (seq_lengths, hidden, wq, gu, w_out, w_shared_down, w_experts_in, w_experts_out, cosines, sines),
        [
            ((num_seqs, shard_len, width), F32),
            ((num_seqs, full_len, width), BF),
            ((num_seqs, full_len, 3 * head_width), BF),
            ((num_seqs, full_len, head_width), BF),
            ((width, wqkv_width), BF),
            ((head_width, width), BF),
            ((width, 2 * own_units), BF),
            ((own_units, width), BF),
            ((width, 2 * half_units), BF),
            ((half_units, width), BF),
        ],
        [
            vmem(num_seqs, nc, shard_len, width),
            vmem(nc, rows_w, wqkv_width),
            vmem(*blocks, wqkv_width),
            vmem(nc, rows_w, 2 * own_units),
            vmem(*blocks, 2 * own_units),
            vmem(nz, 2, rows_w, width),
            vmem(num_seqs, nc, shard_len, width),
            vmem(num_seqs, nc, shard_len, width, dtype=F32),
            vmem(nc - 1, num_seqs, shard_len, width),
        ],
        [dma((80,)), dma((80,)), dma((nc,)), dma((nc,)), dma((3,))],
        0,
        [sm] + [vm] * 5 + [hbm, hbm, vm, vm],
        [vm] * 8 + [hbm, hbm],
        1_000_000_000,
        "attention_forward",
    )
    slots_all = num_experts * ROWS
    out, d_att, ggu, gsd, gex, gwi, gwo = run(
        functools.partial(middle, nc, nz),
        (att.reshape(tok, width), grads, table, w_all, gu_all, sd_all, wie, woe),
        [
            ((tok, width), BF),
            ((tok, width), F32),
            ((*blocks, 2 * own_units), BF),
            ((nz, 2, down_rows, width), BF),
            ((*blocks, 128), F32),
            ((width, 2 * half_units), BF),
            ((half_units, width), BF),
        ],
        [
            vmem(tok, width),
            vmem(nc, tok, width),
            vmem(nc, tok, width),
            vmem(num_experts, 2, ROWS, width),
            vmem(2, nz, nc, 2, ROWS, width),
            vmem(2 * slots_all, width),
            vmem(2 * slots_all, width),
            vmem(nc - 1, 2, tok, width),
            vmem(nc * tok, own_units),
            vmem(nc * tok, 2 * own_units),
            vmem(nc * tok, width, dtype=F32),
            vmem(nc * tok, width, dtype=F32),
            vmem(2, nc, tok, width),
            vmem(2 * slots_all, half_units),
            vmem(2 * slots_all, 2 * half_units),
            vmem(2 * slots_all, width, dtype=F32),
            vmem(2 * slots_all, width, dtype=F32),
            vmem(num_experts, 2, ROWS, width),
            vmem(num_experts, 2, ROWS, width),
            vmem(num_experts, 2, ROWS, width),
            vmem(num_experts, 2, ROWS, width),
        ],
        [dma((64,)), dma((64,))],
        1,
        [vm] * 8,
        [vm] * 7,
        13_000_000_000,
        "routed_and_shared",
    )
    grad_in, fq, fgu, fsd, fwo, fex, e_in, e_out = run(
        functools.partial(attention_backward, nc, nz),
        (seq_lengths, d_att.reshape(num_seqs, shard_len, width), hidden, normed, qkv, w_all, wo_all,
         context, cosines, sines, gex, ggu, gsd, gwi, gwo),
        [
            ((num_seqs, shard_len, width), F32),
            ((nc, rows_w, 3 * head_width), BF),
            ((nc, rows_w, 2 * own_units), BF),
            ((down_rows, width), F32),
            ((rows_w, width), F32),
            ((rows_w, 128), F32),
            (w_experts_in.shape, BF),
            (w_experts_out.shape, BF),
        ],
        [
            vmem(num_seqs, shard_len, width),
            vmem(num_seqs, nc, shard_len, width),
            vmem(num_seqs, nc, shard_len, width),
            vmem(num_seqs, nc, shard_len, width, dtype=F32),
            vmem(nc - 1, num_seqs, shard_len, width),
            vmem(*blocks, 3 * head_width),
            vmem(nz, 2, rows_w, width),
            vmem(nc, nz, rows_w, 2 * own_units),
            vmem(nc, nz, rows_w, 2 * own_units),
            vmem(nz - 1, nc, rows_w, 2 * own_units),
            vmem(nc, rows_w, 2 * own_units),
            vmem(nc, nz, rows_w, 3 * head_width),
            vmem(nc, nz, rows_w, 3 * head_width),
            vmem(nz - 1, nc, rows_w, 3 * head_width),
            vmem(nc, rows_w, 3 * head_width),
            vmem(nc, nz, rows_w, 128, dtype=F32),
            vmem(nc, nz, rows_w, 128, dtype=F32),
            vmem(nz - 1, nc, rows_w, 128, dtype=F32),
            vmem(nc, rows_w, 128, dtype=F32),
            vmem(nc, rows_w, 128, dtype=F32),
            vmem(nz, down_rows, width),
            vmem(nz, down_rows, width),
            vmem(nz - 1, down_rows, width),
            vmem(nz, rows_w, width),
            vmem(nz, rows_w, width),
            vmem(nz - 1, rows_w, width),
        ],
        [dma((80,)), dma((80,)), dma((nc,)), dma((nc,)), dma((3,))],
        2,
        [sm] + [vm] * 12 + [hbm, hbm],
        [vm] * 6 + [hbm, hbm],
        2_000_000_000,
        "attention_backward",
    )
    grad_qkv = fq.astype(F32).reshape(nc, rows_w, 3, head_width).transpose(1, 2, 0, 3)
    grad_qkv = grad_qkv.reshape(w_qkv.shape)
    grad_gu = fgu.astype(F32).reshape(nc, rows_w, 2, own_units).transpose(1, 2, 0, 3)
    grad_gain = jnp.sum(w_qkv.astype(F32) * grad_qkv, axis=1) / gain_attn.astype(F32)
    return (
        out.reshape(hidden_in.shape),
        grad_in.reshape(hidden_in.shape),
        grad_gain,
        grad_qkv,
        fwo,
        fex[:, 64 : 64 + num_experts],
        fex[:, 80],
        grad_gu.reshape(w_gate_up.shape),
        fsd,
        e_in.astype(F32),
        e_out.astype(F32),
    )


def fits(mesh, hidden_in, w_qkv, w_router, w_gate_up, w_experts_in):
    nc, nz, nf = mesh.shape["ctx"], mesh.shape["exp"], mesh.shape["fsdp"]
    heads = w_qkv.shape[1] // 3 // HS
    return (
        nf == 2
        and nc % 2 == 0
        and heads % nc == 0
        and w_router.shape[1] == nc * nz
        and (heads // nc * HS * 2) % 128 == 0
        and 3 * heads // nc * HS == 576
        and w_router.shape[1] == 16
        and hidden_in.shape[2] // nc == 32
        and hidden_in.shape[0] == 2 * nz * nf
        and hidden_in.shape[3] == 768
        and CAP <= ROWS
    )


def solution(mesh):
    def whole(*args):
        chosen = fast_device if fits(mesh, args[0], args[5], args[7], args[9], args[11]) else per_device
        return placed(mesh, chosen)(*args)

    return whole


def placed(mesh, chosen):
    return jax.shard_map(
        chosen,
        mesh=mesh,
        in_specs=(
            P(("exp", "fsdp"), None, "ctx", None),
            P(("exp", "fsdp")),
            P(("exp", "fsdp"), None, "ctx", None),
            P(("exp", "fsdp"), "ctx", None),
            P(("ctx", "exp", "fsdp")),
            P(("ctx", "exp", "fsdp"), None),
            P(("ctx", "exp", "fsdp"), None),
            P(("ctx", "exp", "fsdp"), None),
            P(("ctx", "exp", "fsdp")),
            P(("ctx", "exp", "fsdp"), None),
            P(("ctx", "exp", "fsdp"), None),
            P("exp", ("ctx", "fsdp"), None),
            P("exp", ("ctx", "fsdp"), None),
            P(("exp", "fsdp"), None, "ctx", None),
        ),
        out_specs=(
            P(("exp", "fsdp"), None, "ctx", None),
            P(("exp", "fsdp"), None, "ctx", None),
            P(("ctx", "exp", "fsdp")),
            P(("ctx", "exp", "fsdp"), None),
            P(("ctx", "exp", "fsdp"), None),
            P(("ctx", "exp", "fsdp"), None),
            P(("ctx", "exp", "fsdp")),
            P(("ctx", "exp", "fsdp"), None),
            P(("ctx", "exp", "fsdp"), None),
            P("exp", ("ctx", "fsdp"), None),
            P("exp", ("ctx", "fsdp"), None),
        ),
        check_vma=False,
    )
```

```python
import functools

import jax
import jax.numpy as jnp
from jax import lax
from jax.experimental import pallas as pl
from jax.experimental.pallas import tpu as pltpu
from jax.sharding import PartitionSpec as P

HS = 64
CAP = 18


epsilon = 1e-06
masked_out = -1e30
highest = lax.Precision.HIGHEST


def rms_norm(values_in, gain_row):
    return (
        values_in
        * lax.rsqrt(jnp.mean(values_in * values_in, axis=-1, keepdims=True) + epsilon)
        * gain_row
    )


def rope_tables(places):
    half_size = HS // 2
    frequency = 10000.0 ** (-jnp.arange(half_size, dtype=jnp.float32) * 2.0 / HS)
    angles = places.astype(jnp.float32)[:, None] * frequency[None, :]
    return (jnp.cos(angles), jnp.sin(angles))


def rotate(values_in, cosines, sine_rows):
    half_size = values_in.shape[-1] // 2
    leading = values_in[..., :half_size]
    trailing = values_in[..., half_size:]
    cos_rows = cosines[:, None, :]
    sin_rows = sine_rows[:, None, :]
    return jnp.concatenate(
        [leading * cos_rows - trailing * sin_rows, leading * sin_rows + trailing * cos_rows],
        axis=-1,
    )


def swiglu(merged_rows):
    gate_part, up_part = jnp.split(merged_rows, 2, axis=-1)
    return jax.nn.silu(gate_part) * up_part


def first_t(left_side, right_side, precision=None):
    return lax.dot_general(
        left_side,
        right_side,
        (((0,), (0,)), ((), ())),
        precision=precision,
        preferred_element_type=jnp.float32,
    )


def second_t(left_side, right_side, precision=None):
    return lax.dot_general(
        left_side,
        right_side,
        (((1,), (1,)), ((), ())),
        precision=precision,
        preferred_element_type=jnp.float32,
    )


def per_device(
    hidden_in,
    seq_lengths,
    expert_ids,
    route_rank,
    gain_attn,
    w_qkv,
    w_out,
    w_router,
    gain_ffn,
    w_gate_up,
    w_shared_down,
    w_experts_in,
    w_experts_out,
    grad_output,
):
    num_seqs, two_ends, half_len, model_width = hidden_in.shape
    shard_len = 2 * half_len
    tok_count = num_seqs * shard_len
    num_heads = model_width // HS
    score_scale = HS ** (-0.5)
    ctx_size = lax.axis_size("ctx")
    full_len = shard_len * ctx_size
    whole_half = half_len * ctx_size
    gain_one, wqkv_all, wout_all, router_all, gain_two, shared_in, shared_down = (
        lax.all_gather(gain_attn, ("ctx", "exp", "fsdp"), axis=0, tiled=True),
        lax.all_gather(w_qkv, ("ctx", "exp", "fsdp"), axis=0, tiled=True),
        lax.all_gather(w_out, ("ctx", "exp", "fsdp"), axis=0, tiled=True),
        lax.all_gather(w_router, ("ctx", "exp", "fsdp"), axis=0, tiled=True),
        lax.all_gather(gain_ffn, ("ctx", "exp", "fsdp"), axis=0, tiled=True),
        lax.all_gather(w_gate_up, ("ctx", "exp", "fsdp"), axis=0, tiled=True),
        lax.all_gather(w_shared_down, ("ctx", "exp", "fsdp"), axis=0, tiled=True),
    )
    experts_in, experts_out = (
        lax.all_gather(w_experts_in, ("ctx", "fsdp"), axis=1, tiled=True),
        lax.all_gather(w_experts_out, ("ctx", "fsdp"), axis=1, tiled=True),
    )
    lower_places = lax.axis_index("ctx") * half_len + jnp.arange(half_len, dtype=jnp.int32)
    places = jnp.concatenate([lower_places, full_len - 1 - lower_places])
    whole_range = jnp.arange(whole_half, dtype=jnp.int32)
    full_places = jnp.concatenate([whole_range, full_len - 1 - whole_range])
    live_mask = (places[None, :] < seq_lengths[:, None]).astype(jnp.float32)
    live_rows = live_mask.reshape(tok_count, 1)
    inputs_f = hidden_in.astype(jnp.float32).reshape(tok_count, model_width)
    gain_attn_f = gain_one.astype(jnp.float32)
    normed_b = rms_norm(inputs_f, gain_attn_f).astype(jnp.bfloat16)
    qkv_merged = jnp.dot(normed_b, wqkv_all, preferred_element_type=jnp.float32).reshape(
        num_seqs, shard_len, 3, num_heads, HS
    )
    cosines, sine_rows = rope_tables(places)
    queries = rotate(qkv_merged[:, :, 0], cosines, sine_rows).astype(jnp.bfloat16)
    keys_local = rotate(qkv_merged[:, :, 1], cosines, sine_rows).astype(jnp.bfloat16)
    values_local = qkv_merged[:, :, 2].astype(jnp.bfloat16)
    end_shape = (num_seqs, 2, half_len, model_width)
    keys_full, values_full = (
        lax.all_gather(keys_local.reshape(end_shape), "ctx", axis=2, tiled=True),
        lax.all_gather(values_local.reshape(end_shape), "ctx", axis=2, tiled=True),
    )
    keys_full = keys_full.reshape(num_seqs, full_len, num_heads, HS)
    values_full = values_full.reshape(num_seqs, full_len, num_heads, HS)
    stat_shape = (num_seqs, num_heads, shard_len)
    block_range = jnp.arange(ctx_size, dtype=jnp.int32)

    def block_scores(query_rows, query_places, key_rows, key_places):
        scores = (
            jnp.einsum("bqhd,bkhd->bhqk", query_rows, key_rows, preferred_element_type=jnp.float32)
            * score_scale
        )
        allowed = (key_places[None, None, :] <= query_places[None, :, None]) & (
            key_places[None, None, :] < seq_lengths[:, None, None]
        )
        return jnp.where(allowed[:, None], scores, masked_out)

    def key_block(block_idx):
        offset = block_idx * shard_len
        return (
            lax.dynamic_slice_in_dim(keys_full, offset, shard_len, 1),
            lax.dynamic_slice_in_dim(values_full, offset, shard_len, 1),
            lax.dynamic_slice_in_dim(full_places, offset, shard_len, 0),
        )

    def lse_step(state_in, block_idx):
        run_max, run_sum = state_in
        key_rows, value_rows, key_places = key_block(block_idx)
        scores = block_scores(queries, places, key_rows, key_places)
        new_max = jnp.maximum(run_max, jnp.max(scores, axis=-1))
        run_sum = run_sum * jnp.exp(run_max - new_max) + jnp.sum(
            jnp.exp(scores - new_max[..., None]), axis=-1
        )
        return ((new_max, run_sum), None)

    (row_max, row_sum), unused = lax.scan(
        lse_step,
        (jnp.full(stat_shape, masked_out, jnp.float32), jnp.zeros(stat_shape, jnp.float32)),
        block_range,
    )
    log_total = row_max + jnp.log(row_sum)

    def context_step(running, block_idx):
        key_rows, value_rows, key_places = key_block(block_idx)
        prob_rows = jnp.exp(
            block_scores(queries, places, key_rows, key_places) - log_total[..., None]
        ).astype(jnp.bfloat16)
        return (
            running
            + jnp.einsum(
                "bhqk,bkhd->bqhd", prob_rows, value_rows, preferred_element_type=jnp.float32
            ),
            None,
        )

    context, unused = lax.scan(
        context_step, jnp.zeros((num_seqs, shard_len, num_heads, HS), jnp.float32), block_range
    )
    context_b = context.reshape(tok_count, model_width).astype(jnp.bfloat16)
    attended = inputs_f + jnp.dot(context_b, wout_all, preferred_element_type=jnp.float32)
    gain_ffn_f = gain_two.astype(jnp.float32)
    normed_two = rms_norm(attended, gain_ffn_f).astype(jnp.bfloat16)
    logits = jnp.dot(normed_two, router_all, preferred_element_type=jnp.float32)
    num_experts = router_all.shape[1]
    expert_range = jnp.arange(num_experts, dtype=jnp.int32)
    picked_ids = expert_ids.reshape(tok_count, 2)
    pick_hot = (picked_ids[:, :, None] == expert_range).astype(jnp.float32)
    chosen = jnp.sum(pick_hot * logits[:, None, :], axis=-1)
    gate_probs = jax.nn.softmax(chosen, axis=-1)
    expert_load = (jnp.sum(pick_hot, axis=1) * live_rows).astype(jnp.bfloat16)
    rank_rows = route_rank.reshape(tok_count)
    earlier = (rank_rows[None, :] < rank_rows[:, None]).astype(jnp.bfloat16)
    position = jnp.dot(earlier, expert_load, preferred_element_type=jnp.float32)
    chosen_pos = jnp.sum(pick_hot * position[:, None, :], axis=-1)
    kept_mask = live_rows * (chosen_pos < CAP).astype(jnp.float32)
    slot_hot = (chosen_pos[:, :, None] == jnp.arange(CAP, dtype=jnp.float32)).astype(jnp.float32)
    dispatch = (
        (pick_hot[:, :, :, None] * slot_hot[:, :, None, :] * kept_mask[:, :, None, None])
        .reshape(tok_count, 2, num_experts * CAP)
        .astype(jnp.bfloat16)
    )
    dispatch_any = dispatch[:, 0] + dispatch[:, 1]
    exp_size = lax.axis_size("exp")
    per_owner = num_experts // exp_size
    send_rows = (
        first_t(dispatch_any, normed_two)
        .astype(jnp.bfloat16)
        .reshape(exp_size, per_owner, CAP, model_width)
    )
    arrived = lax.all_to_all(send_rows, "exp", split_axis=0, concat_axis=0, tiled=True)
    expert_merged = jnp.einsum(
        "secd,edf->secf", arrived, experts_in, preferred_element_type=jnp.float32
    )
    expert_hidden = swiglu(expert_merged).astype(jnp.bfloat16)
    expert_result = jnp.einsum(
        "secf,efd->secd", expert_hidden, experts_out, preferred_element_type=jnp.float32
    ).astype(jnp.bfloat16)
    returned = lax.all_to_all(
        expert_result, "exp", split_axis=0, concat_axis=0, tiled=True
    ).reshape(num_experts * CAP, model_width)
    routed = jnp.einsum("tks,sd->tkd", dispatch, returned, preferred_element_type=jnp.float32)
    mixture = jnp.sum(gate_probs[:, :, None] * routed, axis=1)
    shared_merged = jnp.dot(normed_two, shared_in, preferred_element_type=jnp.float32)
    shared_hidden = swiglu(shared_merged).astype(jnp.bfloat16)
    shared_result = jnp.dot(shared_hidden, shared_down, preferred_element_type=jnp.float32)
    layer_out = (
        (live_rows * (attended + mixture + shared_result)).reshape(end_shape).astype(jnp.bfloat16)
    )
    upstream = grad_output.astype(jnp.float32).reshape(tok_count, model_width) * live_rows
    upstream_b = upstream.astype(jnp.bfloat16)
    upstream_f = upstream_b.astype(jnp.float32)
    d_shared_down = first_t(shared_hidden, upstream_b)
    d_shared_hidden = second_t(upstream_b, shared_down)
    unused, swiglu_pull = jax.vjp(swiglu, shared_merged)
    d_shared_merged = swiglu_pull(d_shared_hidden)[0].astype(jnp.bfloat16)
    d_shared_in = first_t(normed_two, d_shared_merged)
    d_normed_two = second_t(d_shared_merged, shared_in)
    gate_grads = jnp.sum(routed * upstream_f[:, None, :], axis=-1)
    weighted = (gate_probs[:, :, None] * upstream_f[:, None, :]).astype(jnp.bfloat16)
    d_returned = (
        jnp.einsum("tks,tkd->sd", dispatch, weighted, preferred_element_type=jnp.float32)
        .astype(jnp.bfloat16)
        .reshape(exp_size, per_owner, CAP, model_width)
    )
    d_result = lax.all_to_all(d_returned, "exp", split_axis=0, concat_axis=0, tiled=True)
    d_experts_out = jnp.einsum(
        "secf,secd->efd", expert_hidden, d_result, preferred_element_type=jnp.float32
    )
    d_expert_hidden = jnp.einsum(
        "secd,efd->secf", d_result, experts_out, preferred_element_type=jnp.float32
    )
    unused, expert_pull = jax.vjp(swiglu, expert_merged)
    d_expert_merged = expert_pull(d_expert_hidden)[0].astype(jnp.bfloat16)
    d_experts_in = jnp.einsum(
        "secd,secf->edf", arrived, d_expert_merged, preferred_element_type=jnp.float32
    )
    d_arrived = jnp.einsum(
        "secf,edf->secd", d_expert_merged, experts_in, preferred_element_type=jnp.float32
    ).astype(jnp.bfloat16)
    d_sent = lax.all_to_all(d_arrived, "exp", split_axis=0, concat_axis=0, tiled=True).reshape(
        num_experts * CAP, model_width
    )
    d_normed_two = d_normed_two + jnp.dot(dispatch_any, d_sent, preferred_element_type=jnp.float32)
    unused, gate_pull = jax.vjp(lambda chosen_in: jax.nn.softmax(chosen_in, axis=-1), chosen)
    d_chosen = gate_pull(gate_grads)[0]
    d_logits = jnp.sum(pick_hot * d_chosen[:, :, None], axis=1)
    d_router = first_t(normed_two.astype(jnp.float32), d_logits, highest)
    d_normed_two = d_normed_two + second_t(d_logits, router_all.astype(jnp.float32), highest)
    unused, second_pull = jax.vjp(rms_norm, attended, gain_ffn_f)
    d_attended, d_gain_ffn = second_pull(d_normed_two)
    d_attended = d_attended + upstream
    d_attended_b = d_attended.astype(jnp.bfloat16)
    d_out_proj = first_t(context_b, d_attended_b)
    d_context = (
        second_t(d_attended_b, wout_all)
        .astype(jnp.bfloat16)
        .reshape(num_seqs, shard_len, num_heads, HS)
    )

    def score_grads(
        query_rows, query_places, key_rows, value_rows, key_places, d_rows, lse_rows, delta_rows
    ):
        prob_rows = jnp.exp(
            block_scores(query_rows, query_places, key_rows, key_places) - lse_rows[..., None]
        )
        d_probs = jnp.einsum(
            "bqhd,bkhd->bhqk", d_rows, value_rows, preferred_element_type=jnp.float32
        )
        d_scores = (prob_rows * (d_probs - delta_rows[..., None])).astype(jnp.bfloat16)
        return (prob_rows.astype(jnp.bfloat16), d_scores)

    def delta_step(running, block_idx):
        key_rows, value_rows, key_places = key_block(block_idx)
        prob_rows = jnp.exp(
            block_scores(queries, places, key_rows, key_places) - log_total[..., None]
        )
        d_probs = jnp.einsum(
            "bqhd,bkhd->bhqk", d_context, value_rows, preferred_element_type=jnp.float32
        )
        return (running + jnp.sum(prob_rows * d_probs, axis=-1), None)

    row_delta, unused = lax.scan(delta_step, jnp.zeros(stat_shape, jnp.float32), block_range)
    head_shape = (num_seqs, shard_len, num_heads, HS)

    def query_step(d_query, block_idx):
        key_rows, value_rows, key_places = key_block(block_idx)
        prob_b, d_scores = score_grads(
            queries, places, key_rows, value_rows, key_places, d_context, log_total, row_delta
        )
        return (
            d_query
            + jnp.einsum("bhqk,bkhd->bqhd", d_scores, key_rows, preferred_element_type=jnp.float32)
            * score_scale,
            None,
        )

    d_query, unused = lax.scan(query_step, jnp.zeros(head_shape, jnp.float32), block_range)
    query_all, d_context_all = (
        lax.all_gather(queries.reshape(end_shape), "ctx", axis=2, tiled=True),
        lax.all_gather(d_context.reshape(end_shape), "ctx", axis=2, tiled=True),
    )
    stat_ends = (num_seqs, num_heads, 2, half_len)
    lse_all, delta_all = (
        lax.all_gather(log_total.reshape(stat_ends), "ctx", axis=3, tiled=True),
        lax.all_gather(row_delta.reshape(stat_ends), "ctx", axis=3, tiled=True),
    )
    query_all = query_all.reshape(num_seqs, full_len, num_heads, HS)
    d_context_all = d_context_all.reshape(num_seqs, full_len, num_heads, HS)
    lse_all = lse_all.reshape(num_seqs, num_heads, full_len)
    delta_all = delta_all.reshape(num_seqs, num_heads, full_len)

    def owner_step(state_in, block_idx):
        d_keys, d_values = state_in
        offset = block_idx * shard_len
        query_rows = lax.dynamic_slice_in_dim(query_all, offset, shard_len, 1)
        d_rows = lax.dynamic_slice_in_dim(d_context_all, offset, shard_len, 1)
        lse_rows = lax.dynamic_slice_in_dim(lse_all, offset, shard_len, 2)
        delta_rows = lax.dynamic_slice_in_dim(delta_all, offset, shard_len, 2)
        query_places = lax.dynamic_slice_in_dim(full_places, offset, shard_len, 0)
        prob_b, d_scores = score_grads(
            query_rows, query_places, keys_local, values_local, places, d_rows, lse_rows, delta_rows
        )
        d_keys = (
            d_keys
            + jnp.einsum(
                "bhqk,bqhd->bkhd", d_scores, query_rows, preferred_element_type=jnp.float32
            )
            * score_scale
        )
        d_values = d_values + jnp.einsum(
            "bhqk,bqhd->bkhd", prob_b, d_rows, preferred_element_type=jnp.float32
        )
        return ((d_keys, d_values), None)

    (d_keys_local, d_values_local), unused = lax.scan(
        owner_step,
        (jnp.zeros(head_shape, jnp.float32), jnp.zeros(head_shape, jnp.float32)),
        block_range,
    )
    unused, rope_pull = jax.vjp(
        lambda rows_in: rotate(rows_in, cosines, sine_rows), qkv_merged[:, :, 0]
    )
    d_query_pre = rope_pull(d_query)[0]
    d_key_pre = rope_pull(d_keys_local)[0]
    d_qkv_merged = (
        jnp.stack([d_query_pre, d_key_pre, d_values_local], axis=2)
        .reshape(tok_count, 3 * model_width)
        .astype(jnp.bfloat16)
    )
    d_qkv = first_t(normed_b, d_qkv_merged)
    d_normed = second_t(d_qkv_merged, wqkv_all)
    unused, first_pull = jax.vjp(rms_norm, inputs_f, gain_attn_f)
    d_inputs, d_gain_attn = first_pull(d_normed)
    grad_input = (d_attended + d_inputs).reshape(end_shape)
    dense_sums = (
        lax.psum_scatter(d_gain_attn, ("ctx", "exp", "fsdp"), scatter_dimension=0, tiled=True),
        lax.psum_scatter(d_qkv, ("ctx", "exp", "fsdp"), scatter_dimension=0, tiled=True),
        lax.psum_scatter(d_out_proj, ("ctx", "exp", "fsdp"), scatter_dimension=0, tiled=True),
        lax.psum_scatter(d_router, ("ctx", "exp", "fsdp"), scatter_dimension=0, tiled=True),
        lax.psum_scatter(d_gain_ffn, ("ctx", "exp", "fsdp"), scatter_dimension=0, tiled=True),
        lax.psum_scatter(d_shared_in, ("ctx", "exp", "fsdp"), scatter_dimension=0, tiled=True),
        lax.psum_scatter(d_shared_down, ("ctx", "exp", "fsdp"), scatter_dimension=0, tiled=True),
    )
    expert_sums = (
        lax.psum_scatter(
            d_experts_in.astype(jnp.bfloat16), ("ctx", "fsdp"), scatter_dimension=1, tiled=True
        ).astype(jnp.float32),
        lax.psum_scatter(
            d_experts_out.astype(jnp.bfloat16), ("ctx", "fsdp"), scatter_dimension=1, tiled=True
        ).astype(jnp.float32),
    )
    return (
        layer_out,
        grad_input,
        dense_sums[0],
        dense_sums[1],
        dense_sums[2],
        dense_sums[3],
        dense_sums[4],
        dense_sums[5],
        dense_sums[6],
        expert_sums[0],
        expert_sums[1],
    )


F32 = jnp.float32
BF = jnp.bfloat16
MESH = pl.DeviceIdType.MESH
ROWS = 24
SMALL = 64
VMEM_BYTES = 63 * 1024 * 1024


def place():
    return lax.axis_index("ctx"), lax.axis_index("exp"), lax.axis_index("fsdp")


def wrap(value, size):
    return lax.rem(value, size)


def mm(left, right):
    return lax.dot_general(
        left, right, (((1,), (0,)), ((), ())), preferred_element_type=F32
    )


def mm_nt(left, right):
    return lax.dot_general(
        left, right, (((1,), (1,)), ((), ())), preferred_element_type=F32
    )


def mm_tn(left, right):
    return lax.dot_general(
        left, right, (((0,), (0,)), ((), ())), preferred_element_type=F32
    )


def greet(peers):
    barrier = pltpu.get_barrier_semaphore()
    for peer in peers:
        pl.semaphore_signal(barrier, inc=1, device_id=peer, device_id_type=MESH)


def met(peers):
    pl.semaphore_wait(pltpu.get_barrier_semaphore(), len(peers))


class Courier:
    def __init__(self, send, recv):
        self.send, self.recv, self.count, self.sent = send, recv, 0, []

    def push(self, src, dst, device):
        index = self.count
        self.count += 1
        copy = pltpu.make_async_remote_copy(
            src_ref=src,
            dst_ref=dst,
            send_sem=self.send.at[index],
            recv_sem=self.recv.at[index],
            device_id=device,
            device_id_type=MESH,
        )
        copy.start()
        self.sent.append(copy)
        return copy

    def settle(self, copies):
        for copy in copies:
            copy.wait_send()
        done = {id(copy) for copy in copies}
        self.sent = [copy for copy in self.sent if id(copy) not in done]

    def finish(self):
        self.settle(list(self.sent))


def swap_halves(rows):
    width = rows.shape[1]
    lane = lax.broadcasted_iota(jnp.int32, rows.shape, 1)
    ahead = pltpu.roll(rows, width - HS // 2, 1)
    behind = pltpu.roll(rows, HS // 2, 1)
    return jnp.where((lane & (HS - 1)) < HS // 2, -ahead, behind)


def wide(table, times):
    return jnp.concatenate([table] * times, axis=1)


def position_of(index, half_len, full_len):
    block = index // (2 * half_len)
    inside = index & (2 * half_len - 1)
    low = block * half_len + (inside & (half_len - 1))
    return jnp.where(inside >= half_len, full_len - 1 - low, low)


def allowed_keys(length, half_len, full_len):
    shape = (full_len, full_len)
    query_at = position_of(lax.broadcasted_iota(jnp.int32, shape, 0), half_len, full_len)
    key_at = position_of(lax.broadcasted_iota(jnp.int32, shape, 1), half_len, full_len)
    return (key_at <= query_at) & (key_at < length)


def head_probs(query, key, allowed):
    scores = jnp.where(allowed, mm_nt(query, key) * (HS**-0.5), masked_out)
    weights = jnp.exp(scores - jnp.max(scores, axis=1, keepdims=True))
    return weights * (1.0 / jnp.sum(weights, axis=1, keepdims=True))


def column_row(tail, lane):
    pick = (lax.broadcasted_iota(jnp.int32, (8, 128), 1) == lane).astype(BF)
    return mm_nt(pick, tail)[0:1]


def split_dot(dot, left, right, left_wide=True):
    whole = left if left_wide else right
    high = whole.astype(BF)
    low = (whole - high.astype(F32)).astype(BF)
    if left_wide:
        return dot(high, right) + dot(low, right)
    return dot(left, high) + dot(left, low)


def inverse_rms(rows):
    return lax.rsqrt(jnp.mean(rows * rows, axis=1, keepdims=True) + epsilon)


def norm_back(rows, inverse, scaled):
    return inverse * scaled - rows * (inverse * inverse * inverse) * jnp.mean(
        rows * scaled, axis=1, keepdims=True
    )


def join(blocks, shape):
    return blocks.astype(F32).reshape(shape).astype(BF)


def ffn_pass(rows_ref, grads_ref, in_ref, out_ref, hidden_ref, dm_ref, result, back, units, step):
    result[...] = jnp.zeros(result.shape, F32)
    back[...] = jnp.zeros(back.shape, F32)

    def body(j, carry):
        low = pl.multiple_of(j * step, step)
        gate_at, up_at = pl.ds(low, step), pl.ds(pl.multiple_of(units + low, step), step)
        rows, grads = rows_ref[...], grads_ref[...]
        gate, up = mm(rows, in_ref[:, gate_at]), mm(rows, in_ref[:, up_at])
        down = out_ref[gate_at, :]
        d_hidden = mm_nt(grads, down)
        share = 1.0 / (1.0 + jnp.exp(-gate))
        lit = gate * share
        hidden = (lit * up).astype(BF)
        d_gate = (d_hidden * up * (share * (1.0 + gate * (1.0 - share)))).astype(BF)
        d_up = (d_hidden * lit).astype(BF)
        hidden_ref[:, gate_at] = hidden
        dm_ref[:, gate_at] = d_gate
        dm_ref[:, up_at] = d_up
        result[...] += mm(hidden, down)
        back[...] += mm_nt(d_gate, in_ref[:, gate_at]) + mm_nt(d_up, in_ref[:, up_at])
        return carry

    lax.fori_loop(0, units // step, body, 0)


def block_kernel(
    nc, nz,
    len_ref, hid_ref, go_ref, ids_ref, rank_ref, wqkv_ref, small_ref, gu_ref, wo_ref, sd_ref,
    win_ref, wout_ref, turn_ref,
    out_ref, gin_ref, fq_ref, fgu_ref, fsd_ref, fwo_ref, ein_ref, eout_ref,
    hid_all, up_own, up_all, wq_own, wq_st, wq_buf, w_ref, gu_st, gu_buf, gu_all, wo_st, wo_buf,
    wo_all, sd_all, wie, woe, normed_ref, qkv_ref, ctx_all, att_own, nt_all,
    sb, ar, xs, ds, acc_a, acc_b, sh_own, sh_hidden, sh_dm, sh_send, rs_shared,
    ex_hidden, ex_dm, pin, fb, rb, gsd, da_own, dctx_send, dctx_all, part, part_own, rs_in,
    sib_gu, zi_gu, pb_gu, sib_q, zi_q, pb_q, sib_sd, zi_sd, sib_wo, zi_wo, pb_wo, in_wo,
    send, recv, esend, erecv, gsend, grecv, lsem,
):
    c, z, f = place()
    in_plane = [(wrap(c + s, nc), z, f) for s in range(1, nc)]
    in_column = [(c, wrap(z + s, nz), f) for s in range(1, nz)]
    sibling = (c, z, 1 - f)
    across = [(wrap(c + s, nc), z, 1 - f) for s in range(1, nc)]
    ring = [(dz, dc) for dz in range(nz) for dc in range(nc) if dz or dc]
    everyone = [(wrap(c + dc, nc), wrap(z + dz, nz), f) for dz, dc in ring]
    greet(everyone + [sibling] + across)

    num_seqs, shard_len, width = hid_ref.shape
    full_len = nc * shard_len
    half_len = shard_len // 2
    tok = num_seqs * shard_len
    rows_w = wqkv_ref.shape[0]
    head_width = wqkv_ref.shape[1] // 3 // nc
    heads_here = head_width // HS
    wide_cols = wq_own.shape[2]
    units = gu_ref.shape[1] // 2
    own_units = units // nc
    down_rows = sd_ref.shape[0]
    num_experts = nz * nc
    num_slots = num_experts * ROWS
    block_rows = nz * 2 * rows_w
    mail = Courier(send, recv)

    for owner in range(nc):
        wq_own[owner] = jnp.concatenate(
            [
                wqkv_ref[:, side * width + owner * head_width : side * width + (owner + 1) * head_width]
                for side in range(3)
            ]
            + [small_ref[...]],
            axis=1,
        )
    met(everyone + [sibling] + across)

    staged_wq = [
        mail.push(wq_own.at[wrap(c + s, nc)], wq_st.at[c], in_plane[s - 1]) for s in range(1, nc)
    ]
    arriving = [
        [mail.push(hid_ref.at[q], hid_all.at[q, c], peer) for peer in in_plane]
        for q in range(num_seqs)
    ]
    staged_wo = [mail.push(wo_ref, wo_st.at[c], peer) for peer in in_plane]
    staged_gu = []
    for s in range(1, nc):
        owner = wrap(c + s, nc)
        for side in range(2):
            at = pl.ds(pl.multiple_of(side * units + owner * own_units, own_units), own_units)
            staged_gu.append(
                mail.push(
                    gu_ref.at[:, at],
                    gu_st.at[c, :, pl.ds(side * own_units, own_units)],
                    in_plane[s - 1],
                )
            )

    block = 2 * c + f
    shard_rows = win_ref.shape[1]
    half_units = units // 2
    lands = pl.ds(pl.multiple_of(block * shard_rows, shard_rows), shard_rows)
    expert_in, own_in = [], []
    for s in range(nc):
        owner = wrap(c + s, nc)
        for g in range(2):
            core = f if g == 0 else 1 - f
            for side in range(2):
                from_lane = pl.multiple_of(side * units + core * half_units, half_units)
                src = win_ref.at[owner, :, pl.ds(from_lane, half_units)]
                dst = wie.at[lands, pl.ds(side * half_units, half_units)]
                if s == 0 and g == 0:
                    own_in.append(pltpu.make_async_copy(src, dst, lsem.at[side]))
                    own_in[-1].start()
                else:
                    expert_in.append(mail.push(src, dst, (owner, z, core)))
    out_rows = wout_ref.shape[1]
    to_core = block // nc
    slot = wrap(block, nc)
    out_lands = pl.ds(pl.multiple_of(slot * out_rows, out_rows), out_rows)

    def out_copy(s, device, to_slot, lands_at):
        return pltpu.make_async_remote_copy(
            src_ref=wout_ref.at[wrap(c + s, nc)],
            dst_ref=woe.at[lands_at],
            send_sem=esend.at[s],
            recv_sem=erecv.at[to_slot],
            device_id=device,
            device_id_type=MESH,
        )

    for s in range(1, nc):
        out_copy(s, (wrap(c + s, nc), z, to_core), slot, out_lands).start()
    own_out = pltpu.make_async_copy(wout_ref.at[c], woe.at[out_lands], lsem.at[2])

    @pl.when(to_core == f)
    def _():
        own_out.start()

    @pl.when(to_core != f)
    def _():
        out_copy(0, sibling, slot, out_lands).start()

    row_at = lax.broadcasted_iota(jnp.int32, (tok, 1), 0)
    inside = row_at & (shard_len - 1)
    low = c * half_len + (inside & (half_len - 1))
    places = jnp.where(inside >= half_len, full_len - 1 - low, low)
    lengths = jnp.zeros((tok, 1), jnp.int32)
    for q in range(num_seqs):
        lengths = jnp.where(row_at // shard_len == q, len_ref[q], lengths)
    live = (places < lengths).astype(F32)
    lane = lax.broadcasted_iota(jnp.int32, (tok, 128), 1).astype(F32)
    picked = ids_ref[...].astype(F32)
    hots = [(lane == SMALL + picked[:, k : k + 1]).astype(F32) for k in range(2)]
    rank_row = jnp.broadcast_to(rank_ref[...].astype(F32), (tok, tok))
    earlier = (rank_row < jnp.transpose(rank_row, (1, 0))).astype(BF)
    position = mm(earlier, ((hots[0] + hots[1]) * live).astype(BF))
    slot_lane = lax.broadcasted_iota(jnp.int32, (tok, num_slots), 1).astype(F32)
    dispatch = []
    for k in range(2):
        at = jnp.sum(hots[k] * position, axis=1, keepdims=True)
        slot_at = jnp.where((live > 0) & (at < CAP), picked[:, k : k + 1] * ROWS + at, -1.0)
        dispatch.append((slot_lane == slot_at).astype(BF))
    anyone = dispatch[0] + dispatch[1]
    upstream = go_ref[...].reshape(tok, width).astype(F32) * live
    up_b = upstream.astype(BF)
    up_f = up_b.astype(F32)
    up_own[...] = up_b.reshape(num_seqs, shard_len, width)
    up_copies = [mail.push(up_own, up_all.at[:, c], peer) for peer in in_plane]
    for q in range(num_seqs):
        hid_all[q, c] = hid_ref[q]
        up_all[q, c] = up_own[q]

    own_down = pl.ds(pl.multiple_of((z * 2 + f) * down_rows, down_rows), down_rows)
    sd_all[own_down] = sd_ref[...]

    def spread(stage, staged, buffer):
        for copy in staged:
            copy.wait_recv()
        copies = [mail.push(stage, buffer.at[:, z, f], peer) for peer in in_column]
        copies.append(mail.push(stage, buffer.at[:, z, f], sibling))
        for i in range(nc):
            buffer[i, z, f] = stage[i]
        return copies

    def forward(copies, buffer):
        passed = []
        for s in range(1, nz):
            origin = wrap(z + nz - s, nz)
            copies[s - 1].wait_recv()
            passed.append(
                mail.push(buffer.at[:, origin, f], buffer.at[:, origin, f], sibling)
            )
        return passed

    with jax.named_scope("a_stage_wq"):
        wq_st[c] = wq_own[c]
        spread_wq = spread(wq_st, staged_wq, wq_buf)
    with jax.named_scope("a_stage_wo"):
        wo_st[c] = wo_ref[...]
        spread_wo = spread(wo_st, staged_wo, wo_buf)
    with jax.named_scope("a_stage_gu"):
        for side in range(2):
            at = pl.ds(pl.multiple_of(side * units + c * own_units, own_units), own_units)
            gu_st[c, :, side * own_units : (side + 1) * own_units] = gu_ref[:, at]
        spread_gu = spread(gu_st, staged_gu, gu_buf)
    spread_sd = [mail.push(sd_ref, sd_all.at[own_down], peer) for peer in in_column]
    spread_sd.append(mail.push(sd_ref, sd_all.at[own_down], sibling))
    with jax.named_scope("a_forward_wq"):
        passed_wq = forward(spread_wq, wq_buf)
        for copy in passed_wq + spread_wq[-1:]:
            copy.wait_recv()
        for i in range(nc):
            w_ref[i * block_rows : (i + 1) * block_rows, :] = join(
                wq_buf[i], (block_rows, wide_cols)
            )

    cosines = wide(turn_ref[:, :128], 2 * head_width // 128)
    sines = wide(turn_ref[:, 128:], 2 * head_width // 128)
    tail_at = wide_cols - 128
    attn_gain = column_row(w_ref[:, tail_at:], SMALL + num_experts)
    ctx_copies = []
    for q in range(num_seqs):
        with jax.named_scope("a_wait_hidden"):
            for copy in arriving[q]:
                copy.wait_recv()
        with jax.named_scope("a_attention"):
            rows = hid_all[q].reshape(full_len, width).astype(F32)
            normed = (rows * inverse_rms(rows) * attn_gain).astype(BF)
            normed_ref[q] = normed
            merged = mm(normed, w_ref[:, : 3 * head_width])
            both = merged[:, : 2 * head_width]
            both = (both * cosines + swap_halves(both) * sines).astype(BF)
            values = merged[:, 2 * head_width :].astype(BF)
            qkv_ref[q, :, : 2 * head_width] = both
            qkv_ref[q, :, 2 * head_width :] = values
            allowed = allowed_keys(len_ref[q], half_len, full_len)
            heads = []
            for h in range(heads_here):
                probs = head_probs(
                    both[:, h * HS : (h + 1) * HS],
                    both[:, head_width + h * HS : head_width + (h + 1) * HS],
                    allowed,
                ).astype(BF)
                heads.append(mm(probs, values[:, h * HS : (h + 1) * HS]))
            context = jnp.concatenate(heads, axis=1).astype(BF)
            ctx_all[c, q] = context.reshape(nc, shard_len, head_width)
        ctx_copies.append(
            [mail.push(ctx_all.at[c, q], ctx_all.at[c, q], peer) for peer in in_plane]
        )
    with jax.named_scope("a_forward_wo"):
        passed_wo = forward(spread_wo, wo_buf)
        for copy in passed_wo + spread_wo[-1:]:
            copy.wait_recv()
        for i in range(nc):
            wo_all[i * block_rows : (i + 1) * block_rows, :] = join(
                wo_buf[i], (block_rows, width)
            )
    ffn_gain = column_row(w_ref[:, tail_at:], SMALL + num_experts + 1)
    for q in range(num_seqs):
        with jax.named_scope("a_wait_context"):
            for copy in ctx_copies[q]:
                copy.wait_recv()
        with jax.named_scope("a_project"):
            total = hid_all[q].reshape(full_len, width).astype(F32)
            for i in range(nc):
                total = total + mm(
                    ctx_all[i, q].reshape(full_len, head_width),
                    wo_all[i * head_width : (i + 1) * head_width, :],
                )
            acc_a[q * full_len : (q + 1) * full_len] = total
            nt_all[q] = (
                (total * inverse_rms(total) * ffn_gain).astype(BF).reshape(nc, shard_len, width)
            )
    by_block = acc_a.reshape(num_seqs, nc, shard_len, width)
    for q in range(num_seqs):
        att_own[q] = by_block[q, c]

    with jax.named_scope("b_dispatch"):
        normed = jnp.concatenate([nt_all[q, c] for q in range(num_seqs)], axis=0)
        tail = w_ref[:, tail_at:]
        logits = mm(normed, tail)
        chosen = [jnp.sum(hot * logits, axis=1, keepdims=True) for hot in hots]
        top = jnp.maximum(chosen[0], chosen[1])
        raised = [jnp.exp(value - top) for value in chosen]
        gates = [value / (raised[0] + raised[1]) for value in raised]
        weighted = [(gates[k] * up_f).astype(BF) for k in range(2)]
        rows_out = mm_tn(anyone, normed)
        grads_out = mm_tn(dispatch[0], weighted[0]) + mm_tn(dispatch[1], weighted[1])
        sb[:, 0] = rows_out.reshape(num_experts, ROWS, width).astype(BF)
        sb[:, 1] = grads_out.reshape(num_experts, ROWS, width).astype(BF)
        row_copies = [
            mail.push(sb.at[to[1] * nc + to[0]], ar.at[f, z, c], to) for to in everyone
        ]
        ar[f, z, c] = sb[z * nc + c]
        forwards = [mail.push(sb.at[z * nc + c], ar.at[f, z, c], sibling)]

    with jax.named_scope("b_forward_gu"):
        passed_gu = forward(spread_gu, gu_buf)
        passed_sd = []
        for s in range(1, nz):
            origin = wrap(z + nz - s, nz)
            spread_sd[s - 1].wait_recv()
            at = pl.ds(pl.multiple_of((origin * 2 + f) * down_rows, down_rows), down_rows)
            passed_sd.append(mail.push(sd_all.at[at], sd_all.at[at], sibling))
        for copy in passed_gu + spread_gu[-1:] + passed_sd + spread_sd[-1:]:
            copy.wait_recv()
        for i in range(nc):
            gu_all[i * block_rows : (i + 1) * block_rows, :] = join(
                gu_buf[i], (block_rows, 2 * own_units)
            )
    with jax.named_scope("b_wait_upstream"):
        for copy in up_copies:
            copy.wait_recv()
    plane_tok = nc * tok
    shared_rows = nt_all.reshape(plane_tok, width)
    shared_grads = up_all.reshape(plane_tok, width)
    with jax.named_scope("b_shared"):
        first = pl.ds(0, plane_tok)
        ffn_pass(
            shared_rows, shared_grads, gu_all, sd_all, sh_hidden, sh_dm,
            acc_a.at[first], acc_b.at[first], own_units, 256,
        )
        for k, acc in enumerate((acc_a, acc_b)):
            cut = acc.reshape(num_seqs, nc, shard_len, width)
            for q in range(num_seqs):
                sh_own[k, q] = cut[q, c]
            sh_send[k] = cut[...].astype(BF)
    shared_copies = [
        mail.push(sh_send.at[:, :, wrap(c + s, nc)], rs_shared.at[s - 1], in_plane[s - 1])
        for s in range(1, nc)
    ]

    with jax.named_scope("b_forward_rows"):
        for copy, (dz, dc) in zip(row_copies, ring):
            copy.wait_recv()
            oz, oc = wrap(z + nz - dz, nz), wrap(c + nc - dc, nc)
            forwards.append(mail.push(ar.at[f, oz, oc], ar.at[f, oz, oc], sibling))
        for copy in forwards:
            copy.wait_recv()
        for core in range(2):
            at = slice(core * num_slots, (core + 1) * num_slots)
            xs[at] = join(ar[core, :, :, 0], (num_slots, width))
            ds[at] = join(ar[core, :, :, 1], (num_slots, width))
    with jax.named_scope("b_wait_experts"):
        for copy in own_in:
            copy.wait()
        for copy in expert_in:
            copy.wait_recv()
        for at in range(nc):

            @pl.when(f * nc + at != block)
            def _(at=at):
                out_copy(0, sibling, at, pl.ds(at * out_rows, out_rows)).wait_recv()

        @pl.when(to_core == f)
        def _():
            own_out.wait()

    mail.settle(row_copies + forwards[:1])
    pr = sb
    acc = [ref.at[pl.ds(0, num_slots)] for ref in (acc_a, acc_b)]
    for turn in range(2):
        core = 1 - f if turn == 0 else f
        at = pl.ds(pl.multiple_of(core * num_slots, num_slots), num_slots)
        with jax.named_scope("b_experts"):
            ffn_pass(
                xs.at[at], ds.at[at], wie, woe, ex_hidden.at[at], ex_dm.at[at],
                acc[0], acc[1], half_units, 256,
            )
        if turn == 0:
            for k in range(2):
                pr[:, k] = acc[k][...].reshape(num_experts, ROWS, width).astype(BF)
            swap = mail.push(pr, pin, sibling)
    with jax.named_scope("b_sibling_sum"):
        swap.wait_recv()
        for k in range(2):
            fb[:, k] = (
                acc[k][...].reshape(num_experts, ROWS, width) + pin[:, k].astype(F32)
            ).astype(BF)
        returns = [
            mail.push(fb.at[to[1] * nc + to[0]], rb.at[z * nc + c], to) for to in everyone
        ]
        rb[z * nc + c] = fb[z * nc + c]

    gwi, gwo = wie, woe

    def expert_grads(j, carry):
        at = pl.ds(pl.multiple_of(j * 256, 256), 256)
        gwi[:, at] = mm_tn(xs[...], ex_dm[:, at]).astype(BF)
        return carry

    home_in, home_own = [], []
    for side in range(2):
        steps = half_units // 256
        with jax.named_scope("b_gwi"):
            lax.fori_loop(side * steps, (side + 1) * steps, expert_grads, 0)
        for s in range(nc):
            owner = wrap(c + s, nc)
            for g in range(2):
                core = f if g == 0 else 1 - f
                from_rows = pl.ds(
                    pl.multiple_of((2 * owner + core) * shard_rows, shard_rows), shard_rows
                )
                to_lane = pl.multiple_of(side * units + f * half_units, half_units)
                src = gwi.at[from_rows, pl.ds(side * half_units, half_units)]
                dst = ein_ref.at[c, :, pl.ds(to_lane, half_units)]
                if s == 0 and g == 0:
                    home_own.append(pltpu.make_async_copy(src, dst, lsem.at[3 + side]))
                    home_own[-1].start()
                else:
                    home_in.append(mail.push(src, dst, (owner, z, core)))

    def home_out(j, arrives):
        to_block = f * nc + j
        return pltpu.make_async_remote_copy(
            src_ref=gwo.at[pl.ds(j * out_rows, out_rows)],
            dst_ref=eout_ref.at[arrives],
            send_sem=gsend.at[j],
            recv_sem=grecv.at[arrives],
            device_id=(to_block // 2, z, wrap(to_block, 2)),
            device_id_type=MESH,
        )

    def home_out_own(j):
        return pltpu.make_async_copy(
            gwo.at[pl.ds(j * out_rows, out_rows)], eout_ref.at[c], lsem.at[5]
        )

    with jax.named_scope("b_gwo"):
        for j in range(nc):
            gwo[j * out_rows : (j + 1) * out_rows, :] = mm_tn(
                ex_hidden[:, j * out_rows : (j + 1) * out_rows], ds[...]
            ).astype(BF)

            @pl.when(f * nc + j == block)
            def _(j=j):
                home_out_own(j).start()

            @pl.when(f * nc + j != block)
            def _(j=j):
                home_out(j, c).start()

    mail.settle(spread_gu + passed_gu)
    ggu = gu_buf
    with jax.named_scope("b_shared_grads"):

        def gate_up_grads(j, carry):
            at = pl.ds(pl.multiple_of(j * 256, 256), 256)
            piece = mm_tn(shared_rows[...], sh_dm[:, at])
            ggu[:, :, :, :, at] = piece.reshape(ggu.shape[:4] + (256,)).astype(BF)
            return carry

        lax.fori_loop(0, 2 * own_units // 256, gate_up_grads, 0)
        gsd[...] = mm_tn(sh_hidden[...], shared_grads[...]).reshape(gsd.shape).astype(BF)
        sibling_gu = mail.push(ggu.at[:, :, 1 - f], sib_gu, sibling)
        sibling_sd = mail.push(gsd.at[:, 1 - f], sib_sd, sibling)

    with jax.named_scope("c_wait_shared"):
        shared, d_normed = [sh_own[k].reshape(tok, width) for k in range(2)]
        for s in range(1, nc):
            shared_copies[s - 1].wait_recv()
            shared = shared + rs_shared[s - 1, 0].reshape(tok, width).astype(F32)
            d_normed = d_normed + rs_shared[s - 1, 1].reshape(tok, width).astype(F32)
    with jax.named_scope("c_wait_returns"):
        for copy in returns:
            copy.wait_recv()
    with jax.named_scope("c_combine"):
        attended = att_own[...].reshape(tok, width)
        inverse = inverse_rms(attended)
        results = join(rb[:, 0], (num_slots, width))
        d_rows = join(rb[:, 1], (num_slots, width))
        routed = [mm(dispatch[k], results) for k in range(2)]
        mixture = gates[0] * routed[0] + gates[1] * routed[1]
        out_ref[...] = (
            (live * (attended + mixture + shared)).astype(BF).reshape(out_ref.shape)
        )
        d_gates = [jnp.sum(routed[k] * up_f, axis=1, keepdims=True) for k in range(2)]
        mean_gate = gates[0] * d_gates[0] + gates[1] * d_gates[1]
        d_logits = hots[0] * (gates[0] * (d_gates[0] - mean_gate)) + hots[1] * (
            gates[1] * (d_gates[1] - mean_gate)
        )
        d_normed = d_normed + mm(anyone, d_rows) + split_dot(mm_nt, d_logits, tail)
        d_attended = upstream + norm_back(attended, inverse, d_normed * ffn_gain)
        d_att_b = d_attended.astype(BF)
        d_context = mm_nt(d_att_b, wo_all[...]).astype(BF)
        for i in range(nc):
            dctx_send[i] = d_context[:, i * head_width : (i + 1) * head_width].reshape(
                num_seqs, shard_len, head_width
            )
        for q in range(num_seqs):
            dctx_all[q, c] = dctx_send[c, q]
        dctx_copies = [
            mail.push(dctx_send.at[wrap(c + s, nc)], dctx_all.at[:, c], in_plane[s - 1])
            for s in range(1, nc)
        ]
        gin_ref[...] = d_attended.reshape(gin_ref.shape)

    mail.settle(spread_wo + passed_wo)
    gwo_at = wo_buf
    with jax.named_scope("c_reduce"):
        def two_cores(copy, own, inbox):
            copy.wait_recv()
            inbox[...] = (own.astype(F32) + inbox[...].astype(F32)).astype(BF)

        def four_planes(copy, buffer, inbox):
            copy.wait_recv()
            for i in range(nc):
                inbox[i] = (buffer[i, :, f].astype(F32) + inbox[i].astype(F32)).astype(BF)

        for i in range(nc):
            mine = jnp.concatenate([ctx_all[i, q, c] for q in range(num_seqs)], axis=0)
            gwo_at[i] = mm_tn(mine, d_att_b).reshape(gwo_at.shape[1:]).astype(BF)
        sibling_wo = mail.push(gwo_at.at[:, :, 1 - f], sib_wo, sibling)
        d_router = split_dot(mm_tn, normed, d_logits, left_wide=False)
        d_gain = jnp.sum(d_normed * attended * inverse, axis=0, keepdims=True)
        turned = jnp.transpose(jnp.broadcast_to(d_gain, (128, width)), (1, 0))
        extra_lane = lax.broadcasted_iota(jnp.int32, (width, 128), 1)
        extras = jnp.where(extra_lane == SMALL + num_experts + 1, turned, d_router)
        four_planes(sibling_gu, ggu, sib_gu)
        two_cores(sibling_sd, gsd[:, f], sib_sd)
        gu_copies = [
            mail.push(sib_gu.at[:, wrap(z + s, nz)], zi_gu.at[s - 1], in_column[s - 1])
            for s in range(1, nz)
        ]
        sd_copies = [
            mail.push(sib_sd.at[wrap(z + s, nz)], zi_sd.at[s - 1], in_column[s - 1])
            for s in range(1, nz)
        ]
        four_planes(sibling_wo, gwo_at, sib_wo)
        wo_copies = [
            mail.push(sib_wo.at[:, wrap(z + s, nz)], zi_wo.at[s - 1], in_column[s - 1])
            for s in range(1, nz)
        ]

    with jax.named_scope("c_wait_dctx"):
        for copy in dctx_copies:
            copy.wait_recv()
    grad_qkv = jnp.zeros((width, 3 * head_width), F32)
    parting = []
    for q in range(num_seqs):
        with jax.named_scope("c_attention"):
            d_context = dctx_all[q].reshape(full_len, head_width)
            allowed = allowed_keys(len_ref[q], half_len, full_len)
            merged = qkv_ref[q]
            d_query, d_key, d_value = [], [], []
            for h in range(heads_here):
                query = merged[:, h * HS : (h + 1) * HS]
                key = merged[:, head_width + h * HS : head_width + (h + 1) * HS]
                value = merged[:, 2 * head_width + h * HS : 2 * head_width + (h + 1) * HS]
                d_head = d_context[:, h * HS : (h + 1) * HS]
                probs = head_probs(query, key, allowed)
                d_probs = mm_nt(d_head, value)
                delta = jnp.sum(probs * d_probs, axis=1, keepdims=True)
                d_scores = (probs * (d_probs - delta)).astype(BF)
                d_query.append(mm(d_scores, key) * (HS**-0.5))
                d_key.append(mm_tn(d_scores, query) * (HS**-0.5))
                d_value.append(mm_tn(probs.astype(BF), d_head))
            both = jnp.concatenate(d_query + d_key, axis=1)
            both = both * cosines - swap_halves(both) * sines
            d_merged = jnp.concatenate([both] + d_value, axis=1).astype(BF)
            product = mm_nt(d_merged, w_ref[:, : 3 * head_width]).reshape(nc, shard_len, width)
            part_own[q] = product
            part[q] = product.astype(BF)
            parting.append(
                [
                    mail.push(part.at[q, wrap(c + s, nc)], rs_in.at[s - 1, q], in_plane[s - 1])
                    for s in range(1, nc)
                ]
            )
            grad_qkv = grad_qkv + mm_tn(normed_ref[q], d_merged)
    mail.settle(spread_wq + passed_wq)
    gq = wq_buf
    with jax.named_scope("c_reduce_q"):
        last = jnp.concatenate([grad_qkv[:, tail_at:], extras[:, 3 * head_width - tail_at :]], axis=1)
        gq[...] = (
            jnp.concatenate([grad_qkv[:, :tail_at], last], axis=1).reshape(gq.shape).astype(BF)
        )
        sibling_q = mail.push(gq.at[:, :, 1 - f], sib_q, sibling)
        four_planes(sibling_q, gq, sib_q)
        q_copies = [
            mail.push(sib_q.at[:, wrap(z + s, nz)], zi_q.at[s - 1], in_column[s - 1])
            for s in range(1, nz)
        ]

    def column_sum(own, copies, inbox):
        total = own.astype(F32)
        for s in range(1, nz):
            copies[s - 1].wait_recv()
            total = total + inbox[s - 1].astype(F32)
        return total

    def hand_out(box, final):
        final[c] = box[c]
        return [
            mail.push(box.at[wrap(c + s, nc)], final.at[c], in_plane[s - 1])
            for s in range(1, nc)
        ]

    with jax.named_scope("c_column_gu"):
        pb_gu[...] = column_sum(sib_gu[:, z], gu_copies, zi_gu).astype(BF)
        final_gu = hand_out(pb_gu, fgu_ref)
    with jax.named_scope("c_column_sd"):
        fsd_ref[...] = column_sum(sib_sd[z], sd_copies, zi_sd)
    with jax.named_scope("c_column_wo"):
        pb_wo[...] = column_sum(sib_wo[:, z], wo_copies, zi_wo).astype(BF)
        final_wo = hand_out(pb_wo, in_wo)
    with jax.named_scope("c_column_q"):
        pb_q[...] = column_sum(sib_q[:, z], q_copies, zi_q).astype(BF)
        final_q = hand_out(pb_q, fq_ref)
    with jax.named_scope("c_grad_in"):
        for q in range(num_seqs):
            d_normed = part_own[q, c]
            for s in range(1, nc):
                parting[q][s - 1].wait_recv()
                d_normed = d_normed + rs_in[s - 1, q].astype(F32)
            rows = hid_ref[q].astype(F32)
            gin_ref[q] = gin_ref[q] + norm_back(rows, inverse_rms(rows), d_normed * attn_gain)
    with jax.named_scope("c_final"):
        for copy in final_wo:
            copy.wait_recv()
        fwo_ref[...] = jnp.sum(in_wo[...].astype(F32), axis=0)
        for copy in final_gu + final_q:
            copy.wait_recv()
    with jax.named_scope("c_wait_home"):
        for copy in home_own:
            copy.wait()
        for copy in home_in:
            copy.wait_recv()
        for arrives in range(nc):

            @pl.when((arrives != c) | (to_core != f))
            def _(arrives=arrives):
                home_out(0, arrives).wait_recv()

        for j in range(nc):

            @pl.when(f * nc + j == block)
            def _(j=j):
                home_out_own(j).wait()

            @pl.when(f * nc + j != block)
            def _(j=j):
                home_out(j, c).wait_send()

        @pl.when(to_core != f)
        def _():
            out_copy(0, sibling, slot, out_lands).wait_send()

        for s in range(1, nc):
            out_copy(s, (wrap(c + s, nc), z, to_core), slot, out_lands).wait_send()
        mail.finish()


def finish_kernel(
    nc, fq_ref, fgu_ref, wqkv_ref, ga_ref, ein_ref, eout_ref, out_in, gin_in, fsd_in, fwo_in,
    gq_ref, gr_ref, gains_ref, ggu_ref, oin_ref, oout_ref, out_ref, gin_ref, fsd_ref, fwo_ref,
):
    oin_ref[...] = ein_ref[...].astype(F32)
    oout_ref[...] = eout_ref[...].astype(F32)

    @pl.when(pl.program_id(0) == 0)
    def _():
        out_ref[...] = out_in[...]
        gin_ref[...] = gin_in[...]
        fsd_ref[...] = fsd_in[...]
        fwo_ref[...] = fwo_in[...]
        rows_w = wqkv_ref.shape[0]
        head_width = wqkv_ref.shape[1] // 3 // nc
        grads = jnp.concatenate(
            [
                fq_ref[i, :, side * head_width : (side + 1) * head_width].astype(F32)
                for side in range(3)
                for i in range(nc)
            ],
            axis=1,
        )
        gq_ref[...] = grads
        own_units = fgu_ref.shape[2] // 2
        ggu_ref[...] = jnp.concatenate(
            [
                fgu_ref[i, :, side * own_units : (side + 1) * own_units].astype(F32)
                for side in range(2)
                for i in range(nc)
            ],
            axis=1,
        )
        extras = jnp.sum(fq_ref[:, :, 3 * head_width - SMALL :].astype(F32), axis=0)
        num_experts = gr_ref.shape[1]
        gr_ref[...] = extras[:, SMALL : SMALL + num_experts]
        first = jnp.sum(wqkv_ref[...].astype(F32) * grads, axis=1, keepdims=True)
        lane = lax.broadcasted_iota(jnp.int32, (rows_w, 128), 1)
        both = jnp.where(lane == SMALL + num_experts, first, extras)
        turned = jnp.transpose(
            jnp.concatenate([both, jnp.zeros((128 - rows_w, 128), F32)], axis=0), (1, 0)
        )
        gain = ga_ref[...].astype(F32)
        at = SMALL + num_experts
        gains_ref[0:1, :] = turned[at : at + 1, :rows_w] / gain
        gains_ref[1:2, :] = turned[at + 1 : at + 2, :rows_w]


def vmem(*shape, dtype=jnp.bfloat16):
    return pltpu.VMEM(shape, dtype)


def fast_device(
    hidden_in, seq_lengths, expert_ids, route_rank, gain_attn, w_qkv, w_out, w_router, gain_ffn,
    w_gate_up, w_shared_down, w_experts_in, w_experts_out, grad_output,
):
    nc, nz = lax.axis_size("ctx"), lax.axis_size("exp")
    num_seqs, two_ends, half_len, width = hidden_in.shape
    shard_len = 2 * half_len
    full_len = nc * shard_len
    tok = num_seqs * shard_len
    rows_w = w_qkv.shape[0]
    head_width = w_qkv.shape[1] // 3 // nc
    num_experts = w_router.shape[1]
    down_rows = w_shared_down.shape[0]
    own_units = w_gate_up.shape[1] // 2 // nc
    half_units = w_experts_in.shape[2] // 4
    hbm, vm, sm = pl.ANY, pltpu.VMEM, pltpu.SMEM
    dma = pltpu.SemaphoreType.DMA

    small = jnp.concatenate([w_router, gain_attn[:, None], gain_ffn[:, None]], axis=1)
    small = jnp.pad(small, ((0, 0), (0, SMALL - small.shape[1])))
    every = jnp.arange(full_len, dtype=jnp.int32)
    inside = every % shard_len
    low = every // shard_len * half_len + inside % half_len
    cosines, sines = rope_tables(jnp.where(inside >= half_len, full_len - 1 - low, low))
    turns = jnp.concatenate([cosines] * 4 + [sines] * 4, axis=1)

    seq_shape = (num_seqs, shard_len, width)
    group_shape = (num_seqs, nc, shard_len, width)
    blocks = (nc, nz, 2, rows_w)
    half_blocks = (nc, nz, rows_w)
    wide_cols = 3 * head_width + SMALL
    num_slots = num_experts * ROWS
    row_box = (num_experts, 2, ROWS, width)
    plane_tok = nc * tok
    outs = [
        (seq_shape, BF),
        (seq_shape, F32),
        ((nc, rows_w, wide_cols), BF),
        ((nc, rows_w, 2 * own_units), BF),
        ((down_rows, width), F32),
        ((rows_w, width), F32),
        (w_experts_in.shape, BF),
        (w_experts_out.shape, BF),
    ]
    out, gin, fq, fgu, fsd, fwo, ein, eout = pl.pallas_call(
        functools.partial(block_kernel, nc, nz),
        out_shape=[jax.ShapeDtypeStruct(shape, dtype) for shape, dtype in outs],
        in_specs=[
            pl.BlockSpec(memory_space=space) for space in [sm] + [vm] * 9 + [hbm, hbm, vm]
        ],
        out_specs=[pl.BlockSpec(memory_space=space) for space in [vm] * 6 + [hbm, hbm]],
        scratch_shapes=[
            vmem(*group_shape),
            vmem(*seq_shape),
            vmem(*group_shape),
            vmem(nc, rows_w, wide_cols),
            vmem(nc, rows_w, wide_cols),
            vmem(*blocks, wide_cols),
            vmem(width, wide_cols),
            vmem(nc, rows_w, 2 * own_units),
            vmem(*blocks, 2 * own_units),
            vmem(width, 2 * own_units),
            vmem(nc, rows_w, width),
            vmem(*blocks, width),
            vmem(width, width),
            vmem(own_units, width),
            vmem(width, 2 * half_units),
            vmem(half_units, width),
            vmem(num_seqs, full_len, width),
            vmem(num_seqs, full_len, 3 * head_width),
            vmem(nc, num_seqs, nc, shard_len, head_width),
            vmem(*seq_shape, dtype=F32),
            vmem(*group_shape),
            vmem(*row_box),
            vmem(2, nz, nc, 2, ROWS, width),
            vmem(2 * num_slots, width),
            vmem(2 * num_slots, width),
            vmem(plane_tok, width, dtype=F32),
            vmem(plane_tok, width, dtype=F32),
            vmem(2, *seq_shape, dtype=F32),
            vmem(plane_tok, own_units),
            vmem(plane_tok, 2 * own_units),
            vmem(2, *group_shape),
            vmem(nc - 1, 2, *seq_shape),
            vmem(2 * num_slots, half_units),
            vmem(2 * num_slots, 2 * half_units),
            vmem(*row_box),
            vmem(*row_box),
            vmem(*row_box),
            vmem(nz, 2, down_rows, width),
            vmem(*seq_shape),
            vmem(nc, num_seqs, shard_len, head_width),
            vmem(num_seqs, nc, shard_len, head_width),
            vmem(*group_shape),
            vmem(*group_shape, dtype=F32),
            vmem(nc - 1, *seq_shape),
            vmem(*half_blocks, 2 * own_units),
            vmem(nz - 1, nc, rows_w, 2 * own_units),
            vmem(nc, rows_w, 2 * own_units),
            vmem(*half_blocks, wide_cols),
            vmem(nz - 1, nc, rows_w, wide_cols),
            vmem(nc, rows_w, wide_cols),
            vmem(nz, down_rows, width),
            vmem(nz - 1, down_rows, width),
            vmem(*half_blocks, width),
            vmem(nz - 1, nc, rows_w, width),
            vmem(nc, rows_w, width),
            vmem(nc, rows_w, width),
            dma((200,)),
            dma((200,)),
            dma((nc,)),
            dma((nc,)),
            dma((nc,)),
            dma((nc,)),
            dma((6,)),
        ],
        compiler_params=pltpu.CompilerParams(
            collective_id=0, has_side_effects=True, vmem_limit_bytes=VMEM_BYTES
        ),
        cost_estimate=pl.CostEstimate(
            flops=16_000_000_000, bytes_accessed=30_000_000, transcendentals=0
        ),
        name="block_forward_backward",
    )(
        seq_lengths,
        hidden_in.reshape(seq_shape),
        grad_output.reshape(seq_shape),
        expert_ids.reshape(tok, 2),
        route_rank.reshape(1, tok),
        w_qkv, small, w_gate_up, w_out, w_shared_down, w_experts_in, w_experts_out, turns,
    )

    def whole(shape):
        return pl.BlockSpec(shape, lambda e: (0,) * len(shape))

    def one(shape):
        return pl.BlockSpec((1,) + shape[1:], lambda e: (e, 0, 0))

    ins = [fq, fgu, w_qkv, gain_attn.reshape(1, rows_w), ein, eout, out, gin, fsd, fwo]
    results = [
        (w_qkv.shape, F32),
        (w_router.shape, F32),
        ((2, rows_w), F32),
        (w_gate_up.shape, F32),
        (ein.shape, F32),
        (eout.shape, F32),
        (seq_shape, BF),
        (seq_shape, F32),
        (fsd.shape, F32),
        (fwo.shape, F32),
    ]
    grad_qkv, grad_router, gains, grad_gu, grad_in, grad_out, out, gin, fsd, fwo = pl.pallas_call(
        functools.partial(finish_kernel, nc),
        grid=(ein.shape[0],),
        out_shape=[jax.ShapeDtypeStruct(shape, dtype) for shape, dtype in results],
        in_specs=[one(x.shape) if i in (4, 5) else whole(x.shape) for i, x in enumerate(ins)],
        out_specs=[
            one(shape) if i in (4, 5) else whole(shape) for i, (shape, _) in enumerate(results)
        ],
        compiler_params=pltpu.CompilerParams(vmem_limit_bytes=VMEM_BYTES),
        name="widen_gradients",
    )(*ins)
    return (
        out.reshape(hidden_in.shape),
        gin.reshape(hidden_in.shape),
        gains[0],
        grad_qkv,
        fwo,
        grad_router,
        gains[1],
        grad_gu,
        fsd,
        grad_in,
        grad_out,
    )


def fits(mesh, hidden_in, w_qkv, w_router, w_gate_up, w_experts_in):
    nc, nz, nf = mesh.shape["ctx"], mesh.shape["exp"], mesh.shape["fsdp"]
    heads = w_qkv.shape[1] // 3 // HS
    return (
        nf == 2
        and nc == 4
        and nz == 4
        and heads == 12
        and w_router.shape[1] == nc * nz
        and w_qkv.shape[0] == 768
        and hidden_in.shape[2] == 32 * nc
        and hidden_in.shape[0] == 2 * nz * nf
        and hidden_in.shape[3] == 768
        and w_gate_up.shape[1] == w_experts_in.shape[2] == 4096
        and CAP <= ROWS
    )


def solution(mesh):
    def whole(*args):
        chosen = fast_device if fits(mesh, args[0], args[5], args[7], args[9], args[11]) else per_device
        return placed(mesh, chosen)(*args)

    return whole


def placed(mesh, chosen):
    return jax.shard_map(
        chosen,
        mesh=mesh,
        in_specs=(
            P(("exp", "fsdp"), None, "ctx", None),
            P(("exp", "fsdp")),
            P(("exp", "fsdp"), None, "ctx", None),
            P(("exp", "fsdp"), "ctx", None),
            P(("ctx", "exp", "fsdp")),
            P(("ctx", "exp", "fsdp"), None),
            P(("ctx", "exp", "fsdp"), None),
            P(("ctx", "exp", "fsdp"), None),
            P(("ctx", "exp", "fsdp")),
            P(("ctx", "exp", "fsdp"), None),
            P(("ctx", "exp", "fsdp"), None),
            P("exp", ("ctx", "fsdp"), None),
            P("exp", ("ctx", "fsdp"), None),
            P(("exp", "fsdp"), None, "ctx", None),
        ),
        out_specs=(
            P(("exp", "fsdp"), None, "ctx", None),
            P(("exp", "fsdp"), None, "ctx", None),
            P(("ctx", "exp", "fsdp")),
            P(("ctx", "exp", "fsdp"), None),
            P(("ctx", "exp", "fsdp"), None),
            P(("ctx", "exp", "fsdp"), None),
            P(("ctx", "exp", "fsdp")),
            P(("ctx", "exp", "fsdp"), None),
            P(("ctx", "exp", "fsdp"), None),
            P("exp", ("ctx", "fsdp"), None),
            P("exp", ("ctx", "fsdp"), None),
        ),
        check_vma=False,
    )
```

```python
import functools
import math

import jax
import jax.numpy as jnp
from jax import lax
from jax.experimental import pallas as pl
from jax.experimental.pallas import tpu as pltpu
from jax.sharding import PartitionSpec as P

HS = 64
CAP = 18


epsilon = 1e-06
masked_out = -1e30
highest = lax.Precision.HIGHEST


def rms_norm(values_in, gain_row):
    return (
        values_in
        * lax.rsqrt(jnp.mean(values_in * values_in, axis=-1, keepdims=True) + epsilon)
        * gain_row
    )


def rope_tables(places):
    half_size = HS // 2
    frequency = 10000.0 ** (-jnp.arange(half_size, dtype=jnp.float32) * 2.0 / HS)
    angles = places.astype(jnp.float32)[:, None] * frequency[None, :]
    return (jnp.cos(angles), jnp.sin(angles))


def rotate(values_in, cosines, sine_rows):
    half_size = values_in.shape[-1] // 2
    leading = values_in[..., :half_size]
    trailing = values_in[..., half_size:]
    cos_rows = cosines[:, None, :]
    sin_rows = sine_rows[:, None, :]
    return jnp.concatenate(
        [leading * cos_rows - trailing * sin_rows, leading * sin_rows + trailing * cos_rows],
        axis=-1,
    )


def swiglu(merged_rows):
    gate_part, up_part = jnp.split(merged_rows, 2, axis=-1)
    return jax.nn.silu(gate_part) * up_part


def first_t(left_side, right_side, precision=None):
    return lax.dot_general(
        left_side,
        right_side,
        (((0,), (0,)), ((), ())),
        precision=precision,
        preferred_element_type=jnp.float32,
    )


def second_t(left_side, right_side, precision=None):
    return lax.dot_general(
        left_side,
        right_side,
        (((1,), (1,)), ((), ())),
        precision=precision,
        preferred_element_type=jnp.float32,
    )


def per_device(
    hidden_in,
    seq_lengths,
    expert_ids,
    route_rank,
    gain_attn,
    w_qkv,
    w_out,
    w_router,
    gain_ffn,
    w_gate_up,
    w_shared_down,
    w_experts_in,
    w_experts_out,
    grad_output,
):
    num_seqs, two_ends, half_len, model_width = hidden_in.shape
    shard_len = 2 * half_len
    tok_count = num_seqs * shard_len
    num_heads = model_width // HS
    score_scale = HS ** (-0.5)
    ctx_size = lax.axis_size("ctx")
    full_len = shard_len * ctx_size
    whole_half = half_len * ctx_size
    gain_one, wqkv_all, wout_all, router_all, gain_two, shared_in, shared_down = (
        lax.all_gather(gain_attn, ("ctx", "exp", "fsdp"), axis=0, tiled=True),
        lax.all_gather(w_qkv, ("ctx", "exp", "fsdp"), axis=0, tiled=True),
        lax.all_gather(w_out, ("ctx", "exp", "fsdp"), axis=0, tiled=True),
        lax.all_gather(w_router, ("ctx", "exp", "fsdp"), axis=0, tiled=True),
        lax.all_gather(gain_ffn, ("ctx", "exp", "fsdp"), axis=0, tiled=True),
        lax.all_gather(w_gate_up, ("ctx", "exp", "fsdp"), axis=0, tiled=True),
        lax.all_gather(w_shared_down, ("ctx", "exp", "fsdp"), axis=0, tiled=True),
    )
    experts_in, experts_out = (
        lax.all_gather(w_experts_in, ("ctx", "fsdp"), axis=1, tiled=True),
        lax.all_gather(w_experts_out, ("ctx", "fsdp"), axis=1, tiled=True),
    )
    lower_places = lax.axis_index("ctx") * half_len + jnp.arange(half_len, dtype=jnp.int32)
    places = jnp.concatenate([lower_places, full_len - 1 - lower_places])
    whole_range = jnp.arange(whole_half, dtype=jnp.int32)
    full_places = jnp.concatenate([whole_range, full_len - 1 - whole_range])
    live_mask = (places[None, :] < seq_lengths[:, None]).astype(jnp.float32)
    live_rows = live_mask.reshape(tok_count, 1)
    inputs_f = hidden_in.astype(jnp.float32).reshape(tok_count, model_width)
    gain_attn_f = gain_one.astype(jnp.float32)
    normed_b = rms_norm(inputs_f, gain_attn_f).astype(jnp.bfloat16)
    qkv_merged = jnp.dot(normed_b, wqkv_all, preferred_element_type=jnp.float32).reshape(
        num_seqs, shard_len, 3, num_heads, HS
    )
    cosines, sine_rows = rope_tables(places)
    queries = rotate(qkv_merged[:, :, 0], cosines, sine_rows).astype(jnp.bfloat16)
    keys_local = rotate(qkv_merged[:, :, 1], cosines, sine_rows).astype(jnp.bfloat16)
    values_local = qkv_merged[:, :, 2].astype(jnp.bfloat16)
    end_shape = (num_seqs, 2, half_len, model_width)
    keys_full, values_full = (
        lax.all_gather(keys_local.reshape(end_shape), "ctx", axis=2, tiled=True),
        lax.all_gather(values_local.reshape(end_shape), "ctx", axis=2, tiled=True),
    )
    keys_full = keys_full.reshape(num_seqs, full_len, num_heads, HS)
    values_full = values_full.reshape(num_seqs, full_len, num_heads, HS)
    stat_shape = (num_seqs, num_heads, shard_len)
    block_range = jnp.arange(ctx_size, dtype=jnp.int32)

    def block_scores(query_rows, query_places, key_rows, key_places):
        scores = (
            jnp.einsum("bqhd,bkhd->bhqk", query_rows, key_rows, preferred_element_type=jnp.float32)
            * score_scale
        )
        allowed = (key_places[None, None, :] <= query_places[None, :, None]) & (
            key_places[None, None, :] < seq_lengths[:, None, None]
        )
        return jnp.where(allowed[:, None], scores, masked_out)

    def key_block(block_idx):
        offset = block_idx * shard_len
        return (
            lax.dynamic_slice_in_dim(keys_full, offset, shard_len, 1),
            lax.dynamic_slice_in_dim(values_full, offset, shard_len, 1),
            lax.dynamic_slice_in_dim(full_places, offset, shard_len, 0),
        )

    def lse_step(state_in, block_idx):
        run_max, run_sum = state_in
        key_rows, value_rows, key_places = key_block(block_idx)
        scores = block_scores(queries, places, key_rows, key_places)
        new_max = jnp.maximum(run_max, jnp.max(scores, axis=-1))
        run_sum = run_sum * jnp.exp(run_max - new_max) + jnp.sum(
            jnp.exp(scores - new_max[..., None]), axis=-1
        )
        return ((new_max, run_sum), None)

    (row_max, row_sum), unused = lax.scan(
        lse_step,
        (jnp.full(stat_shape, masked_out, jnp.float32), jnp.zeros(stat_shape, jnp.float32)),
        block_range,
    )
    log_total = row_max + jnp.log(row_sum)

    def context_step(running, block_idx):
        key_rows, value_rows, key_places = key_block(block_idx)
        prob_rows = jnp.exp(
            block_scores(queries, places, key_rows, key_places) - log_total[..., None]
        ).astype(jnp.bfloat16)
        return (
            running
            + jnp.einsum(
                "bhqk,bkhd->bqhd", prob_rows, value_rows, preferred_element_type=jnp.float32
            ),
            None,
        )

    context, unused = lax.scan(
        context_step, jnp.zeros((num_seqs, shard_len, num_heads, HS), jnp.float32), block_range
    )
    context_b = context.reshape(tok_count, model_width).astype(jnp.bfloat16)
    attended = inputs_f + jnp.dot(context_b, wout_all, preferred_element_type=jnp.float32)
    gain_ffn_f = gain_two.astype(jnp.float32)
    normed_two = rms_norm(attended, gain_ffn_f).astype(jnp.bfloat16)
    logits = jnp.dot(normed_two, router_all, preferred_element_type=jnp.float32)
    num_experts = router_all.shape[1]
    expert_range = jnp.arange(num_experts, dtype=jnp.int32)
    picked_ids = expert_ids.reshape(tok_count, 2)
    pick_hot = (picked_ids[:, :, None] == expert_range).astype(jnp.float32)
    chosen = jnp.sum(pick_hot * logits[:, None, :], axis=-1)
    gate_probs = jax.nn.softmax(chosen, axis=-1)
    expert_load = (jnp.sum(pick_hot, axis=1) * live_rows).astype(jnp.bfloat16)
    rank_rows = route_rank.reshape(tok_count)
    earlier = (rank_rows[None, :] < rank_rows[:, None]).astype(jnp.bfloat16)
    position = jnp.dot(earlier, expert_load, preferred_element_type=jnp.float32)
    chosen_pos = jnp.sum(pick_hot * position[:, None, :], axis=-1)
    kept_mask = live_rows * (chosen_pos < CAP).astype(jnp.float32)
    slot_hot = (chosen_pos[:, :, None] == jnp.arange(CAP, dtype=jnp.float32)).astype(jnp.float32)
    dispatch = (
        (pick_hot[:, :, :, None] * slot_hot[:, :, None, :] * kept_mask[:, :, None, None])
        .reshape(tok_count, 2, num_experts * CAP)
        .astype(jnp.bfloat16)
    )
    dispatch_any = dispatch[:, 0] + dispatch[:, 1]
    exp_size = lax.axis_size("exp")
    per_owner = num_experts // exp_size
    send_rows = (
        first_t(dispatch_any, normed_two)
        .astype(jnp.bfloat16)
        .reshape(exp_size, per_owner, CAP, model_width)
    )
    arrived = lax.all_to_all(send_rows, "exp", split_axis=0, concat_axis=0, tiled=True)
    expert_merged = jnp.einsum(
        "secd,edf->secf", arrived, experts_in, preferred_element_type=jnp.float32
    )
    expert_hidden = swiglu(expert_merged).astype(jnp.bfloat16)
    expert_result = jnp.einsum(
        "secf,efd->secd", expert_hidden, experts_out, preferred_element_type=jnp.float32
    ).astype(jnp.bfloat16)
    returned = lax.all_to_all(
        expert_result, "exp", split_axis=0, concat_axis=0, tiled=True
    ).reshape(num_experts * CAP, model_width)
    routed = jnp.einsum("tks,sd->tkd", dispatch, returned, preferred_element_type=jnp.float32)
    mixture = jnp.sum(gate_probs[:, :, None] * routed, axis=1)
    shared_merged = jnp.dot(normed_two, shared_in, preferred_element_type=jnp.float32)
    shared_hidden = swiglu(shared_merged).astype(jnp.bfloat16)
    shared_result = jnp.dot(shared_hidden, shared_down, preferred_element_type=jnp.float32)
    layer_out = (
        (live_rows * (attended + mixture + shared_result)).reshape(end_shape).astype(jnp.bfloat16)
    )
    upstream = grad_output.astype(jnp.float32).reshape(tok_count, model_width) * live_rows
    upstream_b = upstream.astype(jnp.bfloat16)
    upstream_f = upstream_b.astype(jnp.float32)
    d_shared_down = first_t(shared_hidden, upstream_b)
    d_shared_hidden = second_t(upstream_b, shared_down)
    unused, swiglu_pull = jax.vjp(swiglu, shared_merged)
    d_shared_merged = swiglu_pull(d_shared_hidden)[0].astype(jnp.bfloat16)
    d_shared_in = first_t(normed_two, d_shared_merged)
    d_normed_two = second_t(d_shared_merged, shared_in)
    gate_grads = jnp.sum(routed * upstream_f[:, None, :], axis=-1)
    weighted = (gate_probs[:, :, None] * upstream_f[:, None, :]).astype(jnp.bfloat16)
    d_returned = (
        jnp.einsum("tks,tkd->sd", dispatch, weighted, preferred_element_type=jnp.float32)
        .astype(jnp.bfloat16)
        .reshape(exp_size, per_owner, CAP, model_width)
    )
    d_result = lax.all_to_all(d_returned, "exp", split_axis=0, concat_axis=0, tiled=True)
    d_experts_out = jnp.einsum(
        "secf,secd->efd", expert_hidden, d_result, preferred_element_type=jnp.float32
    )
    d_expert_hidden = jnp.einsum(
        "secd,efd->secf", d_result, experts_out, preferred_element_type=jnp.float32
    )
    unused, expert_pull = jax.vjp(swiglu, expert_merged)
    d_expert_merged = expert_pull(d_expert_hidden)[0].astype(jnp.bfloat16)
    d_experts_in = jnp.einsum(
        "secd,secf->edf", arrived, d_expert_merged, preferred_element_type=jnp.float32
    )
    d_arrived = jnp.einsum(
        "secf,edf->secd", d_expert_merged, experts_in, preferred_element_type=jnp.float32
    ).astype(jnp.bfloat16)
    d_sent = lax.all_to_all(d_arrived, "exp", split_axis=0, concat_axis=0, tiled=True).reshape(
        num_experts * CAP, model_width
    )
    d_normed_two = d_normed_two + jnp.dot(dispatch_any, d_sent, preferred_element_type=jnp.float32)
    unused, gate_pull = jax.vjp(lambda chosen_in: jax.nn.softmax(chosen_in, axis=-1), chosen)
    d_chosen = gate_pull(gate_grads)[0]
    d_logits = jnp.sum(pick_hot * d_chosen[:, :, None], axis=1)
    d_router = first_t(normed_two.astype(jnp.float32), d_logits, highest)
    d_normed_two = d_normed_two + second_t(d_logits, router_all.astype(jnp.float32), highest)
    unused, second_pull = jax.vjp(rms_norm, attended, gain_ffn_f)
    d_attended, d_gain_ffn = second_pull(d_normed_two)
    d_attended = d_attended + upstream
    d_attended_b = d_attended.astype(jnp.bfloat16)
    d_out_proj = first_t(context_b, d_attended_b)
    d_context = (
        second_t(d_attended_b, wout_all)
        .astype(jnp.bfloat16)
        .reshape(num_seqs, shard_len, num_heads, HS)
    )

    def score_grads(
        query_rows, query_places, key_rows, value_rows, key_places, d_rows, lse_rows, delta_rows
    ):
        prob_rows = jnp.exp(
            block_scores(query_rows, query_places, key_rows, key_places) - lse_rows[..., None]
        )
        d_probs = jnp.einsum(
            "bqhd,bkhd->bhqk", d_rows, value_rows, preferred_element_type=jnp.float32
        )
        d_scores = (prob_rows * (d_probs - delta_rows[..., None])).astype(jnp.bfloat16)
        return (prob_rows.astype(jnp.bfloat16), d_scores)

    def delta_step(running, block_idx):
        key_rows, value_rows, key_places = key_block(block_idx)
        prob_rows = jnp.exp(
            block_scores(queries, places, key_rows, key_places) - log_total[..., None]
        )
        d_probs = jnp.einsum(
            "bqhd,bkhd->bhqk", d_context, value_rows, preferred_element_type=jnp.float32
        )
        return (running + jnp.sum(prob_rows * d_probs, axis=-1), None)

    row_delta, unused = lax.scan(delta_step, jnp.zeros(stat_shape, jnp.float32), block_range)
    head_shape = (num_seqs, shard_len, num_heads, HS)

    def query_step(d_query, block_idx):
        key_rows, value_rows, key_places = key_block(block_idx)
        prob_b, d_scores = score_grads(
            queries, places, key_rows, value_rows, key_places, d_context, log_total, row_delta
        )
        return (
            d_query
            + jnp.einsum("bhqk,bkhd->bqhd", d_scores, key_rows, preferred_element_type=jnp.float32)
            * score_scale,
            None,
        )

    d_query, unused = lax.scan(query_step, jnp.zeros(head_shape, jnp.float32), block_range)
    query_all, d_context_all = (
        lax.all_gather(queries.reshape(end_shape), "ctx", axis=2, tiled=True),
        lax.all_gather(d_context.reshape(end_shape), "ctx", axis=2, tiled=True),
    )
    stat_ends = (num_seqs, num_heads, 2, half_len)
    lse_all, delta_all = (
        lax.all_gather(log_total.reshape(stat_ends), "ctx", axis=3, tiled=True),
        lax.all_gather(row_delta.reshape(stat_ends), "ctx", axis=3, tiled=True),
    )
    query_all = query_all.reshape(num_seqs, full_len, num_heads, HS)
    d_context_all = d_context_all.reshape(num_seqs, full_len, num_heads, HS)
    lse_all = lse_all.reshape(num_seqs, num_heads, full_len)
    delta_all = delta_all.reshape(num_seqs, num_heads, full_len)

    def owner_step(state_in, block_idx):
        d_keys, d_values = state_in
        offset = block_idx * shard_len
        query_rows = lax.dynamic_slice_in_dim(query_all, offset, shard_len, 1)
        d_rows = lax.dynamic_slice_in_dim(d_context_all, offset, shard_len, 1)
        lse_rows = lax.dynamic_slice_in_dim(lse_all, offset, shard_len, 2)
        delta_rows = lax.dynamic_slice_in_dim(delta_all, offset, shard_len, 2)
        query_places = lax.dynamic_slice_in_dim(full_places, offset, shard_len, 0)
        prob_b, d_scores = score_grads(
            query_rows, query_places, keys_local, values_local, places, d_rows, lse_rows, delta_rows
        )
        d_keys = (
            d_keys
            + jnp.einsum(
                "bhqk,bqhd->bkhd", d_scores, query_rows, preferred_element_type=jnp.float32
            )
            * score_scale
        )
        d_values = d_values + jnp.einsum(
            "bhqk,bqhd->bkhd", prob_b, d_rows, preferred_element_type=jnp.float32
        )
        return ((d_keys, d_values), None)

    (d_keys_local, d_values_local), unused = lax.scan(
        owner_step,
        (jnp.zeros(head_shape, jnp.float32), jnp.zeros(head_shape, jnp.float32)),
        block_range,
    )
    unused, rope_pull = jax.vjp(
        lambda rows_in: rotate(rows_in, cosines, sine_rows), qkv_merged[:, :, 0]
    )
    d_query_pre = rope_pull(d_query)[0]
    d_key_pre = rope_pull(d_keys_local)[0]
    d_qkv_merged = (
        jnp.stack([d_query_pre, d_key_pre, d_values_local], axis=2)
        .reshape(tok_count, 3 * model_width)
        .astype(jnp.bfloat16)
    )
    d_qkv = first_t(normed_b, d_qkv_merged)
    d_normed = second_t(d_qkv_merged, wqkv_all)
    unused, first_pull = jax.vjp(rms_norm, inputs_f, gain_attn_f)
    d_inputs, d_gain_attn = first_pull(d_normed)
    grad_input = (d_attended + d_inputs).reshape(end_shape)
    dense_sums = (
        lax.psum_scatter(d_gain_attn, ("ctx", "exp", "fsdp"), scatter_dimension=0, tiled=True),
        lax.psum_scatter(d_qkv, ("ctx", "exp", "fsdp"), scatter_dimension=0, tiled=True),
        lax.psum_scatter(d_out_proj, ("ctx", "exp", "fsdp"), scatter_dimension=0, tiled=True),
        lax.psum_scatter(d_router, ("ctx", "exp", "fsdp"), scatter_dimension=0, tiled=True),
        lax.psum_scatter(d_gain_ffn, ("ctx", "exp", "fsdp"), scatter_dimension=0, tiled=True),
        lax.psum_scatter(d_shared_in, ("ctx", "exp", "fsdp"), scatter_dimension=0, tiled=True),
        lax.psum_scatter(d_shared_down, ("ctx", "exp", "fsdp"), scatter_dimension=0, tiled=True),
    )
    expert_sums = (
        lax.psum_scatter(
            d_experts_in.astype(jnp.bfloat16), ("ctx", "fsdp"), scatter_dimension=1, tiled=True
        ).astype(jnp.float32),
        lax.psum_scatter(
            d_experts_out.astype(jnp.bfloat16), ("ctx", "fsdp"), scatter_dimension=1, tiled=True
        ).astype(jnp.float32),
    )
    return (
        layer_out,
        grad_input,
        dense_sums[0],
        dense_sums[1],
        dense_sums[2],
        dense_sums[3],
        dense_sums[4],
        dense_sums[5],
        dense_sums[6],
        expert_sums[0],
        expert_sums[1],
    )


F32 = jnp.float32
BF = jnp.bfloat16
MESH = pl.DeviceIdType.MESH
BOX = 40
SMALL = 64
VMEM_BYTES = 63 * 1024 * 1024
PUMPS = (2, 10, 8)
POSTS = 64
HOME = 512
WIDEN = 1


def place():
    return lax.axis_index("ctx"), lax.axis_index("exp"), lax.axis_index("fsdp")


def wrap(value, size):
    return lax.rem(value, size)


def mm(left, right):
    return lax.dot_general(
        left, right, (((1,), (0,)), ((), ())), preferred_element_type=F32
    )


def mm_nt(left, right):
    return lax.dot_general(
        left, right, (((1,), (1,)), ((), ())), preferred_element_type=F32
    )


def mm_tn(left, right):
    return lax.dot_general(
        left, right, (((0,), (0,)), ((), ())), preferred_element_type=F32
    )


def greet(peers):
    barrier = pltpu.get_barrier_semaphore()
    for peer in peers:
        pl.semaphore_signal(barrier, inc=1, device_id=peer, device_id_type=MESH)


def met(peers):
    pl.semaphore_wait(pltpu.get_barrier_semaphore(), len(peers))


class Post:
    def __init__(self, send, recv, like, device):
        self.send, self.recv, self.like, self.device = send, recv, like, device

    def add(self, src, dst, device):
        pltpu.make_async_remote_copy(
            src_ref=src,
            dst_ref=dst,
            send_sem=self.send,
            recv_sem=self.recv,
            device_id=device,
            device_id_type=MESH,
        ).start()

    def all_of_it(self, like=None):
        like = self.like if like is None else like
        return pltpu.make_async_remote_copy(
            src_ref=like,
            dst_ref=like,
            send_sem=self.send,
            recv_sem=self.recv,
            device_id=self.device,
            device_id_type=MESH,
        )

    def wait_recv(self, like=None):
        self.all_of_it(like).wait_recv()

    def wait_send(self, like=None):
        self.all_of_it(like).wait_send()


class Courier:
    def __init__(self, send, recv, device):
        self.send, self.recv, self.device, self.count, self.sent = send, recv, device, 0, []

    def open(self, like, keep=True):
        post = Post(self.send.at[self.count], self.recv.at[self.count], like, self.device)
        self.count += 1
        if keep:
            self.sent.append(post)
        return post

    def post(self, like, moves):
        post = self.open(like)
        for src, dst, device in moves:
            post.add(src, dst, device)
        return post

    def settle(self, posts):
        for post in posts:
            post.wait_send()
        done = {id(post) for post in posts}
        self.sent = [post for post in self.sent if id(post) not in done]

    def finish(self):
        self.settle(list(self.sent))


def swap_halves(rows):
    width = rows.shape[1]
    lane = lax.broadcasted_iota(jnp.int32, rows.shape, 1)
    ahead = pltpu.roll(rows, width - HS // 2, 1)
    behind = pltpu.roll(rows, HS // 2, 1)
    return jnp.where((lane & (HS - 1)) < HS // 2, -ahead, behind)


def wide(table, times):
    return jnp.concatenate([table] * times, axis=1)


def position_of(index, half_len, full_len):
    block = index // (2 * half_len)
    inside = index & (2 * half_len - 1)
    low = block * half_len + (inside & (half_len - 1))
    return jnp.where(inside >= half_len, full_len - 1 - low, low)


def allowed_keys(length, half_len, full_len):
    shape = (full_len, full_len)
    query_at = position_of(lax.broadcasted_iota(jnp.int32, shape, 0), half_len, full_len)
    key_at = position_of(lax.broadcasted_iota(jnp.int32, shape, 1), half_len, full_len)
    return (key_at <= query_at) & (key_at < length)


def head_probs(query, key, allowed):
    scores = jnp.where(allowed, mm_nt(query, key) * (HS**-0.5), masked_out)
    weights = jnp.exp(scores - jnp.max(scores, axis=1, keepdims=True))
    return weights * (1.0 / jnp.sum(weights, axis=1, keepdims=True))


def column_row(tail, lane):
    pick = (lax.broadcasted_iota(jnp.int32, (8, 128), 1) == lane).astype(BF)
    return mm_nt(pick, tail)[0:1]


def split_dot(dot, left, right, left_wide=True):
    whole = left if left_wide else right
    high = whole.astype(BF)
    low = (whole - high.astype(F32)).astype(BF)
    if left_wide:
        return dot(high, right) + dot(low, right)
    return dot(left, high) + dot(left, low)


def inverse_rms(rows):
    return lax.rsqrt(jnp.mean(rows * rows, axis=1, keepdims=True) + epsilon)


def norm_back(rows, inverse, scaled):
    return inverse * scaled - rows * (inverse * inverse * inverse) * jnp.mean(
        rows * scaled, axis=1, keepdims=True
    )


def join(blocks, shape):
    return blocks.astype(F32).reshape(shape).astype(BF)


def ffn_block(j, rows, grads, in_ref, out_ref, hidden_ref, dm_ref, result, back, units, step):
    low = pl.multiple_of(j * step, step) if not isinstance(j, int) else j * step
    high = pl.multiple_of(units + low, step) if not isinstance(j, int) else units + low
    gate_at, up_at = pl.ds(low, step), pl.ds(high, step)
    gate, up = mm(rows, in_ref[:, gate_at]), mm(rows, in_ref[:, up_at])
    down = out_ref[gate_at, :]
    d_hidden = mm_nt(grads, down)
    share = 1.0 / (1.0 + jnp.exp(-gate))
    lit = gate * share
    hidden = (lit * up).astype(BF)
    d_gate = (d_hidden * up * (share * (1.0 + gate * (1.0 - share)))).astype(BF)
    d_up = (d_hidden * lit).astype(BF)
    hidden_ref[:, gate_at] = hidden
    dm_ref[:, gate_at] = d_gate
    dm_ref[:, up_at] = d_up
    result[...] += mm(hidden, down)
    back[...] += mm_nt(d_gate, in_ref[:, gate_at]) + mm_nt(d_up, in_ref[:, up_at])


def box_rows(kept_rows, boxes, shift):
    shape = (boxes * kept_rows, boxes * BOX)
    row = lax.broadcasted_iota(jnp.int32, shape, 0)
    column = lax.broadcasted_iota(jnp.int32, shape, 1)
    box = jnp.floor((column.astype(F32) + 0.5) * (1.0 / BOX)).astype(jnp.int32)
    at = column - box * BOX - shift
    return ((at >= 0) & (at < kept_rows) & (row == box * kept_rows + at)).astype(BF)


def block_kernel(
    nc, nz,
    len_ref, hid_ref, go_ref, ids_ref, rank_ref, wqkv_ref, router_ref, ga_ref, gf_ref, gu_ref,
    wo_ref, sd_ref, win_ref, wout_ref,
    out_ref, gin_ref, fq_ref, fgu_ref, fsd_ref, fwo_ref, ein_ref, eout_ref,
    turn_ref, hid_all, up_own, up_all, wq_own, wq_st, wq_buf, w_ref, gu_st, gu_buf, gu_all, wo_st, wo_buf,
    wo_all, sd_all, wie, woe, normed_ref, qkv_ref, ctx_all, att_own, nt_all,
    sb, ar, xs, ds, acc_a, acc_b, sh_own, sh_hidden, sh_dm, sh_send, sh_in, sh_mid, sh_end,
    ex_hidden, ex_dm, pin, fb, rb, gsd, da_own, dctx_send, dctx_all, part, part_own, rs_in, rs_mid, rs_end,
    sib_gu, zi_gu, pb_gu, sib_q, zi_q, pb_q, sib_sd, zi_sd, sib_wo, zi_wo, pb_wo, in_wo,
    send, recv, lsem,
):
    c, z, f = place()
    near_x, near_y = c + 1 - 2 * wrap(c, 2), wrap(c + 2, nc)
    far = wrap(near_x + 2, nc)
    to_x, to_y = (near_x, z, f), (near_y, z, f)
    in_plane = [(wrap(c + s, nc), z, f) for s in range(1, nc)]
    in_column = [(c, wrap(z + s, nz), f) for s in range(1, nz)]
    sibling = (c, z, 1 - f)
    across = [(wrap(c + s, nc), z, 1 - f) for s in range(1, nc)]
    ring = [(dz, dc) for dz in range(nz) for dc in range(nc) if dz or dc]
    everyone = [(wrap(c + dc, nc), wrap(z + dz, nz), f) for dz, dc in ring]
    with jax.named_scope("s_greet"):
        greet(everyone + [sibling] + across)

    num_seqs, shard_len, width = hid_ref.shape
    full_len = nc * shard_len
    half_len = shard_len // 2
    tok = num_seqs * shard_len
    rows_w = wqkv_ref.shape[0]
    head_width = wqkv_ref.shape[1] // 3 // nc
    heads_here = head_width // HS
    wide_cols = wq_own.shape[2]
    units = gu_ref.shape[1] // 2
    own_units = units // nc
    down_rows = sd_ref.shape[0]
    num_experts = nz * nc
    num_slots = num_experts * CAP
    box_slots = num_experts * BOX
    block_rows = nz * 2 * rows_w
    mail = Courier(send, recv, sibling)

    small = jnp.concatenate(
        [
            router_ref[...].astype(F32),
            ga_ref[...].astype(F32),
            gf_ref[...].astype(F32),
            jnp.zeros((128 - num_experts - 2, rows_w), F32),
        ],
        axis=0,
    )
    small = jnp.concatenate([small, jnp.zeros((128, 128 - rows_w), F32)], axis=1)
    small = jnp.transpose(small, (1, 0))[:rows_w, :SMALL].astype(BF)
    for owner in range(nc):
        wq_own[owner] = jnp.concatenate(
            [
                wqkv_ref[:, side * width + owner * head_width : side * width + (owner + 1) * head_width]
                for side in range(3)
            ]
            + [small],
            axis=1,
        )
    with jax.named_scope("s_met"):
        met(everyone + [sibling] + across)

    others = pl.ds(0, nc - 1)
    staged_wq = mail.post(
        wq_st.at[others],
        [(wq_own.at[wrap(c + s, nc)], wq_st.at[c], in_plane[s - 1]) for s in range(1, nc)],
    )
    arriving = [
        mail.post(
            hid_all.at[q, pl.ds(0, 2)],
            [(hid_ref.at[q], hid_all.at[q, c], peer) for peer in (to_x, to_y)],
        )
        for q in range(num_seqs)
    ]
    staged_wo = mail.post(wo_st.at[others], [(wo_ref, wo_st.at[c], peer) for peer in in_plane])
    staged_gu = mail.open(gu_st.at[others])
    for s in range(1, nc):
        owner = wrap(c + s, nc)
        for side in range(2):
            at = pl.ds(pl.multiple_of(side * units + owner * own_units, own_units), own_units)
            staged_gu.add(
                gu_ref.at[:, at],
                gu_st.at[c, :, pl.ds(side * own_units, own_units)],
                in_plane[s - 1],
            )

    block = 2 * c + f
    shard_rows = win_ref.shape[1]
    half_units = units // 2
    step = 256
    steps = half_units // step
    lands = pl.ds(pl.multiple_of(block * shard_rows, shard_rows), shard_rows)
    out_rows = wout_ref.shape[1]
    to_core = block // nc
    slot = wrap(block, nc)
    out_lands = pl.ds(pl.multiple_of(slot * out_rows, out_rows), out_rows)
    remote_rows = (2 * nc - 1) * shard_rows
    expert_in = [
        mail.open(wie.at[pl.ds(0, remote_rows), pl.ds(0, 2 * step)]) for _ in range(steps)
    ]
    expert_out = mail.open(woe, keep=False)
    remote_out = woe.at[pl.ds(0, (nc - 1) * out_rows)]
    own_out = pltpu.make_async_copy(wout_ref.at[c], woe.at[out_lands], lsem.at[0])

    def send_out(s):
        owner = wrap(c + s, nc)
        expert_out.add(wout_ref.at[owner], woe.at[out_lands], (owner, z, to_core))

    def send_out_own():
        @pl.when(to_core == f)
        def _():
            own_out.start()

        @pl.when(to_core != f)
        def _():
            expert_out.add(wout_ref.at[c], woe.at[out_lands], sibling)

    def own_in(j):
        like = wie.at[pl.ds(0, shard_rows), pl.ds(0, 2 * step)]
        return pltpu.make_async_copy(like, like, lsem.at[1 + j])

    def send_in(j, s, g, side):
        owner = wrap(c + s, nc)
        core = f if g == 0 else 1 - f
        from_lane = pl.multiple_of(side * units + core * half_units + j * step, step)
        src = win_ref.at[owner, :, pl.ds(from_lane, step)]
        dst = wie.at[lands, pl.ds(side * half_units + j * step, step)]
        if s == 0 and g == 0:
            pltpu.make_async_copy(src, dst, lsem.at[1 + j]).start()
        else:
            expert_in[j].add(src, dst, (owner, z, core))

    bulk = [functools.partial(send_out, s) for s in range(1, nc)] + [send_out_own]
    for j in range(steps):
        for s in range(1, nc + 1):
            for g in range(2):
                for side in range(2):
                    bulk.append(functools.partial(send_in, j, s % nc, g, side))

    def pump(queue, count):
        for _ in range(min(count, len(queue))):
            queue.pop(0)()

    with jax.named_scope("s_turns"):
        row = lax.broadcasted_iota(jnp.int32, (full_len, 128), 0)
        lane = lax.broadcasted_iota(jnp.int32, (full_len, 128), 1) & (HS // 2 - 1)
        frequency = jnp.exp(lane.astype(F32) * (-2.0 * math.log(10000.0) / HS))
        angles = position_of(row, half_len, full_len).astype(F32) * frequency
        turn_ref[:, :128] = jnp.cos(angles)
        turn_ref[:, 128:] = jnp.sin(angles)
    row_at = lax.broadcasted_iota(jnp.int32, (tok, 1), 0)
    inside = row_at & (shard_len - 1)
    low = c * half_len + (inside & (half_len - 1))
    places = jnp.where(inside >= half_len, full_len - 1 - low, low)
    lengths = jnp.zeros((tok, 1), jnp.int32)
    for q in range(num_seqs):
        lengths = jnp.where(row_at // shard_len == q, len_ref[q], lengths)
    live = (places < lengths).astype(F32)
    lane = lax.broadcasted_iota(jnp.int32, (tok, 128), 1).astype(F32)
    picked = []
    for k in range(2):
        ids = jnp.concatenate(
            [ids_ref[q, e, k : k + 1, :] for q in range(num_seqs) for e in range(2)], axis=1
        ).astype(F32)
        picked.append(jnp.transpose(jnp.broadcast_to(ids, (tok, tok)), (1, 0)))
    hots = [(lane == SMALL + picked[k]).astype(F32) for k in range(2)]
    rank_row = jnp.broadcast_to(rank_ref[...].astype(F32), (tok, tok))
    earlier = (rank_row < jnp.transpose(rank_row, (1, 0))).astype(BF)
    position = mm(earlier, ((hots[0] + hots[1]) * live).astype(BF))
    slot_lane = lax.broadcasted_iota(jnp.int32, (tok, box_slots), 1).astype(F32)
    dispatch, dispatch_d = [], []
    for k in range(2):
        at = jnp.sum(hots[k] * position, axis=1, keepdims=True)
        slot_at = jnp.where((live > 0) & (at < CAP), picked[k][:, :1] * BOX + at, -BOX)
        dispatch.append((slot_lane == slot_at).astype(BF))
        dispatch_d.append((slot_lane == slot_at + CAP).astype(BF))
    anyone = dispatch[0] + dispatch[1]
    anyone_d = dispatch_d[0] + dispatch_d[1]
    upstream = go_ref[...].reshape(tok, width).astype(F32) * live
    up_b = upstream.astype(BF)
    up_f = up_b.astype(F32)
    up_own[...] = up_b.reshape(num_seqs, shard_len, width)
    for q in range(num_seqs):
        hid_all[q, c] = hid_ref[q]
        up_all[q, c] = up_own[q]

    def pass_on(post, buffer, q, at):
        post.wait_recv()
        origin, peer = (near_x, to_y) if q == 0 else (near_y, to_x)
        block_at = at(buffer, q, origin)
        return mail.post(block_at, [(block_at, block_at, peer)])

    def by_seq(buffer, q, chip):
        return buffer.at[q, chip]

    def by_chip(buffer, q, chip):
        return buffer.at[chip, q]

    sd_all[z, f] = sd_ref[...]
    planes = pl.ds(0, nz - 1)

    def spread(stage, staged, buffer):
        staged.wait_recv()
        post = mail.post(
            buffer.at[:, planes, 0],
            [(stage, buffer.at[:, z, f], peer) for peer in in_column],
        )
        for i in range(nc):
            buffer[i, z, f] = stage[i]
        return post

    def forward(post, buffer):
        post.wait_recv()
        both = buffer.at[:, :, f]
        return mail.post(both, [(both, both, sibling)])

    with jax.named_scope("a_stage_wq"):
        wq_st[c] = wq_own[c]
        spread_wq = spread(wq_st, staged_wq, wq_buf)
    with jax.named_scope("a_pass_hidden"):
        passing = [pass_on(arriving[q], hid_all, q, by_seq) for q in range(num_seqs)]
    up_copies = [
        mail.post(
            up_all.at[q, pl.ds(0, 2)],
            [(up_own.at[q], up_all.at[q, c], peer) for peer in (to_x, to_y)],
        )
        for q in range(num_seqs)
    ]
    with jax.named_scope("a_stage_wo"):
        wo_st[c] = wo_ref[...]
        spread_wo = spread(wo_st, staged_wo, wo_buf)
    with jax.named_scope("a_stage_gu"):
        for side in range(2):
            at = pl.ds(pl.multiple_of(side * units + c * own_units, own_units), own_units)
            gu_st[c, :, side * own_units : (side + 1) * own_units] = gu_ref[:, at]
        spread_gu = spread(gu_st, staged_gu, gu_buf)
    spread_sd = mail.post(
        sd_all.at[planes, 0], [(sd_ref, sd_all.at[z, f], peer) for peer in in_column]
    )
    with jax.named_scope("a_forward_wq"):
        passed_wq = forward(spread_wq, wq_buf)
        passed_wq.wait_recv()
        for i in range(nc):
            w_ref[i * block_rows : (i + 1) * block_rows, :] = join(
                wq_buf[i], (block_rows, wide_cols)
            )

    cosines = wide(turn_ref[:, :128], 2 * head_width // 128)
    sines = wide(turn_ref[:, 128:], 2 * head_width // 128)
    tail_at = wide_cols - 128
    attn_gain = column_row(w_ref[:, tail_at:], SMALL + num_experts)
    ctx_copies = []
    for q in range(num_seqs):
        with jax.named_scope("a_wait_hidden"):
            passing[q].wait_recv()
        with jax.named_scope("a_attention"):
            rows = hid_all[q].reshape(full_len, width).astype(F32)
            normed = (rows * inverse_rms(rows) * attn_gain).astype(BF)
            normed_ref[q] = normed
            merged = mm(normed, w_ref[:, : 3 * head_width])
            both = merged[:, : 2 * head_width]
            both = (both * cosines + swap_halves(both) * sines).astype(BF)
            values = merged[:, 2 * head_width :].astype(BF)
            qkv_ref[q, :, : 2 * head_width] = both
            qkv_ref[q, :, 2 * head_width :] = values
            allowed = allowed_keys(len_ref[q], half_len, full_len)
            heads = []
            for h in range(heads_here):
                probs = head_probs(
                    both[:, h * HS : (h + 1) * HS],
                    both[:, head_width + h * HS : head_width + (h + 1) * HS],
                    allowed,
                ).astype(BF)
                heads.append(mm(probs, values[:, h * HS : (h + 1) * HS]))
            context = jnp.concatenate(heads, axis=1).astype(BF)
            ctx_all[c, q] = context.reshape(nc, shard_len, head_width)
        ctx_copies.append(
            mail.post(
                ctx_all.at[pl.ds(0, 2), q],
                [(ctx_all.at[c, q], ctx_all.at[c, q], peer) for peer in (to_x, to_y)],
            )
        )
    with jax.named_scope("a_pass_upstream"):
        up_passing = [pass_on(up_copies[q], up_all, q, by_seq) for q in range(num_seqs)]
    with jax.named_scope("a_pass_context"):
        ctx_passing = [pass_on(ctx_copies[q], ctx_all, q, by_chip) for q in range(num_seqs)]
    pump(bulk, PUMPS[0])
    with jax.named_scope("a_forward_wo"):
        passed_wo = forward(spread_wo, wo_buf)
        passed_wo.wait_recv()
        for i in range(nc):
            wo_all[i * block_rows : (i + 1) * block_rows, :] = join(
                wo_buf[i], (block_rows, width)
            )
    ffn_gain = column_row(w_ref[:, tail_at:], SMALL + num_experts + 1)
    for q in range(num_seqs):
        with jax.named_scope("a_wait_context"):
            ctx_passing[q].wait_recv()
        with jax.named_scope("a_project"):
            total = hid_all[q].reshape(full_len, width).astype(F32)
            for i in range(nc):
                total = total + mm(
                    ctx_all[i, q].reshape(full_len, head_width),
                    wo_all[i * head_width : (i + 1) * head_width, :],
                )
            acc_a[q * full_len : (q + 1) * full_len] = total
            nt_all[q] = (
                (total * inverse_rms(total) * ffn_gain).astype(BF).reshape(nc, shard_len, width)
            )
    by_block = acc_a.at[pl.ds(0, nc * tok)].reshape(num_seqs, nc, shard_len, width)
    for q in range(num_seqs):
        att_own[q] = by_block[q, c]

    with jax.named_scope("b_dispatch"):
        normed = jnp.concatenate([nt_all[q, c] for q in range(num_seqs)], axis=0)
        tail = w_ref[:, tail_at:]
        logits = mm(normed, tail)
        chosen = [jnp.sum(hot * logits, axis=1, keepdims=True) for hot in hots]
        top = jnp.maximum(chosen[0], chosen[1])
        raised = [jnp.exp(value - top) for value in chosen]
        gates = [value / (raised[0] + raised[1]) for value in raised]
        weighted = [(gates[k] * up_f).astype(BF) for k in range(2)]
        boxes = mm_tn(anyone, normed)
        boxes = boxes + mm_tn(dispatch_d[0], weighted[0]) + mm_tn(dispatch_d[1], weighted[1])
        sb[...] = boxes.reshape(num_experts, BOX, width).astype(BF)
        row_copies = []
        for dz in range(nz):
            post = mail.open(ar.at[f, 0] if dz else ar.at[f, 0, others])
            for dc in range(nc):
                if dz or dc:
                    to = (wrap(c + dc, nc), wrap(z + dz, nz), f)
                    post.add(sb.at[to[1] * nc + to[0]], ar.at[f, z, c], to)
            row_copies.append(post)
        ar[f, z, c] = sb[z * nc + c]
    pump(bulk, len(bulk))

    with jax.named_scope("b_forward_gu"):
        passed_gu = forward(spread_gu, gu_buf)
        spread_sd.wait_recv()
        passed_sd = mail.post(sd_all.at[:, f], [(sd_all.at[:, f], sd_all.at[:, f], sibling)])
        passed_gu.wait_recv()
        passed_sd.wait_recv()
        for i in range(nc):
            gu_all[i * block_rows : (i + 1) * block_rows, :] = join(
                gu_buf[i], (block_rows, 2 * own_units)
            )
    with jax.named_scope("b_wait_upstream"):
        for post in up_passing:
            post.wait_recv()
    plane_tok = nc * tok
    shared_rows = nt_all.reshape(plane_tok, width)
    shared_grads = up_all.reshape(plane_tok, width)
    shared_down = sd_all.reshape(own_units, width)
    with jax.named_scope("b_shared"):
        first = pl.ds(0, plane_tok)
        acc_a[...] = jnp.zeros(acc_a.shape, F32)
        acc_b[...] = jnp.zeros(acc_b.shape, F32)

        def shared_block(j, carry):
            ffn_block(
                j, shared_rows[...], shared_grads[...], gu_all, shared_down, sh_hidden, sh_dm,
                acc_a.at[first], acc_b.at[first], own_units, 256,
            )
            return carry

        lax.fori_loop(0, own_units // 256, shared_block, 0)
        for k, acc in enumerate((acc_a, acc_b)):
            cut = acc.at[first].reshape(num_seqs, nc, shard_len, width)
            for q in range(num_seqs):
                sh_own[k, q, 0] = cut[q, c]
                sh_own[k, q, 1] = cut[q, near_y if q == 0 else near_x]
            sh_send[k] = cut[...].astype(BF)

    def first_leg(inbox, box, lead):
        post = mail.open(inbox)
        for q in range(num_seqs):
            peer = to_x if q == 0 else to_y
            for at, chip in enumerate((near_x if q == 0 else near_y, far)):
                post.add(box.at[lead + (q, chip)], inbox.at[lead + (q, at)], peer)
        return post

    shared_first = first_leg(sh_in, sh_send, (slice(None),))

    mail.settle([spread_gu, passed_gu])
    ggu = gu_buf
    with jax.named_scope("b_shared_grads"):

        def gate_up_grads(j, carry):
            at = pl.ds(pl.multiple_of(j * 256, 256), 256)
            piece = mm_tn(shared_rows[...], sh_dm[:, at])
            ggu[:, :, :, :, at] = piece.reshape(ggu.shape[:4] + (256,)).astype(BF)
            return carry

        lax.fori_loop(0, 2 * own_units // 256, gate_up_grads, 0)
        gsd[...] = mm_tn(sh_hidden[...], shared_grads[...]).reshape(gsd.shape).astype(BF)
        sibling_gu = mail.post(sib_gu, [(ggu.at[:, :, 1 - f], sib_gu, sibling)])
        sibling_sd = mail.post(sib_sd, [(gsd.at[:, 1 - f], sib_sd, sibling)])

    with jax.named_scope("b_reduce_shared"):
        def two_cores(copy, own, inbox):
            copy.wait_recv()
            inbox[...] = (own.astype(F32) + inbox[...].astype(F32)).astype(BF)

        def four_planes(copy, buffer, inbox):
            copy.wait_recv()
            for i in range(nc):
                inbox[i] = (buffer[i, :, f].astype(F32) + inbox[i].astype(F32)).astype(BF)

        four_planes(sibling_gu, ggu, sib_gu)
        two_cores(sibling_sd, gsd[:, f], sib_sd)
        gu_copies = mail.post(
            zi_gu,
            [
                (sib_gu.at[:, wrap(z + s, nz)], zi_gu.at[s - 1], in_column[s - 1])
                for s in range(1, nz)
            ],
        )
        sd_copies = mail.post(
            zi_sd,
            [(sib_sd.at[wrap(z + s, nz)], zi_sd.at[s - 1], in_column[s - 1]) for s in range(1, nz)],
        )

    with jax.named_scope("b_forward_rows"):
        forwards = mail.open(ar.at[f])
        for dz in range(nz):
            row_copies[dz].wait_recv()
            origin = wrap(z + nz - dz, nz)
            forwards.add(ar.at[f, origin], ar.at[f, origin], sibling)
        forwards.wait_recv()
        keep_x, keep_d = (box_rows(CAP, num_experts, shift) for shift in (0, CAP))
        for core in range(2):
            at = slice(core * num_slots, (core + 1) * num_slots)
            boxes = join(ar[core], (box_slots, width))
            xs[at] = mm(keep_x, boxes).astype(BF)
            ds[at] = mm(keep_d, boxes).astype(BF)
    with jax.named_scope("b_wait_down"):
        @pl.when(to_core == f)
        def _():
            expert_out.wait_recv(remote_out)
            own_out.wait()

        @pl.when(to_core != f)
        def _():
            expert_out.wait_recv()

    acc_a[...] = jnp.zeros(acc_a.shape, F32)
    acc_b[...] = jnp.zeros(acc_b.shape, F32)
    for j in range(steps):
        with jax.named_scope("b_wait_experts"):
            own_in(j).wait()
            expert_in[j].wait_recv()
        with jax.named_scope("b_experts"):
            ffn_block(
                j, xs[...], ds[...], wie, woe, ex_hidden, ex_dm, acc_a, acc_b, half_units, step
            )
    mail.settle(row_copies)
    pr = sb
    with jax.named_scope("b_sibling_sum"):

        def boxed(core):
            at = pl.ds(pl.multiple_of(core * num_slots, num_slots), num_slots)
            return (
                mm_tn(keep_x, acc_a[at].astype(BF)) + mm_tn(keep_d, acc_b[at].astype(BF))
            ).reshape(num_experts, BOX, width)

        pr[...] = boxed(1 - f).astype(BF)
        swap = mail.post(pin, [(pr, pin, sibling)])
        ours = boxed(f)
        swap.wait_recv()
        fb[...] = (ours + pin[...].astype(F32)).astype(BF)
        returns = mail.post(
            rb.at[pl.ds(0, num_experts - 1)],
            [(fb.at[to[1] * nc + to[0]], rb.at[z * nc + c], to) for to in everyone],
        )
        rb[z * nc + c] = fb[z * nc + c]
    with jax.named_scope("b_second_leg"):
        shared_first.wait_recv()
        for k in range(2):
            for q in range(num_seqs):
                sh_mid[k, q] = (sh_own[k, q, 1] + sh_in[k, q, 1].astype(F32)).astype(BF)
        shared_second = mail.post(
            sh_end,
            [
                (sh_mid.at[:, q], sh_end.at[:, q], to_y if q == 0 else to_x)
                for q in range(num_seqs)
            ],
        )

    gwi, gwo = wie, woe

    def expert_grads(j, carry):
        at = pl.ds(pl.multiple_of(j * 256, 256), 256)
        gwi[:, at] = mm_tn(xs[...], ex_dm[:, at]).astype(BF)
        return carry

    home = []
    home_in = mail.open(gwi.at[pl.ds(0, remote_rows)])
    home_out = mail.open(gwo, keep=False)
    remote_home = gwo.at[pl.ds(0, (nc - 1) * out_rows)]
    home_in_own = pltpu.make_async_copy(
        gwi.at[pl.ds(0, shard_rows)], gwi.at[pl.ds(0, shard_rows)], lsem.at[1]
    )

    def send_home_in(j, s, g, side):
        owner = wrap(c + s, nc)
        core = f if g == 0 else 1 - f
        from_rows = pl.ds(
            pl.multiple_of((2 * owner + core) * shard_rows, shard_rows), shard_rows
        )
        to_lane = pl.multiple_of(side * units + f * half_units + j * HOME, HOME)
        src = gwi.at[from_rows, pl.ds(side * half_units + j * HOME, HOME)]
        dst = ein_ref.at[c, :, pl.ds(to_lane, HOME)]
        if s == 0 and g == 0:
            pltpu.make_async_copy(src, dst, lsem.at[1]).start()
        else:
            home_in.add(src, dst, (owner, z, core))

    def home_out_own(j):
        return pltpu.make_async_copy(
            gwo.at[pl.ds(j * out_rows, out_rows)], eout_ref.at[c], lsem.at[0]
        )

    def send_home_out(j):
        to_block = f * nc + j

        @pl.when(to_block == block)
        def _():
            home_out_own(j).start()

        @pl.when(to_block != block)
        def _():
            home_out.add(
                gwo.at[pl.ds(j * out_rows, out_rows)],
                eout_ref.at[c],
                (to_block // 2, z, wrap(to_block, 2)),
            )

    for side in range(2):
        for j in range(half_units // HOME):
            for s in range(1, nc + 1):
                for g in range(2):
                    home.append(functools.partial(send_home_in, j, s % nc, g, side))
    for j in range(nc):
        home.append(functools.partial(send_home_out, j))
    with jax.named_scope("b_gwi"):
        lax.fori_loop(0, 2 * half_units // 256, expert_grads, 0)
    pump(home, PUMPS[1])
    with jax.named_scope("b_gwo"):
        for j in range(nc):
            gwo[j * out_rows : (j + 1) * out_rows, :] = mm_tn(
                ex_hidden[:, j * out_rows : (j + 1) * out_rows], ds[...]
            ).astype(BF)

    with jax.named_scope("c_wait_shared"):
        shared_second.wait_recv()
        shared, d_normed = [
            jnp.concatenate(
                [
                    sh_own[k, q, 0] + sh_in[k, q, 0].astype(F32) + sh_end[k, q].astype(F32)
                    for q in range(num_seqs)
                ],
                axis=0,
            )
            for k in range(2)
        ]
    with jax.named_scope("c_wait_returns"):
        returns.wait_recv()
    with jax.named_scope("c_combine"):
        attended = att_own[...].reshape(tok, width)
        inverse = inverse_rms(attended)
        results = join(rb[...], (box_slots, width))
        routed = [mm(dispatch[k], results) for k in range(2)]
        mixture = gates[0] * routed[0] + gates[1] * routed[1]
        out_ref[...] = (
            (live * (attended + mixture + shared)).astype(BF).reshape(out_ref.shape)
        )
        d_gates = [jnp.sum(routed[k] * up_f, axis=1, keepdims=True) for k in range(2)]
        mean_gate = gates[0] * d_gates[0] + gates[1] * d_gates[1]
        d_logits = hots[0] * (gates[0] * (d_gates[0] - mean_gate)) + hots[1] * (
            gates[1] * (d_gates[1] - mean_gate)
        )
        d_normed = d_normed + mm(anyone_d, results) + split_dot(mm_nt, d_logits, tail)
        d_attended = upstream + norm_back(attended, inverse, d_normed * ffn_gain)
        d_att_b = d_attended.astype(BF)
        d_context = mm_nt(d_att_b, wo_all[...]).astype(BF)
        for i in range(nc):
            dctx_send[i] = d_context[:, i * head_width : (i + 1) * head_width].reshape(
                num_seqs, shard_len, head_width
            )
        for q in range(num_seqs):
            dctx_all[q, c] = dctx_send[c, q]
        dctx_copies = mail.post(
            dctx_all.at[:, others],
            [
                (dctx_send.at[wrap(c + s, nc)], dctx_all.at[:, c], in_plane[s - 1])
                for s in range(1, nc)
            ],
        )
        gin_ref[...] = d_attended.reshape(gin_ref.shape)
    pump(home, PUMPS[2])

    mail.settle([spread_wo, passed_wo])
    gwo_at = wo_buf
    with jax.named_scope("c_reduce"):
        for i in range(nc):
            mine = jnp.concatenate([ctx_all[i, q, c] for q in range(num_seqs)], axis=0)
            gwo_at[i] = mm_tn(mine, d_att_b).reshape(gwo_at.shape[1:]).astype(BF)
        sibling_wo = mail.post(sib_wo, [(gwo_at.at[:, :, 1 - f], sib_wo, sibling)])
        d_router = split_dot(mm_tn, normed, d_logits, left_wide=False)
        d_gain = jnp.sum(d_normed * attended * inverse, axis=0, keepdims=True)
        turned = jnp.transpose(jnp.broadcast_to(d_gain, (128, width)), (1, 0))
        extra_lane = lax.broadcasted_iota(jnp.int32, (width, 128), 1)
        extras = jnp.where(extra_lane == SMALL + num_experts + 1, turned, d_router)
        four_planes(sibling_wo, gwo_at, sib_wo)
        wo_copies = mail.post(
            zi_wo,
            [
                (sib_wo.at[:, wrap(z + s, nz)], zi_wo.at[s - 1], in_column[s - 1])
                for s in range(1, nz)
            ],
        )

    with jax.named_scope("c_wait_dctx"):
        dctx_copies.wait_recv()
    grad_qkv = jnp.zeros((width, 3 * head_width), F32)
    rs_first = mail.open(rs_in)
    for q in range(num_seqs):
        with jax.named_scope("c_attention"):
            d_context = dctx_all[q].reshape(full_len, head_width)
            allowed = allowed_keys(len_ref[q], half_len, full_len)
            merged = qkv_ref[q]
            d_query, d_key, d_value = [], [], []
            for h in range(heads_here):
                query = merged[:, h * HS : (h + 1) * HS]
                key = merged[:, head_width + h * HS : head_width + (h + 1) * HS]
                value = merged[:, 2 * head_width + h * HS : 2 * head_width + (h + 1) * HS]
                d_head = d_context[:, h * HS : (h + 1) * HS]
                probs = head_probs(query, key, allowed)
                d_probs = mm_nt(d_head, value)
                delta = jnp.sum(probs * d_probs, axis=1, keepdims=True)
                d_scores = (probs * (d_probs - delta)).astype(BF)
                d_query.append(mm(d_scores, key) * (HS**-0.5))
                d_key.append(mm_tn(d_scores, query) * (HS**-0.5))
                d_value.append(mm_tn(probs.astype(BF), d_head))
            both = jnp.concatenate(d_query + d_key, axis=1)
            both = both * cosines - swap_halves(both) * sines
            d_merged = jnp.concatenate([both] + d_value, axis=1).astype(BF)
            product = mm_nt(d_merged, w_ref[:, : 3 * head_width]).reshape(nc, shard_len, width)
            part_own[q] = product
            part[q] = product.astype(BF)
            for at, chip in enumerate((near_x if q == 0 else near_y, far)):
                rs_first.add(part.at[q, chip], rs_in.at[q, at], to_x if q == 0 else to_y)
            grad_qkv = grad_qkv + mm_tn(normed_ref[q], d_merged)
    pump(home, len(home))
    mail.settle([spread_wq, passed_wq])
    gq = wq_buf
    with jax.named_scope("c_reduce_q"):
        last = jnp.concatenate([grad_qkv[:, tail_at:], extras[:, 3 * head_width - tail_at :]], axis=1)
        gq[...] = (
            jnp.concatenate([grad_qkv[:, :tail_at], last], axis=1).reshape(gq.shape).astype(BF)
        )
        sibling_q = mail.post(sib_q, [(gq.at[:, :, 1 - f], sib_q, sibling)])
        four_planes(sibling_q, gq, sib_q)
        q_copies = mail.post(
            zi_q,
            [
                (sib_q.at[:, wrap(z + s, nz)], zi_q.at[s - 1], in_column[s - 1])
                for s in range(1, nz)
            ],
        )
    with jax.named_scope("c_second_leg"):
        rs_first.wait_recv()
        for q in range(num_seqs):
            relay = part_own[q, near_y if q == 0 else near_x]
            rs_mid[q] = (relay + rs_in[q, 1].astype(F32)).astype(BF)
        rs_second = mail.post(
            rs_end,
            [(rs_mid.at[q], rs_end.at[q], to_y if q == 0 else to_x) for q in range(num_seqs)],
        )

    def column_sum(own, copies, inbox):
        copies.wait_recv()
        total = own.astype(F32)
        for s in range(1, nz):
            total = total + inbox[s - 1].astype(F32)
        return total

    def hand_out(box, final):
        final[c] = box[c]
        return mail.post(
            final.at[others],
            [(box.at[wrap(c + s, nc)], final.at[c], in_plane[s - 1]) for s in range(1, nc)],
        )

    with jax.named_scope("c_column_gu"):
        pb_gu[...] = column_sum(sib_gu[:, z], gu_copies, zi_gu).astype(BF)
        final_gu = hand_out(pb_gu, fgu_ref)
    with jax.named_scope("c_column_sd"):
        fsd_ref[...] = column_sum(sib_sd[z], sd_copies, zi_sd)
    with jax.named_scope("c_column_wo"):
        pb_wo[...] = column_sum(sib_wo[:, z], wo_copies, zi_wo).astype(BF)
        final_wo = hand_out(pb_wo, in_wo)
    with jax.named_scope("c_column_q"):
        pb_q[...] = column_sum(sib_q[:, z], q_copies, zi_q).astype(BF)
        final_q = hand_out(pb_q, fq_ref)
    with jax.named_scope("c_grad_in"):
        rs_second.wait_recv()
        for q in range(num_seqs):
            d_normed = part_own[q, c] + rs_in[q, 0].astype(F32) + rs_end[q].astype(F32)
            rows = hid_ref[q].astype(F32)
            gin_ref[q] = gin_ref[q] + norm_back(rows, inverse_rms(rows), d_normed * attn_gain)
    with jax.named_scope("c_final"):
        final_wo.wait_recv()
        fwo_ref[...] = jnp.sum(in_wo[...].astype(F32), axis=0)
        final_gu.wait_recv()
        final_q.wait_recv()
    with jax.named_scope("c_wait_home"):
        home_in_own.wait()
        home_in.wait_recv()

        @pl.when(to_core == f)
        def _():
            home_out_own(0).wait()
            home_out.wait_recv(remote_home)
            home_out.wait_send(remote_home)
            expert_out.wait_send(remote_out)

        @pl.when(to_core != f)
        def _():
            home_out.wait_recv()
            home_out.wait_send()
            expert_out.wait_send()

    assert mail.count <= POSTS, mail.count
    with jax.named_scope("z_finish"):
        mail.finish()


def finish_kernel(
    nc, fq_ref, fgu_ref, wqkv_ref, ga_ref, ein_ref, eout_ref, out_in, gin_in, fsd_in, fwo_in,
    gq_ref, gr_ref, gga_ref, ggf_ref, ggu_ref, oin_ref, oout_ref, out_ref, gin_ref, fsd_ref, fwo_ref,
):
    oin_ref[...] = ein_ref[...].astype(F32)
    oout_ref[...] = eout_ref[...].astype(F32)

    @pl.when((pl.program_id(0) == 0) & (pl.program_id(1) == 0))
    def _():
        out_ref[...] = out_in[...]
        gin_ref[...] = gin_in[...]
        fsd_ref[...] = fsd_in[...]
        fwo_ref[...] = fwo_in[...]
        rows_w = wqkv_ref.shape[0]
        head_width = wqkv_ref.shape[1] // 3 // nc
        grads = jnp.concatenate(
            [
                fq_ref[i, :, side * head_width : (side + 1) * head_width].astype(F32)
                for side in range(3)
                for i in range(nc)
            ],
            axis=1,
        )
        gq_ref[...] = grads
        own_units = fgu_ref.shape[2] // 2
        ggu_ref[...] = jnp.concatenate(
            [
                fgu_ref[i, :, side * own_units : (side + 1) * own_units].astype(F32)
                for side in range(2)
                for i in range(nc)
            ],
            axis=1,
        )
        extras = jnp.sum(fq_ref[:, :, 3 * head_width - SMALL :].astype(F32), axis=0)
        num_experts = gr_ref.shape[0]
        first = jnp.sum(wqkv_ref[...].astype(F32) * grads, axis=1, keepdims=True)
        lane = lax.broadcasted_iota(jnp.int32, (rows_w, 128), 1)
        both = jnp.where(lane == SMALL + num_experts, first, extras)
        turned = jnp.transpose(
            jnp.concatenate([both, jnp.zeros((128 - rows_w, 128), F32)], axis=0), (1, 0)
        )
        gr_ref[...] = turned[SMALL : SMALL + num_experts, :rows_w]
        at = SMALL + num_experts
        gga_ref[...] = turned[at : at + 1, :rows_w] / ga_ref[...].astype(F32)
        ggf_ref[...] = turned[at + 1 : at + 2, :rows_w]


def vmem(*shape, dtype=jnp.bfloat16):
    return pltpu.VMEM(shape, dtype)


def fast_device(
    hidden_in, seq_lengths, expert_ids, route_rank, gain_attn, w_qkv, w_out, w_router, gain_ffn,
    w_gate_up, w_shared_down, w_experts_in, w_experts_out, grad_output,
):
    nc, nz = lax.axis_size("ctx"), lax.axis_size("exp")
    num_seqs, two_ends, half_len, width = hidden_in.shape
    shard_len = 2 * half_len
    full_len = nc * shard_len
    tok = num_seqs * shard_len
    rows_w = w_qkv.shape[0]
    head_width = w_qkv.shape[1] // 3 // nc
    num_experts = w_router.shape[1]
    down_rows = w_shared_down.shape[0]
    own_units = w_gate_up.shape[1] // 2 // nc
    half_units = w_experts_in.shape[2] // 4
    hbm, vm, sm = pl.ANY, pltpu.VMEM, pltpu.SMEM
    dma = pltpu.SemaphoreType.DMA

    seq_shape = (num_seqs, shard_len, width)
    group_shape = (num_seqs, nc, shard_len, width)
    blocks = (nc, nz, 2, rows_w)
    half_blocks = (nc, nz, rows_w)
    wide_cols = 3 * head_width + SMALL
    num_slots = num_experts * CAP
    row_box = (num_experts, BOX, width)
    plane_tok = nc * tok
    outs = [
        (seq_shape, BF),
        (seq_shape, F32),
        ((nc, rows_w, wide_cols), BF),
        ((nc, rows_w, 2 * own_units), BF),
        ((down_rows, width), F32),
        ((rows_w, width), F32),
        (w_experts_in.shape, BF),
        (w_experts_out.shape, BF),
    ]
    out, gin, fq, fgu, fsd, fwo, ein, eout = pl.pallas_call(
        functools.partial(block_kernel, nc, nz),
        out_shape=[jax.ShapeDtypeStruct(shape, dtype) for shape, dtype in outs],
        in_specs=[
            pl.BlockSpec(memory_space=space) for space in [sm] + [vm] * 11 + [hbm, hbm]
        ],
        out_specs=[pl.BlockSpec(memory_space=space) for space in [vm] * 6 + [hbm, hbm]],
        scratch_shapes=[
            vmem(full_len, 256, dtype=F32),
            vmem(*group_shape),
            vmem(*seq_shape),
            vmem(*group_shape),
            vmem(nc, rows_w, wide_cols),
            vmem(nc, rows_w, wide_cols),
            vmem(*blocks, wide_cols),
            vmem(width, wide_cols),
            vmem(nc, rows_w, 2 * own_units),
            vmem(*blocks, 2 * own_units),
            vmem(width, 2 * own_units),
            vmem(nc, rows_w, width),
            vmem(*blocks, width),
            vmem(width, width),
            vmem(nz, 2, down_rows, width),
            vmem(width, 2 * half_units),
            vmem(half_units, width),
            vmem(num_seqs, full_len, width),
            vmem(num_seqs, full_len, 3 * head_width),
            vmem(nc, num_seqs, nc, shard_len, head_width),
            vmem(*seq_shape, dtype=F32),
            vmem(*group_shape),
            vmem(*row_box),
            vmem(2, nz, nc, BOX, width),
            vmem(2 * num_slots, width),
            vmem(2 * num_slots, width),
            vmem(2 * num_slots, width, dtype=F32),
            vmem(2 * num_slots, width, dtype=F32),
            vmem(2, num_seqs, 2, shard_len, width, dtype=F32),
            vmem(plane_tok, own_units),
            vmem(plane_tok, 2 * own_units),
            vmem(2, *group_shape),
            vmem(2, num_seqs, 2, shard_len, width),
            vmem(2, *seq_shape),
            vmem(2, *seq_shape),
            vmem(2 * num_slots, half_units),
            vmem(2 * num_slots, 2 * half_units),
            vmem(*row_box),
            vmem(*row_box),
            vmem(*row_box),
            vmem(nz, 2, down_rows, width),
            vmem(*seq_shape),
            vmem(nc, num_seqs, shard_len, head_width),
            vmem(num_seqs, nc, shard_len, head_width),
            vmem(*group_shape),
            vmem(*group_shape, dtype=F32),
            vmem(num_seqs, 2, shard_len, width),
            vmem(*seq_shape),
            vmem(*seq_shape),
            vmem(*half_blocks, 2 * own_units),
            vmem(nz - 1, nc, rows_w, 2 * own_units),
            vmem(nc, rows_w, 2 * own_units),
            vmem(*half_blocks, wide_cols),
            vmem(nz - 1, nc, rows_w, wide_cols),
            vmem(nc, rows_w, wide_cols),
            vmem(nz, down_rows, width),
            vmem(nz - 1, down_rows, width),
            vmem(*half_blocks, width),
            vmem(nz - 1, nc, rows_w, width),
            vmem(nc, rows_w, width),
            vmem(nc, rows_w, width),
            dma((POSTS,)),
            dma((POSTS,)),
            dma((1 + half_units // 256,)),
        ],
        compiler_params=pltpu.CompilerParams(
            collective_id=0, has_side_effects=True, vmem_limit_bytes=VMEM_BYTES
        ),
        cost_estimate=pl.CostEstimate(
            flops=16_000_000_000, bytes_accessed=30_000_000, transcendentals=0
        ),
        name="block_forward_backward",
    )(
        seq_lengths,
        hidden_in.reshape(seq_shape),
        grad_output.reshape(seq_shape),
        expert_ids.transpose(0, 1, 3, 2),
        route_rank.reshape(1, tok),
        w_qkv, w_router.T, gain_attn.reshape(1, rows_w), gain_ffn.reshape(1, rows_w),
        w_gate_up, w_out, w_shared_down, w_experts_in, w_experts_out,
    )

    def whole(shape):
        return pl.BlockSpec(shape, lambda e, j: (0,) * len(shape))

    def one(shape):
        return pl.BlockSpec((1, shape[1], shape[2] // WIDEN), lambda e, j: (e, 0, j))

    ins = [fq, fgu, w_qkv, gain_attn.reshape(1, rows_w), ein, eout, out, gin, fsd, fwo]
    results = [
        (w_qkv.shape, F32),
        (w_router.shape[::-1], F32),
        ((1, rows_w), F32),
        ((1, rows_w), F32),
        (w_gate_up.shape, F32),
        (ein.shape, F32),
        (eout.shape, F32),
        (seq_shape, BF),
        (seq_shape, F32),
        (fsd.shape, F32),
        (fwo.shape, F32),
    ]
    grad_qkv, grad_router, grad_ga, grad_gf, grad_gu, grad_in, grad_out, out, gin, fsd, fwo = pl.pallas_call(
        functools.partial(finish_kernel, nc),
        grid=(ein.shape[0], WIDEN),
        out_shape=[jax.ShapeDtypeStruct(shape, dtype) for shape, dtype in results],
        in_specs=[one(x.shape) if i in (4, 5) else whole(x.shape) for i, x in enumerate(ins)],
        out_specs=[
            one(shape) if i in (5, 6) else whole(shape) for i, (shape, _) in enumerate(results)
        ],
        compiler_params=pltpu.CompilerParams(vmem_limit_bytes=VMEM_BYTES),
        name="widen_gradients",
    )(*ins)
    return (
        out.reshape(hidden_in.shape),
        gin.reshape(hidden_in.shape),
        grad_ga.reshape(rows_w),
        grad_qkv,
        fwo,
        grad_router.T,
        grad_gf.reshape(rows_w),
        grad_gu,
        fsd,
        grad_in,
        grad_out,
    )


def fits(mesh, hidden_in, w_qkv, w_router, w_gate_up, w_experts_in):
    nc, nz, nf = mesh.shape["ctx"], mesh.shape["exp"], mesh.shape["fsdp"]
    heads = w_qkv.shape[1] // 3 // HS
    return (
        nf == 2
        and nc == 4
        and nz == 4
        and heads == 12
        and w_router.shape[1] == nc * nz
        and w_qkv.shape[0] == 768
        and hidden_in.shape[2] == 32 * nc
        and hidden_in.shape[0] == 2 * nz * nf
        and hidden_in.shape[3] == 768
        and w_gate_up.shape[1] == w_experts_in.shape[2] == 4096
        and 2 * CAP <= BOX
    )


def solution(mesh):
    def whole(*args):
        chosen = fast_device if fits(mesh, args[0], args[5], args[7], args[9], args[11]) else per_device
        return placed(mesh, chosen)(*args)

    return whole


def placed(mesh, chosen):
    return jax.shard_map(
        chosen,
        mesh=mesh,
        in_specs=(
            P(("exp", "fsdp"), None, "ctx", None),
            P(("exp", "fsdp")),
            P(("exp", "fsdp"), None, "ctx", None),
            P(("exp", "fsdp"), "ctx", None),
            P(("ctx", "exp", "fsdp")),
            P(("ctx", "exp", "fsdp"), None),
            P(("ctx", "exp", "fsdp"), None),
            P(("ctx", "exp", "fsdp"), None),
            P(("ctx", "exp", "fsdp")),
            P(("ctx", "exp", "fsdp"), None),
            P(("ctx", "exp", "fsdp"), None),
            P("exp", ("ctx", "fsdp"), None),
            P("exp", ("ctx", "fsdp"), None),
            P(("exp", "fsdp"), None, "ctx", None),
        ),
        out_specs=(
            P(("exp", "fsdp"), None, "ctx", None),
            P(("exp", "fsdp"), None, "ctx", None),
            P(("ctx", "exp", "fsdp")),
            P(("ctx", "exp", "fsdp"), None),
            P(("ctx", "exp", "fsdp"), None),
            P(("ctx", "exp", "fsdp"), None),
            P(("ctx", "exp", "fsdp")),
            P(("ctx", "exp", "fsdp"), None),
            P(("ctx", "exp", "fsdp"), None),
            P("exp", ("ctx", "fsdp"), None),
            P("exp", ("ctx", "fsdp"), None),
        ),
        check_vma=False,
    )
```

```python
import functools
import math

import jax
import jax.numpy as jnp
from jax import lax
from jax.experimental import pallas as pl
from jax.experimental.pallas import tpu as pltpu
from jax.sharding import PartitionSpec as P

HS = 64
CAP = 18


epsilon = 1e-06
masked_out = -1e30
highest = lax.Precision.HIGHEST


def rms_norm(values_in, gain_row):
    return (
        values_in
        * lax.rsqrt(jnp.mean(values_in * values_in, axis=-1, keepdims=True) + epsilon)
        * gain_row
    )


def rope_tables(places):
    half_size = HS // 2
    frequency = 10000.0 ** (-jnp.arange(half_size, dtype=jnp.float32) * 2.0 / HS)
    angles = places.astype(jnp.float32)[:, None] * frequency[None, :]
    return (jnp.cos(angles), jnp.sin(angles))


def rotate(values_in, cosines, sine_rows):
    half_size = values_in.shape[-1] // 2
    leading = values_in[..., :half_size]
    trailing = values_in[..., half_size:]
    cos_rows = cosines[:, None, :]
    sin_rows = sine_rows[:, None, :]
    return jnp.concatenate(
        [leading * cos_rows - trailing * sin_rows, leading * sin_rows + trailing * cos_rows],
        axis=-1,
    )


def swiglu(merged_rows):
    gate_part, up_part = jnp.split(merged_rows, 2, axis=-1)
    return jax.nn.silu(gate_part) * up_part


def first_t(left_side, right_side, precision=None):
    return lax.dot_general(
        left_side,
        right_side,
        (((0,), (0,)), ((), ())),
        precision=precision,
        preferred_element_type=jnp.float32,
    )


def second_t(left_side, right_side, precision=None):
    return lax.dot_general(
        left_side,
        right_side,
        (((1,), (1,)), ((), ())),
        precision=precision,
        preferred_element_type=jnp.float32,
    )


def per_device(
    hidden_in,
    seq_lengths,
    expert_ids,
    route_rank,
    gain_attn,
    w_qkv,
    w_out,
    w_router,
    gain_ffn,
    w_gate_up,
    w_shared_down,
    w_experts_in,
    w_experts_out,
    grad_output,
):
    num_seqs, two_ends, half_len, model_width = hidden_in.shape
    shard_len = 2 * half_len
    tok_count = num_seqs * shard_len
    num_heads = model_width // HS
    score_scale = HS ** (-0.5)
    ctx_size = lax.axis_size("ctx")
    full_len = shard_len * ctx_size
    whole_half = half_len * ctx_size
    gain_one, wqkv_all, wout_all, router_all, gain_two, shared_in, shared_down = (
        lax.all_gather(gain_attn, ("ctx", "exp", "fsdp"), axis=0, tiled=True),
        lax.all_gather(w_qkv, ("ctx", "exp", "fsdp"), axis=0, tiled=True),
        lax.all_gather(w_out, ("ctx", "exp", "fsdp"), axis=0, tiled=True),
        lax.all_gather(w_router, ("ctx", "exp", "fsdp"), axis=0, tiled=True),
        lax.all_gather(gain_ffn, ("ctx", "exp", "fsdp"), axis=0, tiled=True),
        lax.all_gather(w_gate_up, ("ctx", "exp", "fsdp"), axis=0, tiled=True),
        lax.all_gather(w_shared_down, ("ctx", "exp", "fsdp"), axis=0, tiled=True),
    )
    experts_in, experts_out = (
        lax.all_gather(w_experts_in, ("ctx", "fsdp"), axis=1, tiled=True),
        lax.all_gather(w_experts_out, ("ctx", "fsdp"), axis=1, tiled=True),
    )
    lower_places = lax.axis_index("ctx") * half_len + jnp.arange(half_len, dtype=jnp.int32)
    places = jnp.concatenate([lower_places, full_len - 1 - lower_places])
    whole_range = jnp.arange(whole_half, dtype=jnp.int32)
    full_places = jnp.concatenate([whole_range, full_len - 1 - whole_range])
    live_mask = (places[None, :] < seq_lengths[:, None]).astype(jnp.float32)
    live_rows = live_mask.reshape(tok_count, 1)
    inputs_f = hidden_in.astype(jnp.float32).reshape(tok_count, model_width)
    gain_attn_f = gain_one.astype(jnp.float32)
    normed_b = rms_norm(inputs_f, gain_attn_f).astype(jnp.bfloat16)
    qkv_merged = jnp.dot(normed_b, wqkv_all, preferred_element_type=jnp.float32).reshape(
        num_seqs, shard_len, 3, num_heads, HS
    )
    cosines, sine_rows = rope_tables(places)
    queries = rotate(qkv_merged[:, :, 0], cosines, sine_rows).astype(jnp.bfloat16)
    keys_local = rotate(qkv_merged[:, :, 1], cosines, sine_rows).astype(jnp.bfloat16)
    values_local = qkv_merged[:, :, 2].astype(jnp.bfloat16)
    end_shape = (num_seqs, 2, half_len, model_width)
    keys_full, values_full = (
        lax.all_gather(keys_local.reshape(end_shape), "ctx", axis=2, tiled=True),
        lax.all_gather(values_local.reshape(end_shape), "ctx", axis=2, tiled=True),
    )
    keys_full = keys_full.reshape(num_seqs, full_len, num_heads, HS)
    values_full = values_full.reshape(num_seqs, full_len, num_heads, HS)
    stat_shape = (num_seqs, num_heads, shard_len)
    block_range = jnp.arange(ctx_size, dtype=jnp.int32)

    def block_scores(query_rows, query_places, key_rows, key_places):
        scores = (
            jnp.einsum("bqhd,bkhd->bhqk", query_rows, key_rows, preferred_element_type=jnp.float32)
            * score_scale
        )
        allowed = (key_places[None, None, :] <= query_places[None, :, None]) & (
            key_places[None, None, :] < seq_lengths[:, None, None]
        )
        return jnp.where(allowed[:, None], scores, masked_out)

    def key_block(block_idx):
        offset = block_idx * shard_len
        return (
            lax.dynamic_slice_in_dim(keys_full, offset, shard_len, 1),
            lax.dynamic_slice_in_dim(values_full, offset, shard_len, 1),
            lax.dynamic_slice_in_dim(full_places, offset, shard_len, 0),
        )

    def lse_step(state_in, block_idx):
        run_max, run_sum = state_in
        key_rows, value_rows, key_places = key_block(block_idx)
        scores = block_scores(queries, places, key_rows, key_places)
        new_max = jnp.maximum(run_max, jnp.max(scores, axis=-1))
        run_sum = run_sum * jnp.exp(run_max - new_max) + jnp.sum(
            jnp.exp(scores - new_max[..., None]), axis=-1
        )
        return ((new_max, run_sum), None)

    (row_max, row_sum), unused = lax.scan(
        lse_step,
        (jnp.full(stat_shape, masked_out, jnp.float32), jnp.zeros(stat_shape, jnp.float32)),
        block_range,
    )
    log_total = row_max + jnp.log(row_sum)

    def context_step(running, block_idx):
        key_rows, value_rows, key_places = key_block(block_idx)
        prob_rows = jnp.exp(
            block_scores(queries, places, key_rows, key_places) - log_total[..., None]
        ).astype(jnp.bfloat16)
        return (
            running
            + jnp.einsum(
                "bhqk,bkhd->bqhd", prob_rows, value_rows, preferred_element_type=jnp.float32
            ),
            None,
        )

    context, unused = lax.scan(
        context_step, jnp.zeros((num_seqs, shard_len, num_heads, HS), jnp.float32), block_range
    )
    context_b = context.reshape(tok_count, model_width).astype(jnp.bfloat16)
    attended = inputs_f + jnp.dot(context_b, wout_all, preferred_element_type=jnp.float32)
    gain_ffn_f = gain_two.astype(jnp.float32)
    normed_two = rms_norm(attended, gain_ffn_f).astype(jnp.bfloat16)
    logits = jnp.dot(normed_two, router_all, preferred_element_type=jnp.float32)
    num_experts = router_all.shape[1]
    expert_range = jnp.arange(num_experts, dtype=jnp.int32)
    picked_ids = expert_ids.reshape(tok_count, 2)
    pick_hot = (picked_ids[:, :, None] == expert_range).astype(jnp.float32)
    chosen = jnp.sum(pick_hot * logits[:, None, :], axis=-1)
    gate_probs = jax.nn.softmax(chosen, axis=-1)
    expert_load = (jnp.sum(pick_hot, axis=1) * live_rows).astype(jnp.bfloat16)
    rank_rows = route_rank.reshape(tok_count)
    earlier = (rank_rows[None, :] < rank_rows[:, None]).astype(jnp.bfloat16)
    position = jnp.dot(earlier, expert_load, preferred_element_type=jnp.float32)
    chosen_pos = jnp.sum(pick_hot * position[:, None, :], axis=-1)
    kept_mask = live_rows * (chosen_pos < CAP).astype(jnp.float32)
    slot_hot = (chosen_pos[:, :, None] == jnp.arange(CAP, dtype=jnp.float32)).astype(jnp.float32)
    dispatch = (
        (pick_hot[:, :, :, None] * slot_hot[:, :, None, :] * kept_mask[:, :, None, None])
        .reshape(tok_count, 2, num_experts * CAP)
        .astype(jnp.bfloat16)
    )
    dispatch_any = dispatch[:, 0] + dispatch[:, 1]
    exp_size = lax.axis_size("exp")
    per_owner = num_experts // exp_size
    send_rows = (
        first_t(dispatch_any, normed_two)
        .astype(jnp.bfloat16)
        .reshape(exp_size, per_owner, CAP, model_width)
    )
    arrived = lax.all_to_all(send_rows, "exp", split_axis=0, concat_axis=0, tiled=True)
    expert_merged = jnp.einsum(
        "secd,edf->secf", arrived, experts_in, preferred_element_type=jnp.float32
    )
    expert_hidden = swiglu(expert_merged).astype(jnp.bfloat16)
    expert_result = jnp.einsum(
        "secf,efd->secd", expert_hidden, experts_out, preferred_element_type=jnp.float32
    ).astype(jnp.bfloat16)
    returned = lax.all_to_all(
        expert_result, "exp", split_axis=0, concat_axis=0, tiled=True
    ).reshape(num_experts * CAP, model_width)
    routed = jnp.einsum("tks,sd->tkd", dispatch, returned, preferred_element_type=jnp.float32)
    mixture = jnp.sum(gate_probs[:, :, None] * routed, axis=1)
    shared_merged = jnp.dot(normed_two, shared_in, preferred_element_type=jnp.float32)
    shared_hidden = swiglu(shared_merged).astype(jnp.bfloat16)
    shared_result = jnp.dot(shared_hidden, shared_down, preferred_element_type=jnp.float32)
    layer_out = (
        (live_rows * (attended + mixture + shared_result)).reshape(end_shape).astype(jnp.bfloat16)
    )
    upstream = grad_output.astype(jnp.float32).reshape(tok_count, model_width) * live_rows
    upstream_b = upstream.astype(jnp.bfloat16)
    upstream_f = upstream_b.astype(jnp.float32)
    d_shared_down = first_t(shared_hidden, upstream_b)
    d_shared_hidden = second_t(upstream_b, shared_down)
    unused, swiglu_pull = jax.vjp(swiglu, shared_merged)
    d_shared_merged = swiglu_pull(d_shared_hidden)[0].astype(jnp.bfloat16)
    d_shared_in = first_t(normed_two, d_shared_merged)
    d_normed_two = second_t(d_shared_merged, shared_in)
    gate_grads = jnp.sum(routed * upstream_f[:, None, :], axis=-1)
    weighted = (gate_probs[:, :, None] * upstream_f[:, None, :]).astype(jnp.bfloat16)
    d_returned = (
        jnp.einsum("tks,tkd->sd", dispatch, weighted, preferred_element_type=jnp.float32)
        .astype(jnp.bfloat16)
        .reshape(exp_size, per_owner, CAP, model_width)
    )
    d_result = lax.all_to_all(d_returned, "exp", split_axis=0, concat_axis=0, tiled=True)
    d_experts_out = jnp.einsum(
        "secf,secd->efd", expert_hidden, d_result, preferred_element_type=jnp.float32
    )
    d_expert_hidden = jnp.einsum(
        "secd,efd->secf", d_result, experts_out, preferred_element_type=jnp.float32
    )
    unused, expert_pull = jax.vjp(swiglu, expert_merged)
    d_expert_merged = expert_pull(d_expert_hidden)[0].astype(jnp.bfloat16)
    d_experts_in = jnp.einsum(
        "secd,secf->edf", arrived, d_expert_merged, preferred_element_type=jnp.float32
    )
    d_arrived = jnp.einsum(
        "secf,edf->secd", d_expert_merged, experts_in, preferred_element_type=jnp.float32
    ).astype(jnp.bfloat16)
    d_sent = lax.all_to_all(d_arrived, "exp", split_axis=0, concat_axis=0, tiled=True).reshape(
        num_experts * CAP, model_width
    )
    d_normed_two = d_normed_two + jnp.dot(dispatch_any, d_sent, preferred_element_type=jnp.float32)
    unused, gate_pull = jax.vjp(lambda chosen_in: jax.nn.softmax(chosen_in, axis=-1), chosen)
    d_chosen = gate_pull(gate_grads)[0]
    d_logits = jnp.sum(pick_hot * d_chosen[:, :, None], axis=1)
    d_router = first_t(normed_two.astype(jnp.float32), d_logits, highest)
    d_normed_two = d_normed_two + second_t(d_logits, router_all.astype(jnp.float32), highest)
    unused, second_pull = jax.vjp(rms_norm, attended, gain_ffn_f)
    d_attended, d_gain_ffn = second_pull(d_normed_two)
    d_attended = d_attended + upstream
    d_attended_b = d_attended.astype(jnp.bfloat16)
    d_out_proj = first_t(context_b, d_attended_b)
    d_context = (
        second_t(d_attended_b, wout_all)
        .astype(jnp.bfloat16)
        .reshape(num_seqs, shard_len, num_heads, HS)
    )

    def score_grads(
        query_rows, query_places, key_rows, value_rows, key_places, d_rows, lse_rows, delta_rows
    ):
        prob_rows = jnp.exp(
            block_scores(query_rows, query_places, key_rows, key_places) - lse_rows[..., None]
        )
        d_probs = jnp.einsum(
            "bqhd,bkhd->bhqk", d_rows, value_rows, preferred_element_type=jnp.float32
        )
        d_scores = (prob_rows * (d_probs - delta_rows[..., None])).astype(jnp.bfloat16)
        return (prob_rows.astype(jnp.bfloat16), d_scores)

    def delta_step(running, block_idx):
        key_rows, value_rows, key_places = key_block(block_idx)
        prob_rows = jnp.exp(
            block_scores(queries, places, key_rows, key_places) - log_total[..., None]
        )
        d_probs = jnp.einsum(
            "bqhd,bkhd->bhqk", d_context, value_rows, preferred_element_type=jnp.float32
        )
        return (running + jnp.sum(prob_rows * d_probs, axis=-1), None)

    row_delta, unused = lax.scan(delta_step, jnp.zeros(stat_shape, jnp.float32), block_range)
    head_shape = (num_seqs, shard_len, num_heads, HS)

    def query_step(d_query, block_idx):
        key_rows, value_rows, key_places = key_block(block_idx)
        prob_b, d_scores = score_grads(
            queries, places, key_rows, value_rows, key_places, d_context, log_total, row_delta
        )
        return (
            d_query
            + jnp.einsum("bhqk,bkhd->bqhd", d_scores, key_rows, preferred_element_type=jnp.float32)
            * score_scale,
            None,
        )

    d_query, unused = lax.scan(query_step, jnp.zeros(head_shape, jnp.float32), block_range)
    query_all, d_context_all = (
        lax.all_gather(queries.reshape(end_shape), "ctx", axis=2, tiled=True),
        lax.all_gather(d_context.reshape(end_shape), "ctx", axis=2, tiled=True),
    )
    stat_ends = (num_seqs, num_heads, 2, half_len)
    lse_all, delta_all = (
        lax.all_gather(log_total.reshape(stat_ends), "ctx", axis=3, tiled=True),
        lax.all_gather(row_delta.reshape(stat_ends), "ctx", axis=3, tiled=True),
    )
    query_all = query_all.reshape(num_seqs, full_len, num_heads, HS)
    d_context_all = d_context_all.reshape(num_seqs, full_len, num_heads, HS)
    lse_all = lse_all.reshape(num_seqs, num_heads, full_len)
    delta_all = delta_all.reshape(num_seqs, num_heads, full_len)

    def owner_step(state_in, block_idx):
        d_keys, d_values = state_in
        offset = block_idx * shard_len
        query_rows = lax.dynamic_slice_in_dim(query_all, offset, shard_len, 1)
        d_rows = lax.dynamic_slice_in_dim(d_context_all, offset, shard_len, 1)
        lse_rows = lax.dynamic_slice_in_dim(lse_all, offset, shard_len, 2)
        delta_rows = lax.dynamic_slice_in_dim(delta_all, offset, shard_len, 2)
        query_places = lax.dynamic_slice_in_dim(full_places, offset, shard_len, 0)
        prob_b, d_scores = score_grads(
            query_rows, query_places, keys_local, values_local, places, d_rows, lse_rows, delta_rows
        )
        d_keys = (
            d_keys
            + jnp.einsum(
                "bhqk,bqhd->bkhd", d_scores, query_rows, preferred_element_type=jnp.float32
            )
            * score_scale
        )
        d_values = d_values + jnp.einsum(
            "bhqk,bqhd->bkhd", prob_b, d_rows, preferred_element_type=jnp.float32
        )
        return ((d_keys, d_values), None)

    (d_keys_local, d_values_local), unused = lax.scan(
        owner_step,
        (jnp.zeros(head_shape, jnp.float32), jnp.zeros(head_shape, jnp.float32)),
        block_range,
    )
    unused, rope_pull = jax.vjp(
        lambda rows_in: rotate(rows_in, cosines, sine_rows), qkv_merged[:, :, 0]
    )
    d_query_pre = rope_pull(d_query)[0]
    d_key_pre = rope_pull(d_keys_local)[0]
    d_qkv_merged = (
        jnp.stack([d_query_pre, d_key_pre, d_values_local], axis=2)
        .reshape(tok_count, 3 * model_width)
        .astype(jnp.bfloat16)
    )
    d_qkv = first_t(normed_b, d_qkv_merged)
    d_normed = second_t(d_qkv_merged, wqkv_all)
    unused, first_pull = jax.vjp(rms_norm, inputs_f, gain_attn_f)
    d_inputs, d_gain_attn = first_pull(d_normed)
    grad_input = (d_attended + d_inputs).reshape(end_shape)
    dense_sums = (
        lax.psum_scatter(d_gain_attn, ("ctx", "exp", "fsdp"), scatter_dimension=0, tiled=True),
        lax.psum_scatter(d_qkv, ("ctx", "exp", "fsdp"), scatter_dimension=0, tiled=True),
        lax.psum_scatter(d_out_proj, ("ctx", "exp", "fsdp"), scatter_dimension=0, tiled=True),
        lax.psum_scatter(d_router, ("ctx", "exp", "fsdp"), scatter_dimension=0, tiled=True),
        lax.psum_scatter(d_gain_ffn, ("ctx", "exp", "fsdp"), scatter_dimension=0, tiled=True),
        lax.psum_scatter(d_shared_in, ("ctx", "exp", "fsdp"), scatter_dimension=0, tiled=True),
        lax.psum_scatter(d_shared_down, ("ctx", "exp", "fsdp"), scatter_dimension=0, tiled=True),
    )
    expert_sums = (
        lax.psum_scatter(
            d_experts_in.astype(jnp.bfloat16), ("ctx", "fsdp"), scatter_dimension=1, tiled=True
        ).astype(jnp.float32),
        lax.psum_scatter(
            d_experts_out.astype(jnp.bfloat16), ("ctx", "fsdp"), scatter_dimension=1, tiled=True
        ).astype(jnp.float32),
    )
    return (
        layer_out,
        grad_input,
        dense_sums[0],
        dense_sums[1],
        dense_sums[2],
        dense_sums[3],
        dense_sums[4],
        dense_sums[5],
        dense_sums[6],
        expert_sums[0],
        expert_sums[1],
    )


F32 = jnp.float32
BF = jnp.bfloat16
MESH = pl.DeviceIdType.MESH
BOX = 40
SMALL = 64
VMEM_BYTES = 63 * 1024 * 1024
PUMPS = (2, 10, 8, 1)
POSTS = 64
HOME = 512
WIDEN = 1


def place():
    return lax.axis_index("ctx"), lax.axis_index("exp"), lax.axis_index("fsdp")


def wrap(value, size):
    return lax.rem(value, size)


def mm(left, right):
    return lax.dot_general(
        left, right, (((1,), (0,)), ((), ())), preferred_element_type=F32
    )


def mm_nt(left, right):
    return lax.dot_general(
        left, right, (((1,), (1,)), ((), ())), preferred_element_type=F32
    )


def mm_tn(left, right):
    return lax.dot_general(
        left, right, (((0,), (0,)), ((), ())), preferred_element_type=F32
    )


def greet(peers):
    barrier = pltpu.get_barrier_semaphore()
    for peer in peers:
        pl.semaphore_signal(barrier, inc=1, device_id=peer, device_id_type=MESH)


def met(peers):
    pl.semaphore_wait(pltpu.get_barrier_semaphore(), len(peers))


class Post:
    def __init__(self, send, recv, like, device):
        self.send, self.recv, self.like, self.device = send, recv, like, device

    def add(self, src, dst, device):
        pltpu.make_async_remote_copy(
            src_ref=src,
            dst_ref=dst,
            send_sem=self.send,
            recv_sem=self.recv,
            device_id=device,
            device_id_type=MESH,
        ).start()

    def all_of_it(self, like=None):
        like = self.like if like is None else like
        return pltpu.make_async_remote_copy(
            src_ref=like,
            dst_ref=like,
            send_sem=self.send,
            recv_sem=self.recv,
            device_id=self.device,
            device_id_type=MESH,
        )

    def wait_recv(self, like=None):
        self.all_of_it(like).wait_recv()

    def wait_send(self, like=None):
        self.all_of_it(like).wait_send()


class Courier:
    def __init__(self, send, recv, device):
        self.send, self.recv, self.device, self.count, self.sent = send, recv, device, 0, []

    def open(self, like, keep=True):
        post = Post(self.send.at[self.count], self.recv.at[self.count], like, self.device)
        self.count += 1
        if keep:
            self.sent.append(post)
        return post

    def post(self, like, moves):
        post = self.open(like)
        for src, dst, device in moves:
            post.add(src, dst, device)
        return post

    def settle(self, posts):
        for post in posts:
            post.wait_send()
        done = {id(post) for post in posts}
        self.sent = [post for post in self.sent if id(post) not in done]

    def finish(self):
        self.settle(list(self.sent))


def swap_halves(rows):
    width = rows.shape[1]
    lane = lax.broadcasted_iota(jnp.int32, rows.shape, 1)
    ahead = pltpu.roll(rows, width - HS // 2, 1)
    behind = pltpu.roll(rows, HS // 2, 1)
    return jnp.where((lane & (HS - 1)) < HS // 2, -ahead, behind)


def wide(table, times):
    return jnp.concatenate([table] * times, axis=1)


def position_of(index, half_len, full_len):
    block = index // (2 * half_len)
    inside = index & (2 * half_len - 1)
    low = block * half_len + (inside & (half_len - 1))
    return jnp.where(inside >= half_len, full_len - 1 - low, low)


def allowed_keys(length, half_len, full_len):
    shape = (full_len, full_len)
    query_at = position_of(lax.broadcasted_iota(jnp.int32, shape, 0), half_len, full_len)
    key_at = position_of(lax.broadcasted_iota(jnp.int32, shape, 1), half_len, full_len)
    return (key_at <= query_at) & (key_at < length)


def head_probs(query, key, allowed):
    scores = jnp.where(allowed, mm_nt(query, key) * (HS**-0.5), masked_out)
    weights = jnp.exp(scores - jnp.max(scores, axis=1, keepdims=True))
    return weights * (1.0 / jnp.sum(weights, axis=1, keepdims=True))


def column_row(tail, lane):
    pick = (lax.broadcasted_iota(jnp.int32, (8, 128), 1) == lane).astype(BF)
    return mm_nt(pick, tail)[0:1]


def split_dot(dot, left, right, left_wide=True):
    whole = left if left_wide else right
    high = whole.astype(BF)
    low = (whole - high.astype(F32)).astype(BF)
    if left_wide:
        return dot(high, right) + dot(low, right)
    return dot(left, high) + dot(left, low)


def inverse_rms(rows):
    return lax.rsqrt(jnp.mean(rows * rows, axis=1, keepdims=True) + epsilon)


def norm_back(rows, inverse, scaled):
    return inverse * scaled - rows * (inverse * inverse * inverse) * jnp.mean(
        rows * scaled, axis=1, keepdims=True
    )


def join(blocks, shape):
    return blocks.astype(F32).reshape(shape).astype(BF)


def ffn_block(j, rows, grads, in_ref, out_ref, hidden_ref, dm_ref, result, back, units, step):
    low = pl.multiple_of(j * step, step) if not isinstance(j, int) else j * step
    high = pl.multiple_of(units + low, step) if not isinstance(j, int) else units + low
    gate_at, up_at = pl.ds(low, step), pl.ds(high, step)
    gate, up = mm(rows, in_ref[:, gate_at]), mm(rows, in_ref[:, up_at])
    down = out_ref[gate_at, :]
    d_hidden = mm_nt(grads, down)
    share = 1.0 / (1.0 + jnp.exp(-gate))
    lit = gate * share
    hidden = (lit * up).astype(BF)
    d_gate = (d_hidden * up * (share * (1.0 + gate * (1.0 - share)))).astype(BF)
    d_up = (d_hidden * lit).astype(BF)
    hidden_ref[:, gate_at] = hidden
    dm_ref[:, gate_at] = d_gate
    dm_ref[:, up_at] = d_up
    result[...] += mm(hidden, down)
    back[...] += mm_nt(d_gate, in_ref[:, gate_at]) + mm_nt(d_up, in_ref[:, up_at])


def box_rows(kept_rows, boxes, shift):
    shape = (boxes * kept_rows, boxes * BOX)
    row = lax.broadcasted_iota(jnp.int32, shape, 0)
    column = lax.broadcasted_iota(jnp.int32, shape, 1)
    box = jnp.floor((column.astype(F32) + 0.5) * (1.0 / BOX)).astype(jnp.int32)
    at = column - box * BOX - shift
    return ((at >= 0) & (at < kept_rows) & (row == box * kept_rows + at)).astype(BF)


def block_kernel(
    nc, nz,
    len_ref, hid_ref, go_ref, ids_ref, rank_ref, wqkv_ref, router_ref, ga_ref, gf_ref, gu_ref,
    wo_ref, sd_ref, win_ref, wout_ref,
    out_ref, gin_ref, fq_ref, fgu_ref, fsd_ref, fwo_ref, ein_ref, eout_ref,
    turn_ref, hid_all, up_own, up_all, wq_own, wq_st, wq_buf, w_ref, gu_st, gu_buf, gu_all, wo_st, wo_buf,
    wo_all, sd_all, wie, woe, normed_ref, qkv_ref, ctx_all, att_own, nt_all,
    sb, ar, xs, ds, acc_a, acc_b, sh_own, sh_hidden, sh_dm, sh_send, sh_in, sh_mid, sh_end,
    ex_hidden, ex_dm, pin, fb, rb, gsd, da_own, dctx_send, dctx_all, part, part_own, rs_in, rs_mid, rs_end,
    sib_gu, zi_gu, pb_gu, sib_q, zi_q, pb_q, sib_sd, zi_sd, sib_wo, zi_wo, pb_wo, in_wo,
    send, recv, lsem,
):
    c, z, f = place()
    near_x, near_y = c + 1 - 2 * wrap(c, 2), wrap(c + 2, nc)
    far = wrap(near_x + 2, nc)
    to_x, to_y = (near_x, z, f), (near_y, z, f)
    in_plane = [(wrap(c + s, nc), z, f) for s in range(1, nc)]
    in_column = [(c, wrap(z + s, nz), f) for s in range(1, nz)]
    sibling = (c, z, 1 - f)
    across = [(wrap(c + s, nc), z, 1 - f) for s in range(1, nc)]
    ring = [(dz, dc) for dz in range(nz) for dc in range(nc) if dz or dc]
    everyone = [(wrap(c + dc, nc), wrap(z + dz, nz), f) for dz, dc in ring]
    with jax.named_scope("s_greet"):
        greet(everyone + [sibling] + across)

    num_seqs, shard_len, width = hid_ref.shape
    full_len = nc * shard_len
    half_len = shard_len // 2
    tok = num_seqs * shard_len
    rows_w = wqkv_ref.shape[0]
    head_width = wqkv_ref.shape[1] // 3 // nc
    heads_here = head_width // HS
    wide_cols = wq_own.shape[2]
    units = gu_ref.shape[1] // 2
    own_units = units // nc
    down_rows = sd_ref.shape[0]
    num_experts = nz * nc
    num_slots = num_experts * CAP
    box_slots = num_experts * BOX
    block_rows = nz * 2 * rows_w
    mail = Courier(send, recv, sibling)

    small = jnp.concatenate(
        [
            router_ref[...].astype(F32),
            ga_ref[...].astype(F32),
            gf_ref[...].astype(F32),
            jnp.zeros((128 - num_experts - 2, rows_w), F32),
        ],
        axis=0,
    )
    small = jnp.concatenate([small, jnp.zeros((128, 128 - rows_w), F32)], axis=1)
    small = jnp.transpose(small, (1, 0))[:rows_w, :SMALL].astype(BF)
    for owner in range(nc):
        wq_own[owner] = jnp.concatenate(
            [
                wqkv_ref[:, side * width + owner * head_width : side * width + (owner + 1) * head_width]
                for side in range(3)
            ]
            + [small],
            axis=1,
        )
    with jax.named_scope("s_met"):
        met(everyone + [sibling] + across)

    others = pl.ds(0, nc - 1)
    staged_wq = mail.post(
        wq_st.at[others],
        [(wq_own.at[wrap(c + s, nc)], wq_st.at[c], in_plane[s - 1]) for s in range(1, nc)],
    )
    arriving = [
        mail.post(
            hid_all.at[q, pl.ds(0, 2)],
            [(hid_ref.at[q], hid_all.at[q, c], peer) for peer in (to_x, to_y)],
        )
        for q in range(num_seqs)
    ]
    staged_wo = mail.post(wo_st.at[others], [(wo_ref, wo_st.at[c], peer) for peer in in_plane])
    staged_gu = mail.open(gu_st.at[others])
    for s in range(1, nc):
        owner = wrap(c + s, nc)
        for side in range(2):
            at = pl.ds(pl.multiple_of(side * units + owner * own_units, own_units), own_units)
            staged_gu.add(
                gu_ref.at[:, at],
                gu_st.at[c, :, pl.ds(side * own_units, own_units)],
                in_plane[s - 1],
            )

    block = 2 * c + f
    shard_rows = win_ref.shape[1]
    half_units = units // 2
    step = 256
    steps = half_units // step
    lands = pl.ds(pl.multiple_of(block * shard_rows, shard_rows), shard_rows)
    out_rows = wout_ref.shape[1]
    to_core = block // nc
    slot = wrap(block, nc)
    out_lands = pl.ds(pl.multiple_of(slot * out_rows, out_rows), out_rows)
    remote_rows = (2 * nc - 1) * shard_rows
    expert_in = [
        mail.open(wie.at[pl.ds(0, remote_rows), pl.ds(0, 2 * step)]) for _ in range(steps)
    ]
    expert_out = mail.open(woe, keep=False)
    remote_out = woe.at[pl.ds(0, (nc - 1) * out_rows)]
    own_out = pltpu.make_async_copy(wout_ref.at[c], woe.at[out_lands], lsem.at[0])

    def send_out(s):
        owner = wrap(c + s, nc)
        expert_out.add(wout_ref.at[owner], woe.at[out_lands], (owner, z, to_core))

    def send_out_own():
        @pl.when(to_core == f)
        def _():
            own_out.start()

        @pl.when(to_core != f)
        def _():
            expert_out.add(wout_ref.at[c], woe.at[out_lands], sibling)

    def own_in(j):
        like = wie.at[pl.ds(0, shard_rows), pl.ds(0, 2 * step)]
        return pltpu.make_async_copy(like, like, lsem.at[1 + j])

    def send_in(j, s, g, side):
        owner = wrap(c + s, nc)
        core = f if g == 0 else 1 - f
        from_lane = pl.multiple_of(side * units + core * half_units + j * step, step)
        src = win_ref.at[owner, :, pl.ds(from_lane, step)]
        dst = wie.at[lands, pl.ds(side * half_units + j * step, step)]
        if s == 0 and g == 0:
            pltpu.make_async_copy(src, dst, lsem.at[1 + j]).start()
        else:
            expert_in[j].add(src, dst, (owner, z, core))

    bulk = [functools.partial(send_out, s) for s in range(1, nc)] + [send_out_own]
    for j in range(steps):
        for s in range(1, nc + 1):
            for g in range(2):
                for side in range(2):
                    bulk.append(functools.partial(send_in, j, s % nc, g, side))

    def pump(queue, count):
        for _ in range(min(count, len(queue))):
            queue.pop(0)()

    with jax.named_scope("s_turns"):
        row = lax.broadcasted_iota(jnp.int32, (full_len, 128), 0)
        lane = lax.broadcasted_iota(jnp.int32, (full_len, 128), 1) & (HS // 2 - 1)
        frequency = jnp.exp(lane.astype(F32) * (-2.0 * math.log(10000.0) / HS))
        angles = position_of(row, half_len, full_len).astype(F32) * frequency
        turn_ref[:, :128] = jnp.cos(angles)
        turn_ref[:, 128:] = jnp.sin(angles)
    row_at = lax.broadcasted_iota(jnp.int32, (tok, 1), 0)
    inside = row_at & (shard_len - 1)
    low = c * half_len + (inside & (half_len - 1))
    places = jnp.where(inside >= half_len, full_len - 1 - low, low)
    lengths = jnp.zeros((tok, 1), jnp.int32)
    for q in range(num_seqs):
        lengths = jnp.where(row_at // shard_len == q, len_ref[q], lengths)
    live = (places < lengths).astype(F32)
    lane = lax.broadcasted_iota(jnp.int32, (tok, 128), 1).astype(F32)
    picked = []
    for k in range(2):
        ids = jnp.concatenate(
            [ids_ref[q, e, k : k + 1, :] for q in range(num_seqs) for e in range(2)], axis=1
        ).astype(F32)
        picked.append(jnp.transpose(jnp.broadcast_to(ids, (tok, tok)), (1, 0)))
    hots = [(lane == SMALL + picked[k]).astype(F32) for k in range(2)]
    rank_row = jnp.broadcast_to(rank_ref[...].astype(F32), (tok, tok))
    earlier = (rank_row < jnp.transpose(rank_row, (1, 0))).astype(BF)
    position = mm(earlier, ((hots[0] + hots[1]) * live).astype(BF))
    slot_lane = lax.broadcasted_iota(jnp.int32, (tok, box_slots), 1).astype(F32)
    dispatch, dispatch_d = [], []
    for k in range(2):
        at = jnp.sum(hots[k] * position, axis=1, keepdims=True)
        slot_at = jnp.where((live > 0) & (at < CAP), picked[k][:, :1] * BOX + at, -BOX)
        dispatch.append((slot_lane == slot_at).astype(BF))
        dispatch_d.append((slot_lane == slot_at + CAP).astype(BF))
    anyone = dispatch[0] + dispatch[1]
    anyone_d = dispatch_d[0] + dispatch_d[1]
    upstream = go_ref[...].reshape(tok, width).astype(F32) * live
    up_b = upstream.astype(BF)
    up_f = up_b.astype(F32)
    up_own[...] = up_b.reshape(num_seqs, shard_len, width)
    for q in range(num_seqs):
        hid_all[q, c] = hid_ref[q]
        up_all[q, c] = up_own[q]

    def pass_on(post, buffer, q, at):
        post.wait_recv()
        origin, peer = (near_x, to_y) if q == 0 else (near_y, to_x)
        block_at = at(buffer, q, origin)
        return mail.post(block_at, [(block_at, block_at, peer)])

    def by_seq(buffer, q, chip):
        return buffer.at[q, chip]

    def by_chip(buffer, q, chip):
        return buffer.at[chip, q]

    sd_all[z, f] = sd_ref[...]
    planes = pl.ds(0, nz - 1)

    def spread(stage, staged, buffer):
        staged.wait_recv()
        post = mail.post(
            buffer.at[:, planes, 0],
            [(stage, buffer.at[:, z, f], peer) for peer in in_column],
        )
        for i in range(nc):
            buffer[i, z, f] = stage[i]
        return post

    def forward(post, buffer):
        post.wait_recv()
        both = buffer.at[:, :, f]
        return mail.post(both, [(both, both, sibling)])

    with jax.named_scope("a_stage_wq"):
        wq_st[c] = wq_own[c]
        spread_wq = spread(wq_st, staged_wq, wq_buf)
    with jax.named_scope("a_pass_hidden"):
        passing = [pass_on(arriving[q], hid_all, q, by_seq) for q in range(num_seqs)]
    up_copies = [
        mail.post(
            up_all.at[q, pl.ds(0, 2)],
            [(up_own.at[q], up_all.at[q, c], peer) for peer in (to_x, to_y)],
        )
        for q in range(num_seqs)
    ]
    pump(bulk, PUMPS[3])
    wo_st[c] = wo_ref[...]
    for side in range(2):
        at = pl.ds(pl.multiple_of(side * units + c * own_units, own_units), own_units)
        gu_st[c, :, side * own_units : (side + 1) * own_units] = gu_ref[:, at]
    with jax.named_scope("a_forward_wq"):
        passed_wq = forward(spread_wq, wq_buf)
        passed_wq.wait_recv()
        for i in range(nc):
            w_ref[i * block_rows : (i + 1) * block_rows, :] = join(
                wq_buf[i], (block_rows, wide_cols)
            )

    cosines = wide(turn_ref[:, :128], 2 * head_width // 128)
    sines = wide(turn_ref[:, 128:], 2 * head_width // 128)
    tail_at = wide_cols - 128
    attn_gain = column_row(w_ref[:, tail_at:], SMALL + num_experts)
    ctx_copies = []
    for q in range(num_seqs):
        with jax.named_scope("a_wait_hidden"):
            passing[q].wait_recv()
        with jax.named_scope("a_attention"):
            rows = hid_all[q].reshape(full_len, width).astype(F32)
            normed = (rows * inverse_rms(rows) * attn_gain).astype(BF)
            normed_ref[q] = normed
            merged = mm(normed, w_ref[:, : 3 * head_width])
            both = merged[:, : 2 * head_width]
            both = (both * cosines + swap_halves(both) * sines).astype(BF)
            values = merged[:, 2 * head_width :].astype(BF)
            qkv_ref[q, :, : 2 * head_width] = both
            qkv_ref[q, :, 2 * head_width :] = values
            allowed = allowed_keys(len_ref[q], half_len, full_len)
            heads = []
            for h in range(heads_here):
                probs = head_probs(
                    both[:, h * HS : (h + 1) * HS],
                    both[:, head_width + h * HS : head_width + (h + 1) * HS],
                    allowed,
                ).astype(BF)
                heads.append(mm(probs, values[:, h * HS : (h + 1) * HS]))
            context = jnp.concatenate(heads, axis=1).astype(BF)
            ctx_all[c, q] = context.reshape(nc, shard_len, head_width)
        ctx_copies.append(
            mail.post(
                ctx_all.at[pl.ds(0, 2), q],
                [(ctx_all.at[c, q], ctx_all.at[c, q], peer) for peer in (to_x, to_y)],
            )
        )
    spread_wo = spread(wo_st, staged_wo, wo_buf)
    with jax.named_scope("a_pass_upstream"):
        up_passing = [pass_on(up_copies[q], up_all, q, by_seq) for q in range(num_seqs)]
    with jax.named_scope("a_pass_context"):
        ctx_passing = [pass_on(ctx_copies[q], ctx_all, q, by_chip) for q in range(num_seqs)]
    pump(bulk, PUMPS[0])
    with jax.named_scope("a_forward_wo"):
        passed_wo = forward(spread_wo, wo_buf)
        spread_gu = spread(gu_st, staged_gu, gu_buf)
        spread_sd = mail.post(
            sd_all.at[planes, 0], [(sd_ref, sd_all.at[z, f], peer) for peer in in_column]
        )
        passed_wo.wait_recv()
        for i in range(nc):
            wo_all[i * block_rows : (i + 1) * block_rows, :] = join(
                wo_buf[i], (block_rows, width)
            )
    ffn_gain = column_row(w_ref[:, tail_at:], SMALL + num_experts + 1)
    for q in range(num_seqs):
        with jax.named_scope("a_wait_context"):
            ctx_passing[q].wait_recv()
        with jax.named_scope("a_project"):
            total = hid_all[q].reshape(full_len, width).astype(F32)
            for i in range(nc):
                total = total + mm(
                    ctx_all[i, q].reshape(full_len, head_width),
                    wo_all[i * head_width : (i + 1) * head_width, :],
                )
            acc_a[q * full_len : (q + 1) * full_len] = total
            nt_all[q] = (
                (total * inverse_rms(total) * ffn_gain).astype(BF).reshape(nc, shard_len, width)
            )
    by_block = acc_a.at[pl.ds(0, nc * tok)].reshape(num_seqs, nc, shard_len, width)
    for q in range(num_seqs):
        att_own[q] = by_block[q, c]

    with jax.named_scope("b_dispatch"):
        normed = jnp.concatenate([nt_all[q, c] for q in range(num_seqs)], axis=0)
        tail = w_ref[:, tail_at:]
        logits = mm(normed, tail)
        chosen = [jnp.sum(hot * logits, axis=1, keepdims=True) for hot in hots]
        top = jnp.maximum(chosen[0], chosen[1])
        raised = [jnp.exp(value - top) for value in chosen]
        gates = [value / (raised[0] + raised[1]) for value in raised]
        weighted = [(gates[k] * up_f).astype(BF) for k in range(2)]
        boxes = mm_tn(anyone, normed)
        boxes = boxes + mm_tn(dispatch_d[0], weighted[0]) + mm_tn(dispatch_d[1], weighted[1])
        sb[...] = boxes.reshape(num_experts, BOX, width).astype(BF)
        row_copies = []
        for dz in range(nz):
            post = mail.open(ar.at[f, 0] if dz else ar.at[f, 0, others])
            for dc in range(nc):
                if dz or dc:
                    to = (wrap(c + dc, nc), wrap(z + dz, nz), f)
                    post.add(sb.at[to[1] * nc + to[0]], ar.at[f, z, c], to)
            row_copies.append(post)
        ar[f, z, c] = sb[z * nc + c]
    pump(bulk, len(bulk))

    with jax.named_scope("b_forward_gu"):
        passed_gu = forward(spread_gu, gu_buf)
        spread_sd.wait_recv()
        passed_sd = mail.post(sd_all.at[:, f], [(sd_all.at[:, f], sd_all.at[:, f], sibling)])
        passed_gu.wait_recv()
        passed_sd.wait_recv()
        for i in range(nc):
            gu_all[i * block_rows : (i + 1) * block_rows, :] = join(
                gu_buf[i], (block_rows, 2 * own_units)
            )
    with jax.named_scope("b_wait_upstream"):
        for post in up_passing:
            post.wait_recv()
    plane_tok = nc * tok
    shared_rows = nt_all.reshape(plane_tok, width)
    shared_grads = up_all.reshape(plane_tok, width)
    shared_down = sd_all.reshape(own_units, width)
    with jax.named_scope("b_shared"):
        first = pl.ds(0, plane_tok)
        acc_a[...] = jnp.zeros(acc_a.shape, F32)
        acc_b[...] = jnp.zeros(acc_b.shape, F32)

        def shared_block(j, carry):
            ffn_block(
                j, shared_rows[...], shared_grads[...], gu_all, shared_down, sh_hidden, sh_dm,
                acc_a.at[first], acc_b.at[first], own_units, 256,
            )
            return carry

        lax.fori_loop(0, own_units // 256, shared_block, 0)
        for k, acc in enumerate((acc_a, acc_b)):
            cut = acc.at[first].reshape(num_seqs, nc, shard_len, width)
            for q in range(num_seqs):
                sh_own[k, q, 0] = cut[q, c]
                sh_own[k, q, 1] = cut[q, near_y if q == 0 else near_x]
            sh_send[k] = cut[...].astype(BF)

    def first_leg(inbox, box, lead):
        post = mail.open(inbox)
        for q in range(num_seqs):
            peer = to_x if q == 0 else to_y
            for at, chip in enumerate((near_x if q == 0 else near_y, far)):
                post.add(box.at[lead + (q, chip)], inbox.at[lead + (q, at)], peer)
        return post

    shared_first = first_leg(sh_in, sh_send, (slice(None),))

    mail.settle([spread_gu, passed_gu])
    ggu = gu_buf
    with jax.named_scope("b_shared_grads"):

        def gate_up_grads(j, carry):
            at = pl.ds(pl.multiple_of(j * 256, 256), 256)
            piece = mm_tn(shared_rows[...], sh_dm[:, at])
            ggu[:, :, :, :, at] = piece.reshape(ggu.shape[:4] + (256,)).astype(BF)
            return carry

        lax.fori_loop(0, 2 * own_units // 256, gate_up_grads, 0)
        gsd[...] = mm_tn(sh_hidden[...], shared_grads[...]).reshape(gsd.shape).astype(BF)
        sibling_gu = mail.post(sib_gu, [(ggu.at[:, :, 1 - f], sib_gu, sibling)])
        sibling_sd = mail.post(sib_sd, [(gsd.at[:, 1 - f], sib_sd, sibling)])

    with jax.named_scope("b_reduce_shared"):
        def two_cores(copy, own, inbox):
            copy.wait_recv()
            inbox[...] = (own.astype(F32) + inbox[...].astype(F32)).astype(BF)

        def four_planes(copy, buffer, inbox):
            copy.wait_recv()
            for i in range(nc):
                inbox[i] = (buffer[i, :, f].astype(F32) + inbox[i].astype(F32)).astype(BF)

        four_planes(sibling_gu, ggu, sib_gu)
        two_cores(sibling_sd, gsd[:, f], sib_sd)
        gu_copies = mail.post(
            zi_gu,
            [
                (sib_gu.at[:, wrap(z + s, nz)], zi_gu.at[s - 1], in_column[s - 1])
                for s in range(1, nz)
            ],
        )
        sd_copies = mail.post(
            zi_sd,
            [(sib_sd.at[wrap(z + s, nz)], zi_sd.at[s - 1], in_column[s - 1]) for s in range(1, nz)],
        )

    with jax.named_scope("b_forward_rows"):
        forwards = mail.open(ar.at[f])
        for dz in range(nz):
            row_copies[dz].wait_recv()
            origin = wrap(z + nz - dz, nz)
            forwards.add(ar.at[f, origin], ar.at[f, origin], sibling)
        forwards.wait_recv()
        keep_x, keep_d = (box_rows(CAP, num_experts, shift) for shift in (0, CAP))
        for core in range(2):
            at = slice(core * num_slots, (core + 1) * num_slots)
            boxes = join(ar[core], (box_slots, width))
            xs[at] = mm(keep_x, boxes).astype(BF)
            ds[at] = mm(keep_d, boxes).astype(BF)
    with jax.named_scope("b_wait_down"):
        @pl.when(to_core == f)
        def _():
            expert_out.wait_recv(remote_out)
            own_out.wait()

        @pl.when(to_core != f)
        def _():
            expert_out.wait_recv()

    acc_a[...] = jnp.zeros(acc_a.shape, F32)
    acc_b[...] = jnp.zeros(acc_b.shape, F32)
    for j in range(steps):
        with jax.named_scope("b_wait_experts"):
            own_in(j).wait()
            expert_in[j].wait_recv()
        with jax.named_scope("b_experts"):
            ffn_block(
                j, xs[...], ds[...], wie, woe, ex_hidden, ex_dm, acc_a, acc_b, half_units, step
            )
    mail.settle(row_copies)
    pr = sb
    with jax.named_scope("b_sibling_sum"):

        def boxed(core):
            at = pl.ds(pl.multiple_of(core * num_slots, num_slots), num_slots)
            return (
                mm_tn(keep_x, acc_a[at].astype(BF)) + mm_tn(keep_d, acc_b[at].astype(BF))
            ).reshape(num_experts, BOX, width)

        pr[...] = boxed(1 - f).astype(BF)
        swap = mail.post(pin, [(pr, pin, sibling)])
        ours = boxed(f)
        swap.wait_recv()
        fb[...] = (ours + pin[...].astype(F32)).astype(BF)
        returns = mail.post(
            rb.at[pl.ds(0, num_experts - 1)],
            [(fb.at[to[1] * nc + to[0]], rb.at[z * nc + c], to) for to in everyone],
        )
        rb[z * nc + c] = fb[z * nc + c]
    with jax.named_scope("b_second_leg"):
        shared_first.wait_recv()
        for k in range(2):
            for q in range(num_seqs):
                sh_mid[k, q] = (sh_own[k, q, 1] + sh_in[k, q, 1].astype(F32)).astype(BF)
        shared_second = mail.post(
            sh_end,
            [
                (sh_mid.at[:, q], sh_end.at[:, q], to_y if q == 0 else to_x)
                for q in range(num_seqs)
            ],
        )

    gwi, gwo = wie, woe

    def expert_grads(j, carry):
        at = pl.ds(pl.multiple_of(j * 256, 256), 256)
        gwi[:, at] = mm_tn(xs[...], ex_dm[:, at]).astype(BF)
        return carry

    home = []
    home_in = mail.open(gwi.at[pl.ds(0, remote_rows)])
    home_out = mail.open(gwo, keep=False)
    remote_home = gwo.at[pl.ds(0, (nc - 1) * out_rows)]
    home_in_own = pltpu.make_async_copy(
        gwi.at[pl.ds(0, shard_rows)], gwi.at[pl.ds(0, shard_rows)], lsem.at[1]
    )

    def send_home_in(j, s, g, side):
        owner = wrap(c + s, nc)
        core = f if g == 0 else 1 - f
        from_rows = pl.ds(
            pl.multiple_of((2 * owner + core) * shard_rows, shard_rows), shard_rows
        )
        to_lane = pl.multiple_of(side * units + f * half_units + j * HOME, HOME)
        src = gwi.at[from_rows, pl.ds(side * half_units + j * HOME, HOME)]
        dst = ein_ref.at[c, :, pl.ds(to_lane, HOME)]
        if s == 0 and g == 0:
            pltpu.make_async_copy(src, dst, lsem.at[1]).start()
        else:
            home_in.add(src, dst, (owner, z, core))

    def home_out_own(j):
        return pltpu.make_async_copy(
            gwo.at[pl.ds(j * out_rows, out_rows)], eout_ref.at[c], lsem.at[0]
        )

    def send_home_out(j):
        to_block = f * nc + j

        @pl.when(to_block == block)
        def _():
            home_out_own(j).start()

        @pl.when(to_block != block)
        def _():
            home_out.add(
                gwo.at[pl.ds(j * out_rows, out_rows)],
                eout_ref.at[c],
                (to_block // 2, z, wrap(to_block, 2)),
            )

    for side in range(2):
        for j in range(half_units // HOME):
            for s in range(1, nc + 1):
                for g in range(2):
                    home.append(functools.partial(send_home_in, j, s % nc, g, side))
    for j in range(nc):
        home.append(functools.partial(send_home_out, j))
    with jax.named_scope("b_gwi"):
        lax.fori_loop(0, 2 * half_units // 256, expert_grads, 0)
    pump(home, PUMPS[1])
    with jax.named_scope("b_gwo"):
        for j in range(nc):
            gwo[j * out_rows : (j + 1) * out_rows, :] = mm_tn(
                ex_hidden[:, j * out_rows : (j + 1) * out_rows], ds[...]
            ).astype(BF)

    with jax.named_scope("c_wait_shared"):
        shared_second.wait_recv()
        shared, d_normed = [
            jnp.concatenate(
                [
                    sh_own[k, q, 0] + sh_in[k, q, 0].astype(F32) + sh_end[k, q].astype(F32)
                    for q in range(num_seqs)
                ],
                axis=0,
            )
            for k in range(2)
        ]
    with jax.named_scope("c_wait_returns"):
        returns.wait_recv()
    with jax.named_scope("c_combine"):
        attended = att_own[...].reshape(tok, width)
        inverse = inverse_rms(attended)
        results = join(rb[...], (box_slots, width))
        routed = [mm(dispatch[k], results) for k in range(2)]
        mixture = gates[0] * routed[0] + gates[1] * routed[1]
        out_ref[...] = (
            (live * (attended + mixture + shared)).astype(BF).reshape(out_ref.shape)
        )
        d_gates = [jnp.sum(routed[k] * up_f, axis=1, keepdims=True) for k in range(2)]
        mean_gate = gates[0] * d_gates[0] + gates[1] * d_gates[1]
        d_logits = hots[0] * (gates[0] * (d_gates[0] - mean_gate)) + hots[1] * (
            gates[1] * (d_gates[1] - mean_gate)
        )
        d_normed = d_normed + mm(anyone_d, results) + split_dot(mm_nt, d_logits, tail)
        d_attended = upstream + norm_back(attended, inverse, d_normed * ffn_gain)
        d_att_b = d_attended.astype(BF)
        d_context = mm_nt(d_att_b, wo_all[...]).astype(BF)
        for i in range(nc):
            dctx_send[i] = d_context[:, i * head_width : (i + 1) * head_width].reshape(
                num_seqs, shard_len, head_width
            )
        for q in range(num_seqs):
            dctx_all[q, c] = dctx_send[c, q]
        dctx_copies = mail.post(
            dctx_all.at[:, others],
            [
                (dctx_send.at[wrap(c + s, nc)], dctx_all.at[:, c], in_plane[s - 1])
                for s in range(1, nc)
            ],
        )
        gin_ref[...] = d_attended.reshape(gin_ref.shape)
    pump(home, PUMPS[2])

    mail.settle([spread_wo, passed_wo])
    gwo_at = wo_buf
    with jax.named_scope("c_reduce"):
        for i in range(nc):
            mine = jnp.concatenate([ctx_all[i, q, c] for q in range(num_seqs)], axis=0)
            gwo_at[i] = mm_tn(mine, d_att_b).reshape(gwo_at.shape[1:]).astype(BF)
        sibling_wo = mail.post(sib_wo, [(gwo_at.at[:, :, 1 - f], sib_wo, sibling)])
        d_router = split_dot(mm_tn, normed, d_logits, left_wide=False)
        d_gain = jnp.sum(d_normed * attended * inverse, axis=0, keepdims=True)
        turned = jnp.transpose(jnp.broadcast_to(d_gain, (128, width)), (1, 0))
        extra_lane = lax.broadcasted_iota(jnp.int32, (width, 128), 1)
        extras = jnp.where(extra_lane == SMALL + num_experts + 1, turned, d_router)
        four_planes(sibling_wo, gwo_at, sib_wo)
        wo_copies = mail.post(
            zi_wo,
            [
                (sib_wo.at[:, wrap(z + s, nz)], zi_wo.at[s - 1], in_column[s - 1])
                for s in range(1, nz)
            ],
        )

    with jax.named_scope("c_wait_dctx"):
        dctx_copies.wait_recv()
    grad_qkv = jnp.zeros((width, 3 * head_width), F32)
    rs_first = mail.open(rs_in)
    for q in range(num_seqs):
        with jax.named_scope("c_attention"):
            d_context = dctx_all[q].reshape(full_len, head_width)
            allowed = allowed_keys(len_ref[q], half_len, full_len)
            merged = qkv_ref[q]
            d_query, d_key, d_value = [], [], []
            for h in range(heads_here):
                query = merged[:, h * HS : (h + 1) * HS]
                key = merged[:, head_width + h * HS : head_width + (h + 1) * HS]
                value = merged[:, 2 * head_width + h * HS : 2 * head_width + (h + 1) * HS]
                d_head = d_context[:, h * HS : (h + 1) * HS]
                probs = head_probs(query, key, allowed)
                d_probs = mm_nt(d_head, value)
                delta = jnp.sum(probs * d_probs, axis=1, keepdims=True)
                d_scores = (probs * (d_probs - delta)).astype(BF)
                d_query.append(mm(d_scores, key) * (HS**-0.5))
                d_key.append(mm_tn(d_scores, query) * (HS**-0.5))
                d_value.append(mm_tn(probs.astype(BF), d_head))
            both = jnp.concatenate(d_query + d_key, axis=1)
            both = both * cosines - swap_halves(both) * sines
            d_merged = jnp.concatenate([both] + d_value, axis=1).astype(BF)
            product = mm_nt(d_merged, w_ref[:, : 3 * head_width]).reshape(nc, shard_len, width)
            part_own[q] = product
            part[q] = product.astype(BF)
            for at, chip in enumerate((near_x if q == 0 else near_y, far)):
                rs_first.add(part.at[q, chip], rs_in.at[q, at], to_x if q == 0 else to_y)
            grad_qkv = grad_qkv + mm_tn(normed_ref[q], d_merged)
    pump(home, len(home) - 2)
    mail.settle([spread_wq, passed_wq])
    gq = wq_buf
    with jax.named_scope("c_reduce_q"):
        last = jnp.concatenate([grad_qkv[:, tail_at:], extras[:, 3 * head_width - tail_at :]], axis=1)
        gq[...] = (
            jnp.concatenate([grad_qkv[:, :tail_at], last], axis=1).reshape(gq.shape).astype(BF)
        )
        sibling_q = mail.post(sib_q, [(gq.at[:, :, 1 - f], sib_q, sibling)])
        four_planes(sibling_q, gq, sib_q)
        q_copies = mail.post(
            zi_q,
            [
                (sib_q.at[:, wrap(z + s, nz)], zi_q.at[s - 1], in_column[s - 1])
                for s in range(1, nz)
            ],
        )
    with jax.named_scope("c_second_leg"):
        rs_first.wait_recv()
        for q in range(num_seqs):
            relay = part_own[q, near_y if q == 0 else near_x]
            rs_mid[q] = (relay + rs_in[q, 1].astype(F32)).astype(BF)
        rs_second = mail.post(
            rs_end,
            [(rs_mid.at[q], rs_end.at[q], to_y if q == 0 else to_x) for q in range(num_seqs)],
        )

    def column_sum(own, copies, inbox):
        copies.wait_recv()
        total = own.astype(F32)
        for s in range(1, nz):
            total = total + inbox[s - 1].astype(F32)
        return total

    def hand_out(box, final):
        final[c] = box[c]
        return mail.post(
            final.at[others],
            [(box.at[wrap(c + s, nc)], final.at[c], in_plane[s - 1]) for s in range(1, nc)],
        )

    with jax.named_scope("c_column_gu"):
        pb_gu[...] = column_sum(sib_gu[:, z], gu_copies, zi_gu).astype(BF)
        final_gu = hand_out(pb_gu, fgu_ref)
    with jax.named_scope("c_column_sd"):
        fsd_ref[...] = column_sum(sib_sd[z], sd_copies, zi_sd)
    with jax.named_scope("c_column_wo"):
        pb_wo[...] = column_sum(sib_wo[:, z], wo_copies, zi_wo).astype(BF)
        final_wo = hand_out(pb_wo, in_wo)
    with jax.named_scope("c_column_q"):
        pb_q[...] = column_sum(sib_q[:, z], q_copies, zi_q).astype(BF)
        final_q = hand_out(pb_q, fq_ref)
    pump(home, len(home))
    with jax.named_scope("c_grad_in"):
        rs_second.wait_recv()
        for q in range(num_seqs):
            d_normed = part_own[q, c] + rs_in[q, 0].astype(F32) + rs_end[q].astype(F32)
            rows = hid_ref[q].astype(F32)
            gin_ref[q] = gin_ref[q] + norm_back(rows, inverse_rms(rows), d_normed * attn_gain)
    with jax.named_scope("c_final"):
        final_wo.wait_recv()
        fwo_ref[...] = jnp.sum(in_wo[...].astype(F32), axis=0)
        final_gu.wait_recv()
        final_q.wait_recv()
    with jax.named_scope("c_wait_home"):
        home_in_own.wait()
        home_in.wait_recv()

        @pl.when(to_core == f)
        def _():
            home_out_own(0).wait()
            home_out.wait_recv(remote_home)
            home_out.wait_send(remote_home)
            expert_out.wait_send(remote_out)

        @pl.when(to_core != f)
        def _():
            home_out.wait_recv()
            home_out.wait_send()
            expert_out.wait_send()

    assert mail.count <= POSTS, mail.count
    with jax.named_scope("z_finish"):
        mail.finish()


def finish_kernel(
    nc, fq_ref, fgu_ref, wqkv_ref, ga_ref, ein_ref, eout_ref, out_in, gin_in, fsd_in, fwo_in,
    gq_ref, gr_ref, gga_ref, ggf_ref, ggu_ref, oin_ref, oout_ref, out_ref, gin_ref, fsd_ref, fwo_ref,
):
    oin_ref[...] = ein_ref[...].astype(F32)
    oout_ref[...] = eout_ref[...].astype(F32)

    @pl.when((pl.program_id(0) == 0) & (pl.program_id(1) == 0))
    def _():
        out_ref[...] = out_in[...]
        gin_ref[...] = gin_in[...]
        fsd_ref[...] = fsd_in[...]
        fwo_ref[...] = fwo_in[...]
        rows_w = wqkv_ref.shape[0]
        head_width = wqkv_ref.shape[1] // 3 // nc
        grads = jnp.concatenate(
            [
                fq_ref[i, :, side * head_width : (side + 1) * head_width].astype(F32)
                for side in range(3)
                for i in range(nc)
            ],
            axis=1,
        )
        gq_ref[...] = grads
        own_units = fgu_ref.shape[2] // 2
        ggu_ref[...] = jnp.concatenate(
            [
                fgu_ref[i, :, side * own_units : (side + 1) * own_units].astype(F32)
                for side in range(2)
                for i in range(nc)
            ],
            axis=1,
        )
        extras = jnp.sum(fq_ref[:, :, 3 * head_width - SMALL :].astype(F32), axis=0)
        num_experts = gr_ref.shape[0]
        first = jnp.sum(wqkv_ref[...].astype(F32) * grads, axis=1, keepdims=True)
        lane = lax.broadcasted_iota(jnp.int32, (rows_w, 128), 1)
        both = jnp.where(lane == SMALL + num_experts, first, extras)
        turned = jnp.transpose(
            jnp.concatenate([both, jnp.zeros((128 - rows_w, 128), F32)], axis=0), (1, 0)
        )
        gr_ref[...] = turned[SMALL : SMALL + num_experts, :rows_w]
        at = SMALL + num_experts
        gga_ref[...] = turned[at : at + 1, :rows_w] / ga_ref[...].astype(F32)
        ggf_ref[...] = turned[at + 1 : at + 2, :rows_w]


def vmem(*shape, dtype=jnp.bfloat16):
    return pltpu.VMEM(shape, dtype)


def fast_device(
    hidden_in, seq_lengths, expert_ids, route_rank, gain_attn, w_qkv, w_out, w_router, gain_ffn,
    w_gate_up, w_shared_down, w_experts_in, w_experts_out, grad_output,
):
    nc, nz = lax.axis_size("ctx"), lax.axis_size("exp")
    num_seqs, two_ends, half_len, width = hidden_in.shape
    shard_len = 2 * half_len
    full_len = nc * shard_len
    tok = num_seqs * shard_len
    rows_w = w_qkv.shape[0]
    head_width = w_qkv.shape[1] // 3 // nc
    num_experts = w_router.shape[1]
    down_rows = w_shared_down.shape[0]
    own_units = w_gate_up.shape[1] // 2 // nc
    half_units = w_experts_in.shape[2] // 4
    hbm, vm, sm = pl.ANY, pltpu.VMEM, pltpu.SMEM
    dma = pltpu.SemaphoreType.DMA

    seq_shape = (num_seqs, shard_len, width)
    group_shape = (num_seqs, nc, shard_len, width)
    blocks = (nc, nz, 2, rows_w)
    half_blocks = (nc, nz, rows_w)
    wide_cols = 3 * head_width + SMALL
    num_slots = num_experts * CAP
    row_box = (num_experts, BOX, width)
    plane_tok = nc * tok
    outs = [
        (seq_shape, BF),
        (seq_shape, F32),
        ((nc, rows_w, wide_cols), BF),
        ((nc, rows_w, 2 * own_units), BF),
        ((down_rows, width), F32),
        ((rows_w, width), F32),
        (w_experts_in.shape, BF),
        (w_experts_out.shape, BF),
    ]
    out, gin, fq, fgu, fsd, fwo, ein, eout = pl.pallas_call(
        functools.partial(block_kernel, nc, nz),
        out_shape=[jax.ShapeDtypeStruct(shape, dtype) for shape, dtype in outs],
        in_specs=[
            pl.BlockSpec(memory_space=space) for space in [sm] + [vm] * 11 + [hbm, hbm]
        ],
        out_specs=[pl.BlockSpec(memory_space=space) for space in [vm] * 6 + [hbm, hbm]],
        scratch_shapes=[
            vmem(full_len, 256, dtype=F32),
            vmem(*group_shape),
            vmem(*seq_shape),
            vmem(*group_shape),
            vmem(nc, rows_w, wide_cols),
            vmem(nc, rows_w, wide_cols),
            vmem(*blocks, wide_cols),
            vmem(width, wide_cols),
            vmem(nc, rows_w, 2 * own_units),
            vmem(*blocks, 2 * own_units),
            vmem(width, 2 * own_units),
            vmem(nc, rows_w, width),
            vmem(*blocks, width),
            vmem(width, width),
            vmem(nz, 2, down_rows, width),
            vmem(width, 2 * half_units),
            vmem(half_units, width),
            vmem(num_seqs, full_len, width),
            vmem(num_seqs, full_len, 3 * head_width),
            vmem(nc, num_seqs, nc, shard_len, head_width),
            vmem(*seq_shape, dtype=F32),
            vmem(*group_shape),
            vmem(*row_box),
            vmem(2, nz, nc, BOX, width),
            vmem(2 * num_slots, width),
            vmem(2 * num_slots, width),
            vmem(2 * num_slots, width, dtype=F32),
            vmem(2 * num_slots, width, dtype=F32),
            vmem(2, num_seqs, 2, shard_len, width, dtype=F32),
            vmem(plane_tok, own_units),
            vmem(plane_tok, 2 * own_units),
            vmem(2, *group_shape),
            vmem(2, num_seqs, 2, shard_len, width),
            vmem(2, *seq_shape),
            vmem(2, *seq_shape),
            vmem(2 * num_slots, half_units),
            vmem(2 * num_slots, 2 * half_units),
            vmem(*row_box),
            vmem(*row_box),
            vmem(*row_box),
            vmem(nz, 2, down_rows, width),
            vmem(*seq_shape),
            vmem(nc, num_seqs, shard_len, head_width),
            vmem(num_seqs, nc, shard_len, head_width),
            vmem(*group_shape),
            vmem(*group_shape, dtype=F32),
            vmem(num_seqs, 2, shard_len, width),
            vmem(*seq_shape),
            vmem(*seq_shape),
            vmem(*half_blocks, 2 * own_units),
            vmem(nz - 1, nc, rows_w, 2 * own_units),
            vmem(nc, rows_w, 2 * own_units),
            vmem(*half_blocks, wide_cols),
            vmem(nz - 1, nc, rows_w, wide_cols),
            vmem(nc, rows_w, wide_cols),
            vmem(nz, down_rows, width),
            vmem(nz - 1, down_rows, width),
            vmem(*half_blocks, width),
            vmem(nz - 1, nc, rows_w, width),
            vmem(nc, rows_w, width),
            vmem(nc, rows_w, width),
            dma((POSTS,)),
            dma((POSTS,)),
            dma((1 + half_units // 256,)),
        ],
        compiler_params=pltpu.CompilerParams(
            collective_id=0, has_side_effects=True, vmem_limit_bytes=VMEM_BYTES
        ),
        cost_estimate=pl.CostEstimate(
            flops=16_000_000_000, bytes_accessed=30_000_000, transcendentals=0
        ),
        name="block_forward_backward",
    )(
        seq_lengths,
        hidden_in.reshape(seq_shape),
        grad_output.reshape(seq_shape),
        expert_ids.transpose(0, 1, 3, 2),
        route_rank.reshape(1, tok),
        w_qkv, w_router.T, gain_attn.reshape(1, rows_w), gain_ffn.reshape(1, rows_w),
        w_gate_up, w_out, w_shared_down, w_experts_in, w_experts_out,
    )

    def whole(shape):
        return pl.BlockSpec(shape, lambda e, j: (0,) * len(shape))

    def one(shape):
        return pl.BlockSpec((1, shape[1], shape[2] // WIDEN), lambda e, j: (e, 0, j))

    ins = [fq, fgu, w_qkv, gain_attn.reshape(1, rows_w), ein, eout, out, gin, fsd, fwo]
    results = [
        (w_qkv.shape, F32),
        (w_router.shape[::-1], F32),
        ((1, rows_w), F32),
        ((1, rows_w), F32),
        (w_gate_up.shape, F32),
        (ein.shape, F32),
        (eout.shape, F32),
        (seq_shape, BF),
        (seq_shape, F32),
        (fsd.shape, F32),
        (fwo.shape, F32),
    ]
    grad_qkv, grad_router, grad_ga, grad_gf, grad_gu, grad_in, grad_out, out, gin, fsd, fwo = pl.pallas_call(
        functools.partial(finish_kernel, nc),
        grid=(ein.shape[0], WIDEN),
        out_shape=[jax.ShapeDtypeStruct(shape, dtype) for shape, dtype in results],
        in_specs=[one(x.shape) if i in (4, 5) else whole(x.shape) for i, x in enumerate(ins)],
        out_specs=[
            one(shape) if i in (5, 6) else whole(shape) for i, (shape, _) in enumerate(results)
        ],
        compiler_params=pltpu.CompilerParams(vmem_limit_bytes=VMEM_BYTES),
        name="widen_gradients",
    )(*ins)
    return (
        out.reshape(hidden_in.shape),
        gin.reshape(hidden_in.shape),
        grad_ga.reshape(rows_w),
        grad_qkv,
        fwo,
        grad_router.T,
        grad_gf.reshape(rows_w),
        grad_gu,
        fsd,
        grad_in,
        grad_out,
    )


def fits(mesh, hidden_in, w_qkv, w_router, w_gate_up, w_experts_in):
    nc, nz, nf = mesh.shape["ctx"], mesh.shape["exp"], mesh.shape["fsdp"]
    heads = w_qkv.shape[1] // 3 // HS
    return (
        nf == 2
        and nc == 4
        and nz == 4
        and heads == 12
        and w_router.shape[1] == nc * nz
        and w_qkv.shape[0] == 768
        and hidden_in.shape[2] == 32 * nc
        and hidden_in.shape[0] == 2 * nz * nf
        and hidden_in.shape[3] == 768
        and w_gate_up.shape[1] == w_experts_in.shape[2] == 4096
        and 2 * CAP <= BOX
    )


def solution(mesh):
    def whole(*args):
        chosen = fast_device if fits(mesh, args[0], args[5], args[7], args[9], args[11]) else per_device
        return placed(mesh, chosen)(*args)

    return whole


def placed(mesh, chosen):
    return jax.shard_map(
        chosen,
        mesh=mesh,
        in_specs=(
            P(("exp", "fsdp"), None, "ctx", None),
            P(("exp", "fsdp")),
            P(("exp", "fsdp"), None, "ctx", None),
            P(("exp", "fsdp"), "ctx", None),
            P(("ctx", "exp", "fsdp")),
            P(("ctx", "exp", "fsdp"), None),
            P(("ctx", "exp", "fsdp"), None),
            P(("ctx", "exp", "fsdp"), None),
            P(("ctx", "exp", "fsdp")),
            P(("ctx", "exp", "fsdp"), None),
            P(("ctx", "exp", "fsdp"), None),
            P("exp", ("ctx", "fsdp"), None),
            P("exp", ("ctx", "fsdp"), None),
            P(("exp", "fsdp"), None, "ctx", None),
        ),
        out_specs=(
            P(("exp", "fsdp"), None, "ctx", None),
            P(("exp", "fsdp"), None, "ctx", None),
            P(("ctx", "exp", "fsdp")),
            P(("ctx", "exp", "fsdp"), None),
            P(("ctx", "exp", "fsdp"), None),
            P(("ctx", "exp", "fsdp"), None),
            P(("ctx", "exp", "fsdp")),
            P(("ctx", "exp", "fsdp"), None),
            P(("ctx", "exp", "fsdp"), None),
            P("exp", ("ctx", "fsdp"), None),
            P("exp", ("ctx", "fsdp"), None),
        ),
        check_vma=False,
    )
```

```python
import functools
import math

import jax
import jax.numpy as jnp
from jax import lax
from jax.experimental import pallas as pl
from jax.experimental.pallas import tpu as pltpu
from jax.sharding import PartitionSpec as P

HS = 64
CAP = 18


epsilon = 1e-06
masked_out = -1e30
highest = lax.Precision.HIGHEST


def rms_norm(values_in, gain_row):
    return (
        values_in
        * lax.rsqrt(jnp.mean(values_in * values_in, axis=-1, keepdims=True) + epsilon)
        * gain_row
    )


def rope_tables(places):
    half_size = HS // 2
    frequency = 10000.0 ** (-jnp.arange(half_size, dtype=jnp.float32) * 2.0 / HS)
    angles = places.astype(jnp.float32)[:, None] * frequency[None, :]
    return (jnp.cos(angles), jnp.sin(angles))


def rotate(values_in, cosines, sine_rows):
    half_size = values_in.shape[-1] // 2
    leading = values_in[..., :half_size]
    trailing = values_in[..., half_size:]
    cos_rows = cosines[:, None, :]
    sin_rows = sine_rows[:, None, :]
    return jnp.concatenate(
        [leading * cos_rows - trailing * sin_rows, leading * sin_rows + trailing * cos_rows],
        axis=-1,
    )


def swiglu(merged_rows):
    gate_part, up_part = jnp.split(merged_rows, 2, axis=-1)
    return jax.nn.silu(gate_part) * up_part


def first_t(left_side, right_side, precision=None):
    return lax.dot_general(
        left_side,
        right_side,
        (((0,), (0,)), ((), ())),
        precision=precision,
        preferred_element_type=jnp.float32,
    )


def second_t(left_side, right_side, precision=None):
    return lax.dot_general(
        left_side,
        right_side,
        (((1,), (1,)), ((), ())),
        precision=precision,
        preferred_element_type=jnp.float32,
    )


def per_device(
    hidden_in,
    seq_lengths,
    expert_ids,
    route_rank,
    gain_attn,
    w_qkv,
    w_out,
    w_router,
    gain_ffn,
    w_gate_up,
    w_shared_down,
    w_experts_in,
    w_experts_out,
    grad_output,
):
    num_seqs, two_ends, half_len, model_width = hidden_in.shape
    shard_len = 2 * half_len
    tok_count = num_seqs * shard_len
    num_heads = model_width // HS
    score_scale = HS ** (-0.5)
    ctx_size = lax.axis_size("ctx")
    full_len = shard_len * ctx_size
    whole_half = half_len * ctx_size
    gain_one, wqkv_all, wout_all, router_all, gain_two, shared_in, shared_down = (
        lax.all_gather(gain_attn, ("ctx", "exp", "fsdp"), axis=0, tiled=True),
        lax.all_gather(w_qkv, ("ctx", "exp", "fsdp"), axis=0, tiled=True),
        lax.all_gather(w_out, ("ctx", "exp", "fsdp"), axis=0, tiled=True),
        lax.all_gather(w_router, ("ctx", "exp", "fsdp"), axis=0, tiled=True),
        lax.all_gather(gain_ffn, ("ctx", "exp", "fsdp"), axis=0, tiled=True),
        lax.all_gather(w_gate_up, ("ctx", "exp", "fsdp"), axis=0, tiled=True),
        lax.all_gather(w_shared_down, ("ctx", "exp", "fsdp"), axis=0, tiled=True),
    )
    experts_in, experts_out = (
        lax.all_gather(w_experts_in, ("ctx", "fsdp"), axis=1, tiled=True),
        lax.all_gather(w_experts_out, ("ctx", "fsdp"), axis=1, tiled=True),
    )
    lower_places = lax.axis_index("ctx") * half_len + jnp.arange(half_len, dtype=jnp.int32)
    places = jnp.concatenate([lower_places, full_len - 1 - lower_places])
    whole_range = jnp.arange(whole_half, dtype=jnp.int32)
    full_places = jnp.concatenate([whole_range, full_len - 1 - whole_range])
    live_mask = (places[None, :] < seq_lengths[:, None]).astype(jnp.float32)
    live_rows = live_mask.reshape(tok_count, 1)
    inputs_f = hidden_in.astype(jnp.float32).reshape(tok_count, model_width)
    gain_attn_f = gain_one.astype(jnp.float32)
    normed_b = rms_norm(inputs_f, gain_attn_f).astype(jnp.bfloat16)
    qkv_merged = jnp.dot(normed_b, wqkv_all, preferred_element_type=jnp.float32).reshape(
        num_seqs, shard_len, 3, num_heads, HS
    )
    cosines, sine_rows = rope_tables(places)
    queries = rotate(qkv_merged[:, :, 0], cosines, sine_rows).astype(jnp.bfloat16)
    keys_local = rotate(qkv_merged[:, :, 1], cosines, sine_rows).astype(jnp.bfloat16)
    values_local = qkv_merged[:, :, 2].astype(jnp.bfloat16)
    end_shape = (num_seqs, 2, half_len, model_width)
    keys_full, values_full = (
        lax.all_gather(keys_local.reshape(end_shape), "ctx", axis=2, tiled=True),
        lax.all_gather(values_local.reshape(end_shape), "ctx", axis=2, tiled=True),
    )
    keys_full = keys_full.reshape(num_seqs, full_len, num_heads, HS)
    values_full = values_full.reshape(num_seqs, full_len, num_heads, HS)
    stat_shape = (num_seqs, num_heads, shard_len)
    block_range = jnp.arange(ctx_size, dtype=jnp.int32)

    def block_scores(query_rows, query_places, key_rows, key_places):
        scores = (
            jnp.einsum("bqhd,bkhd->bhqk", query_rows, key_rows, preferred_element_type=jnp.float32)
            * score_scale
        )
        allowed = (key_places[None, None, :] <= query_places[None, :, None]) & (
            key_places[None, None, :] < seq_lengths[:, None, None]
        )
        return jnp.where(allowed[:, None], scores, masked_out)

    def key_block(block_idx):
        offset = block_idx * shard_len
        return (
            lax.dynamic_slice_in_dim(keys_full, offset, shard_len, 1),
            lax.dynamic_slice_in_dim(values_full, offset, shard_len, 1),
            lax.dynamic_slice_in_dim(full_places, offset, shard_len, 0),
        )

    def lse_step(state_in, block_idx):
        run_max, run_sum = state_in
        key_rows, value_rows, key_places = key_block(block_idx)
        scores = block_scores(queries, places, key_rows, key_places)
        new_max = jnp.maximum(run_max, jnp.max(scores, axis=-1))
        run_sum = run_sum * jnp.exp(run_max - new_max) + jnp.sum(
            jnp.exp(scores - new_max[..., None]), axis=-1
        )
        return ((new_max, run_sum), None)

    (row_max, row_sum), unused = lax.scan(
        lse_step,
        (jnp.full(stat_shape, masked_out, jnp.float32), jnp.zeros(stat_shape, jnp.float32)),
        block_range,
    )
    log_total = row_max + jnp.log(row_sum)

    def context_step(running, block_idx):
        key_rows, value_rows, key_places = key_block(block_idx)
        prob_rows = jnp.exp(
            block_scores(queries, places, key_rows, key_places) - log_total[..., None]
        ).astype(jnp.bfloat16)
        return (
            running
            + jnp.einsum(
                "bhqk,bkhd->bqhd", prob_rows, value_rows, preferred_element_type=jnp.float32
            ),
            None,
        )

    context, unused = lax.scan(
        context_step, jnp.zeros((num_seqs, shard_len, num_heads, HS), jnp.float32), block_range
    )
    context_b = context.reshape(tok_count, model_width).astype(jnp.bfloat16)
    attended = inputs_f + jnp.dot(context_b, wout_all, preferred_element_type=jnp.float32)
    gain_ffn_f = gain_two.astype(jnp.float32)
    normed_two = rms_norm(attended, gain_ffn_f).astype(jnp.bfloat16)
    logits = jnp.dot(normed_two, router_all, preferred_element_type=jnp.float32)
    num_experts = router_all.shape[1]
    expert_range = jnp.arange(num_experts, dtype=jnp.int32)
    picked_ids = expert_ids.reshape(tok_count, 2)
    pick_hot = (picked_ids[:, :, None] == expert_range).astype(jnp.float32)
    chosen = jnp.sum(pick_hot * logits[:, None, :], axis=-1)
    gate_probs = jax.nn.softmax(chosen, axis=-1)
    expert_load = (jnp.sum(pick_hot, axis=1) * live_rows).astype(jnp.bfloat16)
    rank_rows = route_rank.reshape(tok_count)
    earlier = (rank_rows[None, :] < rank_rows[:, None]).astype(jnp.bfloat16)
    position = jnp.dot(earlier, expert_load, preferred_element_type=jnp.float32)
    chosen_pos = jnp.sum(pick_hot * position[:, None, :], axis=-1)
    kept_mask = live_rows * (chosen_pos < CAP).astype(jnp.float32)
    slot_hot = (chosen_pos[:, :, None] == jnp.arange(CAP, dtype=jnp.float32)).astype(jnp.float32)
    dispatch = (
        (pick_hot[:, :, :, None] * slot_hot[:, :, None, :] * kept_mask[:, :, None, None])
        .reshape(tok_count, 2, num_experts * CAP)
        .astype(jnp.bfloat16)
    )
    dispatch_any = dispatch[:, 0] + dispatch[:, 1]
    exp_size = lax.axis_size("exp")
    per_owner = num_experts // exp_size
    send_rows = (
        first_t(dispatch_any, normed_two)
        .astype(jnp.bfloat16)
        .reshape(exp_size, per_owner, CAP, model_width)
    )
    arrived = lax.all_to_all(send_rows, "exp", split_axis=0, concat_axis=0, tiled=True)
    expert_merged = jnp.einsum(
        "secd,edf->secf", arrived, experts_in, preferred_element_type=jnp.float32
    )
    expert_hidden = swiglu(expert_merged).astype(jnp.bfloat16)
    expert_result = jnp.einsum(
        "secf,efd->secd", expert_hidden, experts_out, preferred_element_type=jnp.float32
    ).astype(jnp.bfloat16)
    returned = lax.all_to_all(
        expert_result, "exp", split_axis=0, concat_axis=0, tiled=True
    ).reshape(num_experts * CAP, model_width)
    routed = jnp.einsum("tks,sd->tkd", dispatch, returned, preferred_element_type=jnp.float32)
    mixture = jnp.sum(gate_probs[:, :, None] * routed, axis=1)
    shared_merged = jnp.dot(normed_two, shared_in, preferred_element_type=jnp.float32)
    shared_hidden = swiglu(shared_merged).astype(jnp.bfloat16)
    shared_result = jnp.dot(shared_hidden, shared_down, preferred_element_type=jnp.float32)
    layer_out = (
        (live_rows * (attended + mixture + shared_result)).reshape(end_shape).astype(jnp.bfloat16)
    )
    upstream = grad_output.astype(jnp.float32).reshape(tok_count, model_width) * live_rows
    upstream_b = upstream.astype(jnp.bfloat16)
    upstream_f = upstream_b.astype(jnp.float32)
    d_shared_down = first_t(shared_hidden, upstream_b)
    d_shared_hidden = second_t(upstream_b, shared_down)
    unused, swiglu_pull = jax.vjp(swiglu, shared_merged)
    d_shared_merged = swiglu_pull(d_shared_hidden)[0].astype(jnp.bfloat16)
    d_shared_in = first_t(normed_two, d_shared_merged)
    d_normed_two = second_t(d_shared_merged, shared_in)
    gate_grads = jnp.sum(routed * upstream_f[:, None, :], axis=-1)
    weighted = (gate_probs[:, :, None] * upstream_f[:, None, :]).astype(jnp.bfloat16)
    d_returned = (
        jnp.einsum("tks,tkd->sd", dispatch, weighted, preferred_element_type=jnp.float32)
        .astype(jnp.bfloat16)
        .reshape(exp_size, per_owner, CAP, model_width)
    )
    d_result = lax.all_to_all(d_returned, "exp", split_axis=0, concat_axis=0, tiled=True)
    d_experts_out = jnp.einsum(
        "secf,secd->efd", expert_hidden, d_result, preferred_element_type=jnp.float32
    )
    d_expert_hidden = jnp.einsum(
        "secd,efd->secf", d_result, experts_out, preferred_element_type=jnp.float32
    )
    unused, expert_pull = jax.vjp(swiglu, expert_merged)
    d_expert_merged = expert_pull(d_expert_hidden)[0].astype(jnp.bfloat16)
    d_experts_in = jnp.einsum(
        "secd,secf->edf", arrived, d_expert_merged, preferred_element_type=jnp.float32
    )
    d_arrived = jnp.einsum(
        "secf,edf->secd", d_expert_merged, experts_in, preferred_element_type=jnp.float32
    ).astype(jnp.bfloat16)
    d_sent = lax.all_to_all(d_arrived, "exp", split_axis=0, concat_axis=0, tiled=True).reshape(
        num_experts * CAP, model_width
    )
    d_normed_two = d_normed_two + jnp.dot(dispatch_any, d_sent, preferred_element_type=jnp.float32)
    unused, gate_pull = jax.vjp(lambda chosen_in: jax.nn.softmax(chosen_in, axis=-1), chosen)
    d_chosen = gate_pull(gate_grads)[0]
    d_logits = jnp.sum(pick_hot * d_chosen[:, :, None], axis=1)
    d_router = first_t(normed_two.astype(jnp.float32), d_logits, highest)
    d_normed_two = d_normed_two + second_t(d_logits, router_all.astype(jnp.float32), highest)
    unused, second_pull = jax.vjp(rms_norm, attended, gain_ffn_f)
    d_attended, d_gain_ffn = second_pull(d_normed_two)
    d_attended = d_attended + upstream
    d_attended_b = d_attended.astype(jnp.bfloat16)
    d_out_proj = first_t(context_b, d_attended_b)
    d_context = (
        second_t(d_attended_b, wout_all)
        .astype(jnp.bfloat16)
        .reshape(num_seqs, shard_len, num_heads, HS)
    )

    def score_grads(
        query_rows, query_places, key_rows, value_rows, key_places, d_rows, lse_rows, delta_rows
    ):
        prob_rows = jnp.exp(
            block_scores(query_rows, query_places, key_rows, key_places) - lse_rows[..., None]
        )
        d_probs = jnp.einsum(
            "bqhd,bkhd->bhqk", d_rows, value_rows, preferred_element_type=jnp.float32
        )
        d_scores = (prob_rows * (d_probs - delta_rows[..., None])).astype(jnp.bfloat16)
        return (prob_rows.astype(jnp.bfloat16), d_scores)

    def delta_step(running, block_idx):
        key_rows, value_rows, key_places = key_block(block_idx)
        prob_rows = jnp.exp(
            block_scores(queries, places, key_rows, key_places) - log_total[..., None]
        )
        d_probs = jnp.einsum(
            "bqhd,bkhd->bhqk", d_context, value_rows, preferred_element_type=jnp.float32
        )
        return (running + jnp.sum(prob_rows * d_probs, axis=-1), None)

    row_delta, unused = lax.scan(delta_step, jnp.zeros(stat_shape, jnp.float32), block_range)
    head_shape = (num_seqs, shard_len, num_heads, HS)

    def query_step(d_query, block_idx):
        key_rows, value_rows, key_places = key_block(block_idx)
        prob_b, d_scores = score_grads(
            queries, places, key_rows, value_rows, key_places, d_context, log_total, row_delta
        )
        return (
            d_query
            + jnp.einsum("bhqk,bkhd->bqhd", d_scores, key_rows, preferred_element_type=jnp.float32)
            * score_scale,
            None,
        )

    d_query, unused = lax.scan(query_step, jnp.zeros(head_shape, jnp.float32), block_range)
    query_all, d_context_all = (
        lax.all_gather(queries.reshape(end_shape), "ctx", axis=2, tiled=True),
        lax.all_gather(d_context.reshape(end_shape), "ctx", axis=2, tiled=True),
    )
    stat_ends = (num_seqs, num_heads, 2, half_len)
    lse_all, delta_all = (
        lax.all_gather(log_total.reshape(stat_ends), "ctx", axis=3, tiled=True),
        lax.all_gather(row_delta.reshape(stat_ends), "ctx", axis=3, tiled=True),
    )
    query_all = query_all.reshape(num_seqs, full_len, num_heads, HS)
    d_context_all = d_context_all.reshape(num_seqs, full_len, num_heads, HS)
    lse_all = lse_all.reshape(num_seqs, num_heads, full_len)
    delta_all = delta_all.reshape(num_seqs, num_heads, full_len)

    def owner_step(state_in, block_idx):
        d_keys, d_values = state_in
        offset = block_idx * shard_len
        query_rows = lax.dynamic_slice_in_dim(query_all, offset, shard_len, 1)
        d_rows = lax.dynamic_slice_in_dim(d_context_all, offset, shard_len, 1)
        lse_rows = lax.dynamic_slice_in_dim(lse_all, offset, shard_len, 2)
        delta_rows = lax.dynamic_slice_in_dim(delta_all, offset, shard_len, 2)
        query_places = lax.dynamic_slice_in_dim(full_places, offset, shard_len, 0)
        prob_b, d_scores = score_grads(
            query_rows, query_places, keys_local, values_local, places, d_rows, lse_rows, delta_rows
        )
        d_keys = (
            d_keys
            + jnp.einsum(
                "bhqk,bqhd->bkhd", d_scores, query_rows, preferred_element_type=jnp.float32
            )
            * score_scale
        )
        d_values = d_values + jnp.einsum(
            "bhqk,bqhd->bkhd", prob_b, d_rows, preferred_element_type=jnp.float32
        )
        return ((d_keys, d_values), None)

    (d_keys_local, d_values_local), unused = lax.scan(
        owner_step,
        (jnp.zeros(head_shape, jnp.float32), jnp.zeros(head_shape, jnp.float32)),
        block_range,
    )
    unused, rope_pull = jax.vjp(
        lambda rows_in: rotate(rows_in, cosines, sine_rows), qkv_merged[:, :, 0]
    )
    d_query_pre = rope_pull(d_query)[0]
    d_key_pre = rope_pull(d_keys_local)[0]
    d_qkv_merged = (
        jnp.stack([d_query_pre, d_key_pre, d_values_local], axis=2)
        .reshape(tok_count, 3 * model_width)
        .astype(jnp.bfloat16)
    )
    d_qkv = first_t(normed_b, d_qkv_merged)
    d_normed = second_t(d_qkv_merged, wqkv_all)
    unused, first_pull = jax.vjp(rms_norm, inputs_f, gain_attn_f)
    d_inputs, d_gain_attn = first_pull(d_normed)
    grad_input = (d_attended + d_inputs).reshape(end_shape)
    dense_sums = (
        lax.psum_scatter(d_gain_attn, ("ctx", "exp", "fsdp"), scatter_dimension=0, tiled=True),
        lax.psum_scatter(d_qkv, ("ctx", "exp", "fsdp"), scatter_dimension=0, tiled=True),
        lax.psum_scatter(d_out_proj, ("ctx", "exp", "fsdp"), scatter_dimension=0, tiled=True),
        lax.psum_scatter(d_router, ("ctx", "exp", "fsdp"), scatter_dimension=0, tiled=True),
        lax.psum_scatter(d_gain_ffn, ("ctx", "exp", "fsdp"), scatter_dimension=0, tiled=True),
        lax.psum_scatter(d_shared_in, ("ctx", "exp", "fsdp"), scatter_dimension=0, tiled=True),
        lax.psum_scatter(d_shared_down, ("ctx", "exp", "fsdp"), scatter_dimension=0, tiled=True),
    )
    expert_sums = (
        lax.psum_scatter(
            d_experts_in.astype(jnp.bfloat16), ("ctx", "fsdp"), scatter_dimension=1, tiled=True
        ).astype(jnp.float32),
        lax.psum_scatter(
            d_experts_out.astype(jnp.bfloat16), ("ctx", "fsdp"), scatter_dimension=1, tiled=True
        ).astype(jnp.float32),
    )
    return (
        layer_out,
        grad_input,
        dense_sums[0],
        dense_sums[1],
        dense_sums[2],
        dense_sums[3],
        dense_sums[4],
        dense_sums[5],
        dense_sums[6],
        expert_sums[0],
        expert_sums[1],
    )


F32 = jnp.float32
BF = jnp.bfloat16
MESH = pl.DeviceIdType.MESH
BOX = 40
SMALL = 64
VMEM_BYTES = 63 * 1024 * 1024
PUMPS = (3, 17, 6, 0, 6, 6)
POSTS = 64
EARLY = 2
GATE_UP, DOWN = 1, 2
WIDEN = 1


def place():
    return lax.axis_index("ctx"), lax.axis_index("exp"), lax.axis_index("fsdp")


def wrap(value, size):
    return lax.rem(value, size)


def mm(left, right):
    return lax.dot_general(
        left, right, (((1,), (0,)), ((), ())), preferred_element_type=F32
    )


def mm_nt(left, right):
    return lax.dot_general(
        left, right, (((1,), (1,)), ((), ())), preferred_element_type=F32
    )


def mm_tn(left, right):
    return lax.dot_general(
        left, right, (((0,), (0,)), ((), ())), preferred_element_type=F32
    )


def greet(peers):
    barrier = pltpu.get_barrier_semaphore()
    for peer in peers:
        pl.semaphore_signal(barrier, inc=1, device_id=peer, device_id_type=MESH)


def met(peers):
    pl.semaphore_wait(pltpu.get_barrier_semaphore(), len(peers))


class Post:
    def __init__(self, send, recv, like, device):
        self.send, self.recv, self.like, self.device = send, recv, like, device

    def add(self, src, dst, device):
        pltpu.make_async_remote_copy(
            src_ref=src,
            dst_ref=dst,
            send_sem=self.send,
            recv_sem=self.recv,
            device_id=device,
            device_id_type=MESH,
        ).start()

    def all_of_it(self, like=None):
        like = self.like if like is None else like
        return pltpu.make_async_remote_copy(
            src_ref=like,
            dst_ref=like,
            send_sem=self.send,
            recv_sem=self.recv,
            device_id=self.device,
            device_id_type=MESH,
        )

    def wait_recv(self, like=None):
        self.all_of_it(like).wait_recv()

    def wait_send(self, like=None):
        self.all_of_it(like).wait_send()


class Courier:
    def __init__(self, send, recv, device):
        self.send, self.recv, self.device, self.count, self.sent = send, recv, device, 0, []

    def open(self, like, keep=True):
        post = Post(self.send.at[self.count], self.recv.at[self.count], like, self.device)
        self.count += 1
        if keep:
            self.sent.append(post)
        return post

    def post(self, like, moves):
        post = self.open(like)
        for src, dst, device in moves:
            post.add(src, dst, device)
        return post

    def settle(self, posts):
        for post in posts:
            post.wait_send()
        done = {id(post) for post in posts}
        self.sent = [post for post in self.sent if id(post) not in done]

    def finish(self):
        self.settle(list(self.sent))


def swap_halves(rows):
    width = rows.shape[1]
    lane = lax.broadcasted_iota(jnp.int32, rows.shape, 1)
    ahead = pltpu.roll(rows, width - HS // 2, 1)
    behind = pltpu.roll(rows, HS // 2, 1)
    return jnp.where((lane & (HS - 1)) < HS // 2, -ahead, behind)


def wide(table, times):
    return jnp.concatenate([table] * times, axis=1)


def position_of(index, half_len, full_len):
    block = index // (2 * half_len)
    inside = index & (2 * half_len - 1)
    low = block * half_len + (inside & (half_len - 1))
    return jnp.where(inside >= half_len, full_len - 1 - low, low)


def allowed_keys(length, half_len, full_len):
    shape = (full_len, full_len)
    query_at = position_of(lax.broadcasted_iota(jnp.int32, shape, 0), half_len, full_len)
    key_at = position_of(lax.broadcasted_iota(jnp.int32, shape, 1), half_len, full_len)
    return (key_at <= query_at) & (key_at < length)


def head_probs(query, key, allowed):
    scores = jnp.where(allowed, mm_nt(query, key) * (HS**-0.5), masked_out)
    weights = jnp.exp(scores - jnp.max(scores, axis=1, keepdims=True))
    return weights * (1.0 / jnp.sum(weights, axis=1, keepdims=True))


def column_row(tail, lane):
    pick = (lax.broadcasted_iota(jnp.int32, (8, 128), 1) == lane).astype(BF)
    return mm_nt(pick, tail)[0:1]


def split_dot(dot, left, right, left_wide=True):
    whole = left if left_wide else right
    high = whole.astype(BF)
    low = (whole - high.astype(F32)).astype(BF)
    if left_wide:
        return dot(high, right) + dot(low, right)
    return dot(left, high) + dot(left, low)


def inverse_rms(rows):
    return lax.rsqrt(jnp.mean(rows * rows, axis=1, keepdims=True) + epsilon)


def norm_back(rows, inverse, scaled):
    return inverse * scaled - rows * (inverse * inverse * inverse) * jnp.mean(
        rows * scaled, axis=1, keepdims=True
    )


def join(blocks, shape):
    return blocks.astype(F32).reshape(shape).astype(BF)


def ffn_block(j, rows, grads, in_ref, out_ref, hidden_ref, dm_ref, result, back, units, step):
    low = pl.multiple_of(j * step, step) if not isinstance(j, int) else j * step
    high = pl.multiple_of(units + low, step) if not isinstance(j, int) else units + low
    gate_at, up_at = pl.ds(low, step), pl.ds(high, step)
    gate, up = mm(rows, in_ref[:, gate_at]), mm(rows, in_ref[:, up_at])
    down = out_ref[gate_at, :]
    d_hidden = mm_nt(grads, down)
    share = 1.0 / (1.0 + jnp.exp(-gate))
    lit = gate * share
    hidden = (lit * up).astype(BF)
    d_gate = (d_hidden * up * (share * (1.0 + gate * (1.0 - share)))).astype(BF)
    d_up = (d_hidden * lit).astype(BF)
    hidden_ref[:, gate_at] = hidden
    dm_ref[:, gate_at] = d_gate
    dm_ref[:, up_at] = d_up
    result[...] += mm(hidden, down)
    back[...] += mm_nt(d_gate, in_ref[:, gate_at]) + mm_nt(d_up, in_ref[:, up_at])


def box_rows(kept_rows, boxes, shift):
    shape = (boxes * kept_rows, boxes * BOX)
    row = lax.broadcasted_iota(jnp.int32, shape, 0)
    column = lax.broadcasted_iota(jnp.int32, shape, 1)
    box = jnp.floor((column.astype(F32) + 0.5) * (1.0 / BOX)).astype(jnp.int32)
    at = column - box * BOX - shift
    return ((at >= 0) & (at < kept_rows) & (row == box * kept_rows + at)).astype(BF)


def block_kernel(
    nc, nz,
    len_ref, hid_ref, go_ref, ids_ref, rank_ref, wqkv_ref, router_ref, ga_ref, gf_ref, gu_ref,
    wo_ref, sd_ref, win_ref, wout_ref,
    out_ref, gin_ref, fq_ref, fgu_ref, fsd_ref, fwo_ref, ein_ref, eout_ref,
    turn_ref, meta_own, meta_all, picks, hot_x, hot_d, dg_send, dg_in, hid_all, up_own, up_all, wq_own, wq_st, wq_buf, w_ref, gu_st, gu_buf, gu_all, wo_st, wo_buf,
    wo_all, sd_all, wie, woe, normed_ref, qkv_ref, ctx_all, att_own, nt_all,
    sb, ar, xs, ds, acc_a, acc_b, sh_own, sh_hidden, sh_dm, sh_send, sh_in, sh_mid, sh_end,
    ex_hidden, ex_dm, pin, fb, rb, gsd, da_own, dctx_send, dctx_all, part, part_own, rs_in, rs_mid, rs_end,
    sib_gu, zi_gu, pb_gu, sib_q, zi_q, pb_q, sib_sd, zi_sd, sib_wo, zi_wo, pb_wo, in_wo,
    send, recv, lsem,
):
    c, z, f = place()
    near_x, near_y = c + 1 - 2 * wrap(c, 2), wrap(c + 2, nc)
    far = wrap(near_x + 2, nc)
    to_x, to_y = (near_x, z, f), (near_y, z, f)
    in_plane = [(wrap(c + s, nc), z, f) for s in range(1, nc)]
    in_column = [(c, wrap(z + s, nz), f) for s in range(1, nz)]
    steps_up = list(range(1, nz))
    sibling = (c, z, 1 - f)
    across = [(wrap(c + s, nc), z, 1 - f) for s in range(1, nc)]
    partners = in_plane + in_column + [sibling] + across
    with jax.named_scope("s_greet"):
        greet(partners)

    num_seqs, shard_len, width = hid_ref.shape
    full_len = nc * shard_len
    half_len = shard_len // 2
    tok = num_seqs * shard_len
    rows_w = wqkv_ref.shape[0]
    head_width = wqkv_ref.shape[1] // 3 // nc
    heads_here = head_width // HS
    wide_cols = wq_own.shape[2]
    units = gu_ref.shape[1] // 2
    own_units = units // nc
    down_rows = sd_ref.shape[0]
    num_experts = nz * nc
    num_slots = num_experts * CAP
    column_slots = nz * BOX
    block_rows = nz * 2 * rows_w
    mail = Courier(send, recv, sibling)

    small = jnp.concatenate(
        [
            router_ref[...].astype(F32),
            ga_ref[...].astype(F32),
            gf_ref[...].astype(F32),
            jnp.zeros((128 - num_experts - 2, rows_w), F32),
        ],
        axis=0,
    )
    small = jnp.concatenate([small, jnp.zeros((128, 128 - rows_w), F32)], axis=1)
    small = jnp.transpose(small, (1, 0))[:rows_w, :SMALL].astype(BF)
    for owner in range(nc):
        wq_own[owner] = jnp.concatenate(
            [
                wqkv_ref[:, side * width + owner * head_width : side * width + (owner + 1) * head_width]
                for side in range(3)
            ]
            + [small],
            axis=1,
        )
    meta_own[...] = jnp.concatenate(
        [
            jnp.concatenate(
                [ids_ref[q, e, k : k + 1, :] for q in range(num_seqs) for e in range(2)], axis=1
            )
            for k in range(2)
        ]
        + [rank_ref[...], jnp.zeros((5, tok), jnp.int32)],
        axis=0,
    )
    with jax.named_scope("s_met"):
        met(partners)

    others = pl.ds(0, nc - 1)
    staged_wq = mail.post(
        wq_st.at[others],
        [(wq_own.at[wrap(c + s, nc)], wq_st.at[c], in_plane[s - 1]) for s in range(1, nc)],
    )
    arriving = [
        mail.post(
            hid_all.at[q, pl.ds(0, 2)],
            [(hid_ref.at[q], hid_all.at[q, c], peer) for peer in (to_x, to_y)],
        )
        for q in range(num_seqs)
    ]
    meta_copies = mail.post(
        meta_all.at[others], [(meta_own, meta_all.at[c], peer) for peer in in_plane]
    )
    staged_wo = mail.post(wo_st.at[others], [(wo_ref, wo_st.at[c], peer) for peer in in_plane])
    staged_gu = mail.open(gu_st.at[others])
    for s in range(1, nc):
        owner = wrap(c + s, nc)
        for side in range(2):
            at = pl.ds(pl.multiple_of(side * units + owner * own_units, own_units), own_units)
            staged_gu.add(
                gu_ref.at[:, at],
                gu_st.at[c, :, pl.ds(side * own_units, own_units)],
                in_plane[s - 1],
            )

    block = 2 * c + f
    shard_rows = win_ref.shape[1]
    half_units = units // 2
    step = 256
    steps = half_units // step
    lands = pl.ds(pl.multiple_of(block * shard_rows, shard_rows), shard_rows)
    out_rows = wout_ref.shape[1]
    to_core = block // nc
    slot = wrap(block, nc)
    out_lands = pl.ds(pl.multiple_of(slot * out_rows, out_rows), out_rows)
    remote_rows = (2 * nc - 1) * shard_rows
    expert_in = [
        mail.open(wie.at[pl.ds(0, remote_rows), pl.ds(0, 2 * step)]) for _ in range(steps)
    ]
    expert_out = mail.open(woe, keep=False)
    remote_out = woe.at[pl.ds(0, (nc - 1) * out_rows)]
    own_out = pltpu.make_async_copy(wout_ref.at[c], woe.at[out_lands], lsem.at[0])

    def send_out(s):
        owner = wrap(c + s, nc)
        expert_out.add(wout_ref.at[owner], woe.at[out_lands], (owner, z, to_core))

    def send_out_own():
        @pl.when(to_core == f)
        def _():
            own_out.start()

        @pl.when(to_core != f)
        def _():
            expert_out.add(wout_ref.at[c], woe.at[out_lands], sibling)

    def own_in(j):
        like = wie.at[pl.ds(0, shard_rows), pl.ds(0, 2 * step)]
        return pltpu.make_async_copy(like, like, lsem.at[1 + j])

    def send_in(j, s, g, side):
        owner = wrap(c + s, nc)
        core = f if g == 0 else 1 - f
        from_lane = pl.multiple_of(side * units + core * half_units + j * step, step)
        src = win_ref.at[owner, :, pl.ds(from_lane, step)]
        dst = wie.at[lands, pl.ds(side * half_units + j * step, step)]
        if s == 0 and g == 0:
            pltpu.make_async_copy(src, dst, lsem.at[1 + j]).start()
        else:
            expert_in[j].add(src, dst, (owner, z, core))

    bulk = [functools.partial(send_out, s) for s in range(1, nc)] + [send_out_own]
    for j in range(steps):
        for s in range(1, nc + 1):
            for g in range(2):
                for side in range(2):
                    bulk.append(functools.partial(send_in, j, s % nc, g, side))

    def pump(queue, count):
        for _ in range(min(count, len(queue))):
            queue.pop(0)()

    with jax.named_scope("s_turns"):
        row = lax.broadcasted_iota(jnp.int32, (full_len, 128), 0)
        lane = lax.broadcasted_iota(jnp.int32, (full_len, 128), 1) & (HS // 2 - 1)
        frequency = jnp.exp(lane.astype(F32) * (-2.0 * math.log(10000.0) / HS))
        angles = position_of(row, half_len, full_len).astype(F32) * frequency
        turn_ref[:, :128] = jnp.cos(angles)
        turn_ref[:, 128:] = jnp.sin(angles)
    lane = lax.broadcasted_iota(jnp.int32, (tok, 128), 1).astype(F32)

    def live_rows(chip):
        row_at = lax.broadcasted_iota(jnp.int32, (tok, 1), 0)
        inside = row_at & (shard_len - 1)
        low = chip * half_len + (inside & (half_len - 1))
        places = jnp.where(inside >= half_len, full_len - 1 - low, low)
        lengths = jnp.zeros((tok, 1), jnp.int32)
        for q in range(num_seqs):
            lengths = jnp.where(row_at // shard_len == q, len_ref[q], lengths)
        return (places < lengths).astype(F32)

    def turned(rows):
        return jnp.transpose(
            jnp.concatenate([rows, jnp.zeros((128 - rows.shape[0], tok), F32)], axis=0), (1, 0)
        )

    def hot_lanes(columns):
        return [(lane == SMALL + columns[:, k : k + 1]).astype(F32) for k in range(2)]

    def gates_of(hots, logits):
        chosen = [jnp.sum(hot * logits, axis=1, keepdims=True) for hot in hots]
        top = jnp.maximum(chosen[0], chosen[1])
        raised = [jnp.exp(value - top) for value in chosen]
        return [value / (raised[0] + raised[1]) for value in raised]

    def route(chip):
        rows = meta_all[chip].astype(F32)
        columns = turned(rows)
        picks[chip] = columns
        hots = hot_lanes(columns)
        rank_row = jnp.broadcast_to(rows[2:3], (tok, tok))
        earlier = (rank_row < columns[:, 2:3]).astype(BF)
        live = live_rows(chip)
        position = mm(earlier, ((hots[0] + hots[1]) * live).astype(BF))
        slot_lane = lax.broadcasted_iota(jnp.int32, (tok, column_slots), 1).astype(F32)
        for k in range(2):
            at = jnp.sum(hots[k] * position, axis=1, keepdims=True)
            plane = jnp.floor((columns[:, k : k + 1] + 0.5) * (1.0 / nc))
            here = columns[:, k : k + 1] - plane * nc == c.astype(F32)
            slot_at = jnp.where((live > 0) & (at < CAP) & here, plane * BOX + at, -BOX)
            hot_x[chip, k] = (slot_lane == slot_at).astype(BF)
            hot_d[chip, k] = (slot_lane == slot_at + CAP).astype(BF)

    live = live_rows(c)
    upstream = go_ref[...].reshape(tok, width).astype(F32) * live
    up_b = upstream.astype(BF)
    up_own[...] = up_b.reshape(num_seqs, shard_len, width)
    for q in range(num_seqs):
        hid_all[q, c] = hid_ref[q]
        up_all[q, c] = up_own[q]

    def pass_on(post, buffer, q, at):
        post.wait_recv()
        origin, peer = (near_x, to_y) if q == 0 else (near_y, to_x)
        block_at = at(buffer, q, origin)
        return mail.post(block_at, [(block_at, block_at, peer)])

    def by_seq(buffer, q, chip):
        return buffer.at[q, chip]

    def by_chip(buffer, q, chip):
        return buffer.at[chip, q]

    sd_all[z, f] = sd_ref[...]
    planes = pl.ds(0, nz - 1)

    def spread(stage, staged, buffer):
        staged.wait_recv()
        post = mail.post(
            buffer.at[:, planes, 0],
            [(stage, buffer.at[:, z, f], peer) for peer in in_column],
        )
        for i in range(nc):
            buffer[i, z, f] = stage[i]
        return post

    def spread_gate_up(side):
        at = pl.ds(side * own_units, own_units)
        return mail.post(
            gu_buf.at[:, planes, 0, :, at],
            [(gu_st.at[:, :, at], gu_buf.at[:, z, f, :, at], peer) for peer in in_column],
        )

    def forward(posts, buffer):
        for post in posts:
            post.wait_recv()
        both = buffer.at[:, :, f]
        return mail.post(both, [(both, both, sibling)])

    with jax.named_scope("a_stage_wq"):
        wq_st[c] = wq_own[c]
        spread_wq = spread(wq_st, staged_wq, wq_buf)
    with jax.named_scope("a_pass_hidden"):
        passing = [pass_on(arriving[q], hid_all, q, by_seq) for q in range(num_seqs)]
    up_copies = [
        mail.post(
            up_all.at[q, pl.ds(0, 2)],
            [(up_own.at[q], up_all.at[q, c], peer) for peer in (to_x, to_y)],
        )
        for q in range(num_seqs)
    ]
    pump(bulk, PUMPS[3])
    with jax.named_scope("a_route"):
        meta_copies.wait_recv()
        meta_all[c] = meta_own[...]
        for chip in range(nc):
            route(chip)
    wo_st[c] = wo_ref[...]
    for side in range(2):
        at = pl.ds(pl.multiple_of(side * units + c * own_units, own_units), own_units)
        gu_st[c, :, side * own_units : (side + 1) * own_units] = gu_ref[:, at]
    with jax.named_scope("a_forward_wq"):
        passed_wq = forward([spread_wq], wq_buf)
        passed_wq.wait_recv()
        for i in range(nc):
            w_ref[i * block_rows : (i + 1) * block_rows, :] = join(
                wq_buf[i], (block_rows, wide_cols)
            )

    cosines = wide(turn_ref[:, :128], 2 * head_width // 128)
    sines = wide(turn_ref[:, 128:], 2 * head_width // 128)
    tail_at = wide_cols - 128
    attn_gain = column_row(w_ref[:, tail_at:], SMALL + num_experts)
    ctx_copies = []
    for q in range(num_seqs):
        with jax.named_scope("a_wait_hidden"):
            passing[q].wait_recv()
        with jax.named_scope("a_attention"):
            rows = hid_all[q].reshape(full_len, width).astype(F32)
            normed = (rows * inverse_rms(rows) * attn_gain).astype(BF)
            normed_ref[q] = normed
            merged = mm(normed, w_ref[:, : 3 * head_width])
            both = merged[:, : 2 * head_width]
            both = (both * cosines + swap_halves(both) * sines).astype(BF)
            values = merged[:, 2 * head_width :].astype(BF)
            qkv_ref[q, :, : 2 * head_width] = both
            qkv_ref[q, :, 2 * head_width :] = values
            allowed = allowed_keys(len_ref[q], half_len, full_len)
            heads = []
            for h in range(heads_here):
                probs = head_probs(
                    both[:, h * HS : (h + 1) * HS],
                    both[:, head_width + h * HS : head_width + (h + 1) * HS],
                    allowed,
                ).astype(BF)
                heads.append(mm(probs, values[:, h * HS : (h + 1) * HS]))
            context = jnp.concatenate(heads, axis=1).astype(BF)
            ctx_all[c, q] = context.reshape(nc, shard_len, head_width)
        ctx_copies.append(
            mail.post(
                ctx_all.at[pl.ds(0, 2), q],
                [(ctx_all.at[c, q], ctx_all.at[c, q], peer) for peer in (to_x, to_y)],
            )
        )
    spread_wo = spread(wo_st, staged_wo, wo_buf)
    with jax.named_scope("a_pass_upstream"):
        up_passing = [pass_on(up_copies[q], up_all, q, by_seq) for q in range(num_seqs)]
    with jax.named_scope("a_pass_context"):
        ctx_passing = [pass_on(ctx_copies[q], ctx_all, q, by_chip) for q in range(num_seqs)]
    pump(bulk, PUMPS[0])
    with jax.named_scope("a_forward_wo"):
        passed_wo = forward([spread_wo], wo_buf)
        staged_gu.wait_recv()
        for i in range(nc):
            gu_buf[i, z, f] = gu_st[i]
        spread_gu = [spread_gate_up(0)]
        passed_wo.wait_recv()
        for i in range(nc):
            wo_all[i * block_rows : (i + 1) * block_rows, :] = join(
                wo_buf[i], (block_rows, width)
            )
    ffn_gain = column_row(w_ref[:, tail_at:], SMALL + num_experts + 1)
    for q in range(num_seqs):
        with jax.named_scope("a_wait_context"):
            ctx_passing[q].wait_recv()
        with jax.named_scope("a_project"):
            total = hid_all[q].reshape(full_len, width).astype(F32)
            for i in range(nc):
                total = total + mm(
                    ctx_all[i, q].reshape(full_len, head_width),
                    wo_all[i * head_width : (i + 1) * head_width, :],
                )
            acc_a[q * full_len : (q + 1) * full_len] = total
            nt_all[q] = (
                (total * inverse_rms(total) * ffn_gain).astype(BF).reshape(nc, shard_len, width)
            )
    by_block = acc_a.at[pl.ds(0, nc * tok)].reshape(num_seqs, nc, shard_len, width)
    for q in range(num_seqs):
        att_own[q] = by_block[q, c]

    with jax.named_scope("b_wait_upstream"):
        for post in up_passing:
            post.wait_recv()
    with jax.named_scope("b_dispatch"):
        tail = w_ref[:, tail_at:]
        gates = []
        for chip in range(nc):
            normed = jnp.concatenate([nt_all[q, chip] for q in range(num_seqs)], axis=0)
            gates.append(gates_of(hot_lanes(picks[chip]), mm(normed, tail)))
            up_f = jnp.concatenate([up_all[q, chip] for q in range(num_seqs)], axis=0).astype(F32)
            boxes = mm_tn(hot_x[chip, 0] + hot_x[chip, 1], normed)
            for k in range(2):
                boxes = boxes + mm_tn(hot_d[chip, k], (gates[chip][k] * up_f).astype(BF))
            sb[:, chip] = boxes.reshape(nz, BOX, width).astype(BF)
        row_copies = [
            mail.post(ar.at[f, 0], [(sb.at[to[1]], ar.at[f, z], to)]) for to in in_column
        ]
        ar[f, z] = sb[z]
        normed = jnp.concatenate([nt_all[q, c] for q in range(num_seqs)], axis=0)
    pump(bulk, len(bulk))

    with jax.named_scope("b_forward_rows"):
        forwards = mail.open(ar.at[f])
        forwards.add(ar.at[f, z], ar.at[f, z], sibling)
        for s in range(1, nz):
            row_copies[s - 1].wait_recv()
            origin = wrap(z + nz - s, nz)
            forwards.add(ar.at[f, origin], ar.at[f, origin], sibling)
        forwards.wait_recv()
        keep_x, keep_d = (box_rows(CAP, num_experts, shift) for shift in (0, CAP))
        for core in range(2):
            at = slice(core * num_slots, (core + 1) * num_slots)
            boxes = join(ar[core], (num_experts * BOX, width))
            xs[at] = mm(keep_x, boxes).astype(BF)
            ds[at] = mm(keep_d, boxes).astype(BF)
    with jax.named_scope("b_wait_down"):
        @pl.when(to_core == f)
        def _():
            expert_out.wait_recv(remote_out)
            own_out.wait()

        @pl.when(to_core != f)
        def _():
            expert_out.wait_recv()

    gwi, gwo = wie, woe

    def expert_grads(j):
        for side in range(2):
            at = pl.ds(side * half_units + j * step, step)
            gwi[:, at] = mm_tn(xs[...], ex_dm[:, at]).astype(BF)
        at = pl.ds(j * step, step)
        gwo[at, :] = mm_tn(ex_hidden[:, at], ds[...]).astype(BF)
        for s in range(1, nc + 1):
            for g in range(2):
                for side in range(2):
                    home.append(functools.partial(send_home_in, j, s % nc, g, side))
        home.append(functools.partial(send_home_out, j))

    home = []
    home_in = mail.open(gwi.at[pl.ds(0, remote_rows)])
    home_out = mail.open(gwo, keep=False)
    remote_home = gwo.at[pl.ds(0, (nc - 1) * out_rows)]
    home_in_own = pltpu.make_async_copy(
        gwi.at[pl.ds(0, shard_rows)], gwi.at[pl.ds(0, shard_rows)], lsem.at[1]
    )

    def send_home_in(j, s, g, side):
        owner = wrap(c + s, nc)
        core = f if g == 0 else 1 - f
        from_rows = pl.ds(
            pl.multiple_of((2 * owner + core) * shard_rows, shard_rows), shard_rows
        )
        to_lane = pl.multiple_of(side * units + f * half_units + j * step, step)
        src = gwi.at[from_rows, pl.ds(side * half_units + j * step, step)]
        dst = ein_ref.at[c, :, pl.ds(to_lane, step)]
        if s == 0 and g == 0:
            pltpu.make_async_copy(src, dst, lsem.at[1]).start()
        else:
            home_in.add(src, dst, (owner, z, core))

    def home_out_own(j):
        return pltpu.make_async_copy(
            gwo.at[pl.ds(j * out_rows, out_rows)], eout_ref.at[c], lsem.at[0]
        )

    def send_home_out(j):
        to_block = f * nc + j

        @pl.when(to_block == block)
        def _():
            home_out_own(j).start()

        @pl.when(to_block != block)
        def _():
            home_out.add(
                gwo.at[pl.ds(j * out_rows, out_rows)],
                eout_ref.at[c],
                (to_block // 2, z, wrap(to_block, 2)),
            )

    acc_a[...] = jnp.zeros(acc_a.shape, F32)
    acc_b[...] = jnp.zeros(acc_b.shape, F32)
    for j in range(steps):
        with jax.named_scope("b_wait_experts"):
            own_in(j).wait()
            expert_in[j].wait_recv()
        if j == steps - 1:
            pump(home, len(home))
        with jax.named_scope("b_experts"):
            ffn_block(
                j, xs[...], ds[...], wie, woe, ex_hidden, ex_dm, acc_a, acc_b, half_units, step
            )
        if j < EARLY:
            with jax.named_scope("b_early_grads"):
                expert_grads(j)
        if j == GATE_UP:
            spread_gu.append(spread_gate_up(1))
        if j == DOWN:
            spread_sd = mail.post(
                sd_all.at[planes, 0], [(sd_ref, sd_all.at[z, f], peer) for peer in in_column]
            )
    mail.settle(row_copies)
    pr = sb
    with jax.named_scope("b_sibling_sum"):

        def boxed(core):
            at = pl.ds(pl.multiple_of(core * num_slots, num_slots), num_slots)
            return (
                mm_tn(keep_x, acc_a[at].astype(BF)) + mm_tn(keep_d, acc_b[at].astype(BF))
            ).reshape(nz, nc, BOX, width)

        pr[...] = boxed(1 - f).astype(BF)
        swap = mail.post(pin, [(pr, pin, sibling)])
        ours = boxed(f)
        swap.wait_recv()
        fb[...] = (ours + pin[...].astype(F32)).astype(BF)
        returns = mail.post(
            rb.at[planes], [(fb.at[to[1]], rb.at[z], to) for to in in_column]
        )
        rb[z] = fb[z]
    with jax.named_scope("b_expert_grads"):
        for j in range(EARLY, steps):
            expert_grads(j)
    pump(home, PUMPS[1])

    with jax.named_scope("b_forward_gu"):
        passed_gu = forward(spread_gu, gu_buf)
        spread_sd.wait_recv()
        passed_sd = mail.post(sd_all.at[:, f], [(sd_all.at[:, f], sd_all.at[:, f], sibling)])
        passed_gu.wait_recv()
        passed_sd.wait_recv()
        for i in range(nc):
            gu_all[i * block_rows : (i + 1) * block_rows, :] = join(
                gu_buf[i], (block_rows, 2 * own_units)
            )
    plane_tok = nc * tok
    shared_rows = nt_all.reshape(plane_tok, width)
    shared_grads = up_all.reshape(plane_tok, width)
    shared_down = sd_all.reshape(own_units, width)
    with jax.named_scope("b_shared"):
        first = pl.ds(0, plane_tok)
        acc_a[...] = jnp.zeros(acc_a.shape, F32)
        acc_b[...] = jnp.zeros(acc_b.shape, F32)

        def shared_block(j, carry):
            ffn_block(
                j, shared_rows[...], shared_grads[...], gu_all, shared_down, sh_hidden, sh_dm,
                acc_a.at[first], acc_b.at[first], own_units, 256,
            )
            return carry

        lax.fori_loop(0, own_units // 256, shared_block, 0)
    mail.settle(spread_gu + [passed_gu])
    ggu = gu_buf
    with jax.named_scope("b_shared_grads"):

        def gate_up_grads(j, carry):
            at = pl.ds(pl.multiple_of(j * 256, 256), 256)
            piece = mm_tn(shared_rows[...], sh_dm[:, at])
            ggu[:, :, :, :, at] = piece.reshape(ggu.shape[:4] + (256,)).astype(BF)
            return carry

        lax.fori_loop(0, 2 * own_units // 256, gate_up_grads, 0)
        gsd[...] = mm_tn(sh_hidden[...], shared_grads[...]).reshape(gsd.shape).astype(BF)
        sibling_gu = mail.post(sib_gu, [(ggu.at[:, :, 1 - f], sib_gu, sibling)])
        sibling_sd = mail.post(sib_sd, [(gsd.at[:, 1 - f], sib_sd, sibling)])

    with jax.named_scope("c_wait_returns"):
        returns.wait_recv()
    with jax.named_scope("c_column_mixture"):
        cuts = [
            acc.at[first].reshape(num_seqs, nc, shard_len, width) for acc in (acc_a, acc_b)
        ]
        for chip in range(nc):
            results = join(rb[:, chip], (column_slots, width))
            up_f = jnp.concatenate([up_all[q, chip] for q in range(num_seqs)], axis=0).astype(F32)
            routed = [mm(hot_x[chip, k], results) for k in range(2)]
            mixture = gates[chip][0] * routed[0] + gates[chip][1] * routed[1]
            d_rows = mm(hot_d[chip, 0] + hot_d[chip, 1], results)
            for q in range(num_seqs):
                at = slice(q * shard_len, (q + 1) * shard_len)
                cuts[0][q, chip] = cuts[0][q, chip] + mixture[at]
                cuts[1][q, chip] = cuts[1][q, chip] + d_rows[at]
            d_gates = [jnp.sum(routed[k] * up_f, axis=1, keepdims=True) for k in range(2)]
            spread_out = jnp.where(lane == 0, d_gates[0], jnp.where(lane == 1, d_gates[1], 0.0))
            dg_send[chip] = jnp.transpose(spread_out, (1, 0))[:8]
        for k in range(2):
            for q in range(num_seqs):
                sh_own[k, q, 0] = cuts[k][q, c]
                sh_own[k, q, 1] = cuts[k][q, near_y if q == 0 else near_x]
            sh_send[k] = cuts[k][...].astype(BF)

    def first_leg(inbox, box, lead):
        post = mail.open(inbox)
        for q in range(num_seqs):
            peer = to_x if q == 0 else to_y
            for at, chip in enumerate((near_x if q == 0 else near_y, far)):
                post.add(box.at[lead + (q, chip)], inbox.at[lead + (q, at)], peer)
        return post

    shared_first = first_leg(sh_in, sh_send, (slice(None),))
    dg_copies = mail.post(
        dg_in.at[others],
        [(dg_send.at[wrap(c + s, nc)], dg_in.at[c], in_plane[s - 1]) for s in range(1, nc)],
    )
    dg_in[c] = dg_send[c]
    pump(home, PUMPS[4])

    with jax.named_scope("b_reduce_shared"):
        def two_cores(copy, own, inbox):
            copy.wait_recv()
            inbox[...] = (own.astype(F32) + inbox[...].astype(F32)).astype(BF)

        def four_planes(copy, buffer, inbox):
            copy.wait_recv()
            for i in range(nc):
                inbox[i] = (buffer[i, :, f].astype(F32) + inbox[i].astype(F32)).astype(BF)

        four_planes(sibling_gu, ggu, sib_gu)
        two_cores(sibling_sd, gsd[:, f], sib_sd)
        gu_copies = mail.post(
            zi_gu,
            [
                (sib_gu.at[:, to[1]], zi_gu.at[up - 1], to)
                for to, up in zip(in_column, steps_up)
            ],
        )
        sd_copies = mail.post(
            zi_sd,
            [(sib_sd.at[to[1]], zi_sd.at[up - 1], to) for to, up in zip(in_column, steps_up)],
        )

    with jax.named_scope("c_second_sum"):
        shared_first.wait_recv()
        for k in range(2):
            for q in range(num_seqs):
                sh_mid[k, q] = (sh_own[k, q, 1] + sh_in[k, q, 1].astype(F32)).astype(BF)
        shared_second = mail.post(
            sh_end,
            [
                (sh_mid.at[:, q], sh_end.at[:, q], to_y if q == 0 else to_x)
                for q in range(num_seqs)
            ],
        )

    pump(home, PUMPS[5])
    with jax.named_scope("c_wait_shared"):
        dg_copies.wait_recv()
        shared_second.wait_recv()
        added, d_normed = [
            jnp.concatenate(
                [
                    sh_own[k, q, 0] + sh_in[k, q, 0].astype(F32) + sh_end[k, q].astype(F32)
                    for q in range(num_seqs)
                ],
                axis=0,
            )
            for k in range(2)
        ]
    with jax.named_scope("c_combine"):
        attended = att_own[...].reshape(tok, width)
        inverse = inverse_rms(attended)
        out_ref[...] = (live * (attended + added)).astype(BF).reshape(out_ref.shape)
        hots = hot_lanes(picks[c])
        own_gates = gates_of(hots, mm(normed, tail))
        summed = turned(jnp.sum(dg_in[...], axis=0))
        d_gates = [summed[:, k : k + 1] for k in range(2)]
        mean_gate = own_gates[0] * d_gates[0] + own_gates[1] * d_gates[1]
        d_logits = hots[0] * (own_gates[0] * (d_gates[0] - mean_gate)) + hots[1] * (
            own_gates[1] * (d_gates[1] - mean_gate)
        )
        d_normed = d_normed + split_dot(mm_nt, d_logits, tail)
        d_attended = upstream + norm_back(attended, inverse, d_normed * ffn_gain)
        d_att_b = d_attended.astype(BF)
        d_context = mm_nt(d_att_b, wo_all[...]).astype(BF)
        for i in range(nc):
            dctx_send[i] = d_context[:, i * head_width : (i + 1) * head_width].reshape(
                num_seqs, shard_len, head_width
            )
        for q in range(num_seqs):
            dctx_all[q, c] = dctx_send[c, q]
        dctx_copies = mail.post(
            dctx_all.at[:, others],
            [
                (dctx_send.at[wrap(c + s, nc)], dctx_all.at[:, c], in_plane[s - 1])
                for s in range(1, nc)
            ],
        )
        gin_ref[...] = d_attended.reshape(gin_ref.shape)
    pump(home, PUMPS[2])

    mail.settle([spread_wo, passed_wo])
    gwo_at = wo_buf
    with jax.named_scope("c_reduce"):
        for i in range(nc):
            mine = jnp.concatenate([ctx_all[i, q, c] for q in range(num_seqs)], axis=0)
            gwo_at[i] = mm_tn(mine, d_att_b).reshape(gwo_at.shape[1:]).astype(BF)
        sibling_wo = mail.post(sib_wo, [(gwo_at.at[:, :, 1 - f], sib_wo, sibling)])
        d_router = split_dot(mm_tn, normed, d_logits, left_wide=False)
        d_gain = jnp.sum(d_normed * attended * inverse, axis=0, keepdims=True)
        turned = jnp.transpose(jnp.broadcast_to(d_gain, (128, width)), (1, 0))
        extra_lane = lax.broadcasted_iota(jnp.int32, (width, 128), 1)
        extras = jnp.where(extra_lane == SMALL + num_experts + 1, turned, d_router)
        four_planes(sibling_wo, gwo_at, sib_wo)
        wo_copies = mail.post(
            zi_wo,
            [
                (sib_wo.at[:, wrap(z + s, nz)], zi_wo.at[s - 1], in_column[s - 1])
                for s in range(1, nz)
            ],
        )

    with jax.named_scope("c_wait_dctx"):
        dctx_copies.wait_recv()
    grad_qkv = jnp.zeros((width, 3 * head_width), F32)
    rs_first = mail.open(rs_in)
    for q in range(num_seqs):
        with jax.named_scope("c_attention"):
            d_context = dctx_all[q].reshape(full_len, head_width)
            allowed = allowed_keys(len_ref[q], half_len, full_len)
            merged = qkv_ref[q]
            d_query, d_key, d_value = [], [], []
            for h in range(heads_here):
                query = merged[:, h * HS : (h + 1) * HS]
                key = merged[:, head_width + h * HS : head_width + (h + 1) * HS]
                value = merged[:, 2 * head_width + h * HS : 2 * head_width + (h + 1) * HS]
                d_head = d_context[:, h * HS : (h + 1) * HS]
                probs = head_probs(query, key, allowed)
                d_probs = mm_nt(d_head, value)
                delta = jnp.sum(probs * d_probs, axis=1, keepdims=True)
                d_scores = (probs * (d_probs - delta)).astype(BF)
                d_query.append(mm(d_scores, key) * (HS**-0.5))
                d_key.append(mm_tn(d_scores, query) * (HS**-0.5))
                d_value.append(mm_tn(probs.astype(BF), d_head))
            both = jnp.concatenate(d_query + d_key, axis=1)
            both = both * cosines - swap_halves(both) * sines
            d_merged = jnp.concatenate([both] + d_value, axis=1).astype(BF)
            product = mm_nt(d_merged, w_ref[:, : 3 * head_width]).reshape(nc, shard_len, width)
            part_own[q] = product
            part[q] = product.astype(BF)
            for at, chip in enumerate((near_x if q == 0 else near_y, far)):
                rs_first.add(part.at[q, chip], rs_in.at[q, at], to_x if q == 0 else to_y)
            grad_qkv = grad_qkv + mm_tn(normed_ref[q], d_merged)
    pump(home, len(home))
    mail.settle([spread_wq, passed_wq])
    gq = wq_buf
    with jax.named_scope("c_reduce_q"):
        last = jnp.concatenate([grad_qkv[:, tail_at:], extras[:, 3 * head_width - tail_at :]], axis=1)
        gq[...] = (
            jnp.concatenate([grad_qkv[:, :tail_at], last], axis=1).reshape(gq.shape).astype(BF)
        )
        sibling_q = mail.post(sib_q, [(gq.at[:, :, 1 - f], sib_q, sibling)])
        four_planes(sibling_q, gq, sib_q)
        q_copies = mail.post(
            zi_q,
            [
                (sib_q.at[:, to[1]], zi_q.at[up - 1], to)
                for to, up in zip(in_column, steps_up)
            ],
        )
    with jax.named_scope("c_second_leg"):
        rs_first.wait_recv()
        for q in range(num_seqs):
            relay = part_own[q, near_y if q == 0 else near_x]
            rs_mid[q] = (relay + rs_in[q, 1].astype(F32)).astype(BF)
        rs_second = mail.post(
            rs_end,
            [(rs_mid.at[q], rs_end.at[q], to_y if q == 0 else to_x) for q in range(num_seqs)],
        )

    def column_sum(own, copies, inbox):
        copies.wait_recv()
        total = own.astype(F32)
        for s in range(1, nz):
            total = total + inbox[s - 1].astype(F32)
        return total

    def hand_out(box, final):
        final[c] = box[c]
        return mail.post(
            final.at[others],
            [(box.at[wrap(c + s, nc)], final.at[c], in_plane[s - 1]) for s in range(1, nc)],
        )

    with jax.named_scope("c_column_gu"):
        pb_gu[...] = column_sum(sib_gu[:, z], gu_copies, zi_gu).astype(BF)
        final_gu = hand_out(pb_gu, fgu_ref)
    with jax.named_scope("c_column_sd"):
        fsd_ref[...] = column_sum(sib_sd[z], sd_copies, zi_sd)
    with jax.named_scope("c_column_wo"):
        pb_wo[...] = column_sum(sib_wo[:, z], wo_copies, zi_wo).astype(BF)
        final_wo = hand_out(pb_wo, in_wo)
    with jax.named_scope("c_column_q"):
        pb_q[...] = column_sum(sib_q[:, z], q_copies, zi_q).astype(BF)
        final_q = hand_out(pb_q, fq_ref)
    with jax.named_scope("c_grad_in"):
        rs_second.wait_recv()
        for q in range(num_seqs):
            d_normed = part_own[q, c] + rs_in[q, 0].astype(F32) + rs_end[q].astype(F32)
            rows = hid_ref[q].astype(F32)
            gin_ref[q] = gin_ref[q] + norm_back(rows, inverse_rms(rows), d_normed * attn_gain)
    with jax.named_scope("c_final"):
        final_wo.wait_recv()
        fwo_ref[...] = jnp.sum(in_wo[...].astype(F32), axis=0)
        final_gu.wait_recv()
        final_q.wait_recv()
    with jax.named_scope("c_wait_home"):
        home_in_own.wait()
        home_in.wait_recv()

        @pl.when(to_core == f)
        def _():
            home_out_own(0).wait()
            home_out.wait_recv(remote_home)
            home_out.wait_send(remote_home)
            expert_out.wait_send(remote_out)

        @pl.when(to_core != f)
        def _():
            home_out.wait_recv()
            home_out.wait_send()
            expert_out.wait_send()

    assert mail.count <= POSTS, mail.count
    with jax.named_scope("z_finish"):
        mail.finish()


def finish_kernel(
    nc, fq_ref, fgu_ref, wqkv_ref, ga_ref, ein_ref, eout_ref, out_in, gin_in, fsd_in, fwo_in,
    gq_ref, gr_ref, gga_ref, ggf_ref, ggu_ref, oin_ref, oout_ref, out_ref, gin_ref, fsd_ref, fwo_ref,
):
    oin_ref[...] = ein_ref[...].astype(F32)
    oout_ref[...] = eout_ref[...].astype(F32)

    @pl.when((pl.program_id(0) == 0) & (pl.program_id(1) == 0))
    def _():
        out_ref[...] = out_in[...]
        gin_ref[...] = gin_in[...]
        fsd_ref[...] = fsd_in[...]
        fwo_ref[...] = fwo_in[...]
        rows_w = wqkv_ref.shape[0]
        head_width = wqkv_ref.shape[1] // 3 // nc
        grads = jnp.concatenate(
            [
                fq_ref[i, :, side * head_width : (side + 1) * head_width].astype(F32)
                for side in range(3)
                for i in range(nc)
            ],
            axis=1,
        )
        gq_ref[...] = grads
        own_units = fgu_ref.shape[2] // 2
        ggu_ref[...] = jnp.concatenate(
            [
                fgu_ref[i, :, side * own_units : (side + 1) * own_units].astype(F32)
                for side in range(2)
                for i in range(nc)
            ],
            axis=1,
        )
        extras = jnp.sum(fq_ref[:, :, 3 * head_width - SMALL :].astype(F32), axis=0)
        num_experts = gr_ref.shape[0]
        first = jnp.sum(wqkv_ref[...].astype(F32) * grads, axis=1, keepdims=True)
        lane = lax.broadcasted_iota(jnp.int32, (rows_w, 128), 1)
        both = jnp.where(lane == SMALL + num_experts, first, extras)
        turned = jnp.transpose(
            jnp.concatenate([both, jnp.zeros((128 - rows_w, 128), F32)], axis=0), (1, 0)
        )
        gr_ref[...] = turned[SMALL : SMALL + num_experts, :rows_w]
        at = SMALL + num_experts
        gga_ref[...] = turned[at : at + 1, :rows_w] / ga_ref[...].astype(F32)
        ggf_ref[...] = turned[at + 1 : at + 2, :rows_w]


def vmem(*shape, dtype=jnp.bfloat16):
    return pltpu.VMEM(shape, dtype)


def fast_device(
    hidden_in, seq_lengths, expert_ids, route_rank, gain_attn, w_qkv, w_out, w_router, gain_ffn,
    w_gate_up, w_shared_down, w_experts_in, w_experts_out, grad_output,
):
    nc, nz = lax.axis_size("ctx"), lax.axis_size("exp")
    num_seqs, two_ends, half_len, width = hidden_in.shape
    shard_len = 2 * half_len
    full_len = nc * shard_len
    tok = num_seqs * shard_len
    rows_w = w_qkv.shape[0]
    head_width = w_qkv.shape[1] // 3 // nc
    num_experts = w_router.shape[1]
    down_rows = w_shared_down.shape[0]
    own_units = w_gate_up.shape[1] // 2 // nc
    half_units = w_experts_in.shape[2] // 4
    hbm, vm, sm = pl.ANY, pltpu.VMEM, pltpu.SMEM
    dma = pltpu.SemaphoreType.DMA

    seq_shape = (num_seqs, shard_len, width)
    group_shape = (num_seqs, nc, shard_len, width)
    blocks = (nc, nz, 2, rows_w)
    half_blocks = (nc, nz, rows_w)
    wide_cols = 3 * head_width + SMALL
    num_slots = num_experts * CAP
    row_box = (nz, nc, BOX, width)
    plane_tok = nc * tok
    outs = [
        (seq_shape, BF),
        (seq_shape, F32),
        ((nc, rows_w, wide_cols), BF),
        ((nc, rows_w, 2 * own_units), BF),
        ((down_rows, width), F32),
        ((rows_w, width), F32),
        (w_experts_in.shape, BF),
        (w_experts_out.shape, BF),
    ]
    out, gin, fq, fgu, fsd, fwo, ein, eout = pl.pallas_call(
        functools.partial(block_kernel, nc, nz),
        out_shape=[jax.ShapeDtypeStruct(shape, dtype) for shape, dtype in outs],
        in_specs=[
            pl.BlockSpec(memory_space=space) for space in [sm] + [vm] * 11 + [hbm, hbm]
        ],
        out_specs=[pl.BlockSpec(memory_space=space) for space in [vm] * 6 + [hbm, hbm]],
        scratch_shapes=[
            vmem(full_len, 256, dtype=F32),
            vmem(8, tok, dtype=jnp.int32),
            vmem(nc, 8, tok, dtype=jnp.int32),
            vmem(nc, tok, 128, dtype=F32),
            vmem(nc, 2, tok, nz * BOX),
            vmem(nc, 2, tok, nz * BOX),
            vmem(nc, 8, tok, dtype=F32),
            vmem(nc, 8, tok, dtype=F32),
            vmem(*group_shape),
            vmem(*seq_shape),
            vmem(*group_shape),
            vmem(nc, rows_w, wide_cols),
            vmem(nc, rows_w, wide_cols),
            vmem(*blocks, wide_cols),
            vmem(width, wide_cols),
            vmem(nc, rows_w, 2 * own_units),
            vmem(*blocks, 2 * own_units),
            vmem(width, 2 * own_units),
            vmem(nc, rows_w, width),
            vmem(*blocks, width),
            vmem(width, width),
            vmem(nz, 2, down_rows, width),
            vmem(width, 2 * half_units),
            vmem(half_units, width),
            vmem(num_seqs, full_len, width),
            vmem(num_seqs, full_len, 3 * head_width),
            vmem(nc, num_seqs, nc, shard_len, head_width),
            vmem(*seq_shape, dtype=F32),
            vmem(*group_shape),
            vmem(*row_box),
            vmem(2, nz, nc, BOX, width),
            vmem(2 * num_slots, width),
            vmem(2 * num_slots, width),
            vmem(2 * num_slots, width, dtype=F32),
            vmem(2 * num_slots, width, dtype=F32),
            vmem(2, num_seqs, 2, shard_len, width, dtype=F32),
            vmem(plane_tok, own_units),
            vmem(plane_tok, 2 * own_units),
            vmem(2, *group_shape),
            vmem(2, num_seqs, 2, shard_len, width),
            vmem(2, *seq_shape),
            vmem(2, *seq_shape),
            vmem(2 * num_slots, half_units),
            vmem(2 * num_slots, 2 * half_units),
            vmem(*row_box),
            vmem(*row_box),
            vmem(*row_box),
            vmem(nz, 2, down_rows, width),
            vmem(*seq_shape),
            vmem(nc, num_seqs, shard_len, head_width),
            vmem(num_seqs, nc, shard_len, head_width),
            vmem(*group_shape),
            vmem(*group_shape, dtype=F32),
            vmem(num_seqs, 2, shard_len, width),
            vmem(*seq_shape),
            vmem(*seq_shape),
            vmem(*half_blocks, 2 * own_units),
            vmem(nz - 1, nc, rows_w, 2 * own_units),
            vmem(nc, rows_w, 2 * own_units),
            vmem(*half_blocks, wide_cols),
            vmem(nz - 1, nc, rows_w, wide_cols),
            vmem(nc, rows_w, wide_cols),
            vmem(nz, down_rows, width),
            vmem(nz - 1, down_rows, width),
            vmem(*half_blocks, width),
            vmem(nz - 1, nc, rows_w, width),
            vmem(nc, rows_w, width),
            vmem(nc, rows_w, width),
            dma((POSTS,)),
            dma((POSTS,)),
            dma((1 + half_units // 256,)),
        ],
        compiler_params=pltpu.CompilerParams(
            collective_id=0, has_side_effects=True, vmem_limit_bytes=VMEM_BYTES
        ),
        cost_estimate=pl.CostEstimate(
            flops=16_000_000_000, bytes_accessed=30_000_000, transcendentals=0
        ),
        name="block_forward_backward",
    )(
        seq_lengths,
        hidden_in.reshape(seq_shape),
        grad_output.reshape(seq_shape),
        expert_ids.transpose(0, 1, 3, 2),
        route_rank.reshape(1, tok),
        w_qkv, w_router.T, gain_attn.reshape(1, rows_w), gain_ffn.reshape(1, rows_w),
        w_gate_up, w_out, w_shared_down, w_experts_in, w_experts_out,
    )

    def whole(shape):
        return pl.BlockSpec(shape, lambda e, j: (0,) * len(shape))

    def one(shape):
        return pl.BlockSpec((1, shape[1], shape[2] // WIDEN), lambda e, j: (e, 0, j))

    ins = [fq, fgu, w_qkv, gain_attn.reshape(1, rows_w), ein, eout, out, gin, fsd, fwo]
    results = [
        (w_qkv.shape, F32),
        (w_router.shape[::-1], F32),
        ((1, rows_w), F32),
        ((1, rows_w), F32),
        (w_gate_up.shape, F32),
        (ein.shape, F32),
        (eout.shape, F32),
        (seq_shape, BF),
        (seq_shape, F32),
        (fsd.shape, F32),
        (fwo.shape, F32),
    ]
    grad_qkv, grad_router, grad_ga, grad_gf, grad_gu, grad_in, grad_out, out, gin, fsd, fwo = pl.pallas_call(
        functools.partial(finish_kernel, nc),
        grid=(ein.shape[0], WIDEN),
        out_shape=[jax.ShapeDtypeStruct(shape, dtype) for shape, dtype in results],
        in_specs=[one(x.shape) if i in (4, 5) else whole(x.shape) for i, x in enumerate(ins)],
        out_specs=[
            one(shape) if i in (5, 6) else whole(shape) for i, (shape, _) in enumerate(results)
        ],
        compiler_params=pltpu.CompilerParams(vmem_limit_bytes=VMEM_BYTES),
        name="widen_gradients",
    )(*ins)
    return (
        out.reshape(hidden_in.shape),
        gin.reshape(hidden_in.shape),
        grad_ga.reshape(rows_w),
        grad_qkv,
        fwo,
        grad_router.T,
        grad_gf.reshape(rows_w),
        grad_gu,
        fsd,
        grad_in,
        grad_out,
    )


def fits(mesh, hidden_in, w_qkv, w_router, w_gate_up, w_experts_in):
    nc, nz, nf = mesh.shape["ctx"], mesh.shape["exp"], mesh.shape["fsdp"]
    heads = w_qkv.shape[1] // 3 // HS
    return (
        nf == 2
        and nc == 4
        and nz == 4
        and heads == 12
        and w_router.shape[1] == nc * nz
        and w_qkv.shape[0] == 768
        and hidden_in.shape[2] == 32 * nc
        and hidden_in.shape[0] == 2 * nz * nf
        and hidden_in.shape[3] == 768
        and w_gate_up.shape[1] == w_experts_in.shape[2] == 4096
        and 2 * CAP <= BOX
    )


def solution(mesh):
    def whole(*args):
        chosen = fast_device if fits(mesh, args[0], args[5], args[7], args[9], args[11]) else per_device
        return placed(mesh, chosen)(*args)

    return whole


def placed(mesh, chosen):
    return jax.shard_map(
        chosen,
        mesh=mesh,
        in_specs=(
            P(("exp", "fsdp"), None, "ctx", None),
            P(("exp", "fsdp")),
            P(("exp", "fsdp"), None, "ctx", None),
            P(("exp", "fsdp"), "ctx", None),
            P(("ctx", "exp", "fsdp")),
            P(("ctx", "exp", "fsdp"), None),
            P(("ctx", "exp", "fsdp"), None),
            P(("ctx", "exp", "fsdp"), None),
            P(("ctx", "exp", "fsdp")),
            P(("ctx", "exp", "fsdp"), None),
            P(("ctx", "exp", "fsdp"), None),
            P("exp", ("ctx", "fsdp"), None),
            P("exp", ("ctx", "fsdp"), None),
            P(("exp", "fsdp"), None, "ctx", None),
        ),
        out_specs=(
            P(("exp", "fsdp"), None, "ctx", None),
            P(("exp", "fsdp"), None, "ctx", None),
            P(("ctx", "exp", "fsdp")),
            P(("ctx", "exp", "fsdp"), None),
            P(("ctx", "exp", "fsdp"), None),
            P(("ctx", "exp", "fsdp"), None),
            P(("ctx", "exp", "fsdp")),
            P(("ctx", "exp", "fsdp"), None),
            P(("ctx", "exp", "fsdp"), None),
            P("exp", ("ctx", "fsdp"), None),
            P("exp", ("ctx", "fsdp"), None),
        ),
        check_vma=False,
    )
```

```python
import functools
import math

import jax
import jax.numpy as jnp
from jax import lax
from jax.experimental import pallas as pl
from jax.experimental.pallas import tpu as pltpu
from jax.sharding import PartitionSpec as P

HS = 64
CAP = 18


epsilon = 1e-06
masked_out = -1e30
highest = lax.Precision.HIGHEST


def rms_norm(values_in, gain_row):
    return (
        values_in
        * lax.rsqrt(jnp.mean(values_in * values_in, axis=-1, keepdims=True) + epsilon)
        * gain_row
    )


def rope_tables(places):
    half_size = HS // 2
    frequency = 10000.0 ** (-jnp.arange(half_size, dtype=jnp.float32) * 2.0 / HS)
    angles = places.astype(jnp.float32)[:, None] * frequency[None, :]
    return (jnp.cos(angles), jnp.sin(angles))


def rotate(values_in, cosines, sine_rows):
    half_size = values_in.shape[-1] // 2
    leading = values_in[..., :half_size]
    trailing = values_in[..., half_size:]
    cos_rows = cosines[:, None, :]
    sin_rows = sine_rows[:, None, :]
    return jnp.concatenate(
        [leading * cos_rows - trailing * sin_rows, leading * sin_rows + trailing * cos_rows],
        axis=-1,
    )


def swiglu(merged_rows):
    gate_part, up_part = jnp.split(merged_rows, 2, axis=-1)
    return jax.nn.silu(gate_part) * up_part


def first_t(left_side, right_side, precision=None):
    return lax.dot_general(
        left_side,
        right_side,
        (((0,), (0,)), ((), ())),
        precision=precision,
        preferred_element_type=jnp.float32,
    )


def second_t(left_side, right_side, precision=None):
    return lax.dot_general(
        left_side,
        right_side,
        (((1,), (1,)), ((), ())),
        precision=precision,
        preferred_element_type=jnp.float32,
    )


def per_device(
    hidden_in,
    seq_lengths,
    expert_ids,
    route_rank,
    gain_attn,
    w_qkv,
    w_out,
    w_router,
    gain_ffn,
    w_gate_up,
    w_shared_down,
    w_experts_in,
    w_experts_out,
    grad_output,
):
    num_seqs, two_ends, half_len, model_width = hidden_in.shape
    shard_len = 2 * half_len
    tok_count = num_seqs * shard_len
    num_heads = model_width // HS
    score_scale = HS ** (-0.5)
    ctx_size = lax.axis_size("ctx")
    full_len = shard_len * ctx_size
    whole_half = half_len * ctx_size
    gain_one, wqkv_all, wout_all, router_all, gain_two, shared_in, shared_down = (
        lax.all_gather(gain_attn, ("ctx", "exp", "fsdp"), axis=0, tiled=True),
        lax.all_gather(w_qkv, ("ctx", "exp", "fsdp"), axis=0, tiled=True),
        lax.all_gather(w_out, ("ctx", "exp", "fsdp"), axis=0, tiled=True),
        lax.all_gather(w_router, ("ctx", "exp", "fsdp"), axis=0, tiled=True),
        lax.all_gather(gain_ffn, ("ctx", "exp", "fsdp"), axis=0, tiled=True),
        lax.all_gather(w_gate_up, ("ctx", "exp", "fsdp"), axis=0, tiled=True),
        lax.all_gather(w_shared_down, ("ctx", "exp", "fsdp"), axis=0, tiled=True),
    )
    experts_in, experts_out = (
        lax.all_gather(w_experts_in, ("ctx", "fsdp"), axis=1, tiled=True),
        lax.all_gather(w_experts_out, ("ctx", "fsdp"), axis=1, tiled=True),
    )
    lower_places = lax.axis_index("ctx") * half_len + jnp.arange(half_len, dtype=jnp.int32)
    places = jnp.concatenate([lower_places, full_len - 1 - lower_places])
    whole_range = jnp.arange(whole_half, dtype=jnp.int32)
    full_places = jnp.concatenate([whole_range, full_len - 1 - whole_range])
    live_mask = (places[None, :] < seq_lengths[:, None]).astype(jnp.float32)
    live_rows = live_mask.reshape(tok_count, 1)
    inputs_f = hidden_in.astype(jnp.float32).reshape(tok_count, model_width)
    gain_attn_f = gain_one.astype(jnp.float32)
    normed_b = rms_norm(inputs_f, gain_attn_f).astype(jnp.bfloat16)
    qkv_merged = jnp.dot(normed_b, wqkv_all, preferred_element_type=jnp.float32).reshape(
        num_seqs, shard_len, 3, num_heads, HS
    )
    cosines, sine_rows = rope_tables(places)
    queries = rotate(qkv_merged[:, :, 0], cosines, sine_rows).astype(jnp.bfloat16)
    keys_local = rotate(qkv_merged[:, :, 1], cosines, sine_rows).astype(jnp.bfloat16)
    values_local = qkv_merged[:, :, 2].astype(jnp.bfloat16)
    end_shape = (num_seqs, 2, half_len, model_width)
    keys_full, values_full = (
        lax.all_gather(keys_local.reshape(end_shape), "ctx", axis=2, tiled=True),
        lax.all_gather(values_local.reshape(end_shape), "ctx", axis=2, tiled=True),
    )
    keys_full = keys_full.reshape(num_seqs, full_len, num_heads, HS)
    values_full = values_full.reshape(num_seqs, full_len, num_heads, HS)
    stat_shape = (num_seqs, num_heads, shard_len)
    block_range = jnp.arange(ctx_size, dtype=jnp.int32)

    def block_scores(query_rows, query_places, key_rows, key_places):
        scores = (
            jnp.einsum("bqhd,bkhd->bhqk", query_rows, key_rows, preferred_element_type=jnp.float32)
            * score_scale
        )
        allowed = (key_places[None, None, :] <= query_places[None, :, None]) & (
            key_places[None, None, :] < seq_lengths[:, None, None]
        )
        return jnp.where(allowed[:, None], scores, masked_out)

    def key_block(block_idx):
        offset = block_idx * shard_len
        return (
            lax.dynamic_slice_in_dim(keys_full, offset, shard_len, 1),
            lax.dynamic_slice_in_dim(values_full, offset, shard_len, 1),
            lax.dynamic_slice_in_dim(full_places, offset, shard_len, 0),
        )

    def lse_step(state_in, block_idx):
        run_max, run_sum = state_in
        key_rows, value_rows, key_places = key_block(block_idx)
        scores = block_scores(queries, places, key_rows, key_places)
        new_max = jnp.maximum(run_max, jnp.max(scores, axis=-1))
        run_sum = run_sum * jnp.exp(run_max - new_max) + jnp.sum(
            jnp.exp(scores - new_max[..., None]), axis=-1
        )
        return ((new_max, run_sum), None)

    (row_max, row_sum), unused = lax.scan(
        lse_step,
        (jnp.full(stat_shape, masked_out, jnp.float32), jnp.zeros(stat_shape, jnp.float32)),
        block_range,
    )
    log_total = row_max + jnp.log(row_sum)

    def context_step(running, block_idx):
        key_rows, value_rows, key_places = key_block(block_idx)
        prob_rows = jnp.exp(
            block_scores(queries, places, key_rows, key_places) - log_total[..., None]
        ).astype(jnp.bfloat16)
        return (
            running
            + jnp.einsum(
                "bhqk,bkhd->bqhd", prob_rows, value_rows, preferred_element_type=jnp.float32
            ),
            None,
        )

    context, unused = lax.scan(
        context_step, jnp.zeros((num_seqs, shard_len, num_heads, HS), jnp.float32), block_range
    )
    context_b = context.reshape(tok_count, model_width).astype(jnp.bfloat16)
    attended = inputs_f + jnp.dot(context_b, wout_all, preferred_element_type=jnp.float32)
    gain_ffn_f = gain_two.astype(jnp.float32)
    normed_two = rms_norm(attended, gain_ffn_f).astype(jnp.bfloat16)
    logits = jnp.dot(normed_two, router_all, preferred_element_type=jnp.float32)
    num_experts = router_all.shape[1]
    expert_range = jnp.arange(num_experts, dtype=jnp.int32)
    picked_ids = expert_ids.reshape(tok_count, 2)
    pick_hot = (picked_ids[:, :, None] == expert_range).astype(jnp.float32)
    chosen = jnp.sum(pick_hot * logits[:, None, :], axis=-1)
    gate_probs = jax.nn.softmax(chosen, axis=-1)
    expert_load = (jnp.sum(pick_hot, axis=1) * live_rows).astype(jnp.bfloat16)
    rank_rows = route_rank.reshape(tok_count)
    earlier = (rank_rows[None, :] < rank_rows[:, None]).astype(jnp.bfloat16)
    position = jnp.dot(earlier, expert_load, preferred_element_type=jnp.float32)
    chosen_pos = jnp.sum(pick_hot * position[:, None, :], axis=-1)
    kept_mask = live_rows * (chosen_pos < CAP).astype(jnp.float32)
    slot_hot = (chosen_pos[:, :, None] == jnp.arange(CAP, dtype=jnp.float32)).astype(jnp.float32)
    dispatch = (
        (pick_hot[:, :, :, None] * slot_hot[:, :, None, :] * kept_mask[:, :, None, None])
        .reshape(tok_count, 2, num_experts * CAP)
        .astype(jnp.bfloat16)
    )
    dispatch_any = dispatch[:, 0] + dispatch[:, 1]
    exp_size = lax.axis_size("exp")
    per_owner = num_experts // exp_size
    send_rows = (
        first_t(dispatch_any, normed_two)
        .astype(jnp.bfloat16)
        .reshape(exp_size, per_owner, CAP, model_width)
    )
    arrived = lax.all_to_all(send_rows, "exp", split_axis=0, concat_axis=0, tiled=True)
    expert_merged = jnp.einsum(
        "secd,edf->secf", arrived, experts_in, preferred_element_type=jnp.float32
    )
    expert_hidden = swiglu(expert_merged).astype(jnp.bfloat16)
    expert_result = jnp.einsum(
        "secf,efd->secd", expert_hidden, experts_out, preferred_element_type=jnp.float32
    ).astype(jnp.bfloat16)
    returned = lax.all_to_all(
        expert_result, "exp", split_axis=0, concat_axis=0, tiled=True
    ).reshape(num_experts * CAP, model_width)
    routed = jnp.einsum("tks,sd->tkd", dispatch, returned, preferred_element_type=jnp.float32)
    mixture = jnp.sum(gate_probs[:, :, None] * routed, axis=1)
    shared_merged = jnp.dot(normed_two, shared_in, preferred_element_type=jnp.float32)
    shared_hidden = swiglu(shared_merged).astype(jnp.bfloat16)
    shared_result = jnp.dot(shared_hidden, shared_down, preferred_element_type=jnp.float32)
    layer_out = (
        (live_rows * (attended + mixture + shared_result)).reshape(end_shape).astype(jnp.bfloat16)
    )
    upstream = grad_output.astype(jnp.float32).reshape(tok_count, model_width) * live_rows
    upstream_b = upstream.astype(jnp.bfloat16)
    upstream_f = upstream_b.astype(jnp.float32)
    d_shared_down = first_t(shared_hidden, upstream_b)
    d_shared_hidden = second_t(upstream_b, shared_down)
    unused, swiglu_pull = jax.vjp(swiglu, shared_merged)
    d_shared_merged = swiglu_pull(d_shared_hidden)[0].astype(jnp.bfloat16)
    d_shared_in = first_t(normed_two, d_shared_merged)
    d_normed_two = second_t(d_shared_merged, shared_in)
    gate_grads = jnp.sum(routed * upstream_f[:, None, :], axis=-1)
    weighted = (gate_probs[:, :, None] * upstream_f[:, None, :]).astype(jnp.bfloat16)
    d_returned = (
        jnp.einsum("tks,tkd->sd", dispatch, weighted, preferred_element_type=jnp.float32)
        .astype(jnp.bfloat16)
        .reshape(exp_size, per_owner, CAP, model_width)
    )
    d_result = lax.all_to_all(d_returned, "exp", split_axis=0, concat_axis=0, tiled=True)
    d_experts_out = jnp.einsum(
        "secf,secd->efd", expert_hidden, d_result, preferred_element_type=jnp.float32
    )
    d_expert_hidden = jnp.einsum(
        "secd,efd->secf", d_result, experts_out, preferred_element_type=jnp.float32
    )
    unused, expert_pull = jax.vjp(swiglu, expert_merged)
    d_expert_merged = expert_pull(d_expert_hidden)[0].astype(jnp.bfloat16)
    d_experts_in = jnp.einsum(
        "secd,secf->edf", arrived, d_expert_merged, preferred_element_type=jnp.float32
    )
    d_arrived = jnp.einsum(
        "secf,edf->secd", d_expert_merged, experts_in, preferred_element_type=jnp.float32
    ).astype(jnp.bfloat16)
    d_sent = lax.all_to_all(d_arrived, "exp", split_axis=0, concat_axis=0, tiled=True).reshape(
        num_experts * CAP, model_width
    )
    d_normed_two = d_normed_two + jnp.dot(dispatch_any, d_sent, preferred_element_type=jnp.float32)
    unused, gate_pull = jax.vjp(lambda chosen_in: jax.nn.softmax(chosen_in, axis=-1), chosen)
    d_chosen = gate_pull(gate_grads)[0]
    d_logits = jnp.sum(pick_hot * d_chosen[:, :, None], axis=1)
    d_router = first_t(normed_two.astype(jnp.float32), d_logits, highest)
    d_normed_two = d_normed_two + second_t(d_logits, router_all.astype(jnp.float32), highest)
    unused, second_pull = jax.vjp(rms_norm, attended, gain_ffn_f)
    d_attended, d_gain_ffn = second_pull(d_normed_two)
    d_attended = d_attended + upstream
    d_attended_b = d_attended.astype(jnp.bfloat16)
    d_out_proj = first_t(context_b, d_attended_b)
    d_context = (
        second_t(d_attended_b, wout_all)
        .astype(jnp.bfloat16)
        .reshape(num_seqs, shard_len, num_heads, HS)
    )

    def score_grads(
        query_rows, query_places, key_rows, value_rows, key_places, d_rows, lse_rows, delta_rows
    ):
        prob_rows = jnp.exp(
            block_scores(query_rows, query_places, key_rows, key_places) - lse_rows[..., None]
        )
        d_probs = jnp.einsum(
            "bqhd,bkhd->bhqk", d_rows, value_rows, preferred_element_type=jnp.float32
        )
        d_scores = (prob_rows * (d_probs - delta_rows[..., None])).astype(jnp.bfloat16)
        return (prob_rows.astype(jnp.bfloat16), d_scores)

    def delta_step(running, block_idx):
        key_rows, value_rows, key_places = key_block(block_idx)
        prob_rows = jnp.exp(
            block_scores(queries, places, key_rows, key_places) - log_total[..., None]
        )
        d_probs = jnp.einsum(
            "bqhd,bkhd->bhqk", d_context, value_rows, preferred_element_type=jnp.float32
        )
        return (running + jnp.sum(prob_rows * d_probs, axis=-1), None)

    row_delta, unused = lax.scan(delta_step, jnp.zeros(stat_shape, jnp.float32), block_range)
    head_shape = (num_seqs, shard_len, num_heads, HS)

    def query_step(d_query, block_idx):
        key_rows, value_rows, key_places = key_block(block_idx)
        prob_b, d_scores = score_grads(
            queries, places, key_rows, value_rows, key_places, d_context, log_total, row_delta
        )
        return (
            d_query
            + jnp.einsum("bhqk,bkhd->bqhd", d_scores, key_rows, preferred_element_type=jnp.float32)
            * score_scale,
            None,
        )

    d_query, unused = lax.scan(query_step, jnp.zeros(head_shape, jnp.float32), block_range)
    query_all, d_context_all = (
        lax.all_gather(queries.reshape(end_shape), "ctx", axis=2, tiled=True),
        lax.all_gather(d_context.reshape(end_shape), "ctx", axis=2, tiled=True),
    )
    stat_ends = (num_seqs, num_heads, 2, half_len)
    lse_all, delta_all = (
        lax.all_gather(log_total.reshape(stat_ends), "ctx", axis=3, tiled=True),
        lax.all_gather(row_delta.reshape(stat_ends), "ctx", axis=3, tiled=True),
    )
    query_all = query_all.reshape(num_seqs, full_len, num_heads, HS)
    d_context_all = d_context_all.reshape(num_seqs, full_len, num_heads, HS)
    lse_all = lse_all.reshape(num_seqs, num_heads, full_len)
    delta_all = delta_all.reshape(num_seqs, num_heads, full_len)

    def owner_step(state_in, block_idx):
        d_keys, d_values = state_in
        offset = block_idx * shard_len
        query_rows = lax.dynamic_slice_in_dim(query_all, offset, shard_len, 1)
        d_rows = lax.dynamic_slice_in_dim(d_context_all, offset, shard_len, 1)
        lse_rows = lax.dynamic_slice_in_dim(lse_all, offset, shard_len, 2)
        delta_rows = lax.dynamic_slice_in_dim(delta_all, offset, shard_len, 2)
        query_places = lax.dynamic_slice_in_dim(full_places, offset, shard_len, 0)
        prob_b, d_scores = score_grads(
            query_rows, query_places, keys_local, values_local, places, d_rows, lse_rows, delta_rows
        )
        d_keys = (
            d_keys
            + jnp.einsum(
                "bhqk,bqhd->bkhd", d_scores, query_rows, preferred_element_type=jnp.float32
            )
            * score_scale
        )
        d_values = d_values + jnp.einsum(
            "bhqk,bqhd->bkhd", prob_b, d_rows, preferred_element_type=jnp.float32
        )
        return ((d_keys, d_values), None)

    (d_keys_local, d_values_local), unused = lax.scan(
        owner_step,
        (jnp.zeros(head_shape, jnp.float32), jnp.zeros(head_shape, jnp.float32)),
        block_range,
    )
    unused, rope_pull = jax.vjp(
        lambda rows_in: rotate(rows_in, cosines, sine_rows), qkv_merged[:, :, 0]
    )
    d_query_pre = rope_pull(d_query)[0]
    d_key_pre = rope_pull(d_keys_local)[0]
    d_qkv_merged = (
        jnp.stack([d_query_pre, d_key_pre, d_values_local], axis=2)
        .reshape(tok_count, 3 * model_width)
        .astype(jnp.bfloat16)
    )
    d_qkv = first_t(normed_b, d_qkv_merged)
    d_normed = second_t(d_qkv_merged, wqkv_all)
    unused, first_pull = jax.vjp(rms_norm, inputs_f, gain_attn_f)
    d_inputs, d_gain_attn = first_pull(d_normed)
    grad_input = (d_attended + d_inputs).reshape(end_shape)
    dense_sums = (
        lax.psum_scatter(d_gain_attn, ("ctx", "exp", "fsdp"), scatter_dimension=0, tiled=True),
        lax.psum_scatter(d_qkv, ("ctx", "exp", "fsdp"), scatter_dimension=0, tiled=True),
        lax.psum_scatter(d_out_proj, ("ctx", "exp", "fsdp"), scatter_dimension=0, tiled=True),
        lax.psum_scatter(d_router, ("ctx", "exp", "fsdp"), scatter_dimension=0, tiled=True),
        lax.psum_scatter(d_gain_ffn, ("ctx", "exp", "fsdp"), scatter_dimension=0, tiled=True),
        lax.psum_scatter(d_shared_in, ("ctx", "exp", "fsdp"), scatter_dimension=0, tiled=True),
        lax.psum_scatter(d_shared_down, ("ctx", "exp", "fsdp"), scatter_dimension=0, tiled=True),
    )
    expert_sums = (
        lax.psum_scatter(
            d_experts_in.astype(jnp.bfloat16), ("ctx", "fsdp"), scatter_dimension=1, tiled=True
        ).astype(jnp.float32),
        lax.psum_scatter(
            d_experts_out.astype(jnp.bfloat16), ("ctx", "fsdp"), scatter_dimension=1, tiled=True
        ).astype(jnp.float32),
    )
    return (
        layer_out,
        grad_input,
        dense_sums[0],
        dense_sums[1],
        dense_sums[2],
        dense_sums[3],
        dense_sums[4],
        dense_sums[5],
        dense_sums[6],
        expert_sums[0],
        expert_sums[1],
    )


F32 = jnp.float32
BF = jnp.bfloat16
MESH = pl.DeviceIdType.MESH
BOX = 40
SMALL = 64
VMEM_BYTES = 63 * 1024 * 1024
PUMPS = (3, 17, 6, 0, 6, 6)
POSTS = 64
EARLY = 2
LATE = 1
WIDEN = 1


def place():
    return lax.axis_index("ctx"), lax.axis_index("exp"), lax.axis_index("fsdp")


def wrap(value, size):
    return lax.rem(value, size)


def mm(left, right):
    return lax.dot_general(
        left, right, (((1,), (0,)), ((), ())), preferred_element_type=F32
    )


def mm_nt(left, right):
    return lax.dot_general(
        left, right, (((1,), (1,)), ((), ())), preferred_element_type=F32
    )


def mm_tn(left, right):
    return lax.dot_general(
        left, right, (((0,), (0,)), ((), ())), preferred_element_type=F32
    )


def greet(peers):
    barrier = pltpu.get_barrier_semaphore()
    for peer in peers:
        pl.semaphore_signal(barrier, inc=1, device_id=peer, device_id_type=MESH)


def met(peers):
    pl.semaphore_wait(pltpu.get_barrier_semaphore(), len(peers))


class Post:
    def __init__(self, send, recv, like, device):
        self.send, self.recv, self.like, self.device = send, recv, like, device

    def add(self, src, dst, device):
        pltpu.make_async_remote_copy(
            src_ref=src,
            dst_ref=dst,
            send_sem=self.send,
            recv_sem=self.recv,
            device_id=device,
            device_id_type=MESH,
        ).start()

    def all_of_it(self, like=None):
        like = self.like if like is None else like
        return pltpu.make_async_remote_copy(
            src_ref=like,
            dst_ref=like,
            send_sem=self.send,
            recv_sem=self.recv,
            device_id=self.device,
            device_id_type=MESH,
        )

    def wait_recv(self, like=None):
        self.all_of_it(like).wait_recv()

    def wait_send(self, like=None):
        self.all_of_it(like).wait_send()


class Courier:
    def __init__(self, send, recv, device):
        self.send, self.recv, self.device, self.count, self.sent = send, recv, device, 0, []

    def open(self, like, keep=True):
        post = Post(self.send.at[self.count], self.recv.at[self.count], like, self.device)
        self.count += 1
        if keep:
            self.sent.append(post)
        return post

    def at(self, index, like):
        return Post(self.send.at[index], self.recv.at[index], like, self.device)

    def post(self, like, moves):
        post = self.open(like)
        for src, dst, device in moves:
            post.add(src, dst, device)
        return post

    def settle(self, posts):
        for post in posts:
            post.wait_send()
        done = {id(post) for post in posts}
        self.sent = [post for post in self.sent if id(post) not in done]

    def finish(self):
        self.settle(list(self.sent))


def swap_halves(rows):
    width = rows.shape[1]
    lane = lax.broadcasted_iota(jnp.int32, rows.shape, 1)
    ahead = pltpu.roll(rows, width - HS // 2, 1)
    behind = pltpu.roll(rows, HS // 2, 1)
    return jnp.where((lane & (HS - 1)) < HS // 2, -ahead, behind)


def wide(table, times):
    return jnp.concatenate([table] * times, axis=1)


def position_of(index, half_len, full_len):
    block = index // (2 * half_len)
    inside = index & (2 * half_len - 1)
    low = block * half_len + (inside & (half_len - 1))
    return jnp.where(inside >= half_len, full_len - 1 - low, low)


def allowed_keys(length, half_len, full_len):
    shape = (full_len, full_len)
    query_at = position_of(lax.broadcasted_iota(jnp.int32, shape, 0), half_len, full_len)
    key_at = position_of(lax.broadcasted_iota(jnp.int32, shape, 1), half_len, full_len)
    return (key_at <= query_at) & (key_at < length)


def head_probs(query, key, allowed):
    scores = jnp.where(allowed, mm_nt(query, key) * (HS**-0.5), masked_out)
    weights = jnp.exp(scores - jnp.max(scores, axis=1, keepdims=True))
    return weights * (1.0 / jnp.sum(weights, axis=1, keepdims=True))


def column_row(tail, lane):
    pick = (lax.broadcasted_iota(jnp.int32, (8, 128), 1) == lane).astype(BF)
    return mm_nt(pick, tail)[0:1]


def split_dot(dot, left, right, left_wide=True):
    whole = left if left_wide else right
    high = whole.astype(BF)
    low = (whole - high.astype(F32)).astype(BF)
    if left_wide:
        return dot(high, right) + dot(low, right)
    return dot(left, high) + dot(left, low)


def inverse_rms(rows):
    return lax.rsqrt(jnp.mean(rows * rows, axis=1, keepdims=True) + epsilon)


def norm_back(rows, inverse, scaled):
    return inverse * scaled - rows * (inverse * inverse * inverse) * jnp.mean(
        rows * scaled, axis=1, keepdims=True
    )


def join(blocks, shape):
    return blocks.astype(F32).reshape(shape).astype(BF)


def ffn_block(j, rows, grads, in_ref, out_ref, hidden_ref, dm_ref, result, back, units, step):
    low = pl.multiple_of(j * step, step) if not isinstance(j, int) else j * step
    high = pl.multiple_of(units + low, step) if not isinstance(j, int) else units + low
    gate_at, up_at = pl.ds(low, step), pl.ds(high, step)
    gate, up = mm(rows, in_ref[:, gate_at]), mm(rows, in_ref[:, up_at])
    down = out_ref[gate_at, :]
    d_hidden = mm_nt(grads, down)
    share = 1.0 / (1.0 + jnp.exp(-gate))
    lit = gate * share
    hidden = (lit * up).astype(BF)
    d_gate = (d_hidden * up * (share * (1.0 + gate * (1.0 - share)))).astype(BF)
    d_up = (d_hidden * lit).astype(BF)
    hidden_ref[:, gate_at] = hidden
    dm_ref[:, gate_at] = d_gate
    dm_ref[:, up_at] = d_up
    result[...] += mm(hidden, down)
    back[...] += mm_nt(d_gate, in_ref[:, gate_at]) + mm_nt(d_up, in_ref[:, up_at])


def box_rows(kept_rows, boxes, shift):
    shape = (boxes * kept_rows, boxes * BOX)
    row = lax.broadcasted_iota(jnp.int32, shape, 0)
    column = lax.broadcasted_iota(jnp.int32, shape, 1)
    box = jnp.floor((column.astype(F32) + 0.5) * (1.0 / BOX)).astype(jnp.int32)
    at = column - box * BOX - shift
    return ((at >= 0) & (at < kept_rows) & (row == box * kept_rows + at)).astype(BF)


def block_kernel(
    nc, nz,
    len_ref, hid_ref, go_ref, ids_ref, rank_ref, wqkv_ref, router_ref, ga_ref, gf_ref, gu_ref,
    wo_ref, sd_ref, win_ref, wout_ref,
    out_ref, gin_ref, fq_ref, fgu_ref, fsd_ref, fwo_ref, ein_ref, eout_ref,
    turn_ref, meta_own, meta_all, picks, hot_x, hot_d, dg_send, dg_in, hid_all, up_own, up_all, wq_own, wq_st, wq_buf, w_ref, gu_st, gu_buf, gu_all, wo_st, wo_buf,
    wo_all, sd_all, wie, woe, normed_ref, qkv_ref, ctx_all, att_own, nt_all,
    sb, ar, xs, ds, acc_a, acc_b, sh_own, sh_hidden, sh_dm, sh_send, sh_in, sh_mid, sh_end,
    ex_hidden, ex_dm, pin, fb, rb, gsd, da_own, dctx_send, dctx_all, part, part_own, rs_in, rs_mid, rs_end,
    sib_gu, zi_gu, pb_gu, sib_q, zi_q, pb_q, sib_sd, zi_sd, sib_wo, zi_wo, pb_wo, in_wo,
    send, recv, lsem,
):
    c, z, f = place()
    near_x, near_y = c + 1 - 2 * wrap(c, 2), wrap(c + 2, nc)
    far = wrap(near_x + 2, nc)
    to_x, to_y = (near_x, z, f), (near_y, z, f)
    in_plane = [(wrap(c + s, nc), z, f) for s in range(1, nc)]
    in_column = [(c, wrap(z + s, nz), f) for s in range(1, nz)]
    steps_up = list(range(1, nz))
    sibling = (c, z, 1 - f)
    across = [(wrap(c + s, nc), z, 1 - f) for s in range(1, nc)]
    partners = in_plane + in_column + [sibling] + across
    with jax.named_scope("s_greet"):
        greet(partners)

    num_seqs, shard_len, width = hid_ref.shape
    full_len = nc * shard_len
    half_len = shard_len // 2
    tok = num_seqs * shard_len
    rows_w = wqkv_ref.shape[0]
    head_width = wqkv_ref.shape[1] // 3 // nc
    heads_here = head_width // HS
    wide_cols = wq_own.shape[2]
    units = gu_ref.shape[1] // 2
    own_units = units // nc
    down_rows = sd_ref.shape[0]
    num_experts = nz * nc
    num_slots = num_experts * CAP
    column_slots = nz * BOX
    block_rows = nz * 2 * rows_w
    mail = Courier(send, recv, sibling)

    small = jnp.concatenate(
        [
            router_ref[...].astype(F32),
            ga_ref[...].astype(F32),
            gf_ref[...].astype(F32),
            jnp.zeros((128 - num_experts - 2, rows_w), F32),
        ],
        axis=0,
    )
    small = jnp.concatenate([small, jnp.zeros((128, 128 - rows_w), F32)], axis=1)
    small = jnp.transpose(small, (1, 0))[:rows_w, :SMALL].astype(BF)
    for owner in range(nc):
        wq_own[owner] = jnp.concatenate(
            [
                wqkv_ref[:, side * width + owner * head_width : side * width + (owner + 1) * head_width]
                for side in range(3)
            ]
            + [small],
            axis=1,
        )
    meta_own[...] = jnp.concatenate(
        [
            jnp.concatenate(
                [ids_ref[q, e, k : k + 1, :] for q in range(num_seqs) for e in range(2)], axis=1
            )
            for k in range(2)
        ]
        + [rank_ref[...], jnp.zeros((5, tok), jnp.int32)],
        axis=0,
    )
    with jax.named_scope("s_met"):
        met(partners)

    others = pl.ds(0, nc - 1)
    staged_wq = mail.post(
        wq_st.at[others],
        [(wq_own.at[wrap(c + s, nc)], wq_st.at[c], in_plane[s - 1]) for s in range(1, nc)],
    )
    arriving = [
        mail.post(
            hid_all.at[q, pl.ds(0, 2)],
            [(hid_ref.at[q], hid_all.at[q, c], peer) for peer in (to_x, to_y)],
        )
        for q in range(num_seqs)
    ]
    meta_copies = mail.post(
        meta_all.at[others], [(meta_own, meta_all.at[c], peer) for peer in in_plane]
    )
    staged_wo = mail.post(wo_st.at[others], [(wo_ref, wo_st.at[c], peer) for peer in in_plane])
    staged_gu = mail.open(gu_st.at[others])
    for s in range(1, nc):
        owner = wrap(c + s, nc)
        for side in range(2):
            at = pl.ds(pl.multiple_of(side * units + owner * own_units, own_units), own_units)
            staged_gu.add(
                gu_ref.at[:, at],
                gu_st.at[c, :, pl.ds(side * own_units, own_units)],
                in_plane[s - 1],
            )

    block = 2 * c + f
    shard_rows = win_ref.shape[1]
    half_units = units // 2
    step = 256
    steps = half_units // step
    lands = pl.ds(pl.multiple_of(block * shard_rows, shard_rows), shard_rows)
    out_rows = wout_ref.shape[1]
    to_core = block // nc
    slot = wrap(block, nc)
    out_lands = pl.ds(pl.multiple_of(slot * out_rows, out_rows), out_rows)
    remote_rows = (2 * nc - 1) * shard_rows
    first_in = mail.count
    expert_in = [
        mail.open(wie.at[pl.ds(0, remote_rows), pl.ds(0, 2 * step)]) for _ in range(steps)
    ]
    expert_out = mail.open(woe, keep=False)
    remote_out = woe.at[pl.ds(0, (nc - 1) * out_rows)]
    own_out = pltpu.make_async_copy(wout_ref.at[c], woe.at[out_lands], lsem.at[0])

    def send_out(s):
        owner = wrap(c + s, nc)
        expert_out.add(wout_ref.at[owner], woe.at[out_lands], (owner, z, to_core))

    def send_out_own():
        @pl.when(to_core == f)
        def _():
            own_out.start()

        @pl.when(to_core != f)
        def _():
            expert_out.add(wout_ref.at[c], woe.at[out_lands], sibling)

    def own_in(j):
        like = wie.at[pl.ds(0, shard_rows), pl.ds(0, 2 * step)]
        return pltpu.make_async_copy(like, like, lsem.at[1 + j])

    def nth_block(j, chip):
        return wrap(2 * j + j // 2 + 2 * wrap(chip, 2), steps)

    def send_in(j, s, g, side):
        owner = wrap(c + s, nc)
        at = nth_block(j, owner) * step
        core = f if g == 0 else 1 - f
        from_lane = pl.multiple_of(side * units + core * half_units + at, step)
        src = win_ref.at[owner, :, pl.ds(from_lane, step)]
        dst = wie.at[lands, pl.ds(pl.multiple_of(side * half_units + at, step), step)]
        if s == 0 and g == 0:
            pltpu.make_async_copy(src, dst, lsem.at[1 + j]).start()
        else:
            expert_in[j].add(src, dst, (owner, z, core))

    bulk = [functools.partial(send_out, s) for s in range(1, nc)] + [send_out_own]
    for j in range(steps):
        for s in range(1, nc + 1):
            for g in range(2):
                for side in range(2):
                    bulk.append(functools.partial(send_in, j, s % nc, g, side))

    def pump(queue, count):
        for _ in range(min(count, len(queue))):
            queue.pop(0)()

    with jax.named_scope("s_turns"):
        row = lax.broadcasted_iota(jnp.int32, (full_len, 128), 0)
        lane = lax.broadcasted_iota(jnp.int32, (full_len, 128), 1) & (HS // 2 - 1)
        frequency = jnp.exp(lane.astype(F32) * (-2.0 * math.log(10000.0) / HS))
        angles = position_of(row, half_len, full_len).astype(F32) * frequency
        turn_ref[:, :128] = jnp.cos(angles)
        turn_ref[:, 128:] = jnp.sin(angles)
    lane = lax.broadcasted_iota(jnp.int32, (tok, 128), 1).astype(F32)

    def live_rows(chip):
        row_at = lax.broadcasted_iota(jnp.int32, (tok, 1), 0)
        inside = row_at & (shard_len - 1)
        low = chip * half_len + (inside & (half_len - 1))
        places = jnp.where(inside >= half_len, full_len - 1 - low, low)
        lengths = jnp.zeros((tok, 1), jnp.int32)
        for q in range(num_seqs):
            lengths = jnp.where(row_at // shard_len == q, len_ref[q], lengths)
        return (places < lengths).astype(F32)

    def turned(rows):
        return jnp.transpose(
            jnp.concatenate([rows, jnp.zeros((128 - rows.shape[0], tok), F32)], axis=0), (1, 0)
        )

    def hot_lanes(columns):
        return [(lane == SMALL + columns[:, k : k + 1]).astype(F32) for k in range(2)]

    def gates_of(hots, logits):
        chosen = [jnp.sum(hot * logits, axis=1, keepdims=True) for hot in hots]
        top = jnp.maximum(chosen[0], chosen[1])
        raised = [jnp.exp(value - top) for value in chosen]
        return [value / (raised[0] + raised[1]) for value in raised]

    def route(chip):
        rows = meta_all[chip].astype(F32)
        columns = turned(rows)
        picks[chip] = columns
        hots = hot_lanes(columns)
        rank_row = jnp.broadcast_to(rows[2:3], (tok, tok))
        earlier = (rank_row < columns[:, 2:3]).astype(BF)
        live = live_rows(chip)
        position = mm(earlier, ((hots[0] + hots[1]) * live).astype(BF))
        slot_lane = lax.broadcasted_iota(jnp.int32, (tok, column_slots), 1).astype(F32)
        for k in range(2):
            at = jnp.sum(hots[k] * position, axis=1, keepdims=True)
            plane = jnp.floor((columns[:, k : k + 1] + 0.5) * (1.0 / nc))
            here = columns[:, k : k + 1] - plane * nc == c.astype(F32)
            slot_at = jnp.where((live > 0) & (at < CAP) & here, plane * BOX + at, -BOX)
            hot_x[chip, k] = (slot_lane == slot_at).astype(BF)
            hot_d[chip, k] = (slot_lane == slot_at + CAP).astype(BF)

    live = live_rows(c)
    upstream = go_ref[...].reshape(tok, width).astype(F32) * live
    up_b = upstream.astype(BF)
    up_own[...] = up_b.reshape(num_seqs, shard_len, width)
    for q in range(num_seqs):
        hid_all[q, c] = hid_ref[q]
        up_all[q, c] = up_own[q]

    def pass_on(post, buffer, q, at):
        post.wait_recv()
        origin, peer = (near_x, to_y) if q == 0 else (near_y, to_x)
        block_at = at(buffer, q, origin)
        return mail.post(block_at, [(block_at, block_at, peer)])

    def by_seq(buffer, q, chip):
        return buffer.at[q, chip]

    def by_chip(buffer, q, chip):
        return buffer.at[chip, q]

    sd_all[z, f] = sd_ref[...]
    planes = pl.ds(0, nz - 1)

    def spread(stage, staged, buffer):
        staged.wait_recv()
        post = mail.post(
            buffer.at[:, planes, 0],
            [(stage, buffer.at[:, z, f], peer) for peer in in_column],
        )
        for i in range(nc):
            buffer[i, z, f] = stage[i]
        return post

    def spread_gate_up(side):
        at = pl.ds(side * own_units, own_units)
        return mail.post(
            gu_buf.at[:, planes, 0, :, at],
            [(gu_st.at[:, :, at], gu_buf.at[:, z, f, :, at], peer) for peer in in_column],
        )

    def forward(posts, buffer):
        for post in posts:
            post.wait_recv()
        both = buffer.at[:, :, f]
        return mail.post(both, [(both, both, sibling)])

    with jax.named_scope("a_stage_wq"):
        wq_st[c] = wq_own[c]
        spread_wq = spread(wq_st, staged_wq, wq_buf)
    with jax.named_scope("a_pass_hidden"):
        passing = [pass_on(arriving[q], hid_all, q, by_seq) for q in range(num_seqs)]
    up_copies = [
        mail.post(
            up_all.at[q, pl.ds(0, 2)],
            [(up_own.at[q], up_all.at[q, c], peer) for peer in (to_x, to_y)],
        )
        for q in range(num_seqs)
    ]
    pump(bulk, PUMPS[3])
    with jax.named_scope("a_route"):
        meta_copies.wait_recv()
        meta_all[c] = meta_own[...]

        def route_one(chip, carry):
            route(chip)
            return carry

        lax.fori_loop(0, nc, route_one, 0)
    wo_st[c] = wo_ref[...]
    for side in range(2):
        at = pl.ds(pl.multiple_of(side * units + c * own_units, own_units), own_units)
        gu_st[c, :, side * own_units : (side + 1) * own_units] = gu_ref[:, at]
    with jax.named_scope("a_forward_wq"):
        passed_wq = forward([spread_wq], wq_buf)
        passed_wq.wait_recv()
        for i in range(nc):
            w_ref[i * block_rows : (i + 1) * block_rows, :] = join(
                wq_buf[i], (block_rows, wide_cols)
            )

    cosines = wide(turn_ref[:, :128], 2 * head_width // 128)
    sines = wide(turn_ref[:, 128:], 2 * head_width // 128)
    tail_at = wide_cols - 128
    attn_gain = column_row(w_ref[:, tail_at:], SMALL + num_experts)
    ctx_copies = []
    for q in range(num_seqs):
        with jax.named_scope("a_wait_hidden"):
            passing[q].wait_recv()
        with jax.named_scope("a_attention"):
            rows = hid_all[q].reshape(full_len, width).astype(F32)
            normed = (rows * inverse_rms(rows) * attn_gain).astype(BF)
            normed_ref[q] = normed
            merged = mm(normed, w_ref[:, : 3 * head_width])
            both = merged[:, : 2 * head_width]
            both = (both * cosines + swap_halves(both) * sines).astype(BF)
            values = merged[:, 2 * head_width :].astype(BF)
            qkv_ref[q, :, : 2 * head_width] = both
            qkv_ref[q, :, 2 * head_width :] = values
            allowed = allowed_keys(len_ref[q], half_len, full_len)
            heads = []
            for h in range(heads_here):
                probs = head_probs(
                    both[:, h * HS : (h + 1) * HS],
                    both[:, head_width + h * HS : head_width + (h + 1) * HS],
                    allowed,
                ).astype(BF)
                heads.append(mm(probs, values[:, h * HS : (h + 1) * HS]))
            context = jnp.concatenate(heads, axis=1).astype(BF)
            ctx_all[c, q] = context.reshape(nc, shard_len, head_width)
        ctx_copies.append(
            mail.post(
                ctx_all.at[pl.ds(0, 2), q],
                [(ctx_all.at[c, q], ctx_all.at[c, q], peer) for peer in (to_x, to_y)],
            )
        )
    spread_wo = spread(wo_st, staged_wo, wo_buf)
    with jax.named_scope("a_pass_upstream"):
        up_passing = [pass_on(up_copies[q], up_all, q, by_seq) for q in range(num_seqs)]
    with jax.named_scope("a_pass_context"):
        ctx_passing = [pass_on(ctx_copies[q], ctx_all, q, by_chip) for q in range(num_seqs)]
    pump(bulk, PUMPS[0])
    with jax.named_scope("a_forward_wo"):
        passed_wo = forward([spread_wo], wo_buf)
        staged_gu.wait_recv()
        for i in range(nc):
            gu_buf[i, z, f] = gu_st[i]
        spread_gu = [spread_gate_up(0)]
        passed_wo.wait_recv()
        for i in range(nc):
            wo_all[i * block_rows : (i + 1) * block_rows, :] = join(
                wo_buf[i], (block_rows, width)
            )
    ffn_gain = column_row(w_ref[:, tail_at:], SMALL + num_experts + 1)
    for q in range(num_seqs):
        with jax.named_scope("a_wait_context"):
            ctx_passing[q].wait_recv()
        with jax.named_scope("a_project"):
            total = hid_all[q].reshape(full_len, width).astype(F32)
            for i in range(nc):
                total = total + mm(
                    ctx_all[i, q].reshape(full_len, head_width),
                    wo_all[i * head_width : (i + 1) * head_width, :],
                )
            acc_a[q * full_len : (q + 1) * full_len] = total
            nt_all[q] = (
                (total * inverse_rms(total) * ffn_gain).astype(BF).reshape(nc, shard_len, width)
            )
    by_block = acc_a.at[pl.ds(0, nc * tok)].reshape(num_seqs, nc, shard_len, width)
    for q in range(num_seqs):
        att_own[q] = by_block[q, c]

    with jax.named_scope("b_wait_upstream"):
        for post in up_passing:
            post.wait_recv()
    with jax.named_scope("b_dispatch"):
        tail = w_ref[:, tail_at:]

        def box_rows_of(chip, carry):
            normed = jnp.concatenate([nt_all[q, chip] for q in range(num_seqs)], axis=0)
            columns = picks[chip]
            gates = gates_of(hot_lanes(columns), mm(normed, tail))
            picks[chip] = jnp.where(lane == 3, gates[0], jnp.where(lane == 4, gates[1], columns))
            up_f = jnp.concatenate([up_all[q, chip] for q in range(num_seqs)], axis=0).astype(F32)
            boxes = mm_tn(hot_x[chip, 0] + hot_x[chip, 1], normed)
            for k in range(2):
                boxes = boxes + mm_tn(hot_d[chip, k], (gates[k] * up_f).astype(BF))
            boxes = boxes.reshape(nz, BOX, width).astype(BF)
            for plane in range(nz):
                sb[plane, chip] = boxes[plane]
            return carry

        lax.fori_loop(0, nc, box_rows_of, 0)
        row_copies = [
            mail.post(ar.at[f, 0], [(sb.at[to[1]], ar.at[f, z], to)]) for to in in_column
        ]
        ar[f, z] = sb[z]
        normed = jnp.concatenate([nt_all[q, c] for q in range(num_seqs)], axis=0)
    pump(bulk, len(bulk))

    with jax.named_scope("b_forward_rows"):
        forwards = mail.open(ar.at[f])
        forwards.add(ar.at[f, z], ar.at[f, z], sibling)
        for s in range(1, nz):
            row_copies[s - 1].wait_recv()
            origin = wrap(z + nz - s, nz)
            forwards.add(ar.at[f, origin], ar.at[f, origin], sibling)
        forwards.wait_recv()
        keep_x, keep_d = (box_rows(CAP, num_experts, shift) for shift in (0, CAP))
        for core in range(2):
            at = slice(core * num_slots, (core + 1) * num_slots)
            boxes = join(ar[core], (num_experts * BOX, width))
            xs[at] = mm(keep_x, boxes).astype(BF)
            ds[at] = mm(keep_d, boxes).astype(BF)
    with jax.named_scope("b_wait_down"):
        @pl.when(to_core == f)
        def _():
            expert_out.wait_recv(remote_out)
            own_out.wait()

        @pl.when(to_core != f)
        def _():
            expert_out.wait_recv()

    gwi, gwo = wie, woe

    def expert_grads(j):
        low = nth_block(j, c) * step
        for side in range(2):
            at = pl.ds(pl.multiple_of(side * half_units + low, step), step)
            gwi[:, at] = mm_tn(xs[...], ex_dm[:, at]).astype(BF)
        at = pl.ds(pl.multiple_of(low, step), step)
        gwo[at, :] = mm_tn(ex_hidden[:, at], ds[...]).astype(BF)

    def homeward(j):
        moves = [
            functools.partial(send_home_in, j, s % nc, g, side)
            for s in range(1, nc + 1)
            for g in range(2)
            for side in range(2)
        ]
        return moves + [functools.partial(send_home_out, j)]

    home = []
    home_in = mail.open(gwi.at[pl.ds(0, remote_rows)])
    home_out = mail.open(gwo, keep=False)
    remote_home = gwo.at[pl.ds(0, (nc - 1) * out_rows)]
    home_in_own = pltpu.make_async_copy(
        gwi.at[pl.ds(0, shard_rows)], gwi.at[pl.ds(0, shard_rows)], lsem.at[1]
    )

    def send_home_in(j, s, g, side):
        owner = wrap(c + s, nc)
        core = f if g == 0 else 1 - f
        from_rows = pl.ds(
            pl.multiple_of((2 * owner + core) * shard_rows, shard_rows), shard_rows
        )
        low = nth_block(j, c) * step
        to_lane = pl.multiple_of(side * units + f * half_units + low, step)
        src = gwi.at[from_rows, pl.ds(pl.multiple_of(side * half_units + low, step), step)]
        dst = ein_ref.at[c, :, pl.ds(to_lane, step)]
        if s == 0 and g == 0:
            pltpu.make_async_copy(src, dst, lsem.at[1]).start()
        else:
            home_in.add(src, dst, (owner, z, core))

    def home_rows(j):
        return gwo.at[pl.ds(pl.multiple_of(nth_block(j, c) * out_rows, out_rows), out_rows)]

    def home_out_own(j):
        return pltpu.make_async_copy(home_rows(j), eout_ref.at[c], lsem.at[0])

    def send_home_out(j):
        to_block = f * nc + nth_block(j, c)

        @pl.when(to_block == block)
        def _():
            home_out_own(j).start()

        @pl.when(to_block != block)
        def _():
            home_out.add(
                home_rows(j),
                eout_ref.at[c],
                (to_block // 2, z, wrap(to_block, 2)),
            )

    acc_a[...] = jnp.zeros(acc_a.shape, F32)
    acc_b[...] = jnp.zeros(acc_b.shape, F32)
    early = [move for j in range(EARLY) for move in homeward(j)]
    home = [move for j in range(EARLY, steps) for move in homeward(j)]
    late_gate_up = mail.open(gu_buf.at[:, planes, 0, :, pl.ds(0, own_units)])
    spread_sd = mail.open(sd_all.at[planes, 0])
    spread_gu.append(late_gate_up)

    def expert_block(j, carry):
        with jax.named_scope("b_wait_experts"):
            own_in(j).wait()
            mail.at(first_in + j, expert_in[0].like).wait_recv()

        @pl.when(j == steps - 1)
        def _():
            pump(early, len(early))

        with jax.named_scope("b_experts"):
            ffn_block(
                nth_block(j, c), xs[...], ds[...], wie, woe, ex_hidden, ex_dm, acc_a, acc_b,
                half_units, step,
            )

        @pl.when(j < EARLY)
        def _():
            with jax.named_scope("b_early_grads"):
                expert_grads(j)

        @pl.when(j == LATE)
        def _():
            at = pl.ds(own_units, own_units)
            for peer in in_column:
                late_gate_up.add(gu_st.at[:, :, at], gu_buf.at[:, z, f, :, at], peer)
                spread_sd.add(sd_ref, sd_all.at[z, f], peer)

        return carry

    lax.fori_loop(0, steps, expert_block, 0)
    mail.settle(row_copies)
    pr = sb
    with jax.named_scope("b_sibling_sum"):

        def boxed(core):
            at = pl.ds(pl.multiple_of(core * num_slots, num_slots), num_slots)
            return (
                mm_tn(keep_x, acc_a[at].astype(BF)) + mm_tn(keep_d, acc_b[at].astype(BF))
            ).reshape(nz, nc, BOX, width)

        pr[...] = boxed(1 - f).astype(BF)
        swap = mail.post(pin, [(pr, pin, sibling)])
        ours = boxed(f)
        swap.wait_recv()
        fb[...] = (ours + pin[...].astype(F32)).astype(BF)
        returns = mail.post(
            rb.at[planes], [(fb.at[to[1]], rb.at[z], to) for to in in_column]
        )
        rb[z] = fb[z]
    with jax.named_scope("b_expert_grads"):

        def late_grads(j, carry):
            expert_grads(j)
            return carry

        lax.fori_loop(EARLY, steps, late_grads, 0)
    pump(home, PUMPS[1])

    with jax.named_scope("b_forward_gu"):
        passed_gu = forward(spread_gu, gu_buf)
        spread_sd.wait_recv()
        passed_sd = mail.post(sd_all.at[:, f], [(sd_all.at[:, f], sd_all.at[:, f], sibling)])
        passed_gu.wait_recv()
        passed_sd.wait_recv()
        for i in range(nc):
            gu_all[i * block_rows : (i + 1) * block_rows, :] = join(
                gu_buf[i], (block_rows, 2 * own_units)
            )
    plane_tok = nc * tok
    shared_rows = nt_all.reshape(plane_tok, width)
    shared_grads = up_all.reshape(plane_tok, width)
    shared_down = sd_all.reshape(own_units, width)
    with jax.named_scope("b_shared"):
        first = pl.ds(0, plane_tok)
        acc_a[...] = jnp.zeros(acc_a.shape, F32)
        acc_b[...] = jnp.zeros(acc_b.shape, F32)

        def shared_block(j, carry):
            ffn_block(
                j, shared_rows[...], shared_grads[...], gu_all, shared_down, sh_hidden, sh_dm,
                acc_a.at[first], acc_b.at[first], own_units, 256,
            )
            return carry

        lax.fori_loop(0, own_units // 256, shared_block, 0)
    mail.settle(spread_gu + [passed_gu])
    ggu = gu_buf
    with jax.named_scope("b_shared_grads"):

        def gate_up_grads(j, carry):
            at = pl.ds(pl.multiple_of(j * 256, 256), 256)
            piece = mm_tn(shared_rows[...], sh_dm[:, at])
            ggu[:, :, :, :, at] = piece.reshape(ggu.shape[:4] + (256,)).astype(BF)
            return carry

        lax.fori_loop(0, 2 * own_units // 256, gate_up_grads, 0)
        gsd[...] = mm_tn(sh_hidden[...], shared_grads[...]).reshape(gsd.shape).astype(BF)
        sibling_gu = mail.post(sib_gu, [(ggu.at[:, :, 1 - f], sib_gu, sibling)])
        sibling_sd = mail.post(sib_sd, [(gsd.at[:, 1 - f], sib_sd, sibling)])

    with jax.named_scope("c_wait_returns"):
        returns.wait_recv()
    with jax.named_scope("c_column_mixture"):
        cuts = [
            acc.at[first].reshape(num_seqs, nc, shard_len, width) for acc in (acc_a, acc_b)
        ]

        def add_results(chip, carry):
            results = join(
                jnp.concatenate([rb[plane, chip].astype(F32) for plane in range(nz)], axis=0),
                (column_slots, width),
            )
            up_f = jnp.concatenate([up_all[q, chip] for q in range(num_seqs)], axis=0).astype(F32)
            gates = [picks[chip][:, 3 + k : 4 + k] for k in range(2)]
            routed = [mm(hot_x[chip, k], results) for k in range(2)]
            mixture = gates[0] * routed[0] + gates[1] * routed[1]
            d_rows = mm(hot_d[chip, 0] + hot_d[chip, 1], results)
            for q in range(num_seqs):
                at = slice(q * shard_len, (q + 1) * shard_len)
                cuts[0][q, chip] = cuts[0][q, chip] + mixture[at]
                cuts[1][q, chip] = cuts[1][q, chip] + d_rows[at]
            d_gates = [jnp.sum(routed[k] * up_f, axis=1, keepdims=True) for k in range(2)]
            spread_out = jnp.where(lane == 0, d_gates[0], jnp.where(lane == 1, d_gates[1], 0.0))
            dg_send[chip] = jnp.transpose(spread_out, (1, 0))[:8]
            return carry

        lax.fori_loop(0, nc, add_results, 0)
        for k in range(2):
            for q in range(num_seqs):
                sh_own[k, q, 0] = cuts[k][q, c]
                sh_own[k, q, 1] = cuts[k][q, near_y if q == 0 else near_x]
            sh_send[k] = cuts[k][...].astype(BF)

    def first_leg(inbox, box, lead):
        post = mail.open(inbox)
        for q in range(num_seqs):
            peer = to_x if q == 0 else to_y
            for at, chip in enumerate((near_x if q == 0 else near_y, far)):
                post.add(box.at[lead + (q, chip)], inbox.at[lead + (q, at)], peer)
        return post

    shared_first = first_leg(sh_in, sh_send, (slice(None),))
    dg_copies = mail.post(
        dg_in.at[others],
        [(dg_send.at[wrap(c + s, nc)], dg_in.at[c], in_plane[s - 1]) for s in range(1, nc)],
    )
    dg_in[c] = dg_send[c]
    pump(home, PUMPS[4])

    with jax.named_scope("b_reduce_shared"):
        def two_cores(copy, own, inbox):
            copy.wait_recv()
            inbox[...] = (own.astype(F32) + inbox[...].astype(F32)).astype(BF)

        def four_planes(copy, buffer, inbox):
            copy.wait_recv()
            for i in range(nc):
                inbox[i] = (buffer[i, :, f].astype(F32) + inbox[i].astype(F32)).astype(BF)

        four_planes(sibling_gu, ggu, sib_gu)
        two_cores(sibling_sd, gsd[:, f], sib_sd)
        gu_copies = mail.post(
            zi_gu,
            [
                (sib_gu.at[:, to[1]], zi_gu.at[up - 1], to)
                for to, up in zip(in_column, steps_up)
            ],
        )
        sd_copies = mail.post(
            zi_sd,
            [(sib_sd.at[to[1]], zi_sd.at[up - 1], to) for to, up in zip(in_column, steps_up)],
        )

    with jax.named_scope("c_second_sum"):
        shared_first.wait_recv()
        for k in range(2):
            for q in range(num_seqs):
                sh_mid[k, q] = (sh_own[k, q, 1] + sh_in[k, q, 1].astype(F32)).astype(BF)
        shared_second = mail.post(
            sh_end,
            [
                (sh_mid.at[:, q], sh_end.at[:, q], to_y if q == 0 else to_x)
                for q in range(num_seqs)
            ],
        )

    pump(home, PUMPS[5])
    with jax.named_scope("c_wait_shared"):
        dg_copies.wait_recv()
        shared_second.wait_recv()
        added, d_normed = [
            jnp.concatenate(
                [
                    sh_own[k, q, 0] + sh_in[k, q, 0].astype(F32) + sh_end[k, q].astype(F32)
                    for q in range(num_seqs)
                ],
                axis=0,
            )
            for k in range(2)
        ]
    with jax.named_scope("c_combine"):
        attended = att_own[...].reshape(tok, width)
        inverse = inverse_rms(attended)
        out_ref[...] = (live * (attended + added)).astype(BF).reshape(out_ref.shape)
        hots = hot_lanes(picks[c])
        own_gates = gates_of(hots, mm(normed, tail))
        summed = turned(jnp.sum(dg_in[...], axis=0))
        d_gates = [summed[:, k : k + 1] for k in range(2)]
        mean_gate = own_gates[0] * d_gates[0] + own_gates[1] * d_gates[1]
        d_logits = hots[0] * (own_gates[0] * (d_gates[0] - mean_gate)) + hots[1] * (
            own_gates[1] * (d_gates[1] - mean_gate)
        )
        d_normed = d_normed + split_dot(mm_nt, d_logits, tail)
        d_attended = upstream + norm_back(attended, inverse, d_normed * ffn_gain)
        d_att_b = d_attended.astype(BF)
        d_context = mm_nt(d_att_b, wo_all[...]).astype(BF)
        for i in range(nc):
            dctx_send[i] = d_context[:, i * head_width : (i + 1) * head_width].reshape(
                num_seqs, shard_len, head_width
            )
        for q in range(num_seqs):
            dctx_all[q, c] = dctx_send[c, q]
        dctx_copies = mail.post(
            dctx_all.at[:, others],
            [
                (dctx_send.at[wrap(c + s, nc)], dctx_all.at[:, c], in_plane[s - 1])
                for s in range(1, nc)
            ],
        )
        gin_ref[...] = d_attended.reshape(gin_ref.shape)
    pump(home, PUMPS[2])

    mail.settle([spread_wo, passed_wo])
    gwo_at = wo_buf
    with jax.named_scope("c_reduce"):
        for i in range(nc):
            mine = jnp.concatenate([ctx_all[i, q, c] for q in range(num_seqs)], axis=0)
            gwo_at[i] = mm_tn(mine, d_att_b).reshape(gwo_at.shape[1:]).astype(BF)
        sibling_wo = mail.post(sib_wo, [(gwo_at.at[:, :, 1 - f], sib_wo, sibling)])
        d_router = split_dot(mm_tn, normed, d_logits, left_wide=False)
        d_gain = jnp.sum(d_normed * attended * inverse, axis=0, keepdims=True)
        turned = jnp.transpose(jnp.broadcast_to(d_gain, (128, width)), (1, 0))
        extra_lane = lax.broadcasted_iota(jnp.int32, (width, 128), 1)
        extras = jnp.where(extra_lane == SMALL + num_experts + 1, turned, d_router)
        four_planes(sibling_wo, gwo_at, sib_wo)
        wo_copies = mail.post(
            zi_wo,
            [
                (sib_wo.at[:, wrap(z + s, nz)], zi_wo.at[s - 1], in_column[s - 1])
                for s in range(1, nz)
            ],
        )

    with jax.named_scope("c_wait_dctx"):
        dctx_copies.wait_recv()
    grad_qkv = jnp.zeros((width, 3 * head_width), F32)
    rs_first = mail.open(rs_in)
    for q in range(num_seqs):
        with jax.named_scope("c_attention"):
            d_context = dctx_all[q].reshape(full_len, head_width)
            allowed = allowed_keys(len_ref[q], half_len, full_len)
            merged = qkv_ref[q]
            d_query, d_key, d_value = [], [], []
            for h in range(heads_here):
                query = merged[:, h * HS : (h + 1) * HS]
                key = merged[:, head_width + h * HS : head_width + (h + 1) * HS]
                value = merged[:, 2 * head_width + h * HS : 2 * head_width + (h + 1) * HS]
                d_head = d_context[:, h * HS : (h + 1) * HS]
                probs = head_probs(query, key, allowed)
                d_probs = mm_nt(d_head, value)
                delta = jnp.sum(probs * d_probs, axis=1, keepdims=True)
                d_scores = (probs * (d_probs - delta)).astype(BF)
                d_query.append(mm(d_scores, key) * (HS**-0.5))
                d_key.append(mm_tn(d_scores, query) * (HS**-0.5))
                d_value.append(mm_tn(probs.astype(BF), d_head))
            both = jnp.concatenate(d_query + d_key, axis=1)
            both = both * cosines - swap_halves(both) * sines
            d_merged = jnp.concatenate([both] + d_value, axis=1).astype(BF)
            product = mm_nt(d_merged, w_ref[:, : 3 * head_width]).reshape(nc, shard_len, width)
            part_own[q] = product
            part[q] = product.astype(BF)
            for at, chip in enumerate((near_x if q == 0 else near_y, far)):
                rs_first.add(part.at[q, chip], rs_in.at[q, at], to_x if q == 0 else to_y)
            grad_qkv = grad_qkv + mm_tn(normed_ref[q], d_merged)
    pump(home, len(home))
    mail.settle([spread_wq, passed_wq])
    gq = wq_buf
    with jax.named_scope("c_reduce_q"):
        last = jnp.concatenate([grad_qkv[:, tail_at:], extras[:, 3 * head_width - tail_at :]], axis=1)
        gq[...] = (
            jnp.concatenate([grad_qkv[:, :tail_at], last], axis=1).reshape(gq.shape).astype(BF)
        )
        sibling_q = mail.post(sib_q, [(gq.at[:, :, 1 - f], sib_q, sibling)])
        four_planes(sibling_q, gq, sib_q)
        q_copies = mail.post(
            zi_q,
            [
                (sib_q.at[:, to[1]], zi_q.at[up - 1], to)
                for to, up in zip(in_column, steps_up)
            ],
        )
    with jax.named_scope("c_second_leg"):
        rs_first.wait_recv()
        for q in range(num_seqs):
            relay = part_own[q, near_y if q == 0 else near_x]
            rs_mid[q] = (relay + rs_in[q, 1].astype(F32)).astype(BF)
        rs_second = mail.post(
            rs_end,
            [(rs_mid.at[q], rs_end.at[q], to_y if q == 0 else to_x) for q in range(num_seqs)],
        )

    def column_sum(own, copies, inbox):
        copies.wait_recv()
        total = own.astype(F32)
        for s in range(1, nz):
            total = total + inbox[s - 1].astype(F32)
        return total

    def hand_out(box, final):
        final[c] = box[c]
        return mail.post(
            final.at[others],
            [(box.at[wrap(c + s, nc)], final.at[c], in_plane[s - 1]) for s in range(1, nc)],
        )

    with jax.named_scope("c_column_gu"):
        pb_gu[...] = column_sum(sib_gu[:, z], gu_copies, zi_gu).astype(BF)
        final_gu = hand_out(pb_gu, fgu_ref)
    with jax.named_scope("c_column_sd"):
        fsd_ref[...] = column_sum(sib_sd[z], sd_copies, zi_sd)
    with jax.named_scope("c_column_wo"):
        pb_wo[...] = column_sum(sib_wo[:, z], wo_copies, zi_wo).astype(BF)
        final_wo = hand_out(pb_wo, in_wo)
    with jax.named_scope("c_column_q"):
        pb_q[...] = column_sum(sib_q[:, z], q_copies, zi_q).astype(BF)
        final_q = hand_out(pb_q, fq_ref)
    with jax.named_scope("c_grad_in"):
        rs_second.wait_recv()
        for q in range(num_seqs):
            d_normed = part_own[q, c] + rs_in[q, 0].astype(F32) + rs_end[q].astype(F32)
            rows = hid_ref[q].astype(F32)
            gin_ref[q] = gin_ref[q] + norm_back(rows, inverse_rms(rows), d_normed * attn_gain)
    with jax.named_scope("c_final"):
        final_wo.wait_recv()
        fwo_ref[...] = jnp.sum(in_wo[...].astype(F32), axis=0)
        final_gu.wait_recv()
        final_q.wait_recv()
    with jax.named_scope("c_wait_home"):
        home_in_own.wait()
        home_in.wait_recv()

        @pl.when(to_core == f)
        def _():
            home_out_own(0).wait()
            home_out.wait_recv(remote_home)
            home_out.wait_send(remote_home)
            expert_out.wait_send(remote_out)

        @pl.when(to_core != f)
        def _():
            home_out.wait_recv()
            home_out.wait_send()
            expert_out.wait_send()

    assert mail.count <= POSTS, mail.count
    with jax.named_scope("z_finish"):
        mail.finish()


def finish_kernel(
    nc, fq_ref, fgu_ref, wqkv_ref, ga_ref, ein_ref, eout_ref, out_in, gin_in, fsd_in, fwo_in,
    gq_ref, gr_ref, gga_ref, ggf_ref, ggu_ref, oin_ref, oout_ref, out_ref, gin_ref, fsd_ref, fwo_ref,
    narrow_in, narrow_out, wide_in, wide_out, sems,
):
    pieces = []
    for e in range(ein_ref.shape[0]):
        for source, narrow, widened, target in (
            (ein_ref, narrow_in, wide_in, oin_ref),
            (eout_ref, narrow_out, wide_out, oout_ref),
        ):
            rows = source.shape[1] // WIDEN
            for k in range(WIDEN):
                at = (e, pl.ds(k * rows, rows))
                pieces.append((at, source, narrow, widened, target))
    arriving = []
    for i, (at, source, narrow, _, _) in enumerate(pieces):
        arriving.append(pltpu.make_async_copy(source.at[at], narrow.at[at], sems.at[0, i]))
        arriving[-1].start()
    out_ref[...] = out_in[...]
    gin_ref[...] = gin_in[...]
    fsd_ref[...] = fsd_in[...]
    fwo_ref[...] = fwo_in[...]
    rows_w = wqkv_ref.shape[0]
    head_width = wqkv_ref.shape[1] // 3 // nc
    grads = jnp.concatenate(
        [
            fq_ref[i, :, side * head_width : (side + 1) * head_width].astype(F32)
            for side in range(3)
            for i in range(nc)
        ],
        axis=1,
    )
    gq_ref[...] = grads
    own_units = fgu_ref.shape[2] // 2
    ggu_ref[...] = jnp.concatenate(
        [
            fgu_ref[i, :, side * own_units : (side + 1) * own_units].astype(F32)
            for side in range(2)
            for i in range(nc)
        ],
        axis=1,
    )
    extras = jnp.sum(fq_ref[:, :, 3 * head_width - SMALL :].astype(F32), axis=0)
    num_experts = gr_ref.shape[0]
    first = jnp.sum(wqkv_ref[...].astype(F32) * grads, axis=1, keepdims=True)
    lane = lax.broadcasted_iota(jnp.int32, (rows_w, 128), 1)
    both = jnp.where(lane == SMALL + num_experts, first, extras)
    turned = jnp.transpose(
        jnp.concatenate([both, jnp.zeros((128 - rows_w, 128), F32)], axis=0), (1, 0)
    )
    gr_ref[...] = turned[SMALL : SMALL + num_experts, :rows_w]
    at = SMALL + num_experts
    gga_ref[...] = turned[at : at + 1, :rows_w] / ga_ref[...].astype(F32)
    ggf_ref[...] = turned[at + 1 : at + 2, :rows_w]

    leaving = []
    for i, (at, _, narrow, widened, target) in enumerate(pieces):
        arriving[i].wait()
        widened[at] = narrow[at].astype(F32)
        leaving.append(pltpu.make_async_copy(widened.at[at], target.at[at], sems.at[1, i]))
        leaving[-1].start()
    for copy in leaving:
        copy.wait()


def vmem(*shape, dtype=jnp.bfloat16):
    return pltpu.VMEM(shape, dtype)


def fast_device(
    hidden_in, seq_lengths, expert_ids, route_rank, gain_attn, w_qkv, w_out, w_router, gain_ffn,
    w_gate_up, w_shared_down, w_experts_in, w_experts_out, grad_output,
):
    nc, nz = lax.axis_size("ctx"), lax.axis_size("exp")
    num_seqs, two_ends, half_len, width = hidden_in.shape
    shard_len = 2 * half_len
    full_len = nc * shard_len
    tok = num_seqs * shard_len
    rows_w = w_qkv.shape[0]
    head_width = w_qkv.shape[1] // 3 // nc
    num_experts = w_router.shape[1]
    down_rows = w_shared_down.shape[0]
    own_units = w_gate_up.shape[1] // 2 // nc
    half_units = w_experts_in.shape[2] // 4
    hbm, vm, sm = pl.ANY, pltpu.VMEM, pltpu.SMEM
    dma = pltpu.SemaphoreType.DMA

    seq_shape = (num_seqs, shard_len, width)
    group_shape = (num_seqs, nc, shard_len, width)
    blocks = (nc, nz, 2, rows_w)
    half_blocks = (nc, nz, rows_w)
    wide_cols = 3 * head_width + SMALL
    num_slots = num_experts * CAP
    row_box = (nz, nc, BOX, width)
    plane_tok = nc * tok
    outs = [
        (seq_shape, BF),
        (seq_shape, F32),
        ((nc, rows_w, wide_cols), BF),
        ((nc, rows_w, 2 * own_units), BF),
        ((down_rows, width), F32),
        ((rows_w, width), F32),
        (w_experts_in.shape, BF),
        (w_experts_out.shape, BF),
    ]
    out, gin, fq, fgu, fsd, fwo, ein, eout = pl.pallas_call(
        functools.partial(block_kernel, nc, nz),
        out_shape=[jax.ShapeDtypeStruct(shape, dtype) for shape, dtype in outs],
        in_specs=[
            pl.BlockSpec(memory_space=space) for space in [sm] + [vm] * 11 + [hbm, hbm]
        ],
        out_specs=[pl.BlockSpec(memory_space=space) for space in [vm] * 6 + [hbm, hbm]],
        scratch_shapes=[
            vmem(full_len, 256, dtype=F32),
            vmem(8, tok, dtype=jnp.int32),
            vmem(nc, 8, tok, dtype=jnp.int32),
            vmem(nc, tok, 128, dtype=F32),
            vmem(nc, 2, tok, nz * BOX),
            vmem(nc, 2, tok, nz * BOX),
            vmem(nc, 8, tok, dtype=F32),
            vmem(nc, 8, tok, dtype=F32),
            vmem(*group_shape),
            vmem(*seq_shape),
            vmem(*group_shape),
            vmem(nc, rows_w, wide_cols),
            vmem(nc, rows_w, wide_cols),
            vmem(*blocks, wide_cols),
            vmem(width, wide_cols),
            vmem(nc, rows_w, 2 * own_units),
            vmem(*blocks, 2 * own_units),
            vmem(width, 2 * own_units),
            vmem(nc, rows_w, width),
            vmem(*blocks, width),
            vmem(width, width),
            vmem(nz, 2, down_rows, width),
            vmem(width, 2 * half_units),
            vmem(half_units, width),
            vmem(num_seqs, full_len, width),
            vmem(num_seqs, full_len, 3 * head_width),
            vmem(nc, num_seqs, nc, shard_len, head_width),
            vmem(*seq_shape, dtype=F32),
            vmem(*group_shape),
            vmem(*row_box),
            vmem(2, nz, nc, BOX, width),
            vmem(2 * num_slots, width),
            vmem(2 * num_slots, width),
            vmem(2 * num_slots, width, dtype=F32),
            vmem(2 * num_slots, width, dtype=F32),
            vmem(2, num_seqs, 2, shard_len, width, dtype=F32),
            vmem(plane_tok, own_units),
            vmem(plane_tok, 2 * own_units),
            vmem(2, *group_shape),
            vmem(2, num_seqs, 2, shard_len, width),
            vmem(2, *seq_shape),
            vmem(2, *seq_shape),
            vmem(2 * num_slots, half_units),
            vmem(2 * num_slots, 2 * half_units),
            vmem(*row_box),
            vmem(*row_box),
            vmem(*row_box),
            vmem(nz, 2, down_rows, width),
            vmem(*seq_shape),
            vmem(nc, num_seqs, shard_len, head_width),
            vmem(num_seqs, nc, shard_len, head_width),
            vmem(*group_shape),
            vmem(*group_shape, dtype=F32),
            vmem(num_seqs, 2, shard_len, width),
            vmem(*seq_shape),
            vmem(*seq_shape),
            vmem(*half_blocks, 2 * own_units),
            vmem(nz - 1, nc, rows_w, 2 * own_units),
            vmem(nc, rows_w, 2 * own_units),
            vmem(*half_blocks, wide_cols),
            vmem(nz - 1, nc, rows_w, wide_cols),
            vmem(nc, rows_w, wide_cols),
            vmem(nz, down_rows, width),
            vmem(nz - 1, down_rows, width),
            vmem(*half_blocks, width),
            vmem(nz - 1, nc, rows_w, width),
            vmem(nc, rows_w, width),
            vmem(nc, rows_w, width),
            dma((POSTS,)),
            dma((POSTS,)),
            dma((1 + half_units // 256,)),
        ],
        compiler_params=pltpu.CompilerParams(
            collective_id=0, has_side_effects=True, vmem_limit_bytes=VMEM_BYTES
        ),
        cost_estimate=pl.CostEstimate(
            flops=16_000_000_000, bytes_accessed=30_000_000, transcendentals=0
        ),
        name="block_forward_backward",
    )(
        seq_lengths,
        hidden_in.reshape(seq_shape),
        grad_output.reshape(seq_shape),
        expert_ids.transpose(0, 1, 3, 2),
        route_rank.reshape(1, tok),
        w_qkv, w_router.T, gain_attn.reshape(1, rows_w), gain_ffn.reshape(1, rows_w),
        w_gate_up, w_out, w_shared_down, w_experts_in, w_experts_out,
    )

    ins = [fq, fgu, w_qkv, gain_attn.reshape(1, rows_w), ein, eout, out, gin, fsd, fwo]
    results = [
        (w_qkv.shape, F32),
        (w_router.shape[::-1], F32),
        ((1, rows_w), F32),
        ((1, rows_w), F32),
        (w_gate_up.shape, F32),
        (ein.shape, F32),
        (eout.shape, F32),
        (seq_shape, BF),
        (seq_shape, F32),
        (fsd.shape, F32),
        (fwo.shape, F32),
    ]
    grad_qkv, grad_router, grad_ga, grad_gf, grad_gu, grad_in, grad_out, out, gin, fsd, fwo = pl.pallas_call(
        functools.partial(finish_kernel, nc),
        out_shape=[jax.ShapeDtypeStruct(shape, dtype) for shape, dtype in results],
        in_specs=[pl.BlockSpec(memory_space=hbm if i in (4, 5) else vm) for i in range(len(ins))],
        out_specs=[
            pl.BlockSpec(memory_space=hbm if i in (5, 6) else vm) for i in range(len(results))
        ],
        scratch_shapes=[
            vmem(*ein.shape),
            vmem(*eout.shape),
            vmem(*ein.shape, dtype=F32),
            vmem(*eout.shape, dtype=F32),
            dma((2, 2 * ein.shape[0] * WIDEN)),
        ],
        compiler_params=pltpu.CompilerParams(vmem_limit_bytes=VMEM_BYTES),
        name="widen_gradients",
    )(*ins)
    return (
        out.reshape(hidden_in.shape),
        gin.reshape(hidden_in.shape),
        grad_ga.reshape(rows_w),
        grad_qkv,
        fwo,
        grad_router.T,
        grad_gf.reshape(rows_w),
        grad_gu,
        fsd,
        grad_in,
        grad_out,
    )


def fits(mesh, hidden_in, w_qkv, w_router, w_gate_up, w_experts_in):
    nc, nz, nf = mesh.shape["ctx"], mesh.shape["exp"], mesh.shape["fsdp"]
    heads = w_qkv.shape[1] // 3 // HS
    return (
        nf == 2
        and nc == 4
        and nz == 4
        and heads == 12
        and w_router.shape[1] == nc * nz
        and w_qkv.shape[0] == 768
        and hidden_in.shape[2] == 32 * nc
        and hidden_in.shape[0] == 2 * nz * nf
        and hidden_in.shape[3] == 768
        and w_gate_up.shape[1] == w_experts_in.shape[2] == 4096
        and 2 * CAP <= BOX
    )


def solution(mesh):
    def whole(*args):
        chosen = fast_device if fits(mesh, args[0], args[5], args[7], args[9], args[11]) else per_device
        return placed(mesh, chosen)(*args)

    return whole


def placed(mesh, chosen):
    return jax.shard_map(
        chosen,
        mesh=mesh,
        in_specs=(
            P(("exp", "fsdp"), None, "ctx", None),
            P(("exp", "fsdp")),
            P(("exp", "fsdp"), None, "ctx", None),
            P(("exp", "fsdp"), "ctx", None),
            P(("ctx", "exp", "fsdp")),
            P(("ctx", "exp", "fsdp"), None),
            P(("ctx", "exp", "fsdp"), None),
            P(("ctx", "exp", "fsdp"), None),
            P(("ctx", "exp", "fsdp")),
            P(("ctx", "exp", "fsdp"), None),
            P(("ctx", "exp", "fsdp"), None),
            P("exp", ("ctx", "fsdp"), None),
            P("exp", ("ctx", "fsdp"), None),
            P(("exp", "fsdp"), None, "ctx", None),
        ),
        out_specs=(
            P(("exp", "fsdp"), None, "ctx", None),
            P(("exp", "fsdp"), None, "ctx", None),
            P(("ctx", "exp", "fsdp")),
            P(("ctx", "exp", "fsdp"), None),
            P(("ctx", "exp", "fsdp"), None),
            P(("ctx", "exp", "fsdp"), None),
            P(("ctx", "exp", "fsdp")),
            P(("ctx", "exp", "fsdp"), None),
            P(("ctx", "exp", "fsdp"), None),
            P("exp", ("ctx", "fsdp"), None),
            P("exp", ("ctx", "fsdp"), None),
        ),
        check_vma=False,
    )
```

```python
import functools
import math

import jax
import jax.numpy as jnp
from jax import lax
from jax.experimental import pallas as pl
from jax.experimental.pallas import tpu as pltpu
from jax.sharding import PartitionSpec as P

HS = 64
CAP = 18


epsilon = 1e-06
masked_out = -1e30
highest = lax.Precision.HIGHEST


def rms_norm(values_in, gain_row):
    return (
        values_in
        * lax.rsqrt(jnp.mean(values_in * values_in, axis=-1, keepdims=True) + epsilon)
        * gain_row
    )


def rope_tables(places):
    half_size = HS // 2
    frequency = 10000.0 ** (-jnp.arange(half_size, dtype=jnp.float32) * 2.0 / HS)
    angles = places.astype(jnp.float32)[:, None] * frequency[None, :]
    return (jnp.cos(angles), jnp.sin(angles))


def rotate(values_in, cosines, sine_rows):
    half_size = values_in.shape[-1] // 2
    leading = values_in[..., :half_size]
    trailing = values_in[..., half_size:]
    cos_rows = cosines[:, None, :]
    sin_rows = sine_rows[:, None, :]
    return jnp.concatenate(
        [leading * cos_rows - trailing * sin_rows, leading * sin_rows + trailing * cos_rows],
        axis=-1,
    )


def swiglu(merged_rows):
    gate_part, up_part = jnp.split(merged_rows, 2, axis=-1)
    return jax.nn.silu(gate_part) * up_part


def first_t(left_side, right_side, precision=None):
    return lax.dot_general(
        left_side,
        right_side,
        (((0,), (0,)), ((), ())),
        precision=precision,
        preferred_element_type=jnp.float32,
    )


def second_t(left_side, right_side, precision=None):
    return lax.dot_general(
        left_side,
        right_side,
        (((1,), (1,)), ((), ())),
        precision=precision,
        preferred_element_type=jnp.float32,
    )


def per_device(
    hidden_in,
    seq_lengths,
    expert_ids,
    route_rank,
    gain_attn,
    w_qkv,
    w_out,
    w_router,
    gain_ffn,
    w_gate_up,
    w_shared_down,
    w_experts_in,
    w_experts_out,
    grad_output,
):
    num_seqs, two_ends, half_len, model_width = hidden_in.shape
    shard_len = 2 * half_len
    tok_count = num_seqs * shard_len
    num_heads = model_width // HS
    score_scale = HS ** (-0.5)
    ctx_size = lax.axis_size("ctx")
    full_len = shard_len * ctx_size
    whole_half = half_len * ctx_size
    gain_one, wqkv_all, wout_all, router_all, gain_two, shared_in, shared_down = (
        lax.all_gather(gain_attn, ("ctx", "exp", "fsdp"), axis=0, tiled=True),
        lax.all_gather(w_qkv, ("ctx", "exp", "fsdp"), axis=0, tiled=True),
        lax.all_gather(w_out, ("ctx", "exp", "fsdp"), axis=0, tiled=True),
        lax.all_gather(w_router, ("ctx", "exp", "fsdp"), axis=0, tiled=True),
        lax.all_gather(gain_ffn, ("ctx", "exp", "fsdp"), axis=0, tiled=True),
        lax.all_gather(w_gate_up, ("ctx", "exp", "fsdp"), axis=0, tiled=True),
        lax.all_gather(w_shared_down, ("ctx", "exp", "fsdp"), axis=0, tiled=True),
    )
    experts_in, experts_out = (
        lax.all_gather(w_experts_in, ("ctx", "fsdp"), axis=1, tiled=True),
        lax.all_gather(w_experts_out, ("ctx", "fsdp"), axis=1, tiled=True),
    )
    lower_places = lax.axis_index("ctx") * half_len + jnp.arange(half_len, dtype=jnp.int32)
    places = jnp.concatenate([lower_places, full_len - 1 - lower_places])
    whole_range = jnp.arange(whole_half, dtype=jnp.int32)
    full_places = jnp.concatenate([whole_range, full_len - 1 - whole_range])
    live_mask = (places[None, :] < seq_lengths[:, None]).astype(jnp.float32)
    live_rows = live_mask.reshape(tok_count, 1)
    inputs_f = hidden_in.astype(jnp.float32).reshape(tok_count, model_width)
    gain_attn_f = gain_one.astype(jnp.float32)
    normed_b = rms_norm(inputs_f, gain_attn_f).astype(jnp.bfloat16)
    qkv_merged = jnp.dot(normed_b, wqkv_all, preferred_element_type=jnp.float32).reshape(
        num_seqs, shard_len, 3, num_heads, HS
    )
    cosines, sine_rows = rope_tables(places)
    queries = rotate(qkv_merged[:, :, 0], cosines, sine_rows).astype(jnp.bfloat16)
    keys_local = rotate(qkv_merged[:, :, 1], cosines, sine_rows).astype(jnp.bfloat16)
    values_local = qkv_merged[:, :, 2].astype(jnp.bfloat16)
    end_shape = (num_seqs, 2, half_len, model_width)
    keys_full, values_full = (
        lax.all_gather(keys_local.reshape(end_shape), "ctx", axis=2, tiled=True),
        lax.all_gather(values_local.reshape(end_shape), "ctx", axis=2, tiled=True),
    )
    keys_full = keys_full.reshape(num_seqs, full_len, num_heads, HS)
    values_full = values_full.reshape(num_seqs, full_len, num_heads, HS)
    stat_shape = (num_seqs, num_heads, shard_len)
    block_range = jnp.arange(ctx_size, dtype=jnp.int32)

    def block_scores(query_rows, query_places, key_rows, key_places):
        scores = (
            jnp.einsum("bqhd,bkhd->bhqk", query_rows, key_rows, preferred_element_type=jnp.float32)
            * score_scale
        )
        allowed = (key_places[None, None, :] <= query_places[None, :, None]) & (
            key_places[None, None, :] < seq_lengths[:, None, None]
        )
        return jnp.where(allowed[:, None], scores, masked_out)

    def key_block(block_idx):
        offset = block_idx * shard_len
        return (
            lax.dynamic_slice_in_dim(keys_full, offset, shard_len, 1),
            lax.dynamic_slice_in_dim(values_full, offset, shard_len, 1),
            lax.dynamic_slice_in_dim(full_places, offset, shard_len, 0),
        )

    def lse_step(state_in, block_idx):
        run_max, run_sum = state_in
        key_rows, value_rows, key_places = key_block(block_idx)
        scores = block_scores(queries, places, key_rows, key_places)
        new_max = jnp.maximum(run_max, jnp.max(scores, axis=-1))
        run_sum = run_sum * jnp.exp(run_max - new_max) + jnp.sum(
            jnp.exp(scores - new_max[..., None]), axis=-1
        )
        return ((new_max, run_sum), None)

    (row_max, row_sum), unused = lax.scan(
        lse_step,
        (jnp.full(stat_shape, masked_out, jnp.float32), jnp.zeros(stat_shape, jnp.float32)),
        block_range,
    )
    log_total = row_max + jnp.log(row_sum)

    def context_step(running, block_idx):
        key_rows, value_rows, key_places = key_block(block_idx)
        prob_rows = jnp.exp(
            block_scores(queries, places, key_rows, key_places) - log_total[..., None]
        ).astype(jnp.bfloat16)
        return (
            running
            + jnp.einsum(
                "bhqk,bkhd->bqhd", prob_rows, value_rows, preferred_element_type=jnp.float32
            ),
            None,
        )

    context, unused = lax.scan(
        context_step, jnp.zeros((num_seqs, shard_len, num_heads, HS), jnp.float32), block_range
    )
    context_b = context.reshape(tok_count, model_width).astype(jnp.bfloat16)
    attended = inputs_f + jnp.dot(context_b, wout_all, preferred_element_type=jnp.float32)
    gain_ffn_f = gain_two.astype(jnp.float32)
    normed_two = rms_norm(attended, gain_ffn_f).astype(jnp.bfloat16)
    logits = jnp.dot(normed_two, router_all, preferred_element_type=jnp.float32)
    num_experts = router_all.shape[1]
    expert_range = jnp.arange(num_experts, dtype=jnp.int32)
    picked_ids = expert_ids.reshape(tok_count, 2)
    pick_hot = (picked_ids[:, :, None] == expert_range).astype(jnp.float32)
    chosen = jnp.sum(pick_hot * logits[:, None, :], axis=-1)
    gate_probs = jax.nn.softmax(chosen, axis=-1)
    expert_load = (jnp.sum(pick_hot, axis=1) * live_rows).astype(jnp.bfloat16)
    rank_rows = route_rank.reshape(tok_count)
    earlier = (rank_rows[None, :] < rank_rows[:, None]).astype(jnp.bfloat16)
    position = jnp.dot(earlier, expert_load, preferred_element_type=jnp.float32)
    chosen_pos = jnp.sum(pick_hot * position[:, None, :], axis=-1)
    kept_mask = live_rows * (chosen_pos < CAP).astype(jnp.float32)
    slot_hot = (chosen_pos[:, :, None] == jnp.arange(CAP, dtype=jnp.float32)).astype(jnp.float32)
    dispatch = (
        (pick_hot[:, :, :, None] * slot_hot[:, :, None, :] * kept_mask[:, :, None, None])
        .reshape(tok_count, 2, num_experts * CAP)
        .astype(jnp.bfloat16)
    )
    dispatch_any = dispatch[:, 0] + dispatch[:, 1]
    exp_size = lax.axis_size("exp")
    per_owner = num_experts // exp_size
    send_rows = (
        first_t(dispatch_any, normed_two)
        .astype(jnp.bfloat16)
        .reshape(exp_size, per_owner, CAP, model_width)
    )
    arrived = lax.all_to_all(send_rows, "exp", split_axis=0, concat_axis=0, tiled=True)
    expert_merged = jnp.einsum(
        "secd,edf->secf", arrived, experts_in, preferred_element_type=jnp.float32
    )
    expert_hidden = swiglu(expert_merged).astype(jnp.bfloat16)
    expert_result = jnp.einsum(
        "secf,efd->secd", expert_hidden, experts_out, preferred_element_type=jnp.float32
    ).astype(jnp.bfloat16)
    returned = lax.all_to_all(
        expert_result, "exp", split_axis=0, concat_axis=0, tiled=True
    ).reshape(num_experts * CAP, model_width)
    routed = jnp.einsum("tks,sd->tkd", dispatch, returned, preferred_element_type=jnp.float32)
    mixture = jnp.sum(gate_probs[:, :, None] * routed, axis=1)
    shared_merged = jnp.dot(normed_two, shared_in, preferred_element_type=jnp.float32)
    shared_hidden = swiglu(shared_merged).astype(jnp.bfloat16)
    shared_result = jnp.dot(shared_hidden, shared_down, preferred_element_type=jnp.float32)
    layer_out = (
        (live_rows * (attended + mixture + shared_result)).reshape(end_shape).astype(jnp.bfloat16)
    )
    upstream = grad_output.astype(jnp.float32).reshape(tok_count, model_width) * live_rows
    upstream_b = upstream.astype(jnp.bfloat16)
    upstream_f = upstream_b.astype(jnp.float32)
    d_shared_down = first_t(shared_hidden, upstream_b)
    d_shared_hidden = second_t(upstream_b, shared_down)
    unused, swiglu_pull = jax.vjp(swiglu, shared_merged)
    d_shared_merged = swiglu_pull(d_shared_hidden)[0].astype(jnp.bfloat16)
    d_shared_in = first_t(normed_two, d_shared_merged)
    d_normed_two = second_t(d_shared_merged, shared_in)
    gate_grads = jnp.sum(routed * upstream_f[:, None, :], axis=-1)
    weighted = (gate_probs[:, :, None] * upstream_f[:, None, :]).astype(jnp.bfloat16)
    d_returned = (
        jnp.einsum("tks,tkd->sd", dispatch, weighted, preferred_element_type=jnp.float32)
        .astype(jnp.bfloat16)
        .reshape(exp_size, per_owner, CAP, model_width)
    )
    d_result = lax.all_to_all(d_returned, "exp", split_axis=0, concat_axis=0, tiled=True)
    d_experts_out = jnp.einsum(
        "secf,secd->efd", expert_hidden, d_result, preferred_element_type=jnp.float32
    )
    d_expert_hidden = jnp.einsum(
        "secd,efd->secf", d_result, experts_out, preferred_element_type=jnp.float32
    )
    unused, expert_pull = jax.vjp(swiglu, expert_merged)
    d_expert_merged = expert_pull(d_expert_hidden)[0].astype(jnp.bfloat16)
    d_experts_in = jnp.einsum(
        "secd,secf->edf", arrived, d_expert_merged, preferred_element_type=jnp.float32
    )
    d_arrived = jnp.einsum(
        "secf,edf->secd", d_expert_merged, experts_in, preferred_element_type=jnp.float32
    ).astype(jnp.bfloat16)
    d_sent = lax.all_to_all(d_arrived, "exp", split_axis=0, concat_axis=0, tiled=True).reshape(
        num_experts * CAP, model_width
    )
    d_normed_two = d_normed_two + jnp.dot(dispatch_any, d_sent, preferred_element_type=jnp.float32)
    unused, gate_pull = jax.vjp(lambda chosen_in: jax.nn.softmax(chosen_in, axis=-1), chosen)
    d_chosen = gate_pull(gate_grads)[0]
    d_logits = jnp.sum(pick_hot * d_chosen[:, :, None], axis=1)
    d_router = first_t(normed_two.astype(jnp.float32), d_logits, highest)
    d_normed_two = d_normed_two + second_t(d_logits, router_all.astype(jnp.float32), highest)
    unused, second_pull = jax.vjp(rms_norm, attended, gain_ffn_f)
    d_attended, d_gain_ffn = second_pull(d_normed_two)
    d_attended = d_attended + upstream
    d_attended_b = d_attended.astype(jnp.bfloat16)
    d_out_proj = first_t(context_b, d_attended_b)
    d_context = (
        second_t(d_attended_b, wout_all)
        .astype(jnp.bfloat16)
        .reshape(num_seqs, shard_len, num_heads, HS)
    )

    def score_grads(
        query_rows, query_places, key_rows, value_rows, key_places, d_rows, lse_rows, delta_rows
    ):
        prob_rows = jnp.exp(
            block_scores(query_rows, query_places, key_rows, key_places) - lse_rows[..., None]
        )
        d_probs = jnp.einsum(
            "bqhd,bkhd->bhqk", d_rows, value_rows, preferred_element_type=jnp.float32
        )
        d_scores = (prob_rows * (d_probs - delta_rows[..., None])).astype(jnp.bfloat16)
        return (prob_rows.astype(jnp.bfloat16), d_scores)

    def delta_step(running, block_idx):
        key_rows, value_rows, key_places = key_block(block_idx)
        prob_rows = jnp.exp(
            block_scores(queries, places, key_rows, key_places) - log_total[..., None]
        )
        d_probs = jnp.einsum(
            "bqhd,bkhd->bhqk", d_context, value_rows, preferred_element_type=jnp.float32
        )
        return (running + jnp.sum(prob_rows * d_probs, axis=-1), None)

    row_delta, unused = lax.scan(delta_step, jnp.zeros(stat_shape, jnp.float32), block_range)
    head_shape = (num_seqs, shard_len, num_heads, HS)

    def query_step(d_query, block_idx):
        key_rows, value_rows, key_places = key_block(block_idx)
        prob_b, d_scores = score_grads(
            queries, places, key_rows, value_rows, key_places, d_context, log_total, row_delta
        )
        return (
            d_query
            + jnp.einsum("bhqk,bkhd->bqhd", d_scores, key_rows, preferred_element_type=jnp.float32)
            * score_scale,
            None,
        )

    d_query, unused = lax.scan(query_step, jnp.zeros(head_shape, jnp.float32), block_range)
    query_all, d_context_all = (
        lax.all_gather(queries.reshape(end_shape), "ctx", axis=2, tiled=True),
        lax.all_gather(d_context.reshape(end_shape), "ctx", axis=2, tiled=True),
    )
    stat_ends = (num_seqs, num_heads, 2, half_len)
    lse_all, delta_all = (
        lax.all_gather(log_total.reshape(stat_ends), "ctx", axis=3, tiled=True),
        lax.all_gather(row_delta.reshape(stat_ends), "ctx", axis=3, tiled=True),
    )
    query_all = query_all.reshape(num_seqs, full_len, num_heads, HS)
    d_context_all = d_context_all.reshape(num_seqs, full_len, num_heads, HS)
    lse_all = lse_all.reshape(num_seqs, num_heads, full_len)
    delta_all = delta_all.reshape(num_seqs, num_heads, full_len)

    def owner_step(state_in, block_idx):
        d_keys, d_values = state_in
        offset = block_idx * shard_len
        query_rows = lax.dynamic_slice_in_dim(query_all, offset, shard_len, 1)
        d_rows = lax.dynamic_slice_in_dim(d_context_all, offset, shard_len, 1)
        lse_rows = lax.dynamic_slice_in_dim(lse_all, offset, shard_len, 2)
        delta_rows = lax.dynamic_slice_in_dim(delta_all, offset, shard_len, 2)
        query_places = lax.dynamic_slice_in_dim(full_places, offset, shard_len, 0)
        prob_b, d_scores = score_grads(
            query_rows, query_places, keys_local, values_local, places, d_rows, lse_rows, delta_rows
        )
        d_keys = (
            d_keys
            + jnp.einsum(
                "bhqk,bqhd->bkhd", d_scores, query_rows, preferred_element_type=jnp.float32
            )
            * score_scale
        )
        d_values = d_values + jnp.einsum(
            "bhqk,bqhd->bkhd", prob_b, d_rows, preferred_element_type=jnp.float32
        )
        return ((d_keys, d_values), None)

    (d_keys_local, d_values_local), unused = lax.scan(
        owner_step,
        (jnp.zeros(head_shape, jnp.float32), jnp.zeros(head_shape, jnp.float32)),
        block_range,
    )
    unused, rope_pull = jax.vjp(
        lambda rows_in: rotate(rows_in, cosines, sine_rows), qkv_merged[:, :, 0]
    )
    d_query_pre = rope_pull(d_query)[0]
    d_key_pre = rope_pull(d_keys_local)[0]
    d_qkv_merged = (
        jnp.stack([d_query_pre, d_key_pre, d_values_local], axis=2)
        .reshape(tok_count, 3 * model_width)
        .astype(jnp.bfloat16)
    )
    d_qkv = first_t(normed_b, d_qkv_merged)
    d_normed = second_t(d_qkv_merged, wqkv_all)
    unused, first_pull = jax.vjp(rms_norm, inputs_f, gain_attn_f)
    d_inputs, d_gain_attn = first_pull(d_normed)
    grad_input = (d_attended + d_inputs).reshape(end_shape)
    dense_sums = (
        lax.psum_scatter(d_gain_attn, ("ctx", "exp", "fsdp"), scatter_dimension=0, tiled=True),
        lax.psum_scatter(d_qkv, ("ctx", "exp", "fsdp"), scatter_dimension=0, tiled=True),
        lax.psum_scatter(d_out_proj, ("ctx", "exp", "fsdp"), scatter_dimension=0, tiled=True),
        lax.psum_scatter(d_router, ("ctx", "exp", "fsdp"), scatter_dimension=0, tiled=True),
        lax.psum_scatter(d_gain_ffn, ("ctx", "exp", "fsdp"), scatter_dimension=0, tiled=True),
        lax.psum_scatter(d_shared_in, ("ctx", "exp", "fsdp"), scatter_dimension=0, tiled=True),
        lax.psum_scatter(d_shared_down, ("ctx", "exp", "fsdp"), scatter_dimension=0, tiled=True),
    )
    expert_sums = (
        lax.psum_scatter(
            d_experts_in.astype(jnp.bfloat16), ("ctx", "fsdp"), scatter_dimension=1, tiled=True
        ).astype(jnp.float32),
        lax.psum_scatter(
            d_experts_out.astype(jnp.bfloat16), ("ctx", "fsdp"), scatter_dimension=1, tiled=True
        ).astype(jnp.float32),
    )
    return (
        layer_out,
        grad_input,
        dense_sums[0],
        dense_sums[1],
        dense_sums[2],
        dense_sums[3],
        dense_sums[4],
        dense_sums[5],
        dense_sums[6],
        expert_sums[0],
        expert_sums[1],
    )


F32 = jnp.float32
BF = jnp.bfloat16
MESH = pl.DeviceIdType.MESH
BOX = 40
SMALL = 64
VMEM_BYTES = 63 * 1024 * 1024
PUMPS = (3, 6, 6, 0, 6, 6)
POSTS = 64
EARLY = 2
LATE = 1
WIDEN = 1


def place():
    return lax.axis_index("ctx"), lax.axis_index("exp"), lax.axis_index("fsdp")


def wrap(value, size):
    return lax.rem(value, size)


def mm(left, right):
    return lax.dot_general(
        left, right, (((1,), (0,)), ((), ())), preferred_element_type=F32
    )


def mm_nt(left, right):
    return lax.dot_general(
        left, right, (((1,), (1,)), ((), ())), preferred_element_type=F32
    )


def mm_tn(left, right):
    return lax.dot_general(
        left, right, (((0,), (0,)), ((), ())), preferred_element_type=F32
    )


def greet(peers):
    barrier = pltpu.get_barrier_semaphore()
    for peer in peers:
        pl.semaphore_signal(barrier, inc=1, device_id=peer, device_id_type=MESH)


def met(peers):
    pl.semaphore_wait(pltpu.get_barrier_semaphore(), len(peers))


class Post:
    def __init__(self, send, recv, like, device):
        self.send, self.recv, self.like, self.device = send, recv, like, device

    def add(self, src, dst, device):
        pltpu.make_async_remote_copy(
            src_ref=src,
            dst_ref=dst,
            send_sem=self.send,
            recv_sem=self.recv,
            device_id=device,
            device_id_type=MESH,
        ).start()

    def all_of_it(self, like=None):
        like = self.like if like is None else like
        return pltpu.make_async_remote_copy(
            src_ref=like,
            dst_ref=like,
            send_sem=self.send,
            recv_sem=self.recv,
            device_id=self.device,
            device_id_type=MESH,
        )

    def wait_recv(self, like=None):
        self.all_of_it(like).wait_recv()

    def wait_send(self, like=None):
        self.all_of_it(like).wait_send()


class Courier:
    def __init__(self, send, recv, device):
        self.send, self.recv, self.device, self.count, self.sent = send, recv, device, 0, []

    def open(self, like, keep=True):
        post = Post(self.send.at[self.count], self.recv.at[self.count], like, self.device)
        self.count += 1
        if keep:
            self.sent.append(post)
        return post

    def at(self, index, like):
        return Post(self.send.at[index], self.recv.at[index], like, self.device)

    def post(self, like, moves):
        post = self.open(like)
        for src, dst, device in moves:
            post.add(src, dst, device)
        return post

    def settle(self, posts):
        for post in posts:
            post.wait_send()
        done = {id(post) for post in posts}
        self.sent = [post for post in self.sent if id(post) not in done]

    def finish(self):
        self.settle(list(self.sent))


def swap_halves(rows):
    width = rows.shape[1]
    lane = lax.broadcasted_iota(jnp.int32, rows.shape, 1)
    ahead = pltpu.roll(rows, width - HS // 2, 1)
    behind = pltpu.roll(rows, HS // 2, 1)
    return jnp.where((lane & (HS - 1)) < HS // 2, -ahead, behind)


def wide(table, times):
    return jnp.concatenate([table] * times, axis=1)


def position_of(index, half_len, full_len):
    block = index // (2 * half_len)
    inside = index & (2 * half_len - 1)
    low = block * half_len + (inside & (half_len - 1))
    return jnp.where(inside >= half_len, full_len - 1 - low, low)


def allowed_keys(length, half_len, full_len):
    shape = (full_len, full_len)
    query_at = position_of(lax.broadcasted_iota(jnp.int32, shape, 0), half_len, full_len)
    key_at = position_of(lax.broadcasted_iota(jnp.int32, shape, 1), half_len, full_len)
    return (key_at <= query_at) & (key_at < length)


def head_probs(query, key, allowed):
    scores = jnp.where(allowed, mm_nt(query, key) * (HS**-0.5), masked_out)
    weights = jnp.exp(scores - jnp.max(scores, axis=1, keepdims=True))
    return weights * (1.0 / jnp.sum(weights, axis=1, keepdims=True))


def column_row(tail, lane):
    pick = (lax.broadcasted_iota(jnp.int32, (8, 128), 1) == lane).astype(BF)
    return mm_nt(pick, tail)[0:1]


def split_dot(dot, left, right, left_wide=True):
    whole = left if left_wide else right
    high = whole.astype(BF)
    low = (whole - high.astype(F32)).astype(BF)
    if left_wide:
        return dot(high, right) + dot(low, right)
    return dot(left, high) + dot(left, low)


def inverse_rms(rows):
    return lax.rsqrt(jnp.mean(rows * rows, axis=1, keepdims=True) + epsilon)


def norm_back(rows, inverse, scaled):
    return inverse * scaled - rows * (inverse * inverse * inverse) * jnp.mean(
        rows * scaled, axis=1, keepdims=True
    )


def join(blocks, shape):
    return blocks.astype(F32).reshape(shape).astype(BF)


def ffn_block(j, rows, grads, in_ref, out_ref, hidden_ref, dm_ref, result, back, units, step):
    low = pl.multiple_of(j * step, step) if not isinstance(j, int) else j * step
    high = pl.multiple_of(units + low, step) if not isinstance(j, int) else units + low
    gate_at, up_at = pl.ds(low, step), pl.ds(high, step)
    gate, up = mm(rows, in_ref[:, gate_at]), mm(rows, in_ref[:, up_at])
    down = out_ref[gate_at, :]
    d_hidden = mm_nt(grads, down)
    share = 1.0 / (1.0 + jnp.exp(-gate))
    lit = gate * share
    hidden = (lit * up).astype(BF)
    d_gate = (d_hidden * up * (share * (1.0 + gate * (1.0 - share)))).astype(BF)
    d_up = (d_hidden * lit).astype(BF)
    hidden_ref[:, gate_at] = hidden
    dm_ref[:, gate_at] = d_gate
    dm_ref[:, up_at] = d_up
    result[...] += mm(hidden, down)
    back[...] += mm_nt(d_gate, in_ref[:, gate_at]) + mm_nt(d_up, in_ref[:, up_at])


def box_rows(kept_rows, boxes, shift):
    shape = (boxes * kept_rows, boxes * BOX)
    row = lax.broadcasted_iota(jnp.int32, shape, 0)
    column = lax.broadcasted_iota(jnp.int32, shape, 1)
    box = jnp.floor((column.astype(F32) + 0.5) * (1.0 / BOX)).astype(jnp.int32)
    at = column - box * BOX - shift
    return ((at >= 0) & (at < kept_rows) & (row == box * kept_rows + at)).astype(BF)


def block_kernel(
    nc, nz,
    len_ref, ids_in, rank_in, wqkv_in, router_in, ga_in, gf_in, hid_in, gu_in, wo_in, sd_in, go_in,
    win_ref, wout_ref,
    out_to, gin_to, fq_ref, fgu_ref, fsd_to, fwo_to, ein_ref, eout_ref,
    ids_ref, rank_ref, wqkv_ref, router_ref, ga_ref, gf_ref, hid_ref, gu_ref, wo_ref, sd_ref, go_ref,
    out_ref, gin_ref, fsd_ref, fwo_ref,
    turn_ref, meta_own, meta_all, picks, hot_x, hot_d, dg_send, dg_in, hid_all, up_own, up_all, wq_own, wq_st, wq_buf, w_ref, gu_st, gu_buf, gu_all, wo_st, wo_buf,
    wo_all, sd_all, wie, woe, normed_ref, qkv_ref, ctx_all, att_own, nt_all,
    sb, ar, xs, ds, acc_a, acc_b, sh_own, sh_hidden, sh_dm, sh_send, sh_in, sh_mid, sh_end,
    ex_hidden, ex_dm, pin, fb, rb, gsd, da_own, dctx_send, dctx_all, part, part_own, rs_in, rs_mid, rs_end,
    sib_gu, zi_gu, pb_gu, sib_q, zi_q, pb_q, sib_sd, zi_sd, sib_wo, zi_wo, pb_wo, in_wo,
    send, recv, lsem, isem, osem,
):
    c, z, f = place()
    near_x, near_y = c + 1 - 2 * wrap(c, 2), wrap(c + 2, nc)
    far = wrap(near_x + 2, nc)
    to_x, to_y = (near_x, z, f), (near_y, z, f)
    in_plane = [(wrap(c + s, nc), z, f) for s in range(1, nc)]
    in_column = [(c, wrap(z + s, nz), f) for s in range(1, nz)]
    steps_up = list(range(1, nz))
    sibling = (c, z, 1 - f)
    across = [(wrap(c + s, nc), z, 1 - f) for s in range(1, nc)]
    partners = in_plane + in_column + [sibling] + across
    with jax.named_scope("s_greet"):
        greet(partners)

    loads = [
        pltpu.make_async_copy(source, target, isem.at[i])
        for i, (source, target) in enumerate(
            (
                (ids_in, ids_ref), (rank_in, rank_ref), (wqkv_in, wqkv_ref),
                (router_in, router_ref), (ga_in, ga_ref), (gf_in, gf_ref), (hid_in, hid_ref),
                (gu_in, gu_ref), (wo_in, wo_ref), (sd_in, sd_ref), (go_in, go_ref),
            )
        )
    ]
    for load in loads:
        load.start()
    stores = []

    def store(source, target):
        stores.append(pltpu.make_async_copy(source, target, osem.at[len(stores)]))
        stores[-1].start()

    num_seqs, shard_len, width = hid_ref.shape
    full_len = nc * shard_len
    half_len = shard_len // 2
    tok = num_seqs * shard_len
    rows_w = wqkv_ref.shape[0]
    head_width = wqkv_ref.shape[1] // 3 // nc
    heads_here = head_width // HS
    wide_cols = wq_own.shape[2]
    units = gu_ref.shape[1] // 2
    own_units = units // nc
    down_rows = sd_ref.shape[0]
    num_experts = nz * nc
    num_slots = num_experts * CAP
    column_slots = nz * BOX
    block_rows = nz * 2 * rows_w
    mail = Courier(send, recv, sibling)

    for load in loads:
        load.wait()
    small = jnp.concatenate(
        [
            router_ref[...].astype(F32),
            ga_ref[...].astype(F32),
            gf_ref[...].astype(F32),
            jnp.zeros((128 - num_experts - 2, rows_w), F32),
        ],
        axis=0,
    )
    small = jnp.concatenate([small, jnp.zeros((128, 128 - rows_w), F32)], axis=1)
    small = jnp.transpose(small, (1, 0))[:rows_w, :SMALL].astype(BF)
    for owner in range(nc):
        wq_own[owner] = jnp.concatenate(
            [
                wqkv_ref[:, side * width + owner * head_width : side * width + (owner + 1) * head_width]
                for side in range(3)
            ]
            + [small],
            axis=1,
        )
    meta_own[...] = jnp.concatenate(
        [
            jnp.concatenate(
                [ids_ref[q, e, k : k + 1, :] for q in range(num_seqs) for e in range(2)], axis=1
            )
            for k in range(2)
        ]
        + [rank_ref[...], jnp.zeros((5, tok), jnp.int32)],
        axis=0,
    )
    with jax.named_scope("s_met"):
        met(partners)

    others = pl.ds(0, nc - 1)
    staged_wq = mail.post(
        wq_st.at[others],
        [(wq_own.at[wrap(c + s, nc)], wq_st.at[c], in_plane[s - 1]) for s in range(1, nc)],
    )
    arriving = [
        mail.post(
            hid_all.at[q, pl.ds(0, 2)],
            [(hid_ref.at[q], hid_all.at[q, c], peer) for peer in (to_x, to_y)],
        )
        for q in range(num_seqs)
    ]
    meta_copies = mail.post(
        meta_all.at[others], [(meta_own, meta_all.at[c], peer) for peer in in_plane]
    )
    staged_wo = mail.post(wo_st.at[others], [(wo_ref, wo_st.at[c], peer) for peer in in_plane])
    staged_gu = mail.open(gu_st.at[others])
    for s in range(1, nc):
        owner = wrap(c + s, nc)
        for side in range(2):
            at = pl.ds(pl.multiple_of(side * units + owner * own_units, own_units), own_units)
            staged_gu.add(
                gu_ref.at[:, at],
                gu_st.at[c, :, pl.ds(side * own_units, own_units)],
                in_plane[s - 1],
            )

    block = 2 * c + f
    shard_rows = win_ref.shape[1]
    half_units = units // 2
    step = 256
    steps = half_units // step
    lands = pl.ds(pl.multiple_of(block * shard_rows, shard_rows), shard_rows)
    out_rows = wout_ref.shape[1]
    to_core = block // nc
    slot = wrap(block, nc)
    out_lands = pl.ds(pl.multiple_of(slot * out_rows, out_rows), out_rows)
    remote_rows = (2 * nc - 1) * shard_rows
    first_in = mail.count
    expert_in = [
        mail.open(wie.at[pl.ds(0, remote_rows), pl.ds(0, 2 * step)]) for _ in range(steps)
    ]
    expert_out = mail.open(woe, keep=False)
    remote_out = woe.at[pl.ds(0, (nc - 1) * out_rows)]
    own_out = pltpu.make_async_copy(wout_ref.at[c], woe.at[out_lands], lsem.at[0])

    def send_out(s):
        owner = wrap(c + s, nc)
        expert_out.add(wout_ref.at[owner], woe.at[out_lands], (owner, z, to_core))

    def send_out_own():
        @pl.when(to_core == f)
        def _():
            own_out.start()

        @pl.when(to_core != f)
        def _():
            expert_out.add(wout_ref.at[c], woe.at[out_lands], sibling)

    def own_in(j):
        like = wie.at[pl.ds(0, shard_rows), pl.ds(0, 2 * step)]
        return pltpu.make_async_copy(like, like, lsem.at[1 + j])

    def nth_block(j, chip):
        return wrap(2 * j + j // 2 + 2 * wrap(chip, 2), steps)

    def send_in(j, s, g, side):
        owner = wrap(c + s, nc)
        at = nth_block(j, owner) * step
        core = f if g == 0 else 1 - f
        from_lane = pl.multiple_of(side * units + core * half_units + at, step)
        src = win_ref.at[owner, :, pl.ds(from_lane, step)]
        dst = wie.at[lands, pl.ds(pl.multiple_of(side * half_units + at, step), step)]
        if s == 0 and g == 0:
            pltpu.make_async_copy(src, dst, lsem.at[1 + j]).start()
        else:
            expert_in[j].add(src, dst, (owner, z, core))

    bulk = [functools.partial(send_out, s) for s in range(1, nc)] + [send_out_own]
    for j in range(steps):
        for s in range(1, nc + 1):
            for g in range(2):
                for side in range(2):
                    bulk.append(functools.partial(send_in, j, s % nc, g, side))

    def pump(queue, count):
        for _ in range(min(count, len(queue))):
            queue.pop(0)()

    with jax.named_scope("s_turns"):
        row = lax.broadcasted_iota(jnp.int32, (full_len, 128), 0)
        lane = lax.broadcasted_iota(jnp.int32, (full_len, 128), 1) & (HS // 2 - 1)
        frequency = jnp.exp(lane.astype(F32) * (-2.0 * math.log(10000.0) / HS))
        angles = position_of(row, half_len, full_len).astype(F32) * frequency
        turn_ref[:, :128] = jnp.cos(angles)
        turn_ref[:, 128:] = jnp.sin(angles)
    lane = lax.broadcasted_iota(jnp.int32, (tok, 128), 1).astype(F32)

    def live_rows(chip):
        row_at = lax.broadcasted_iota(jnp.int32, (tok, 1), 0)
        inside = row_at & (shard_len - 1)
        low = chip * half_len + (inside & (half_len - 1))
        places = jnp.where(inside >= half_len, full_len - 1 - low, low)
        lengths = jnp.zeros((tok, 1), jnp.int32)
        for q in range(num_seqs):
            lengths = jnp.where(row_at // shard_len == q, len_ref[q], lengths)
        return (places < lengths).astype(F32)

    def turned(rows):
        return jnp.transpose(
            jnp.concatenate([rows, jnp.zeros((128 - rows.shape[0], tok), F32)], axis=0), (1, 0)
        )

    def hot_lanes(columns):
        return [(lane == SMALL + columns[:, k : k + 1]).astype(F32) for k in range(2)]

    def gates_of(hots, logits):
        chosen = [jnp.sum(hot * logits, axis=1, keepdims=True) for hot in hots]
        top = jnp.maximum(chosen[0], chosen[1])
        raised = [jnp.exp(value - top) for value in chosen]
        return [value / (raised[0] + raised[1]) for value in raised]

    def route(chip):
        rows = meta_all[chip].astype(F32)
        columns = turned(rows)
        picks[chip] = columns
        hots = hot_lanes(columns)
        rank_row = jnp.broadcast_to(rows[2:3], (tok, tok))
        earlier = (rank_row < columns[:, 2:3]).astype(BF)
        live = live_rows(chip)
        position = mm(earlier, ((hots[0] + hots[1]) * live).astype(BF))
        slot_lane = lax.broadcasted_iota(jnp.int32, (tok, column_slots), 1).astype(F32)
        for k in range(2):
            at = jnp.sum(hots[k] * position, axis=1, keepdims=True)
            plane = jnp.floor((columns[:, k : k + 1] + 0.5) * (1.0 / nc))
            here = columns[:, k : k + 1] - plane * nc == c.astype(F32)
            slot_at = jnp.where((live > 0) & (at < CAP) & here, plane * BOX + at, -BOX)
            hot_x[chip, k] = (slot_lane == slot_at).astype(BF)
            hot_d[chip, k] = (slot_lane == slot_at + CAP).astype(BF)

    live = live_rows(c)
    upstream = go_ref[...].reshape(tok, width).astype(F32) * live
    up_b = upstream.astype(BF)
    up_own[...] = up_b.reshape(num_seqs, shard_len, width)
    for q in range(num_seqs):
        hid_all[q, c] = hid_ref[q]
        up_all[q, c] = up_own[q]

    def pass_on(post, buffer, q, at):
        post.wait_recv()
        origin, peer = (near_x, to_y) if q == 0 else (near_y, to_x)
        block_at = at(buffer, q, origin)
        return mail.post(block_at, [(block_at, block_at, peer)])

    def by_seq(buffer, q, chip):
        return buffer.at[q, chip]

    def by_chip(buffer, q, chip):
        return buffer.at[chip, q]

    sd_all[z, f] = sd_ref[...]
    planes = pl.ds(0, nz - 1)

    def spread(stage, staged, buffer):
        staged.wait_recv()
        post = mail.post(
            buffer.at[:, planes, 0],
            [(stage, buffer.at[:, z, f], peer) for peer in in_column],
        )
        for i in range(nc):
            buffer[i, z, f] = stage[i]
        return post

    def spread_gate_up(side):
        at = pl.ds(side * own_units, own_units)
        return mail.post(
            gu_buf.at[:, planes, 0, :, at],
            [(gu_st.at[:, :, at], gu_buf.at[:, z, f, :, at], peer) for peer in in_column],
        )

    def forward(posts, buffer):
        for post in posts:
            post.wait_recv()
        both = buffer.at[:, :, f]
        return mail.post(both, [(both, both, sibling)])

    with jax.named_scope("a_stage_wq"):
        wq_st[c] = wq_own[c]
        spread_wq = spread(wq_st, staged_wq, wq_buf)
    with jax.named_scope("a_pass_hidden"):
        passing = [pass_on(arriving[q], hid_all, q, by_seq) for q in range(num_seqs)]
    up_copies = [
        mail.post(
            up_all.at[q, pl.ds(0, 2)],
            [(up_own.at[q], up_all.at[q, c], peer) for peer in (to_x, to_y)],
        )
        for q in range(num_seqs)
    ]
    pump(bulk, PUMPS[3])
    with jax.named_scope("a_route"):
        meta_copies.wait_recv()
        meta_all[c] = meta_own[...]

        def route_one(chip, carry):
            route(chip)
            return carry

        lax.fori_loop(0, nc, route_one, 0)
    wo_st[c] = wo_ref[...]
    for side in range(2):
        at = pl.ds(pl.multiple_of(side * units + c * own_units, own_units), own_units)
        gu_st[c, :, side * own_units : (side + 1) * own_units] = gu_ref[:, at]
    with jax.named_scope("a_forward_wq"):
        passed_wq = forward([spread_wq], wq_buf)
        passed_wq.wait_recv()
        for i in range(nc):
            w_ref[i * block_rows : (i + 1) * block_rows, :] = join(
                wq_buf[i], (block_rows, wide_cols)
            )

    cosines = wide(turn_ref[:, :128], 2 * head_width // 128)
    sines = wide(turn_ref[:, 128:], 2 * head_width // 128)
    tail_at = wide_cols - 128
    attn_gain = column_row(w_ref[:, tail_at:], SMALL + num_experts)
    ctx_copies = []
    for q in range(num_seqs):
        with jax.named_scope("a_wait_hidden"):
            passing[q].wait_recv()
        with jax.named_scope("a_attention"):
            rows = hid_all[q].reshape(full_len, width).astype(F32)
            normed = (rows * inverse_rms(rows) * attn_gain).astype(BF)
            normed_ref[q] = normed
            merged = mm(normed, w_ref[:, : 3 * head_width])
            both = merged[:, : 2 * head_width]
            both = (both * cosines + swap_halves(both) * sines).astype(BF)
            values = merged[:, 2 * head_width :].astype(BF)
            qkv_ref[q, :, : 2 * head_width] = both
            qkv_ref[q, :, 2 * head_width :] = values
            allowed = allowed_keys(len_ref[q], half_len, full_len)
            heads = []
            for h in range(heads_here):
                probs = head_probs(
                    both[:, h * HS : (h + 1) * HS],
                    both[:, head_width + h * HS : head_width + (h + 1) * HS],
                    allowed,
                ).astype(BF)
                heads.append(mm(probs, values[:, h * HS : (h + 1) * HS]))
            context = jnp.concatenate(heads, axis=1).astype(BF)
            ctx_all[c, q] = context.reshape(nc, shard_len, head_width)
        ctx_copies.append(
            mail.post(
                ctx_all.at[pl.ds(0, 2), q],
                [(ctx_all.at[c, q], ctx_all.at[c, q], peer) for peer in (to_x, to_y)],
            )
        )
    spread_wo = spread(wo_st, staged_wo, wo_buf)
    with jax.named_scope("a_pass_upstream"):
        up_passing = [pass_on(up_copies[q], up_all, q, by_seq) for q in range(num_seqs)]
    with jax.named_scope("a_pass_context"):
        ctx_passing = [pass_on(ctx_copies[q], ctx_all, q, by_chip) for q in range(num_seqs)]
    pump(bulk, PUMPS[0])
    with jax.named_scope("a_forward_wo"):
        passed_wo = forward([spread_wo], wo_buf)
        staged_gu.wait_recv()
        for i in range(nc):
            gu_buf[i, z, f] = gu_st[i]
        spread_gu = [spread_gate_up(0)]
        passed_wo.wait_recv()
        for i in range(nc):
            wo_all[i * block_rows : (i + 1) * block_rows, :] = join(
                wo_buf[i], (block_rows, width)
            )
    ffn_gain = column_row(w_ref[:, tail_at:], SMALL + num_experts + 1)
    for q in range(num_seqs):
        with jax.named_scope("a_wait_context"):
            ctx_passing[q].wait_recv()
        with jax.named_scope("a_project"):
            total = hid_all[q].reshape(full_len, width).astype(F32)
            for i in range(nc):
                total = total + mm(
                    ctx_all[i, q].reshape(full_len, head_width),
                    wo_all[i * head_width : (i + 1) * head_width, :],
                )
            acc_a[q * full_len : (q + 1) * full_len] = total
            nt_all[q] = (
                (total * inverse_rms(total) * ffn_gain).astype(BF).reshape(nc, shard_len, width)
            )
    by_block = acc_a.at[pl.ds(0, nc * tok)].reshape(num_seqs, nc, shard_len, width)
    for q in range(num_seqs):
        att_own[q] = by_block[q, c]

    with jax.named_scope("b_wait_upstream"):
        for post in up_passing:
            post.wait_recv()
    with jax.named_scope("b_dispatch"):
        tail = w_ref[:, tail_at:]

        def box_rows_of(chip, carry):
            normed = jnp.concatenate([nt_all[q, chip] for q in range(num_seqs)], axis=0)
            columns = picks[chip]
            gates = gates_of(hot_lanes(columns), mm(normed, tail))
            picks[chip] = jnp.where(lane == 3, gates[0], jnp.where(lane == 4, gates[1], columns))
            up_f = jnp.concatenate([up_all[q, chip] for q in range(num_seqs)], axis=0).astype(F32)
            boxes = mm_tn(hot_x[chip, 0] + hot_x[chip, 1], normed)
            for k in range(2):
                boxes = boxes + mm_tn(hot_d[chip, k], (gates[k] * up_f).astype(BF))
            boxes = boxes.reshape(nz, BOX, width).astype(BF)
            for plane in range(nz):
                sb[plane, chip] = boxes[plane]
            return carry

        lax.fori_loop(0, nc, box_rows_of, 0)
        row_copies = [
            mail.post(ar.at[f, 0], [(sb.at[to[1]], ar.at[f, z], to)]) for to in in_column
        ]
        ar[f, z] = sb[z]
        normed = jnp.concatenate([nt_all[q, c] for q in range(num_seqs)], axis=0)
    pump(bulk, len(bulk))

    with jax.named_scope("b_forward_rows"):
        forwards = mail.open(ar.at[f])
        forwards.add(ar.at[f, z], ar.at[f, z], sibling)
        for s in range(1, nz):
            row_copies[s - 1].wait_recv()
            origin = wrap(z + nz - s, nz)
            forwards.add(ar.at[f, origin], ar.at[f, origin], sibling)
        forwards.wait_recv()
        keep_x, keep_d = (box_rows(CAP, num_experts, shift) for shift in (0, CAP))
        for core in range(2):
            at = slice(core * num_slots, (core + 1) * num_slots)
            boxes = join(ar[core], (num_experts * BOX, width))
            xs[at] = mm(keep_x, boxes).astype(BF)
            ds[at] = mm(keep_d, boxes).astype(BF)
    with jax.named_scope("b_wait_down"):
        @pl.when(to_core == f)
        def _():
            expert_out.wait_recv(remote_out)
            own_out.wait()

        @pl.when(to_core != f)
        def _():
            expert_out.wait_recv()

    gwi, gwo = wie, woe

    def expert_grads(j):
        low = nth_block(j, c) * step
        for side in range(2):
            at = pl.ds(pl.multiple_of(side * half_units + low, step), step)
            gwi[:, at] = mm_tn(xs[...], ex_dm[:, at]).astype(BF)
        at = pl.ds(pl.multiple_of(low, step), step)
        gwo[at, :] = mm_tn(ex_hidden[:, at], ds[...]).astype(BF)

    def homeward(j):
        moves = [
            functools.partial(send_home_in, j, s % nc, g, side)
            for s in range(1, nc + 1)
            for g in range(2)
            for side in range(2)
        ]
        return moves + [functools.partial(send_home_out, j)]

    home = []
    home_in = mail.open(gwi.at[pl.ds(0, remote_rows)])
    home_out = mail.open(gwo, keep=False)
    remote_home = gwo.at[pl.ds(0, (nc - 1) * out_rows)]
    home_in_own = pltpu.make_async_copy(
        gwi.at[pl.ds(0, shard_rows)], gwi.at[pl.ds(0, shard_rows)], lsem.at[1]
    )

    def send_home_in(j, s, g, side):
        owner = wrap(c + s, nc)
        core = f if g == 0 else 1 - f
        from_rows = pl.ds(
            pl.multiple_of((2 * owner + core) * shard_rows, shard_rows), shard_rows
        )
        low = nth_block(j, c) * step
        to_lane = pl.multiple_of(side * units + f * half_units + low, step)
        src = gwi.at[from_rows, pl.ds(pl.multiple_of(side * half_units + low, step), step)]
        dst = ein_ref.at[c, :, pl.ds(to_lane, step)]
        if s == 0 and g == 0:
            pltpu.make_async_copy(src, dst, lsem.at[1]).start()
        else:
            home_in.add(src, dst, (owner, z, core))

    def home_rows(j):
        return gwo.at[pl.ds(pl.multiple_of(nth_block(j, c) * out_rows, out_rows), out_rows)]

    def home_out_own(j):
        return pltpu.make_async_copy(home_rows(j), eout_ref.at[c], lsem.at[0])

    def send_home_out(j):
        to_block = f * nc + nth_block(j, c)

        @pl.when(to_block == block)
        def _():
            home_out_own(j).start()

        @pl.when(to_block != block)
        def _():
            home_out.add(
                home_rows(j),
                eout_ref.at[c],
                (to_block // 2, z, wrap(to_block, 2)),
            )

    acc_a[...] = jnp.zeros(acc_a.shape, F32)
    acc_b[...] = jnp.zeros(acc_b.shape, F32)
    early = [move for j in range(EARLY) for move in homeward(j)]
    home = [move for j in range(EARLY, steps) for move in homeward(j)]
    late_gate_up = mail.open(gu_buf.at[:, planes, 0, :, pl.ds(0, own_units)])
    spread_sd = mail.open(sd_all.at[planes, 0])
    spread_gu.append(late_gate_up)

    def expert_block(j, carry):
        with jax.named_scope("b_wait_experts"):
            own_in(j).wait()
            mail.at(first_in + j, expert_in[0].like).wait_recv()

        @pl.when(j == steps - 1)
        def _():
            pump(early, len(early))

        with jax.named_scope("b_experts"):
            ffn_block(
                nth_block(j, c), xs[...], ds[...], wie, woe, ex_hidden, ex_dm, acc_a, acc_b,
                half_units, step,
            )

        @pl.when(j < EARLY)
        def _():
            with jax.named_scope("b_early_grads"):
                expert_grads(j)

        @pl.when(j == LATE)
        def _():
            at = pl.ds(own_units, own_units)
            for peer in in_column:
                late_gate_up.add(gu_st.at[:, :, at], gu_buf.at[:, z, f, :, at], peer)
                spread_sd.add(sd_ref, sd_all.at[z, f], peer)

        return carry

    lax.fori_loop(0, steps, expert_block, 0)
    mail.settle(row_copies)
    pr = sb
    with jax.named_scope("b_sibling_sum"):

        def boxed(core):
            at = pl.ds(pl.multiple_of(core * num_slots, num_slots), num_slots)
            return (
                mm_tn(keep_x, acc_a[at].astype(BF)) + mm_tn(keep_d, acc_b[at].astype(BF))
            ).reshape(nz, nc, BOX, width)

        pr[...] = boxed(1 - f).astype(BF)
        swap = mail.post(pin, [(pr, pin, sibling)])
        ours = boxed(f)
        swap.wait_recv()
        fb[...] = (ours + pin[...].astype(F32)).astype(BF)
        returns = mail.post(
            rb.at[planes], [(fb.at[to[1]], rb.at[z], to) for to in in_column]
        )
        rb[z] = fb[z]
    with jax.named_scope("b_expert_grads"):

        def late_grads(j, carry):
            expert_grads(j)
            return carry

        lax.fori_loop(EARLY, steps, late_grads, 0)
    pump(home, PUMPS[1])

    with jax.named_scope("b_forward_gu"):
        passed_gu = forward(spread_gu, gu_buf)
        spread_sd.wait_recv()
        passed_sd = mail.post(sd_all.at[:, f], [(sd_all.at[:, f], sd_all.at[:, f], sibling)])
        passed_gu.wait_recv()
        passed_sd.wait_recv()
        for i in range(nc):
            gu_all[i * block_rows : (i + 1) * block_rows, :] = join(
                gu_buf[i], (block_rows, 2 * own_units)
            )
    plane_tok = nc * tok
    shared_rows = nt_all.reshape(plane_tok, width)
    shared_grads = up_all.reshape(plane_tok, width)
    shared_down = sd_all.reshape(own_units, width)
    with jax.named_scope("b_shared"):
        first = pl.ds(0, plane_tok)
        acc_a[...] = jnp.zeros(acc_a.shape, F32)
        acc_b[...] = jnp.zeros(acc_b.shape, F32)

        def shared_block(j, carry):
            ffn_block(
                j, shared_rows[...], shared_grads[...], gu_all, shared_down, sh_hidden, sh_dm,
                acc_a.at[first], acc_b.at[first], own_units, 256,
            )
            return carry

        lax.fori_loop(0, own_units // 256, shared_block, 0)
    mail.settle(spread_gu + [passed_gu])
    ggu = gu_buf
    with jax.named_scope("b_shared_grads"):

        def gate_up_grads(j, carry):
            at = pl.ds(pl.multiple_of(j * 256, 256), 256)
            piece = mm_tn(shared_rows[...], sh_dm[:, at])
            ggu[:, :, :, :, at] = piece.reshape(ggu.shape[:4] + (256,)).astype(BF)
            return carry

        lax.fori_loop(0, 2 * own_units // 256, gate_up_grads, 0)
        gsd[...] = mm_tn(sh_hidden[...], shared_grads[...]).reshape(gsd.shape).astype(BF)
        sibling_gu = mail.post(sib_gu, [(ggu.at[:, :, 1 - f], sib_gu, sibling)])
        sibling_sd = mail.post(sib_sd, [(gsd.at[:, 1 - f], sib_sd, sibling)])

    with jax.named_scope("c_wait_returns"):
        returns.wait_recv()
    with jax.named_scope("c_column_mixture"):
        cuts = [
            acc.at[first].reshape(num_seqs, nc, shard_len, width) for acc in (acc_a, acc_b)
        ]

        def add_results(chip, carry):
            results = join(
                jnp.concatenate([rb[plane, chip].astype(F32) for plane in range(nz)], axis=0),
                (column_slots, width),
            )
            up_f = jnp.concatenate([up_all[q, chip] for q in range(num_seqs)], axis=0).astype(F32)
            gates = [picks[chip][:, 3 + k : 4 + k] for k in range(2)]
            routed = [mm(hot_x[chip, k], results) for k in range(2)]
            mixture = gates[0] * routed[0] + gates[1] * routed[1]
            d_rows = mm(hot_d[chip, 0] + hot_d[chip, 1], results)
            for q in range(num_seqs):
                at = slice(q * shard_len, (q + 1) * shard_len)
                cuts[0][q, chip] = cuts[0][q, chip] + mixture[at]
                cuts[1][q, chip] = cuts[1][q, chip] + d_rows[at]
            d_gates = [jnp.sum(routed[k] * up_f, axis=1, keepdims=True) for k in range(2)]
            spread_out = jnp.where(lane == 0, d_gates[0], jnp.where(lane == 1, d_gates[1], 0.0))
            dg_send[chip] = jnp.transpose(spread_out, (1, 0))[:8]
            return carry

        lax.fori_loop(0, nc, add_results, 0)
        for k in range(2):
            for q in range(num_seqs):
                sh_own[k, q, 0] = cuts[k][q, c]
                sh_own[k, q, 1] = cuts[k][q, near_y if q == 0 else near_x]
            sh_send[k] = cuts[k][...].astype(BF)

    def first_leg(inbox, box, lead):
        post = mail.open(inbox)
        for q in range(num_seqs):
            peer = to_x if q == 0 else to_y
            for at, chip in enumerate((near_x if q == 0 else near_y, far)):
                post.add(box.at[lead + (q, chip)], inbox.at[lead + (q, at)], peer)
        return post

    shared_first = first_leg(sh_in, sh_send, (slice(None),))
    dg_copies = mail.post(
        dg_in.at[others],
        [(dg_send.at[wrap(c + s, nc)], dg_in.at[c], in_plane[s - 1]) for s in range(1, nc)],
    )
    dg_in[c] = dg_send[c]
    pump(home, PUMPS[4])

    with jax.named_scope("b_reduce_shared"):
        def two_cores(copy, own, inbox):
            copy.wait_recv()
            inbox[...] = (own.astype(F32) + inbox[...].astype(F32)).astype(BF)

        def four_planes(copy, buffer, inbox):
            copy.wait_recv()
            for i in range(nc):
                inbox[i] = (buffer[i, :, f].astype(F32) + inbox[i].astype(F32)).astype(BF)

        four_planes(sibling_gu, ggu, sib_gu)
        two_cores(sibling_sd, gsd[:, f], sib_sd)
        gu_copies = mail.post(
            zi_gu,
            [
                (sib_gu.at[:, to[1]], zi_gu.at[up - 1], to)
                for to, up in zip(in_column, steps_up)
            ],
        )
        sd_copies = mail.post(
            zi_sd,
            [(sib_sd.at[to[1]], zi_sd.at[up - 1], to) for to, up in zip(in_column, steps_up)],
        )

    with jax.named_scope("c_second_sum"):
        shared_first.wait_recv()
        for k in range(2):
            for q in range(num_seqs):
                sh_mid[k, q] = (sh_own[k, q, 1] + sh_in[k, q, 1].astype(F32)).astype(BF)
        shared_second = mail.post(
            sh_end,
            [
                (sh_mid.at[:, q], sh_end.at[:, q], to_y if q == 0 else to_x)
                for q in range(num_seqs)
            ],
        )

    pump(home, PUMPS[5])
    with jax.named_scope("c_wait_shared"):
        dg_copies.wait_recv()
        shared_second.wait_recv()
        added, d_normed = [
            jnp.concatenate(
                [
                    sh_own[k, q, 0] + sh_in[k, q, 0].astype(F32) + sh_end[k, q].astype(F32)
                    for q in range(num_seqs)
                ],
                axis=0,
            )
            for k in range(2)
        ]
    with jax.named_scope("c_combine"):
        attended = att_own[...].reshape(tok, width)
        inverse = inverse_rms(attended)
        out_ref[...] = (live * (attended + added)).astype(BF).reshape(out_ref.shape)
        store(out_ref, out_to)
        hots = hot_lanes(picks[c])
        own_gates = gates_of(hots, mm(normed, tail))
        summed = turned(jnp.sum(dg_in[...], axis=0))
        d_gates = [summed[:, k : k + 1] for k in range(2)]
        mean_gate = own_gates[0] * d_gates[0] + own_gates[1] * d_gates[1]
        d_logits = hots[0] * (own_gates[0] * (d_gates[0] - mean_gate)) + hots[1] * (
            own_gates[1] * (d_gates[1] - mean_gate)
        )
        d_normed = d_normed + split_dot(mm_nt, d_logits, tail)
        d_attended = upstream + norm_back(attended, inverse, d_normed * ffn_gain)
        d_att_b = d_attended.astype(BF)
        d_context = mm_nt(d_att_b, wo_all[...]).astype(BF)
        for i in range(nc):
            dctx_send[i] = d_context[:, i * head_width : (i + 1) * head_width].reshape(
                num_seqs, shard_len, head_width
            )
        for q in range(num_seqs):
            dctx_all[q, c] = dctx_send[c, q]
        dctx_copies = mail.post(
            dctx_all.at[:, others],
            [
                (dctx_send.at[wrap(c + s, nc)], dctx_all.at[:, c], in_plane[s - 1])
                for s in range(1, nc)
            ],
        )
        gin_ref[...] = d_attended.reshape(gin_ref.shape)
    pump(home, PUMPS[2])

    mail.settle([spread_wo, passed_wo])
    gwo_at = wo_buf
    with jax.named_scope("c_reduce"):
        for i in range(nc):
            mine = jnp.concatenate([ctx_all[i, q, c] for q in range(num_seqs)], axis=0)
            gwo_at[i] = mm_tn(mine, d_att_b).reshape(gwo_at.shape[1:]).astype(BF)
        sibling_wo = mail.post(sib_wo, [(gwo_at.at[:, :, 1 - f], sib_wo, sibling)])
        d_router = split_dot(mm_tn, normed, d_logits, left_wide=False)
        d_gain = jnp.sum(d_normed * attended * inverse, axis=0, keepdims=True)
        turned = jnp.transpose(jnp.broadcast_to(d_gain, (128, width)), (1, 0))
        extra_lane = lax.broadcasted_iota(jnp.int32, (width, 128), 1)
        extras = jnp.where(extra_lane == SMALL + num_experts + 1, turned, d_router)
        four_planes(sibling_wo, gwo_at, sib_wo)
        wo_copies = mail.post(
            zi_wo,
            [
                (sib_wo.at[:, wrap(z + s, nz)], zi_wo.at[s - 1], in_column[s - 1])
                for s in range(1, nz)
            ],
        )

    with jax.named_scope("c_wait_dctx"):
        dctx_copies.wait_recv()
    def column_sum(own, copies, inbox):
        copies.wait_recv()
        total = own.astype(F32)
        for s in range(1, nz):
            total = total + inbox[s - 1].astype(F32)
        return total

    def hand_out(box, final):
        store(box.at[c], final.at[c])
        return mail.post(
            final.at[others],
            [(box.at[wrap(c + s, nc)], final.at[c], in_plane[s - 1]) for s in range(1, nc)],
        )

    with jax.named_scope("c_column_gu"):
        pb_gu[...] = column_sum(sib_gu[:, z], gu_copies, zi_gu).astype(BF)
        final_gu = hand_out(pb_gu, fgu_ref)
    grad_qkv = jnp.zeros((width, 3 * head_width), F32)
    rs_first = mail.open(rs_in)
    for q in range(num_seqs):
        with jax.named_scope("c_attention"):
            d_context = dctx_all[q].reshape(full_len, head_width)
            allowed = allowed_keys(len_ref[q], half_len, full_len)
            merged = qkv_ref[q]
            d_query, d_key, d_value = [], [], []
            for h in range(heads_here):
                query = merged[:, h * HS : (h + 1) * HS]
                key = merged[:, head_width + h * HS : head_width + (h + 1) * HS]
                value = merged[:, 2 * head_width + h * HS : 2 * head_width + (h + 1) * HS]
                d_head = d_context[:, h * HS : (h + 1) * HS]
                probs = head_probs(query, key, allowed)
                d_probs = mm_nt(d_head, value)
                delta = jnp.sum(probs * d_probs, axis=1, keepdims=True)
                d_scores = (probs * (d_probs - delta)).astype(BF)
                d_query.append(mm(d_scores, key) * (HS**-0.5))
                d_key.append(mm_tn(d_scores, query) * (HS**-0.5))
                d_value.append(mm_tn(probs.astype(BF), d_head))
            both = jnp.concatenate(d_query + d_key, axis=1)
            both = both * cosines - swap_halves(both) * sines
            d_merged = jnp.concatenate([both] + d_value, axis=1).astype(BF)
            product = mm_nt(d_merged, w_ref[:, : 3 * head_width]).reshape(nc, shard_len, width)
            part_own[q] = product
            part[q] = product.astype(BF)
            for at, chip in enumerate((near_x if q == 0 else near_y, far)):
                rs_first.add(part.at[q, chip], rs_in.at[q, at], to_x if q == 0 else to_y)
            grad_qkv = grad_qkv + mm_tn(normed_ref[q], d_merged)
    pump(home, len(home))
    mail.settle([spread_wq, passed_wq])
    gq = wq_buf
    with jax.named_scope("c_reduce_q"):
        last = jnp.concatenate([grad_qkv[:, tail_at:], extras[:, 3 * head_width - tail_at :]], axis=1)
        gq[...] = (
            jnp.concatenate([grad_qkv[:, :tail_at], last], axis=1).reshape(gq.shape).astype(BF)
        )
        sibling_q = mail.post(sib_q, [(gq.at[:, :, 1 - f], sib_q, sibling)])
        four_planes(sibling_q, gq, sib_q)
        q_copies = mail.post(
            zi_q,
            [
                (sib_q.at[:, to[1]], zi_q.at[up - 1], to)
                for to, up in zip(in_column, steps_up)
            ],
        )
    with jax.named_scope("c_second_leg"):
        rs_first.wait_recv()
        for q in range(num_seqs):
            relay = part_own[q, near_y if q == 0 else near_x]
            rs_mid[q] = (relay + rs_in[q, 1].astype(F32)).astype(BF)
        rs_second = mail.post(
            rs_end,
            [(rs_mid.at[q], rs_end.at[q], to_y if q == 0 else to_x) for q in range(num_seqs)],
        )

    with jax.named_scope("c_column_sd"):
        fsd_ref[...] = column_sum(sib_sd[z], sd_copies, zi_sd)
        store(fsd_ref, fsd_to)
    with jax.named_scope("c_column_wo"):
        pb_wo[...] = column_sum(sib_wo[:, z], wo_copies, zi_wo).astype(BF)
        in_wo[c] = pb_wo[c]
        final_wo = mail.post(
            in_wo.at[others],
            [(pb_wo.at[wrap(c + s, nc)], in_wo.at[c], in_plane[s - 1]) for s in range(1, nc)],
        )
    with jax.named_scope("c_column_q"):
        pb_q[...] = column_sum(sib_q[:, z], q_copies, zi_q).astype(BF)
        final_q = hand_out(pb_q, fq_ref)
    with jax.named_scope("c_grad_in"):
        rs_second.wait_recv()
        for q in range(num_seqs):
            d_normed = part_own[q, c] + rs_in[q, 0].astype(F32) + rs_end[q].astype(F32)
            rows = hid_ref[q].astype(F32)
            gin_ref[q] = gin_ref[q] + norm_back(rows, inverse_rms(rows), d_normed * attn_gain)
        store(gin_ref, gin_to)
    with jax.named_scope("c_final"):
        final_wo.wait_recv()
        fwo_ref[...] = jnp.sum(in_wo[...].astype(F32), axis=0)
        store(fwo_ref, fwo_to)
        final_gu.wait_recv()
        final_q.wait_recv()
    with jax.named_scope("c_wait_home"):
        home_in_own.wait()
        home_in.wait_recv()

        @pl.when(to_core == f)
        def _():
            home_out_own(0).wait()
            home_out.wait_recv(remote_home)
            home_out.wait_send(remote_home)
            expert_out.wait_send(remote_out)

        @pl.when(to_core != f)
        def _():
            home_out.wait_recv()
            home_out.wait_send()
            expert_out.wait_send()

    assert mail.count <= POSTS, mail.count
    with jax.named_scope("z_finish"):
        for copy in stores:
            copy.wait()
        mail.finish()


def finish_kernel(
    nc, fq_in, fgu_in, wqkv_in, ga_in, ein_ref, eout_ref, out_in, gin_in, fsd_in, fwo_in,
    gq_to, gr_to, gga_to, ggf_to, ggu_to, oin_ref, oout_ref, out_to, gin_to, fsd_to, fwo_to,
    narrow_in, narrow_out, wide_in, wide_out,
    fq_ref, fgu_ref, wqkv_ref, ga_ref, out_ref, gin_ref, fsd_ref, fwo_ref,
    gq_ref, gr_ref, gga_ref, ggf_ref, ggu_ref, sems, isem, osem,
):
    pieces = []
    for e in range(ein_ref.shape[0]):
        for source, narrow, widened, target in (
            (ein_ref, narrow_in, wide_in, oin_ref),
            (eout_ref, narrow_out, wide_out, oout_ref),
        ):
            rows = source.shape[1] // WIDEN
            for k in range(WIDEN):
                at = (e, pl.ds(k * rows, rows))
                pieces.append((at, source, narrow, widened, target))
    loads = [
        pltpu.make_async_copy(source, target, isem.at[i])
        for i, (source, target) in enumerate(
            (
                (fq_in, fq_ref), (fgu_in, fgu_ref), (wqkv_in, wqkv_ref), (ga_in, ga_ref),
                (out_in, out_ref), (gin_in, gin_ref), (fsd_in, fsd_ref), (fwo_in, fwo_ref),
            )
        )
    ]
    arriving = []
    for i, (at, source, narrow, _, _) in enumerate(pieces):
        arriving.append(pltpu.make_async_copy(source.at[at], narrow.at[at], sems.at[0, i]))
        arriving[-1].start()
        if i == 1:
            for load in loads:
                load.start()
    stores = []

    def store(source, target):
        stores.append(pltpu.make_async_copy(source, target, osem.at[len(stores)]))
        stores[-1].start()

    leaving = []

    def widen(i):
        at, _, narrow, widened, target = pieces[i]
        arriving[i].wait()
        widened[at] = narrow[at].astype(F32)
        leaving.append(pltpu.make_async_copy(widened.at[at], target.at[at], sems.at[1, i]))
        leaving[-1].start()

    for i in range(len(pieces) // 2):
        widen(i)
    for load in loads:
        load.wait()
    for source, target in (
        (out_ref, out_to), (gin_ref, gin_to), (fsd_ref, fsd_to), (fwo_ref, fwo_to)
    ):
        store(source, target)
    rows_w = wqkv_ref.shape[0]
    head_width = wqkv_ref.shape[1] // 3 // nc
    grads = jnp.concatenate(
        [
            fq_ref[i, :, side * head_width : (side + 1) * head_width].astype(F32)
            for side in range(3)
            for i in range(nc)
        ],
        axis=1,
    )
    gq_ref[...] = grads
    own_units = fgu_ref.shape[2] // 2
    ggu_ref[...] = jnp.concatenate(
        [
            fgu_ref[i, :, side * own_units : (side + 1) * own_units].astype(F32)
            for side in range(2)
            for i in range(nc)
        ],
        axis=1,
    )
    extras = jnp.sum(fq_ref[:, :, 3 * head_width - SMALL :].astype(F32), axis=0)
    num_experts = gr_ref.shape[0]
    first = jnp.sum(wqkv_ref[...].astype(F32) * grads, axis=1, keepdims=True)
    lane = lax.broadcasted_iota(jnp.int32, (rows_w, 128), 1)
    both = jnp.where(lane == SMALL + num_experts, first, extras)
    turned = jnp.transpose(
        jnp.concatenate([both, jnp.zeros((128 - rows_w, 128), F32)], axis=0), (1, 0)
    )
    gr_ref[...] = turned[SMALL : SMALL + num_experts, :rows_w]
    at = SMALL + num_experts
    gga_ref[...] = turned[at : at + 1, :rows_w] / ga_ref[...].astype(F32)
    ggf_ref[...] = turned[at + 1 : at + 2, :rows_w]

    for source, target in (
        (gq_ref, gq_to), (gr_ref, gr_to), (gga_ref, gga_to), (ggf_ref, ggf_to), (ggu_ref, ggu_to)
    ):
        store(source, target)
    for i in range(len(pieces) // 2, len(pieces)):
        widen(i)
    for copy in leaving + stores:
        copy.wait()


def vmem(*shape, dtype=jnp.bfloat16):
    return pltpu.VMEM(shape, dtype)


def fast_device(
    hidden_in, seq_lengths, expert_ids, route_rank, gain_attn, w_qkv, w_out, w_router, gain_ffn,
    w_gate_up, w_shared_down, w_experts_in, w_experts_out, grad_output,
):
    nc, nz = lax.axis_size("ctx"), lax.axis_size("exp")
    num_seqs, two_ends, half_len, width = hidden_in.shape
    shard_len = 2 * half_len
    full_len = nc * shard_len
    tok = num_seqs * shard_len
    rows_w = w_qkv.shape[0]
    head_width = w_qkv.shape[1] // 3 // nc
    num_experts = w_router.shape[1]
    down_rows = w_shared_down.shape[0]
    own_units = w_gate_up.shape[1] // 2 // nc
    half_units = w_experts_in.shape[2] // 4
    hbm, vm, sm = pl.ANY, pltpu.VMEM, pltpu.SMEM
    dma = pltpu.SemaphoreType.DMA

    seq_shape = (num_seqs, shard_len, width)
    group_shape = (num_seqs, nc, shard_len, width)
    blocks = (nc, nz, 2, rows_w)
    half_blocks = (nc, nz, rows_w)
    wide_cols = 3 * head_width + SMALL
    num_slots = num_experts * CAP
    row_box = (nz, nc, BOX, width)
    plane_tok = nc * tok
    outs = [
        (seq_shape, BF),
        (seq_shape, F32),
        ((nc, rows_w, wide_cols), BF),
        ((nc, rows_w, 2 * own_units), BF),
        ((down_rows, width), F32),
        ((rows_w, width), F32),
        (w_experts_in.shape, BF),
        (w_experts_out.shape, BF),
    ]
    small_ins = [
        expert_ids.transpose(0, 1, 3, 2),
        route_rank.reshape(1, tok),
        w_qkv,
        w_router.T,
        gain_attn.reshape(1, rows_w),
        gain_ffn.reshape(1, rows_w),
        hidden_in.reshape(seq_shape),
        w_gate_up,
        w_out,
        w_shared_down,
        grad_output.reshape(seq_shape),
    ]
    out, gin, fq, fgu, fsd, fwo, ein, eout = pl.pallas_call(
        functools.partial(block_kernel, nc, nz),
        out_shape=[jax.ShapeDtypeStruct(shape, dtype) for shape, dtype in outs],
        in_specs=[
            pl.BlockSpec(memory_space=space) for space in [sm] + [hbm] * 13
        ],
        out_specs=[pl.BlockSpec(memory_space=hbm) for _ in outs],
        scratch_shapes=[
            *[vmem(*x.shape, dtype=x.dtype) for x in small_ins],
            *[vmem(*outs[i][0], dtype=outs[i][1]) for i in (0, 1, 4, 5)],
            vmem(full_len, 256, dtype=F32),
            vmem(8, tok, dtype=jnp.int32),
            vmem(nc, 8, tok, dtype=jnp.int32),
            vmem(nc, tok, 128, dtype=F32),
            vmem(nc, 2, tok, nz * BOX),
            vmem(nc, 2, tok, nz * BOX),
            vmem(nc, 8, tok, dtype=F32),
            vmem(nc, 8, tok, dtype=F32),
            vmem(*group_shape),
            vmem(*seq_shape),
            vmem(*group_shape),
            vmem(nc, rows_w, wide_cols),
            vmem(nc, rows_w, wide_cols),
            vmem(*blocks, wide_cols),
            vmem(width, wide_cols),
            vmem(nc, rows_w, 2 * own_units),
            vmem(*blocks, 2 * own_units),
            vmem(width, 2 * own_units),
            vmem(nc, rows_w, width),
            vmem(*blocks, width),
            vmem(width, width),
            vmem(nz, 2, down_rows, width),
            vmem(width, 2 * half_units),
            vmem(half_units, width),
            vmem(num_seqs, full_len, width),
            vmem(num_seqs, full_len, 3 * head_width),
            vmem(nc, num_seqs, nc, shard_len, head_width),
            vmem(*seq_shape, dtype=F32),
            vmem(*group_shape),
            vmem(*row_box),
            vmem(2, nz, nc, BOX, width),
            vmem(2 * num_slots, width),
            vmem(2 * num_slots, width),
            vmem(2 * num_slots, width, dtype=F32),
            vmem(2 * num_slots, width, dtype=F32),
            vmem(2, num_seqs, 2, shard_len, width, dtype=F32),
            vmem(plane_tok, own_units),
            vmem(plane_tok, 2 * own_units),
            vmem(2, *group_shape),
            vmem(2, num_seqs, 2, shard_len, width),
            vmem(2, *seq_shape),
            vmem(2, *seq_shape),
            vmem(2 * num_slots, half_units),
            vmem(2 * num_slots, 2 * half_units),
            vmem(*row_box),
            vmem(*row_box),
            vmem(*row_box),
            vmem(nz, 2, down_rows, width),
            vmem(*seq_shape),
            vmem(nc, num_seqs, shard_len, head_width),
            vmem(num_seqs, nc, shard_len, head_width),
            vmem(*group_shape),
            vmem(*group_shape, dtype=F32),
            vmem(num_seqs, 2, shard_len, width),
            vmem(*seq_shape),
            vmem(*seq_shape),
            vmem(*half_blocks, 2 * own_units),
            vmem(nz - 1, nc, rows_w, 2 * own_units),
            vmem(nc, rows_w, 2 * own_units),
            vmem(*half_blocks, wide_cols),
            vmem(nz - 1, nc, rows_w, wide_cols),
            vmem(nc, rows_w, wide_cols),
            vmem(nz, down_rows, width),
            vmem(nz - 1, down_rows, width),
            vmem(*half_blocks, width),
            vmem(nz - 1, nc, rows_w, width),
            vmem(nc, rows_w, width),
            vmem(nc, rows_w, width),
            dma((POSTS,)),
            dma((POSTS,)),
            dma((1 + half_units // 256,)),
            dma((len(small_ins),)),
            dma((6,)),
        ],
        compiler_params=pltpu.CompilerParams(
            collective_id=0, has_side_effects=True, vmem_limit_bytes=VMEM_BYTES
        ),
        cost_estimate=pl.CostEstimate(
            flops=16_000_000_000, bytes_accessed=30_000_000, transcendentals=0
        ),
        name="block_forward_backward",
    )(
        seq_lengths, *small_ins, w_experts_in, w_experts_out
    )

    ins = [fq, fgu, w_qkv, gain_attn.reshape(1, rows_w), ein, eout, out, gin, fsd, fwo]
    results = [
        (w_qkv.shape, F32),
        (w_router.shape[::-1], F32),
        ((1, rows_w), F32),
        ((1, rows_w), F32),
        (w_gate_up.shape, F32),
        (ein.shape, F32),
        (eout.shape, F32),
        (seq_shape, BF),
        (seq_shape, F32),
        (fsd.shape, F32),
        (fwo.shape, F32),
    ]
    grad_qkv, grad_router, grad_ga, grad_gf, grad_gu, grad_in, grad_out, out, gin, fsd, fwo = pl.pallas_call(
        functools.partial(finish_kernel, nc),
        out_shape=[jax.ShapeDtypeStruct(shape, dtype) for shape, dtype in results],
        in_specs=[pl.BlockSpec(memory_space=hbm) for _ in ins],
        out_specs=[pl.BlockSpec(memory_space=hbm) for _ in results],
        scratch_shapes=[
            vmem(*ein.shape),
            vmem(*eout.shape),
            vmem(*ein.shape, dtype=F32),
            vmem(*eout.shape, dtype=F32),
            *[vmem(*ins[i].shape, dtype=ins[i].dtype) for i in (0, 1, 2, 3, 6, 7, 8, 9)],
            *[vmem(*results[i][0], dtype=results[i][1]) for i in range(5)],
            dma((2, 2 * ein.shape[0] * WIDEN)),
            dma((8,)),
            dma((9,)),
        ],
        compiler_params=pltpu.CompilerParams(vmem_limit_bytes=VMEM_BYTES),
        name="widen_gradients",
    )(*ins)
    return (
        out.reshape(hidden_in.shape),
        gin.reshape(hidden_in.shape),
        grad_ga.reshape(rows_w),
        grad_qkv,
        fwo,
        grad_router.T,
        grad_gf.reshape(rows_w),
        grad_gu,
        fsd,
        grad_in,
        grad_out,
    )


def fits(mesh, hidden_in, w_qkv, w_router, w_gate_up, w_experts_in):
    nc, nz, nf = mesh.shape["ctx"], mesh.shape["exp"], mesh.shape["fsdp"]
    heads = w_qkv.shape[1] // 3 // HS
    return (
        nf == 2
        and nc == 4
        and nz == 4
        and heads == 12
        and w_router.shape[1] == nc * nz
        and w_qkv.shape[0] == 768
        and hidden_in.shape[2] == 32 * nc
        and hidden_in.shape[0] == 2 * nz * nf
        and hidden_in.shape[3] == 768
        and w_gate_up.shape[1] == w_experts_in.shape[2] == 4096
        and 2 * CAP <= BOX
    )


def solution(mesh):
    def whole(*args):
        chosen = fast_device if fits(mesh, args[0], args[5], args[7], args[9], args[11]) else per_device
        return placed(mesh, chosen)(*args)

    return whole


def placed(mesh, chosen):
    return jax.shard_map(
        chosen,
        mesh=mesh,
        in_specs=(
            P(("exp", "fsdp"), None, "ctx", None),
            P(("exp", "fsdp")),
            P(("exp", "fsdp"), None, "ctx", None),
            P(("exp", "fsdp"), "ctx", None),
            P(("ctx", "exp", "fsdp")),
            P(("ctx", "exp", "fsdp"), None),
            P(("ctx", "exp", "fsdp"), None),
            P(("ctx", "exp", "fsdp"), None),
            P(("ctx", "exp", "fsdp")),
            P(("ctx", "exp", "fsdp"), None),
            P(("ctx", "exp", "fsdp"), None),
            P("exp", ("ctx", "fsdp"), None),
            P("exp", ("ctx", "fsdp"), None),
            P(("exp", "fsdp"), None, "ctx", None),
        ),
        out_specs=(
            P(("exp", "fsdp"), None, "ctx", None),
            P(("exp", "fsdp"), None, "ctx", None),
            P(("ctx", "exp", "fsdp")),
            P(("ctx", "exp", "fsdp"), None),
            P(("ctx", "exp", "fsdp"), None),
            P(("ctx", "exp", "fsdp"), None),
            P(("ctx", "exp", "fsdp")),
            P(("ctx", "exp", "fsdp"), None),
            P(("ctx", "exp", "fsdp"), None),
            P("exp", ("ctx", "fsdp"), None),
            P("exp", ("ctx", "fsdp"), None),
        ),
        check_vma=False,
    )
```

```python
import functools
import math

import jax
import jax.numpy as jnp
from jax import lax
from jax.experimental import pallas as pl
from jax.experimental.pallas import tpu as pltpu
from jax.sharding import PartitionSpec as P

HS = 64
CAP = 18


epsilon = 1e-06
masked_out = -1e30
highest = lax.Precision.HIGHEST


def rms_norm(values_in, gain_row):
    return (
        values_in
        * lax.rsqrt(jnp.mean(values_in * values_in, axis=-1, keepdims=True) + epsilon)
        * gain_row
    )


def rope_tables(places):
    half_size = HS // 2
    frequency = 10000.0 ** (-jnp.arange(half_size, dtype=jnp.float32) * 2.0 / HS)
    angles = places.astype(jnp.float32)[:, None] * frequency[None, :]
    return (jnp.cos(angles), jnp.sin(angles))


def rotate(values_in, cosines, sine_rows):
    half_size = values_in.shape[-1] // 2
    leading = values_in[..., :half_size]
    trailing = values_in[..., half_size:]
    cos_rows = cosines[:, None, :]
    sin_rows = sine_rows[:, None, :]
    return jnp.concatenate(
        [leading * cos_rows - trailing * sin_rows, leading * sin_rows + trailing * cos_rows],
        axis=-1,
    )


def swiglu(merged_rows):
    gate_part, up_part = jnp.split(merged_rows, 2, axis=-1)
    return jax.nn.silu(gate_part) * up_part


def first_t(left_side, right_side, precision=None):
    return lax.dot_general(
        left_side,
        right_side,
        (((0,), (0,)), ((), ())),
        precision=precision,
        preferred_element_type=jnp.float32,
    )


def second_t(left_side, right_side, precision=None):
    return lax.dot_general(
        left_side,
        right_side,
        (((1,), (1,)), ((), ())),
        precision=precision,
        preferred_element_type=jnp.float32,
    )


def per_device(
    hidden_in,
    seq_lengths,
    expert_ids,
    route_rank,
    gain_attn,
    w_qkv,
    w_out,
    w_router,
    gain_ffn,
    w_gate_up,
    w_shared_down,
    w_experts_in,
    w_experts_out,
    grad_output,
):
    num_seqs, two_ends, half_len, model_width = hidden_in.shape
    shard_len = 2 * half_len
    tok_count = num_seqs * shard_len
    num_heads = model_width // HS
    score_scale = HS ** (-0.5)
    ctx_size = lax.axis_size("ctx")
    full_len = shard_len * ctx_size
    whole_half = half_len * ctx_size
    gain_one, wqkv_all, wout_all, router_all, gain_two, shared_in, shared_down = (
        lax.all_gather(gain_attn, ("ctx", "exp", "fsdp"), axis=0, tiled=True),
        lax.all_gather(w_qkv, ("ctx", "exp", "fsdp"), axis=0, tiled=True),
        lax.all_gather(w_out, ("ctx", "exp", "fsdp"), axis=0, tiled=True),
        lax.all_gather(w_router, ("ctx", "exp", "fsdp"), axis=0, tiled=True),
        lax.all_gather(gain_ffn, ("ctx", "exp", "fsdp"), axis=0, tiled=True),
        lax.all_gather(w_gate_up, ("ctx", "exp", "fsdp"), axis=0, tiled=True),
        lax.all_gather(w_shared_down, ("ctx", "exp", "fsdp"), axis=0, tiled=True),
    )
    experts_in, experts_out = (
        lax.all_gather(w_experts_in, ("ctx", "fsdp"), axis=1, tiled=True),
        lax.all_gather(w_experts_out, ("ctx", "fsdp"), axis=1, tiled=True),
    )
    lower_places = lax.axis_index("ctx") * half_len + jnp.arange(half_len, dtype=jnp.int32)
    places = jnp.concatenate([lower_places, full_len - 1 - lower_places])
    whole_range = jnp.arange(whole_half, dtype=jnp.int32)
    full_places = jnp.concatenate([whole_range, full_len - 1 - whole_range])
    live_mask = (places[None, :] < seq_lengths[:, None]).astype(jnp.float32)
    live_rows = live_mask.reshape(tok_count, 1)
    inputs_f = hidden_in.astype(jnp.float32).reshape(tok_count, model_width)
    gain_attn_f = gain_one.astype(jnp.float32)
    normed_b = rms_norm(inputs_f, gain_attn_f).astype(jnp.bfloat16)
    qkv_merged = jnp.dot(normed_b, wqkv_all, preferred_element_type=jnp.float32).reshape(
        num_seqs, shard_len, 3, num_heads, HS
    )
    cosines, sine_rows = rope_tables(places)
    queries = rotate(qkv_merged[:, :, 0], cosines, sine_rows).astype(jnp.bfloat16)
    keys_local = rotate(qkv_merged[:, :, 1], cosines, sine_rows).astype(jnp.bfloat16)
    values_local = qkv_merged[:, :, 2].astype(jnp.bfloat16)
    end_shape = (num_seqs, 2, half_len, model_width)
    keys_full, values_full = (
        lax.all_gather(keys_local.reshape(end_shape), "ctx", axis=2, tiled=True),
        lax.all_gather(values_local.reshape(end_shape), "ctx", axis=2, tiled=True),
    )
    keys_full = keys_full.reshape(num_seqs, full_len, num_heads, HS)
    values_full = values_full.reshape(num_seqs, full_len, num_heads, HS)
    stat_shape = (num_seqs, num_heads, shard_len)
    block_range = jnp.arange(ctx_size, dtype=jnp.int32)

    def block_scores(query_rows, query_places, key_rows, key_places):
        scores = (
            jnp.einsum("bqhd,bkhd->bhqk", query_rows, key_rows, preferred_element_type=jnp.float32)
            * score_scale
        )
        allowed = (key_places[None, None, :] <= query_places[None, :, None]) & (
            key_places[None, None, :] < seq_lengths[:, None, None]
        )
        return jnp.where(allowed[:, None], scores, masked_out)

    def key_block(block_idx):
        offset = block_idx * shard_len
        return (
            lax.dynamic_slice_in_dim(keys_full, offset, shard_len, 1),
            lax.dynamic_slice_in_dim(values_full, offset, shard_len, 1),
            lax.dynamic_slice_in_dim(full_places, offset, shard_len, 0),
        )

    def lse_step(state_in, block_idx):
        run_max, run_sum = state_in
        key_rows, value_rows, key_places = key_block(block_idx)
        scores = block_scores(queries, places, key_rows, key_places)
        new_max = jnp.maximum(run_max, jnp.max(scores, axis=-1))
        run_sum = run_sum * jnp.exp(run_max - new_max) + jnp.sum(
            jnp.exp(scores - new_max[..., None]), axis=-1
        )
        return ((new_max, run_sum), None)

    (row_max, row_sum), unused = lax.scan(
        lse_step,
        (jnp.full(stat_shape, masked_out, jnp.float32), jnp.zeros(stat_shape, jnp.float32)),
        block_range,
    )
    log_total = row_max + jnp.log(row_sum)

    def context_step(running, block_idx):
        key_rows, value_rows, key_places = key_block(block_idx)
        prob_rows = jnp.exp(
            block_scores(queries, places, key_rows, key_places) - log_total[..., None]
        ).astype(jnp.bfloat16)
        return (
            running
            + jnp.einsum(
                "bhqk,bkhd->bqhd", prob_rows, value_rows, preferred_element_type=jnp.float32
            ),
            None,
        )

    context, unused = lax.scan(
        context_step, jnp.zeros((num_seqs, shard_len, num_heads, HS), jnp.float32), block_range
    )
    context_b = context.reshape(tok_count, model_width).astype(jnp.bfloat16)
    attended = inputs_f + jnp.dot(context_b, wout_all, preferred_element_type=jnp.float32)
    gain_ffn_f = gain_two.astype(jnp.float32)
    normed_two = rms_norm(attended, gain_ffn_f).astype(jnp.bfloat16)
    logits = jnp.dot(normed_two, router_all, preferred_element_type=jnp.float32)
    num_experts = router_all.shape[1]
    expert_range = jnp.arange(num_experts, dtype=jnp.int32)
    picked_ids = expert_ids.reshape(tok_count, 2)
    pick_hot = (picked_ids[:, :, None] == expert_range).astype(jnp.float32)
    chosen = jnp.sum(pick_hot * logits[:, None, :], axis=-1)
    gate_probs = jax.nn.softmax(chosen, axis=-1)
    expert_load = (jnp.sum(pick_hot, axis=1) * live_rows).astype(jnp.bfloat16)
    rank_rows = route_rank.reshape(tok_count)
    earlier = (rank_rows[None, :] < rank_rows[:, None]).astype(jnp.bfloat16)
    position = jnp.dot(earlier, expert_load, preferred_element_type=jnp.float32)
    chosen_pos = jnp.sum(pick_hot * position[:, None, :], axis=-1)
    kept_mask = live_rows * (chosen_pos < CAP).astype(jnp.float32)
    slot_hot = (chosen_pos[:, :, None] == jnp.arange(CAP, dtype=jnp.float32)).astype(jnp.float32)
    dispatch = (
        (pick_hot[:, :, :, None] * slot_hot[:, :, None, :] * kept_mask[:, :, None, None])
        .reshape(tok_count, 2, num_experts * CAP)
        .astype(jnp.bfloat16)
    )
    dispatch_any = dispatch[:, 0] + dispatch[:, 1]
    exp_size = lax.axis_size("exp")
    per_owner = num_experts // exp_size
    send_rows = (
        first_t(dispatch_any, normed_two)
        .astype(jnp.bfloat16)
        .reshape(exp_size, per_owner, CAP, model_width)
    )
    arrived = lax.all_to_all(send_rows, "exp", split_axis=0, concat_axis=0, tiled=True)
    expert_merged = jnp.einsum(
        "secd,edf->secf", arrived, experts_in, preferred_element_type=jnp.float32
    )
    expert_hidden = swiglu(expert_merged).astype(jnp.bfloat16)
    expert_result = jnp.einsum(
        "secf,efd->secd", expert_hidden, experts_out, preferred_element_type=jnp.float32
    ).astype(jnp.bfloat16)
    returned = lax.all_to_all(
        expert_result, "exp", split_axis=0, concat_axis=0, tiled=True
    ).reshape(num_experts * CAP, model_width)
    routed = jnp.einsum("tks,sd->tkd", dispatch, returned, preferred_element_type=jnp.float32)
    mixture = jnp.sum(gate_probs[:, :, None] * routed, axis=1)
    shared_merged = jnp.dot(normed_two, shared_in, preferred_element_type=jnp.float32)
    shared_hidden = swiglu(shared_merged).astype(jnp.bfloat16)
    shared_result = jnp.dot(shared_hidden, shared_down, preferred_element_type=jnp.float32)
    layer_out = (
        (live_rows * (attended + mixture + shared_result)).reshape(end_shape).astype(jnp.bfloat16)
    )
    upstream = grad_output.astype(jnp.float32).reshape(tok_count, model_width) * live_rows
    upstream_b = upstream.astype(jnp.bfloat16)
    upstream_f = upstream_b.astype(jnp.float32)
    d_shared_down = first_t(shared_hidden, upstream_b)
    d_shared_hidden = second_t(upstream_b, shared_down)
    unused, swiglu_pull = jax.vjp(swiglu, shared_merged)
    d_shared_merged = swiglu_pull(d_shared_hidden)[0].astype(jnp.bfloat16)
    d_shared_in = first_t(normed_two, d_shared_merged)
    d_normed_two = second_t(d_shared_merged, shared_in)
    gate_grads = jnp.sum(routed * upstream_f[:, None, :], axis=-1)
    weighted = (gate_probs[:, :, None] * upstream_f[:, None, :]).astype(jnp.bfloat16)
    d_returned = (
        jnp.einsum("tks,tkd->sd", dispatch, weighted, preferred_element_type=jnp.float32)
        .astype(jnp.bfloat16)
        .reshape(exp_size, per_owner, CAP, model_width)
    )
    d_result = lax.all_to_all(d_returned, "exp", split_axis=0, concat_axis=0, tiled=True)
    d_experts_out = jnp.einsum(
        "secf,secd->efd", expert_hidden, d_result, preferred_element_type=jnp.float32
    )
    d_expert_hidden = jnp.einsum(
        "secd,efd->secf", d_result, experts_out, preferred_element_type=jnp.float32
    )
    unused, expert_pull = jax.vjp(swiglu, expert_merged)
    d_expert_merged = expert_pull(d_expert_hidden)[0].astype(jnp.bfloat16)
    d_experts_in = jnp.einsum(
        "secd,secf->edf", arrived, d_expert_merged, preferred_element_type=jnp.float32
    )
    d_arrived = jnp.einsum(
        "secf,edf->secd", d_expert_merged, experts_in, preferred_element_type=jnp.float32
    ).astype(jnp.bfloat16)
    d_sent = lax.all_to_all(d_arrived, "exp", split_axis=0, concat_axis=0, tiled=True).reshape(
        num_experts * CAP, model_width
    )
    d_normed_two = d_normed_two + jnp.dot(dispatch_any, d_sent, preferred_element_type=jnp.float32)
    unused, gate_pull = jax.vjp(lambda chosen_in: jax.nn.softmax(chosen_in, axis=-1), chosen)
    d_chosen = gate_pull(gate_grads)[0]
    d_logits = jnp.sum(pick_hot * d_chosen[:, :, None], axis=1)
    d_router = first_t(normed_two.astype(jnp.float32), d_logits, highest)
    d_normed_two = d_normed_two + second_t(d_logits, router_all.astype(jnp.float32), highest)
    unused, second_pull = jax.vjp(rms_norm, attended, gain_ffn_f)
    d_attended, d_gain_ffn = second_pull(d_normed_two)
    d_attended = d_attended + upstream
    d_attended_b = d_attended.astype(jnp.bfloat16)
    d_out_proj = first_t(context_b, d_attended_b)
    d_context = (
        second_t(d_attended_b, wout_all)
        .astype(jnp.bfloat16)
        .reshape(num_seqs, shard_len, num_heads, HS)
    )

    def score_grads(
        query_rows, query_places, key_rows, value_rows, key_places, d_rows, lse_rows, delta_rows
    ):
        prob_rows = jnp.exp(
            block_scores(query_rows, query_places, key_rows, key_places) - lse_rows[..., None]
        )
        d_probs = jnp.einsum(
            "bqhd,bkhd->bhqk", d_rows, value_rows, preferred_element_type=jnp.float32
        )
        d_scores = (prob_rows * (d_probs - delta_rows[..., None])).astype(jnp.bfloat16)
        return (prob_rows.astype(jnp.bfloat16), d_scores)

    def delta_step(running, block_idx):
        key_rows, value_rows, key_places = key_block(block_idx)
        prob_rows = jnp.exp(
            block_scores(queries, places, key_rows, key_places) - log_total[..., None]
        )
        d_probs = jnp.einsum(
            "bqhd,bkhd->bhqk", d_context, value_rows, preferred_element_type=jnp.float32
        )
        return (running + jnp.sum(prob_rows * d_probs, axis=-1), None)

    row_delta, unused = lax.scan(delta_step, jnp.zeros(stat_shape, jnp.float32), block_range)
    head_shape = (num_seqs, shard_len, num_heads, HS)

    def query_step(d_query, block_idx):
        key_rows, value_rows, key_places = key_block(block_idx)
        prob_b, d_scores = score_grads(
            queries, places, key_rows, value_rows, key_places, d_context, log_total, row_delta
        )
        return (
            d_query
            + jnp.einsum("bhqk,bkhd->bqhd", d_scores, key_rows, preferred_element_type=jnp.float32)
            * score_scale,
            None,
        )

    d_query, unused = lax.scan(query_step, jnp.zeros(head_shape, jnp.float32), block_range)
    query_all, d_context_all = (
        lax.all_gather(queries.reshape(end_shape), "ctx", axis=2, tiled=True),
        lax.all_gather(d_context.reshape(end_shape), "ctx", axis=2, tiled=True),
    )
    stat_ends = (num_seqs, num_heads, 2, half_len)
    lse_all, delta_all = (
        lax.all_gather(log_total.reshape(stat_ends), "ctx", axis=3, tiled=True),
        lax.all_gather(row_delta.reshape(stat_ends), "ctx", axis=3, tiled=True),
    )
    query_all = query_all.reshape(num_seqs, full_len, num_heads, HS)
    d_context_all = d_context_all.reshape(num_seqs, full_len, num_heads, HS)
    lse_all = lse_all.reshape(num_seqs, num_heads, full_len)
    delta_all = delta_all.reshape(num_seqs, num_heads, full_len)

    def owner_step(state_in, block_idx):
        d_keys, d_values = state_in
        offset = block_idx * shard_len
        query_rows = lax.dynamic_slice_in_dim(query_all, offset, shard_len, 1)
        d_rows = lax.dynamic_slice_in_dim(d_context_all, offset, shard_len, 1)
        lse_rows = lax.dynamic_slice_in_dim(lse_all, offset, shard_len, 2)
        delta_rows = lax.dynamic_slice_in_dim(delta_all, offset, shard_len, 2)
        query_places = lax.dynamic_slice_in_dim(full_places, offset, shard_len, 0)
        prob_b, d_scores = score_grads(
            query_rows, query_places, keys_local, values_local, places, d_rows, lse_rows, delta_rows
        )
        d_keys = (
            d_keys
            + jnp.einsum(
                "bhqk,bqhd->bkhd", d_scores, query_rows, preferred_element_type=jnp.float32
            )
            * score_scale
        )
        d_values = d_values + jnp.einsum(
            "bhqk,bqhd->bkhd", prob_b, d_rows, preferred_element_type=jnp.float32
        )
        return ((d_keys, d_values), None)

    (d_keys_local, d_values_local), unused = lax.scan(
        owner_step,
        (jnp.zeros(head_shape, jnp.float32), jnp.zeros(head_shape, jnp.float32)),
        block_range,
    )
    unused, rope_pull = jax.vjp(
        lambda rows_in: rotate(rows_in, cosines, sine_rows), qkv_merged[:, :, 0]
    )
    d_query_pre = rope_pull(d_query)[0]
    d_key_pre = rope_pull(d_keys_local)[0]
    d_qkv_merged = (
        jnp.stack([d_query_pre, d_key_pre, d_values_local], axis=2)
        .reshape(tok_count, 3 * model_width)
        .astype(jnp.bfloat16)
    )
    d_qkv = first_t(normed_b, d_qkv_merged)
    d_normed = second_t(d_qkv_merged, wqkv_all)
    unused, first_pull = jax.vjp(rms_norm, inputs_f, gain_attn_f)
    d_inputs, d_gain_attn = first_pull(d_normed)
    grad_input = (d_attended + d_inputs).reshape(end_shape)
    dense_sums = (
        lax.psum_scatter(d_gain_attn, ("ctx", "exp", "fsdp"), scatter_dimension=0, tiled=True),
        lax.psum_scatter(d_qkv, ("ctx", "exp", "fsdp"), scatter_dimension=0, tiled=True),
        lax.psum_scatter(d_out_proj, ("ctx", "exp", "fsdp"), scatter_dimension=0, tiled=True),
        lax.psum_scatter(d_router, ("ctx", "exp", "fsdp"), scatter_dimension=0, tiled=True),
        lax.psum_scatter(d_gain_ffn, ("ctx", "exp", "fsdp"), scatter_dimension=0, tiled=True),
        lax.psum_scatter(d_shared_in, ("ctx", "exp", "fsdp"), scatter_dimension=0, tiled=True),
        lax.psum_scatter(d_shared_down, ("ctx", "exp", "fsdp"), scatter_dimension=0, tiled=True),
    )
    expert_sums = (
        lax.psum_scatter(
            d_experts_in.astype(jnp.bfloat16), ("ctx", "fsdp"), scatter_dimension=1, tiled=True
        ).astype(jnp.float32),
        lax.psum_scatter(
            d_experts_out.astype(jnp.bfloat16), ("ctx", "fsdp"), scatter_dimension=1, tiled=True
        ).astype(jnp.float32),
    )
    return (
        layer_out,
        grad_input,
        dense_sums[0],
        dense_sums[1],
        dense_sums[2],
        dense_sums[3],
        dense_sums[4],
        dense_sums[5],
        dense_sums[6],
        expert_sums[0],
        expert_sums[1],
    )


F32 = jnp.float32
BF = jnp.bfloat16
MESH = pl.DeviceIdType.MESH
BOX = 40
SMALL = 64
VMEM_BYTES = 63 * 1024 * 1024
PUMPS = (3, 10, 12, 0, 4, 4)
POSTS = 64
EARLY = 2
LATE = 0
WIDEN = 1


def place():
    return lax.axis_index("ctx"), lax.axis_index("exp"), lax.axis_index("fsdp")


def wrap(value, size):
    return lax.rem(value, size)


def mm(left, right):
    return lax.dot_general(
        left, right, (((1,), (0,)), ((), ())), preferred_element_type=F32
    )


def mm_nt(left, right):
    return lax.dot_general(
        left, right, (((1,), (1,)), ((), ())), preferred_element_type=F32
    )


def mm_tn(left, right):
    return lax.dot_general(
        left, right, (((0,), (0,)), ((), ())), preferred_element_type=F32
    )


def greet(peers):
    barrier = pltpu.get_barrier_semaphore()
    for peer in peers:
        pl.semaphore_signal(barrier, inc=1, device_id=peer, device_id_type=MESH)


def met(peers):
    pl.semaphore_wait(pltpu.get_barrier_semaphore(), len(peers))


class Post:
    def __init__(self, send, recv, like, device):
        self.send, self.recv, self.like, self.device = send, recv, like, device

    def add(self, src, dst, device):
        pltpu.make_async_remote_copy(
            src_ref=src,
            dst_ref=dst,
            send_sem=self.send,
            recv_sem=self.recv,
            device_id=device,
            device_id_type=MESH,
        ).start()

    def all_of_it(self, like=None):
        like = self.like if like is None else like
        return pltpu.make_async_remote_copy(
            src_ref=like,
            dst_ref=like,
            send_sem=self.send,
            recv_sem=self.recv,
            device_id=self.device,
            device_id_type=MESH,
        )

    def wait_recv(self, like=None):
        self.all_of_it(like).wait_recv()

    def wait_send(self, like=None):
        self.all_of_it(like).wait_send()


class Courier:
    def __init__(self, send, recv, device):
        self.send, self.recv, self.device, self.count, self.sent = send, recv, device, 0, []

    def open(self, like, keep=True):
        post = Post(self.send.at[self.count], self.recv.at[self.count], like, self.device)
        self.count += 1
        if keep:
            self.sent.append(post)
        return post

    def at(self, index, like):
        return Post(self.send.at[index], self.recv.at[index], like, self.device)

    def post(self, like, moves):
        post = self.open(like)
        for src, dst, device in moves:
            post.add(src, dst, device)
        return post

    def settle(self, posts):
        for post in posts:
            post.wait_send()
        done = {id(post) for post in posts}
        self.sent = [post for post in self.sent if id(post) not in done]

    def finish(self):
        self.settle(list(self.sent))


def swap_halves(rows):
    width = rows.shape[1]
    lane = lax.broadcasted_iota(jnp.int32, rows.shape, 1)
    ahead = pltpu.roll(rows, width - HS // 2, 1)
    behind = pltpu.roll(rows, HS // 2, 1)
    return jnp.where((lane & (HS - 1)) < HS // 2, -ahead, behind)


def wide(table, times):
    return jnp.concatenate([table] * times, axis=1)


def position_of(index, half_len, full_len):
    block = index // (2 * half_len)
    inside = index & (2 * half_len - 1)
    low = block * half_len + (inside & (half_len - 1))
    return jnp.where(inside >= half_len, full_len - 1 - low, low)


def allowed_keys(length, half_len, full_len):
    shape = (full_len, full_len)
    query_at = position_of(lax.broadcasted_iota(jnp.int32, shape, 0), half_len, full_len)
    key_at = position_of(lax.broadcasted_iota(jnp.int32, shape, 1), half_len, full_len)
    return (key_at <= query_at) & (key_at < length)


def head_probs(query, key, allowed):
    scores = jnp.where(allowed, mm_nt(query, key) * (HS**-0.5), masked_out)
    weights = jnp.exp(scores - jnp.max(scores, axis=1, keepdims=True))
    return weights * (1.0 / jnp.sum(weights, axis=1, keepdims=True))


def column_row(tail, lane):
    pick = (lax.broadcasted_iota(jnp.int32, (8, 128), 1) == lane).astype(BF)
    return mm_nt(pick, tail)[0:1]


def split_dot(dot, left, right, left_wide=True):
    whole = left if left_wide else right
    high = whole.astype(BF)
    low = (whole - high.astype(F32)).astype(BF)
    if left_wide:
        return dot(high, right) + dot(low, right)
    return dot(left, high) + dot(left, low)


def inverse_rms(rows):
    return lax.rsqrt(jnp.mean(rows * rows, axis=1, keepdims=True) + epsilon)


def norm_back(rows, inverse, scaled):
    return inverse * scaled - rows * (inverse * inverse * inverse) * jnp.mean(
        rows * scaled, axis=1, keepdims=True
    )


def join(blocks, shape):
    return blocks.astype(F32).reshape(shape).astype(BF)


def ffn_block(j, rows, grads, in_ref, out_ref, hidden_ref, dm_ref, result, back, units, step):
    low = pl.multiple_of(j * step, step) if not isinstance(j, int) else j * step
    high = pl.multiple_of(units + low, step) if not isinstance(j, int) else units + low
    gate_at, up_at = pl.ds(low, step), pl.ds(high, step)
    gate, up = mm(rows, in_ref[:, gate_at]), mm(rows, in_ref[:, up_at])
    down = out_ref[gate_at, :]
    d_hidden = mm_nt(grads, down)
    share = 1.0 / (1.0 + jnp.exp(-gate))
    lit = gate * share
    hidden = (lit * up).astype(BF)
    d_gate = (d_hidden * up * (share * (1.0 + gate * (1.0 - share)))).astype(BF)
    d_up = (d_hidden * lit).astype(BF)
    hidden_ref[:, gate_at] = hidden
    dm_ref[:, gate_at] = d_gate
    dm_ref[:, up_at] = d_up
    result[...] += mm(hidden, down)
    back[...] += mm_nt(d_gate, in_ref[:, gate_at]) + mm_nt(d_up, in_ref[:, up_at])


def box_rows(kept_rows, boxes, shift):
    shape = (boxes * kept_rows, boxes * BOX)
    row = lax.broadcasted_iota(jnp.int32, shape, 0)
    column = lax.broadcasted_iota(jnp.int32, shape, 1)
    box = jnp.floor((column.astype(F32) + 0.5) * (1.0 / BOX)).astype(jnp.int32)
    at = column - box * BOX - shift
    return ((at >= 0) & (at < kept_rows) & (row == box * kept_rows + at)).astype(BF)


def block_kernel(
    nc, nz,
    len_ref, ids_in, rank_in, wqkv_in, router_in, ga_in, gf_in, hid_in, gu_in, wo_in, sd_in, go_in,
    win_ref, wout_ref,
    out_to, gin_to, fq_ref, fgu_ref, fsd_to, fwo_to, ein_ref, eout_ref,
    ids_ref, rank_ref, wqkv_ref, router_ref, ga_ref, gf_ref, hid_ref, gu_ref, wo_ref, sd_ref, go_ref,
    out_ref, gin_ref, fsd_ref, fwo_ref,
    turn_ref, meta_own, meta_all, picks, hot_x, hot_d, dg_send, dg_in, hid_all, up_own, up_all, wq_own, wq_st, wq_buf, w_ref, gu_st, gu_buf, gu_all, wo_st, wo_buf,
    wo_all, sd_all, wie, woe, normed_ref, qkv_ref, probs_all, ctx_all, att_own, nt_all,
    sb, ar, xs, ds, acc_a, acc_b, sh_own, sh_hidden, sh_dm, sh_send, sh_in, sh_mid, sh_end,
    ex_hidden, ex_dm, pin, fb, rb, gsd, da_own, dctx_send, dctx_all, part, part_own, rs_in, rs_mid, rs_end,
    sib_gu, zi_gu, pb_gu, sib_q, zi_q, pb_q, sib_sd, zi_sd, sib_wo, zi_wo, pb_wo, in_wo,
    send, recv, lsem, isem, osem,
):
    c, z, f = place()
    near_x, near_y = c + 1 - 2 * wrap(c, 2), wrap(c + 2, nc)
    far = wrap(near_x + 2, nc)
    to_x, to_y = (near_x, z, f), (near_y, z, f)
    in_plane = [(wrap(c + s, nc), z, f) for s in range(1, nc)]
    in_column = [(c, wrap(z + s, nz), f) for s in range(1, nz)]
    steps_up = list(range(1, nz))
    sibling = (c, z, 1 - f)
    across = [(wrap(c + s, nc), z, 1 - f) for s in range(1, nc)]
    partners = in_plane + in_column + [sibling] + across
    with jax.named_scope("s_greet"):
        greet(partners)

    loads = [
        pltpu.make_async_copy(source, target, isem.at[i])
        for i, (source, target) in enumerate(
            (
                (ids_in, ids_ref), (rank_in, rank_ref), (wqkv_in, wqkv_ref),
                (router_in, router_ref), (ga_in, ga_ref), (gf_in, gf_ref), (hid_in, hid_ref),
                (gu_in, gu_ref), (wo_in, wo_ref), (sd_in, sd_ref), (go_in, go_ref),
            )
        )
    ]
    for load in loads:
        load.start()
    stores = []

    def store(source, target):
        stores.append(pltpu.make_async_copy(source, target, osem.at[len(stores)]))
        stores[-1].start()

    num_seqs, shard_len, width = hid_ref.shape
    full_len = nc * shard_len
    half_len = shard_len // 2
    tok = num_seqs * shard_len
    rows_w = wqkv_ref.shape[0]
    head_width = wqkv_ref.shape[1] // 3 // nc
    heads_here = head_width // HS
    wide_cols = wq_own.shape[2]
    units = gu_ref.shape[1] // 2
    own_units = units // nc
    down_rows = sd_ref.shape[0]
    num_experts = nz * nc
    num_slots = num_experts * CAP
    column_slots = nz * BOX
    block_rows = nz * 2 * rows_w
    mail = Courier(send, recv, sibling)

    for load in loads:
        load.wait()
    small = jnp.concatenate(
        [
            router_ref[...].astype(F32),
            ga_ref[...].astype(F32),
            gf_ref[...].astype(F32),
            jnp.zeros((128 - num_experts - 2, rows_w), F32),
        ],
        axis=0,
    )
    small = jnp.concatenate([small, jnp.zeros((128, 128 - rows_w), F32)], axis=1)
    small = jnp.transpose(small, (1, 0))[:rows_w, :SMALL].astype(BF)
    for owner in range(nc):
        wq_own[owner] = jnp.concatenate(
            [
                wqkv_ref[:, side * width + owner * head_width : side * width + (owner + 1) * head_width]
                for side in range(3)
            ]
            + [small],
            axis=1,
        )
    meta_own[...] = jnp.concatenate(
        [
            jnp.concatenate(
                [ids_ref[q, e, k : k + 1, :] for q in range(num_seqs) for e in range(2)], axis=1
            )
            for k in range(2)
        ]
        + [rank_ref[...], jnp.zeros((5, tok), jnp.int32)],
        axis=0,
    )
    with jax.named_scope("s_met"):
        met(partners)

    others = pl.ds(0, nc - 1)
    staged_wq = mail.post(
        wq_st.at[others],
        [(wq_own.at[wrap(c + s, nc)], wq_st.at[c], in_plane[s - 1]) for s in range(1, nc)],
    )
    arriving = [
        mail.post(
            hid_all.at[q, pl.ds(0, 2)],
            [(hid_ref.at[q], hid_all.at[q, c], peer) for peer in (to_x, to_y)],
        )
        for q in range(num_seqs)
    ]
    meta_copies = mail.post(
        meta_all.at[others], [(meta_own, meta_all.at[c], peer) for peer in in_plane]
    )
    staged_wo = mail.post(wo_st.at[others], [(wo_ref, wo_st.at[c], peer) for peer in in_plane])
    staged_gu = mail.open(gu_st.at[others])
    for s in range(1, nc):
        owner = wrap(c + s, nc)
        for side in range(2):
            at = pl.ds(pl.multiple_of(side * units + owner * own_units, own_units), own_units)
            staged_gu.add(
                gu_ref.at[:, at],
                gu_st.at[c, :, pl.ds(side * own_units, own_units)],
                in_plane[s - 1],
            )

    block = 2 * c + f
    shard_rows = win_ref.shape[1]
    half_units = units // 2
    step = 256
    steps = half_units // step
    lands = pl.ds(pl.multiple_of(block * shard_rows, shard_rows), shard_rows)
    out_rows = wout_ref.shape[1]
    to_core = block // nc
    slot = wrap(block, nc)
    out_lands = pl.ds(pl.multiple_of(slot * out_rows, out_rows), out_rows)
    remote_rows = (2 * nc - 1) * shard_rows
    first_in = mail.count
    expert_in = [
        mail.open(wie.at[pl.ds(0, remote_rows), pl.ds(0, 2 * step)]) for _ in range(steps)
    ]
    expert_out = mail.open(woe, keep=False)
    remote_out = woe.at[pl.ds(0, (nc - 1) * out_rows)]
    own_out = pltpu.make_async_copy(wout_ref.at[c], woe.at[out_lands], lsem.at[0])

    def send_out(s):
        owner = wrap(c + s, nc)
        expert_out.add(wout_ref.at[owner], woe.at[out_lands], (owner, z, to_core))

    def send_out_own():
        @pl.when(to_core == f)
        def _():
            own_out.start()

        @pl.when(to_core != f)
        def _():
            expert_out.add(wout_ref.at[c], woe.at[out_lands], sibling)

    def own_in(j):
        like = wie.at[pl.ds(0, shard_rows), pl.ds(0, 2 * step)]
        return pltpu.make_async_copy(like, like, lsem.at[1 + j])

    def nth_block(j, chip):
        return wrap(2 * j + j // 2 + 2 * wrap(chip, 2), steps)

    def send_in(j, s, g, side):
        owner = wrap(c + s, nc)
        at = nth_block(j, owner) * step
        core = f if g == 0 else 1 - f
        from_lane = pl.multiple_of(side * units + core * half_units + at, step)
        src = win_ref.at[owner, :, pl.ds(from_lane, step)]
        dst = wie.at[lands, pl.ds(pl.multiple_of(side * half_units + at, step), step)]
        if s == 0 and g == 0:
            pltpu.make_async_copy(src, dst, lsem.at[1 + j]).start()
        else:
            expert_in[j].add(src, dst, (owner, z, core))

    bulk = [functools.partial(send_out, s) for s in range(1, nc)] + [send_out_own]
    for j in range(steps):
        for s in range(1, nc + 1):
            for g in range(2):
                for side in range(2):
                    bulk.append(functools.partial(send_in, j, s % nc, g, side))

    def pump(queue, count):
        for _ in range(min(count, len(queue))):
            queue.pop(0)()

    with jax.named_scope("s_turns"):
        row = lax.broadcasted_iota(jnp.int32, (full_len, 128), 0)
        lane = lax.broadcasted_iota(jnp.int32, (full_len, 128), 1) & (HS // 2 - 1)
        frequency = jnp.exp(lane.astype(F32) * (-2.0 * math.log(10000.0) / HS))
        angles = position_of(row, half_len, full_len).astype(F32) * frequency
        turn_ref[:, :128] = jnp.cos(angles)
        turn_ref[:, 128:] = jnp.sin(angles)
    lane = lax.broadcasted_iota(jnp.int32, (tok, 128), 1).astype(F32)

    def live_rows(chip):
        row_at = lax.broadcasted_iota(jnp.int32, (tok, 1), 0)
        inside = row_at & (shard_len - 1)
        low = chip * half_len + (inside & (half_len - 1))
        places = jnp.where(inside >= half_len, full_len - 1 - low, low)
        lengths = jnp.zeros((tok, 1), jnp.int32)
        for q in range(num_seqs):
            lengths = jnp.where(row_at // shard_len == q, len_ref[q], lengths)
        return (places < lengths).astype(F32)

    def turned(rows):
        return jnp.transpose(
            jnp.concatenate([rows, jnp.zeros((128 - rows.shape[0], tok), F32)], axis=0), (1, 0)
        )

    def hot_lanes(columns):
        return [(lane == SMALL + columns[:, k : k + 1]).astype(F32) for k in range(2)]

    def gates_of(hots, logits):
        chosen = [jnp.sum(hot * logits, axis=1, keepdims=True) for hot in hots]
        top = jnp.maximum(chosen[0], chosen[1])
        raised = [jnp.exp(value - top) for value in chosen]
        return [value / (raised[0] + raised[1]) for value in raised]

    def route(chip):
        rows = meta_all[chip].astype(F32)
        columns = turned(rows)
        picks[chip] = columns
        hots = hot_lanes(columns)
        rank_row = jnp.broadcast_to(rows[2:3], (tok, tok))
        earlier = (rank_row < columns[:, 2:3]).astype(BF)
        live = live_rows(chip)
        position = mm(earlier, ((hots[0] + hots[1]) * live).astype(BF))
        slot_lane = lax.broadcasted_iota(jnp.int32, (tok, column_slots), 1).astype(F32)
        for k in range(2):
            at = jnp.sum(hots[k] * position, axis=1, keepdims=True)
            plane = jnp.floor((columns[:, k : k + 1] + 0.5) * (1.0 / nc))
            here = columns[:, k : k + 1] - plane * nc == c.astype(F32)
            slot_at = jnp.where((live > 0) & (at < CAP) & here, plane * BOX + at, -BOX)
            hot_x[chip, k] = (slot_lane == slot_at).astype(BF)
            hot_d[chip, k] = (slot_lane == slot_at + CAP).astype(BF)

    live = live_rows(c)
    upstream = go_ref[...].reshape(tok, width).astype(F32) * live
    up_b = upstream.astype(BF)
    up_own[...] = up_b.reshape(num_seqs, shard_len, width)
    for q in range(num_seqs):
        hid_all[q, c] = hid_ref[q]
        up_all[q, c] = up_own[q]

    def pass_on(post, buffer, q, at):
        post.wait_recv()
        origin, peer = (near_x, to_y) if q == 0 else (near_y, to_x)
        block_at = at(buffer, q, origin)
        return mail.post(block_at, [(block_at, block_at, peer)])

    def by_seq(buffer, q, chip):
        return buffer.at[q, chip]

    def by_chip(buffer, q, chip):
        return buffer.at[chip, q]

    sd_all[z, f] = sd_ref[...]
    planes = pl.ds(0, nz - 1)

    def spread(stage, staged, buffer):
        staged.wait_recv()
        post = mail.post(
            buffer.at[:, planes, 0],
            [(stage, buffer.at[:, z, f], peer) for peer in in_column],
        )
        for i in range(nc):
            buffer[i, z, f] = stage[i]
        return post

    def spread_gate_up(side):
        at = pl.ds(side * own_units, own_units)
        return mail.post(
            gu_buf.at[:, planes, 0, :, at],
            [(gu_st.at[:, :, at], gu_buf.at[:, z, f, :, at], peer) for peer in in_column],
        )

    def forward(posts, buffer):
        for post in posts:
            post.wait_recv()
        both = buffer.at[:, :, f]
        return mail.post(both, [(both, both, sibling)])

    with jax.named_scope("a_stage_wq"):
        wq_st[c] = wq_own[c]
        spread_wq = spread(wq_st, staged_wq, wq_buf)
    with jax.named_scope("a_pass_hidden"):
        passing = [pass_on(arriving[q], hid_all, q, by_seq) for q in range(num_seqs)]
    up_copies = [
        mail.post(
            up_all.at[q, pl.ds(0, 2)],
            [(up_own.at[q], up_all.at[q, c], peer) for peer in (to_x, to_y)],
        )
        for q in range(num_seqs)
    ]
    pump(bulk, PUMPS[3])
    with jax.named_scope("a_route"):
        meta_copies.wait_recv()
        meta_all[c] = meta_own[...]

        def route_one(chip, carry):
            route(chip)
            return carry

        lax.fori_loop(0, nc, route_one, 0)
    wo_st[c] = wo_ref[...]
    for side in range(2):
        at = pl.ds(pl.multiple_of(side * units + c * own_units, own_units), own_units)
        gu_st[c, :, side * own_units : (side + 1) * own_units] = gu_ref[:, at]
    with jax.named_scope("a_forward_wq"):
        passed_wq = forward([spread_wq], wq_buf)
        passed_wq.wait_recv()
        for i in range(nc):
            w_ref[i * block_rows : (i + 1) * block_rows, :] = join(
                wq_buf[i], (block_rows, wide_cols)
            )

    cosines = wide(turn_ref[:, :128], 2 * head_width // 128)
    sines = wide(turn_ref[:, 128:], 2 * head_width // 128)
    tail_at = wide_cols - 128
    attn_gain = column_row(w_ref[:, tail_at:], SMALL + num_experts)
    ctx_copies = []
    for q in range(num_seqs):
        with jax.named_scope("a_wait_hidden"):
            passing[q].wait_recv()
        with jax.named_scope("a_attention"):
            rows = hid_all[q].reshape(full_len, width).astype(F32)
            normed = (rows * inverse_rms(rows) * attn_gain).astype(BF)
            normed_ref[q] = normed
            merged = mm(normed, w_ref[:, : 3 * head_width])
            both = merged[:, : 2 * head_width]
            both = (both * cosines + swap_halves(both) * sines).astype(BF)
            values = merged[:, 2 * head_width :].astype(BF)
            qkv_ref[q, :, : 2 * head_width] = both
            qkv_ref[q, :, 2 * head_width :] = values
            allowed = allowed_keys(len_ref[q], half_len, full_len)
            heads = []
            for h in range(heads_here):
                probs = head_probs(
                    both[:, h * HS : (h + 1) * HS],
                    both[:, head_width + h * HS : head_width + (h + 1) * HS],
                    allowed,
                ).astype(BF)
                heads.append(mm(probs, values[:, h * HS : (h + 1) * HS]))
            context = jnp.concatenate(heads, axis=1).astype(BF)
            ctx_all[c, q] = context.reshape(nc, shard_len, head_width)
        ctx_copies.append(
            mail.post(
                ctx_all.at[pl.ds(0, 2), q],
                [(ctx_all.at[c, q], ctx_all.at[c, q], peer) for peer in (to_x, to_y)],
            )
        )
    spread_wo = spread(wo_st, staged_wo, wo_buf)
    with jax.named_scope("a_pass_upstream"):
        up_passing = [pass_on(up_copies[q], up_all, q, by_seq) for q in range(num_seqs)]
    with jax.named_scope("a_pass_context"):
        ctx_passing = [pass_on(ctx_copies[q], ctx_all, q, by_chip) for q in range(num_seqs)]
    pump(bulk, PUMPS[0])
    with jax.named_scope("a_forward_wo"):
        passed_wo = forward([spread_wo], wo_buf)
        staged_gu.wait_recv()
        for i in range(nc):
            gu_buf[i, z, f] = gu_st[i]
        spread_gu = [spread_gate_up(0)]
        passed_wo.wait_recv()
        for i in range(nc):
            wo_all[i * block_rows : (i + 1) * block_rows, :] = join(
                wo_buf[i], (block_rows, width)
            )
    ffn_gain = column_row(w_ref[:, tail_at:], SMALL + num_experts + 1)
    for q in range(num_seqs):
        with jax.named_scope("a_wait_context"):
            ctx_passing[q].wait_recv()
        with jax.named_scope("a_project"):
            total = hid_all[q].reshape(full_len, width).astype(F32)
            for i in range(nc):
                total = total + mm(
                    ctx_all[i, q].reshape(full_len, head_width),
                    wo_all[i * head_width : (i + 1) * head_width, :],
                )
            acc_a[q * full_len : (q + 1) * full_len] = total
            nt_all[q] = (
                (total * inverse_rms(total) * ffn_gain).astype(BF).reshape(nc, shard_len, width)
            )
    by_block = acc_a.at[pl.ds(0, nc * tok)].reshape(num_seqs, nc, shard_len, width)
    for q in range(num_seqs):
        att_own[q] = by_block[q, c]

    with jax.named_scope("b_wait_upstream"):
        for post in up_passing:
            post.wait_recv()
    with jax.named_scope("b_dispatch"):
        tail = w_ref[:, tail_at:]

        def box_rows_of(chip, carry):
            normed = jnp.concatenate([nt_all[q, chip] for q in range(num_seqs)], axis=0)
            columns = picks[chip]
            gates = gates_of(hot_lanes(columns), mm(normed, tail))
            picks[chip] = jnp.where(lane == 3, gates[0], jnp.where(lane == 4, gates[1], columns))
            up_f = jnp.concatenate([up_all[q, chip] for q in range(num_seqs)], axis=0).astype(F32)
            boxes = mm_tn(hot_x[chip, 0] + hot_x[chip, 1], normed)
            for k in range(2):
                boxes = boxes + mm_tn(hot_d[chip, k], (gates[k] * up_f).astype(BF))
            boxes = boxes.reshape(nz, BOX, width).astype(BF)
            for plane in range(nz):
                sb[plane, chip] = boxes[plane]
            return carry

        lax.fori_loop(0, nc, box_rows_of, 0)
        row_copies = [
            mail.post(ar.at[f, 0], [(sb.at[to[1]], ar.at[f, z], to)]) for to in in_column
        ]
        ar[f, z] = sb[z]
        normed = jnp.concatenate([nt_all[q, c] for q in range(num_seqs)], axis=0)
    pump(bulk, len(bulk))

    with jax.named_scope("b_forward_rows"):
        forwards = mail.open(ar.at[f])
        forwards.add(ar.at[f, z], ar.at[f, z], sibling)
        for s in range(1, nz):
            row_copies[s - 1].wait_recv()
            origin = wrap(z + nz - s, nz)
            forwards.add(ar.at[f, origin], ar.at[f, origin], sibling)
        forwards.wait_recv()
        keep_x, keep_d = (box_rows(CAP, num_experts, shift) for shift in (0, CAP))
        for core in range(2):
            at = slice(core * num_slots, (core + 1) * num_slots)
            boxes = join(ar[core], (num_experts * BOX, width))
            xs[at] = mm(keep_x, boxes).astype(BF)
            ds[at] = mm(keep_d, boxes).astype(BF)
    with jax.named_scope("b_wait_down"):
        @pl.when(to_core == f)
        def _():
            expert_out.wait_recv(remote_out)
            own_out.wait()

        @pl.when(to_core != f)
        def _():
            expert_out.wait_recv()

    gwi, gwo = wie, woe

    def expert_grads(j):
        low = nth_block(j, c) * step
        for side in range(2):
            at = pl.ds(pl.multiple_of(side * half_units + low, step), step)
            gwi[:, at] = mm_tn(xs[...], ex_dm[:, at]).astype(BF)
        at = pl.ds(pl.multiple_of(low, step), step)
        gwo[at, :] = mm_tn(ex_hidden[:, at], ds[...]).astype(BF)

    def homeward(j):
        moves = [
            functools.partial(send_home_in, j, s % nc, g, side)
            for s in range(1, nc + 1)
            for g in range(2)
            for side in range(2)
        ]
        return moves

    home = []
    home_in = mail.open(gwi.at[pl.ds(0, remote_rows)])
    home_out = mail.open(gwo, keep=False)
    remote_home = gwo.at[pl.ds(0, (nc - 1) * out_rows)]
    home_in_own = pltpu.make_async_copy(
        gwi.at[pl.ds(0, shard_rows)], gwi.at[pl.ds(0, shard_rows)], lsem.at[1]
    )

    def send_home_in(j, s, g, side):
        owner = wrap(c + s, nc)
        core = f if g == 0 else 1 - f
        from_rows = pl.ds(
            pl.multiple_of((2 * owner + core) * shard_rows, shard_rows), shard_rows
        )
        low = nth_block(j, c) * step
        to_lane = pl.multiple_of(side * units + f * half_units + low, step)
        src = gwi.at[from_rows, pl.ds(pl.multiple_of(side * half_units + low, step), step)]
        dst = ein_ref.at[c, :, pl.ds(to_lane, step)]
        if s == 0 and g == 0:
            pltpu.make_async_copy(src, dst, lsem.at[1]).start()
        else:
            home_in.add(src, dst, (owner, z, core))

    def home_rows(j):
        return gwo.at[pl.ds(pl.multiple_of(nth_block(j, c) * out_rows, out_rows), out_rows)]

    def home_out_own(j):
        return pltpu.make_async_copy(home_rows(j), eout_ref.at[c], lsem.at[0])

    def send_home_out(j):
        to_block = f * nc + nth_block(j, c)

        @pl.when(to_block == block)
        def _():
            home_out_own(j).start()

        @pl.when(to_block != block)
        def _():
            home_out.add(
                home_rows(j),
                eout_ref.at[c],
                (to_block // 2, z, wrap(to_block, 2)),
            )

    acc_a[...] = jnp.zeros(acc_a.shape, F32)
    acc_b[...] = jnp.zeros(acc_b.shape, F32)
    early = [move for j in range(EARLY) for move in homeward(j)]
    early += [functools.partial(send_home_out, j) for j in range(EARLY)]
    home = [move for j in range(EARLY, steps) for move in homeward(j)]
    home += [functools.partial(send_home_out, j) for j in range(EARLY, steps)]
    late_gate_up = mail.open(gu_buf.at[:, planes, 0, :, pl.ds(0, own_units)])
    spread_sd = mail.open(sd_all.at[planes, 0])
    spread_gu.append(late_gate_up)

    def expert_block(j, carry):
        with jax.named_scope("b_wait_experts"):
            own_in(j).wait()
            mail.at(first_in + j, expert_in[0].like).wait_recv()

        @pl.when(j == steps - 1)
        def _():
            pump(early, len(early))

        with jax.named_scope("b_experts"):
            ffn_block(
                nth_block(j, c), xs[...], ds[...], wie, woe, ex_hidden, ex_dm, acc_a, acc_b,
                half_units, step,
            )

        @pl.when(j < EARLY)
        def _():
            with jax.named_scope("b_early_grads"):
                expert_grads(j)

        @pl.when(j == LATE)
        def _():
            at = pl.ds(own_units, own_units)
            for peer in in_column:
                late_gate_up.add(gu_st.at[:, :, at], gu_buf.at[:, z, f, :, at], peer)
                spread_sd.add(sd_ref, sd_all.at[z, f], peer)

        return carry

    lax.fori_loop(0, steps, expert_block, 0)
    mail.settle(row_copies)
    pr = sb
    with jax.named_scope("b_sibling_sum"):

        def boxed(core):
            at = pl.ds(pl.multiple_of(core * num_slots, num_slots), num_slots)
            return (
                mm_tn(keep_x, acc_a[at].astype(BF)) + mm_tn(keep_d, acc_b[at].astype(BF))
            ).reshape(nz, nc, BOX, width)

        pr[...] = boxed(1 - f).astype(BF)
        swap = mail.post(pin, [(pr, pin, sibling)])
        ours = boxed(f)
        swap.wait_recv()
        fb[...] = (ours + pin[...].astype(F32)).astype(BF)
        returns = mail.post(
            rb.at[planes], [(fb.at[to[1]], rb.at[z], to) for to in in_column]
        )
        rb[z] = fb[z]
    with jax.named_scope("b_expert_grads"):

        def late_grads(j, carry):
            expert_grads(j)
            return carry

        lax.fori_loop(EARLY, steps, late_grads, 0)
    pump(home, PUMPS[1])

    with jax.named_scope("b_forward_gu"):
        passed_gu = forward(spread_gu, gu_buf)
        spread_sd.wait_recv()
        passed_sd = mail.post(sd_all.at[:, f], [(sd_all.at[:, f], sd_all.at[:, f], sibling)])
        passed_gu.wait_recv()
        passed_sd.wait_recv()
        for i in range(nc):
            gu_all[i * block_rows : (i + 1) * block_rows, :] = join(
                gu_buf[i], (block_rows, 2 * own_units)
            )
    plane_tok = nc * tok
    shared_rows = nt_all.reshape(plane_tok, width)
    shared_grads = up_all.reshape(plane_tok, width)
    shared_down = sd_all.reshape(own_units, width)
    with jax.named_scope("b_shared"):
        first = pl.ds(0, plane_tok)
        acc_a[...] = jnp.zeros(acc_a.shape, F32)
        acc_b[...] = jnp.zeros(acc_b.shape, F32)

        def shared_block(j, carry):
            ffn_block(
                j, shared_rows[...], shared_grads[...], gu_all, shared_down, sh_hidden, sh_dm,
                acc_a.at[first], acc_b.at[first], own_units, 256,
            )
            return carry

        lax.fori_loop(0, own_units // 256, shared_block, 0)
    mail.settle(spread_gu + [passed_gu])
    ggu = gu_buf
    with jax.named_scope("b_shared_grads"):

        def gate_up_grads(j, carry):
            at = pl.ds(pl.multiple_of(j * 256, 256), 256)
            piece = mm_tn(shared_rows[...], sh_dm[:, at])
            ggu[:, :, :, :, at] = piece.reshape(ggu.shape[:4] + (256,)).astype(BF)
            return carry

        lax.fori_loop(0, 2 * own_units // 256, gate_up_grads, 0)
        gsd[...] = mm_tn(sh_hidden[...], shared_grads[...]).reshape(gsd.shape).astype(BF)
        sibling_gu = mail.post(sib_gu, [(ggu.at[:, :, 1 - f], sib_gu, sibling)])
        sibling_sd = mail.post(sib_sd, [(gsd.at[:, 1 - f], sib_sd, sibling)])

    with jax.named_scope("c_probs"):
        def probs_of(q, carry):
            allowed = allowed_keys(len_ref[q], half_len, full_len)
            merged = qkv_ref[q]
            for h in range(heads_here):
                probs_all[q, h] = head_probs(
                    merged[:, h * HS : (h + 1) * HS],
                    merged[:, head_width + h * HS : head_width + (h + 1) * HS],
                    allowed,
                )
            return carry

        lax.fori_loop(0, num_seqs, probs_of, 0)
    with jax.named_scope("c_wait_returns"):
        returns.wait_recv()
    with jax.named_scope("c_column_mixture"):
        cuts = [
            acc.at[first].reshape(num_seqs, nc, shard_len, width) for acc in (acc_a, acc_b)
        ]

        def add_results(chip, carry):
            results = join(
                jnp.concatenate([rb[plane, chip].astype(F32) for plane in range(nz)], axis=0),
                (column_slots, width),
            )
            up_f = jnp.concatenate([up_all[q, chip] for q in range(num_seqs)], axis=0).astype(F32)
            gates = [picks[chip][:, 3 + k : 4 + k] for k in range(2)]
            routed = [mm(hot_x[chip, k], results) for k in range(2)]
            mixture = gates[0] * routed[0] + gates[1] * routed[1]
            d_rows = mm(hot_d[chip, 0] + hot_d[chip, 1], results)
            for q in range(num_seqs):
                at = slice(q * shard_len, (q + 1) * shard_len)
                cuts[0][q, chip] = cuts[0][q, chip] + mixture[at]
                cuts[1][q, chip] = cuts[1][q, chip] + d_rows[at]
            d_gates = [jnp.sum(routed[k] * up_f, axis=1, keepdims=True) for k in range(2)]
            spread_out = jnp.where(lane == 0, d_gates[0], jnp.where(lane == 1, d_gates[1], 0.0))
            dg_send[chip] = jnp.transpose(spread_out, (1, 0))[:8]
            return carry

        lax.fori_loop(0, nc, add_results, 0)
        for k in range(2):
            for q in range(num_seqs):
                sh_own[k, q, 0] = cuts[k][q, c]
                sh_own[k, q, 1] = cuts[k][q, near_y if q == 0 else near_x]
            sh_send[k] = cuts[k][...].astype(BF)

    def first_leg(inbox, box, lead):
        post = mail.open(inbox)
        for q in range(num_seqs):
            peer = to_x if q == 0 else to_y
            for at, chip in enumerate((near_x if q == 0 else near_y, far)):
                post.add(box.at[lead + (q, chip)], inbox.at[lead + (q, at)], peer)
        return post

    shared_first = first_leg(sh_in, sh_send, (slice(None),))
    dg_copies = mail.post(
        dg_in.at[others],
        [(dg_send.at[wrap(c + s, nc)], dg_in.at[c], in_plane[s - 1]) for s in range(1, nc)],
    )
    dg_in[c] = dg_send[c]
    pump(home, PUMPS[4])

    with jax.named_scope("b_reduce_shared"):
        def two_cores(copy, own, inbox):
            copy.wait_recv()
            inbox[...] = (own.astype(F32) + inbox[...].astype(F32)).astype(BF)

        def four_planes(copy, buffer, inbox):
            copy.wait_recv()
            for i in range(nc):
                inbox[i] = (buffer[i, :, f].astype(F32) + inbox[i].astype(F32)).astype(BF)

        four_planes(sibling_gu, ggu, sib_gu)
        two_cores(sibling_sd, gsd[:, f], sib_sd)
        gu_copies = mail.post(
            zi_gu,
            [
                (sib_gu.at[:, to[1]], zi_gu.at[up - 1], to)
                for to, up in zip(in_column, steps_up)
            ],
        )
        sd_copies = mail.post(
            zi_sd,
            [(sib_sd.at[to[1]], zi_sd.at[up - 1], to) for to, up in zip(in_column, steps_up)],
        )

    with jax.named_scope("c_second_sum"):
        shared_first.wait_recv()
        for k in range(2):
            for q in range(num_seqs):
                sh_mid[k, q] = (sh_own[k, q, 1] + sh_in[k, q, 1].astype(F32)).astype(BF)
        shared_second = mail.post(
            sh_end,
            [
                (sh_mid.at[:, q], sh_end.at[:, q], to_y if q == 0 else to_x)
                for q in range(num_seqs)
            ],
        )

    pump(home, PUMPS[5])
    with jax.named_scope("c_wait_shared"):
        dg_copies.wait_recv()
        shared_second.wait_recv()
        added, d_normed = [
            jnp.concatenate(
                [
                    sh_own[k, q, 0] + sh_in[k, q, 0].astype(F32) + sh_end[k, q].astype(F32)
                    for q in range(num_seqs)
                ],
                axis=0,
            )
            for k in range(2)
        ]
    with jax.named_scope("c_combine"):
        attended = att_own[...].reshape(tok, width)
        inverse = inverse_rms(attended)
        out_ref[...] = (live * (attended + added)).astype(BF).reshape(out_ref.shape)
        store(out_ref, out_to)
        hots = hot_lanes(picks[c])
        own_gates = gates_of(hots, mm(normed, tail))
        summed = turned(jnp.sum(dg_in[...], axis=0))
        d_gates = [summed[:, k : k + 1] for k in range(2)]
        mean_gate = own_gates[0] * d_gates[0] + own_gates[1] * d_gates[1]
        d_logits = hots[0] * (own_gates[0] * (d_gates[0] - mean_gate)) + hots[1] * (
            own_gates[1] * (d_gates[1] - mean_gate)
        )
        d_normed = d_normed + split_dot(mm_nt, d_logits, tail)
        d_attended = upstream + norm_back(attended, inverse, d_normed * ffn_gain)
        d_att_b = d_attended.astype(BF)
        d_context = mm_nt(d_att_b, wo_all[...]).astype(BF)
        for i in range(nc):
            dctx_send[i] = d_context[:, i * head_width : (i + 1) * head_width].reshape(
                num_seqs, shard_len, head_width
            )
        for q in range(num_seqs):
            dctx_all[q, c] = dctx_send[c, q]
        dctx_copies = mail.post(
            dctx_all.at[:, others],
            [
                (dctx_send.at[wrap(c + s, nc)], dctx_all.at[:, c], in_plane[s - 1])
                for s in range(1, nc)
            ],
        )
        gin_ref[...] = d_attended.reshape(gin_ref.shape)
    pump(home, PUMPS[2])

    mail.settle([spread_wo, passed_wo])
    gwo_at = wo_buf
    with jax.named_scope("c_reduce"):
        for i in range(nc):
            mine = jnp.concatenate([ctx_all[i, q, c] for q in range(num_seqs)], axis=0)
            gwo_at[i] = mm_tn(mine, d_att_b).reshape(gwo_at.shape[1:]).astype(BF)
        sibling_wo = mail.post(sib_wo, [(gwo_at.at[:, :, 1 - f], sib_wo, sibling)])
        d_router = split_dot(mm_tn, normed, d_logits, left_wide=False)
        d_gain = jnp.sum(d_normed * attended * inverse, axis=0, keepdims=True)
        turned = jnp.transpose(jnp.broadcast_to(d_gain, (128, width)), (1, 0))
        extra_lane = lax.broadcasted_iota(jnp.int32, (width, 128), 1)
        extras = jnp.where(extra_lane == SMALL + num_experts + 1, turned, d_router)
        four_planes(sibling_wo, gwo_at, sib_wo)
        wo_copies = mail.post(
            zi_wo,
            [
                (sib_wo.at[:, wrap(z + s, nz)], zi_wo.at[s - 1], in_column[s - 1])
                for s in range(1, nz)
            ],
        )

    with jax.named_scope("c_wait_dctx"):
        dctx_copies.wait_recv()
    def column_sum(own, copies, inbox):
        copies.wait_recv()
        total = own.astype(F32)
        for s in range(1, nz):
            total = total + inbox[s - 1].astype(F32)
        return total

    def hand_out(box, final):
        store(box.at[c], final.at[c])
        return mail.post(
            final.at[others],
            [(box.at[wrap(c + s, nc)], final.at[c], in_plane[s - 1]) for s in range(1, nc)],
        )

    with jax.named_scope("c_column_gu"):
        pb_gu[...] = column_sum(sib_gu[:, z], gu_copies, zi_gu).astype(BF)
        final_gu = hand_out(pb_gu, fgu_ref)
    grad_qkv = jnp.zeros((width, 3 * head_width), F32)
    merged_grads = []
    for q in range(num_seqs):
        with jax.named_scope("c_attention"):
            d_context = dctx_all[q].reshape(full_len, head_width)
            merged = qkv_ref[q]
            d_query, d_key, d_value = [], [], []
            for h in range(heads_here):
                query = merged[:, h * HS : (h + 1) * HS]
                key = merged[:, head_width + h * HS : head_width + (h + 1) * HS]
                value = merged[:, 2 * head_width + h * HS : 2 * head_width + (h + 1) * HS]
                d_head = d_context[:, h * HS : (h + 1) * HS]
                probs = probs_all[q, h]
                d_probs = mm_nt(d_head, value)
                delta = jnp.sum(probs * d_probs, axis=1, keepdims=True)
                d_scores = (probs * (d_probs - delta)).astype(BF)
                d_query.append(mm(d_scores, key) * (HS**-0.5))
                d_key.append(mm_tn(d_scores, query) * (HS**-0.5))
                d_value.append(mm_tn(probs.astype(BF), d_head))
            both = jnp.concatenate(d_query + d_key, axis=1)
            both = both * cosines - swap_halves(both) * sines
            d_merged = jnp.concatenate([both] + d_value, axis=1).astype(BF)
            merged_grads.append(d_merged)
            grad_qkv = grad_qkv + mm_tn(normed_ref[q], d_merged)
    mail.settle([spread_wq, passed_wq])
    gq = wq_buf
    with jax.named_scope("c_reduce_q"):
        last = jnp.concatenate([grad_qkv[:, tail_at:], extras[:, 3 * head_width - tail_at :]], axis=1)
        gq[...] = (
            jnp.concatenate([grad_qkv[:, :tail_at], last], axis=1).reshape(gq.shape).astype(BF)
        )
        sibling_q = mail.post(sib_q, [(gq.at[:, :, 1 - f], sib_q, sibling)])
    with jax.named_scope("c_d_normed"):
        rs_first = mail.open(rs_in)
        for q in range(num_seqs):
            d_merged = merged_grads[q]
            product = mm_nt(d_merged, w_ref[:, : 3 * head_width]).reshape(nc, shard_len, width)
            part_own[q] = product
            part[q] = product.astype(BF)
            for at, chip in enumerate((near_x if q == 0 else near_y, far)):
                rs_first.add(part.at[q, chip], rs_in.at[q, at], to_x if q == 0 else to_y)
    pump(home, len(home))
    with jax.named_scope("c_reduce_q"):
        four_planes(sibling_q, gq, sib_q)
        q_copies = mail.post(
            zi_q,
            [
                (sib_q.at[:, to[1]], zi_q.at[up - 1], to)
                for to, up in zip(in_column, steps_up)
            ],
        )
    with jax.named_scope("c_second_leg"):
        rs_first.wait_recv()
        for q in range(num_seqs):
            relay = part_own[q, near_y if q == 0 else near_x]
            rs_mid[q] = (relay + rs_in[q, 1].astype(F32)).astype(BF)
        rs_second = mail.post(
            rs_end,
            [(rs_mid.at[q], rs_end.at[q], to_y if q == 0 else to_x) for q in range(num_seqs)],
        )

    with jax.named_scope("c_column_sd"):
        fsd_ref[...] = column_sum(sib_sd[z], sd_copies, zi_sd)
        store(fsd_ref, fsd_to)
    with jax.named_scope("c_column_wo"):
        pb_wo[...] = column_sum(sib_wo[:, z], wo_copies, zi_wo).astype(BF)
        in_wo[c] = pb_wo[c]
        final_wo = mail.post(
            in_wo.at[others],
            [(pb_wo.at[wrap(c + s, nc)], in_wo.at[c], in_plane[s - 1]) for s in range(1, nc)],
        )
    with jax.named_scope("c_column_q"):
        pb_q[...] = column_sum(sib_q[:, z], q_copies, zi_q).astype(BF)
        final_q = hand_out(pb_q, fq_ref)
    with jax.named_scope("c_grad_in"):
        rs_second.wait_recv()
        for q in range(num_seqs):
            d_normed = part_own[q, c] + rs_in[q, 0].astype(F32) + rs_end[q].astype(F32)
            rows = hid_ref[q].astype(F32)
            gin_ref[q] = gin_ref[q] + norm_back(rows, inverse_rms(rows), d_normed * attn_gain)
        store(gin_ref, gin_to)
    with jax.named_scope("c_final"):
        final_wo.wait_recv()
        fwo_ref[...] = jnp.sum(in_wo[...].astype(F32), axis=0)
        store(fwo_ref, fwo_to)
        final_gu.wait_recv()
        final_q.wait_recv()
    with jax.named_scope("c_wait_home"):
        home_in_own.wait()
        home_in.wait_recv()

        @pl.when(to_core == f)
        def _():
            home_out_own(0).wait()
            home_out.wait_recv(remote_home)
            home_out.wait_send(remote_home)
            expert_out.wait_send(remote_out)

        @pl.when(to_core != f)
        def _():
            home_out.wait_recv()
            home_out.wait_send()
            expert_out.wait_send()

    assert mail.count <= POSTS, mail.count
    with jax.named_scope("z_finish"):
        for copy in stores:
            copy.wait()
        mail.finish()


def finish_kernel(
    nc, fq_in, fgu_in, wqkv_in, ga_in, ein_ref, eout_ref, out_in, gin_in, fsd_in, fwo_in,
    gq_to, gr_to, gga_to, ggf_to, ggu_to, oin_ref, oout_ref, out_to, gin_to, fsd_to, fwo_to,
    narrow_in, narrow_out, wide_in, wide_out,
    fq_ref, fgu_ref, wqkv_ref, ga_ref, out_ref, gin_ref, fsd_ref, fwo_ref,
    gq_ref, gr_ref, gga_ref, ggf_ref, ggu_ref, sems, isem, osem,
):
    pieces = []
    for e in range(ein_ref.shape[0]):
        for source, narrow, widened, target in (
            (ein_ref, narrow_in, wide_in, oin_ref),
            (eout_ref, narrow_out, wide_out, oout_ref),
        ):
            rows = source.shape[1] // WIDEN
            for k in range(WIDEN):
                at = (e, pl.ds(k * rows, rows))
                pieces.append((at, source, narrow, widened, target))
    loads = [
        pltpu.make_async_copy(source, target, isem.at[i])
        for i, (source, target) in enumerate(
            (
                (fq_in, fq_ref), (fgu_in, fgu_ref), (wqkv_in, wqkv_ref), (ga_in, ga_ref),
                (out_in, out_ref), (gin_in, gin_ref), (fsd_in, fsd_ref), (fwo_in, fwo_ref),
            )
        )
    ]
    arriving = []
    for i, (at, source, narrow, _, _) in enumerate(pieces):
        arriving.append(pltpu.make_async_copy(source.at[at], narrow.at[at], sems.at[0, i]))
        arriving[-1].start()
        if i == 1:
            for load in loads:
                load.start()
    stores = []

    def store(source, target):
        stores.append(pltpu.make_async_copy(source, target, osem.at[len(stores)]))
        stores[-1].start()

    leaving = []

    def widen(i):
        at, _, narrow, widened, target = pieces[i]
        arriving[i].wait()
        widened[at] = narrow[at].astype(F32)
        leaving.append(pltpu.make_async_copy(widened.at[at], target.at[at], sems.at[1, i]))
        leaving[-1].start()

    for i in range(len(pieces) // 2):
        widen(i)
    for load in loads:
        load.wait()
    for source, target in (
        (out_ref, out_to), (gin_ref, gin_to), (fsd_ref, fsd_to), (fwo_ref, fwo_to)
    ):
        store(source, target)
    rows_w = wqkv_ref.shape[0]
    head_width = wqkv_ref.shape[1] // 3 // nc
    grads = jnp.concatenate(
        [
            fq_ref[i, :, side * head_width : (side + 1) * head_width].astype(F32)
            for side in range(3)
            for i in range(nc)
        ],
        axis=1,
    )
    gq_ref[...] = grads
    own_units = fgu_ref.shape[2] // 2
    ggu_ref[...] = jnp.concatenate(
        [
            fgu_ref[i, :, side * own_units : (side + 1) * own_units].astype(F32)
            for side in range(2)
            for i in range(nc)
        ],
        axis=1,
    )
    extras = jnp.sum(fq_ref[:, :, 3 * head_width - SMALL :].astype(F32), axis=0)
    num_experts = gr_ref.shape[0]
    first = jnp.sum(wqkv_ref[...].astype(F32) * grads, axis=1, keepdims=True)
    lane = lax.broadcasted_iota(jnp.int32, (rows_w, 128), 1)
    both = jnp.where(lane == SMALL + num_experts, first, extras)
    turned = jnp.transpose(
        jnp.concatenate([both, jnp.zeros((128 - rows_w, 128), F32)], axis=0), (1, 0)
    )
    gr_ref[...] = turned[SMALL : SMALL + num_experts, :rows_w]
    at = SMALL + num_experts
    gga_ref[...] = turned[at : at + 1, :rows_w] / ga_ref[...].astype(F32)
    ggf_ref[...] = turned[at + 1 : at + 2, :rows_w]

    for source, target in (
        (gq_ref, gq_to), (gr_ref, gr_to), (gga_ref, gga_to), (ggf_ref, ggf_to), (ggu_ref, ggu_to)
    ):
        store(source, target)
    for i in range(len(pieces) // 2, len(pieces)):
        widen(i)
    for copy in leaving + stores:
        copy.wait()


def vmem(*shape, dtype=jnp.bfloat16):
    return pltpu.VMEM(shape, dtype)


def fast_device(
    hidden_in, seq_lengths, expert_ids, route_rank, gain_attn, w_qkv, w_out, w_router, gain_ffn,
    w_gate_up, w_shared_down, w_experts_in, w_experts_out, grad_output,
):
    nc, nz = lax.axis_size("ctx"), lax.axis_size("exp")
    num_seqs, two_ends, half_len, width = hidden_in.shape
    shard_len = 2 * half_len
    full_len = nc * shard_len
    tok = num_seqs * shard_len
    rows_w = w_qkv.shape[0]
    head_width = w_qkv.shape[1] // 3 // nc
    num_experts = w_router.shape[1]
    down_rows = w_shared_down.shape[0]
    own_units = w_gate_up.shape[1] // 2 // nc
    half_units = w_experts_in.shape[2] // 4
    hbm, vm, sm = pl.ANY, pltpu.VMEM, pltpu.SMEM
    dma = pltpu.SemaphoreType.DMA

    seq_shape = (num_seqs, shard_len, width)
    group_shape = (num_seqs, nc, shard_len, width)
    blocks = (nc, nz, 2, rows_w)
    half_blocks = (nc, nz, rows_w)
    wide_cols = 3 * head_width + SMALL
    num_slots = num_experts * CAP
    row_box = (nz, nc, BOX, width)
    plane_tok = nc * tok
    outs = [
        (seq_shape, BF),
        (seq_shape, F32),
        ((nc, rows_w, wide_cols), BF),
        ((nc, rows_w, 2 * own_units), BF),
        ((down_rows, width), F32),
        ((rows_w, width), F32),
        (w_experts_in.shape, BF),
        (w_experts_out.shape, BF),
    ]
    small_ins = [
        expert_ids.transpose(0, 1, 3, 2),
        route_rank.reshape(1, tok),
        w_qkv,
        w_router.T,
        gain_attn.reshape(1, rows_w),
        gain_ffn.reshape(1, rows_w),
        hidden_in.reshape(seq_shape),
        w_gate_up,
        w_out,
        w_shared_down,
        grad_output.reshape(seq_shape),
    ]
    out, gin, fq, fgu, fsd, fwo, ein, eout = pl.pallas_call(
        functools.partial(block_kernel, nc, nz),
        out_shape=[jax.ShapeDtypeStruct(shape, dtype) for shape, dtype in outs],
        in_specs=[
            pl.BlockSpec(memory_space=space) for space in [sm] + [hbm] * 13
        ],
        out_specs=[pl.BlockSpec(memory_space=hbm) for _ in outs],
        scratch_shapes=[
            *[vmem(*x.shape, dtype=x.dtype) for x in small_ins],
            *[vmem(*outs[i][0], dtype=outs[i][1]) for i in (0, 1, 4, 5)],
            vmem(full_len, 256, dtype=F32),
            vmem(8, tok, dtype=jnp.int32),
            vmem(nc, 8, tok, dtype=jnp.int32),
            vmem(nc, tok, 128, dtype=F32),
            vmem(nc, 2, tok, nz * BOX),
            vmem(nc, 2, tok, nz * BOX),
            vmem(nc, 8, tok, dtype=F32),
            vmem(nc, 8, tok, dtype=F32),
            vmem(*group_shape),
            vmem(*seq_shape),
            vmem(*group_shape),
            vmem(nc, rows_w, wide_cols),
            vmem(nc, rows_w, wide_cols),
            vmem(*blocks, wide_cols),
            vmem(width, wide_cols),
            vmem(nc, rows_w, 2 * own_units),
            vmem(*blocks, 2 * own_units),
            vmem(width, 2 * own_units),
            vmem(nc, rows_w, width),
            vmem(*blocks, width),
            vmem(width, width),
            vmem(nz, 2, down_rows, width),
            vmem(width, 2 * half_units),
            vmem(half_units, width),
            vmem(num_seqs, full_len, width),
            vmem(num_seqs, full_len, 3 * head_width),
            vmem(num_seqs, head_width // HS, full_len, full_len, dtype=F32),
            vmem(nc, num_seqs, nc, shard_len, head_width),
            vmem(*seq_shape, dtype=F32),
            vmem(*group_shape),
            vmem(*row_box),
            vmem(2, nz, nc, BOX, width),
            vmem(2 * num_slots, width),
            vmem(2 * num_slots, width),
            vmem(2 * num_slots, width, dtype=F32),
            vmem(2 * num_slots, width, dtype=F32),
            vmem(2, num_seqs, 2, shard_len, width, dtype=F32),
            vmem(plane_tok, own_units),
            vmem(plane_tok, 2 * own_units),
            vmem(2, *group_shape),
            vmem(2, num_seqs, 2, shard_len, width),
            vmem(2, *seq_shape),
            vmem(2, *seq_shape),
            vmem(2 * num_slots, half_units),
            vmem(2 * num_slots, 2 * half_units),
            vmem(*row_box),
            vmem(*row_box),
            vmem(*row_box),
            vmem(nz, 2, down_rows, width),
            vmem(*seq_shape),
            vmem(nc, num_seqs, shard_len, head_width),
            vmem(num_seqs, nc, shard_len, head_width),
            vmem(*group_shape),
            vmem(*group_shape, dtype=F32),
            vmem(num_seqs, 2, shard_len, width),
            vmem(*seq_shape),
            vmem(*seq_shape),
            vmem(*half_blocks, 2 * own_units),
            vmem(nz - 1, nc, rows_w, 2 * own_units),
            vmem(nc, rows_w, 2 * own_units),
            vmem(*half_blocks, wide_cols),
            vmem(nz - 1, nc, rows_w, wide_cols),
            vmem(nc, rows_w, wide_cols),
            vmem(nz, down_rows, width),
            vmem(nz - 1, down_rows, width),
            vmem(*half_blocks, width),
            vmem(nz - 1, nc, rows_w, width),
            vmem(nc, rows_w, width),
            vmem(nc, rows_w, width),
            dma((POSTS,)),
            dma((POSTS,)),
            dma((1 + half_units // 256,)),
            dma((len(small_ins),)),
            dma((6,)),
        ],
        compiler_params=pltpu.CompilerParams(
            collective_id=0, has_side_effects=True, vmem_limit_bytes=VMEM_BYTES
        ),
        cost_estimate=pl.CostEstimate(
            flops=16_000_000_000, bytes_accessed=30_000_000, transcendentals=0
        ),
        name="block_forward_backward",
    )(
        seq_lengths, *small_ins, w_experts_in, w_experts_out
    )

    ins = [fq, fgu, w_qkv, gain_attn.reshape(1, rows_w), ein, eout, out, gin, fsd, fwo]
    results = [
        (w_qkv.shape, F32),
        (w_router.shape[::-1], F32),
        ((1, rows_w), F32),
        ((1, rows_w), F32),
        (w_gate_up.shape, F32),
        (ein.shape, F32),
        (eout.shape, F32),
        (seq_shape, BF),
        (seq_shape, F32),
        (fsd.shape, F32),
        (fwo.shape, F32),
    ]
    grad_qkv, grad_router, grad_ga, grad_gf, grad_gu, grad_in, grad_out, out, gin, fsd, fwo = pl.pallas_call(
        functools.partial(finish_kernel, nc),
        out_shape=[jax.ShapeDtypeStruct(shape, dtype) for shape, dtype in results],
        in_specs=[pl.BlockSpec(memory_space=hbm) for _ in ins],
        out_specs=[pl.BlockSpec(memory_space=hbm) for _ in results],
        scratch_shapes=[
            vmem(*ein.shape),
            vmem(*eout.shape),
            vmem(*ein.shape, dtype=F32),
            vmem(*eout.shape, dtype=F32),
            *[vmem(*ins[i].shape, dtype=ins[i].dtype) for i in (0, 1, 2, 3, 6, 7, 8, 9)],
            *[vmem(*results[i][0], dtype=results[i][1]) for i in range(5)],
            dma((2, 2 * ein.shape[0] * WIDEN)),
            dma((8,)),
            dma((9,)),
        ],
        compiler_params=pltpu.CompilerParams(vmem_limit_bytes=VMEM_BYTES),
        name="widen_gradients",
    )(*ins)
    return (
        out.reshape(hidden_in.shape),
        gin.reshape(hidden_in.shape),
        grad_ga.reshape(rows_w),
        grad_qkv,
        fwo,
        grad_router.T,
        grad_gf.reshape(rows_w),
        grad_gu,
        fsd,
        grad_in,
        grad_out,
    )


def fits(mesh, hidden_in, w_qkv, w_router, w_gate_up, w_experts_in):
    nc, nz, nf = mesh.shape["ctx"], mesh.shape["exp"], mesh.shape["fsdp"]
    heads = w_qkv.shape[1] // 3 // HS
    return (
        nf == 2
        and nc == 4
        and nz == 4
        and heads == 12
        and w_router.shape[1] == nc * nz
        and w_qkv.shape[0] == 768
        and hidden_in.shape[2] == 32 * nc
        and hidden_in.shape[0] == 2 * nz * nf
        and hidden_in.shape[3] == 768
        and w_gate_up.shape[1] == w_experts_in.shape[2] == 4096
        and 2 * CAP <= BOX
    )


def solution(mesh):
    def whole(*args):
        chosen = fast_device if fits(mesh, args[0], args[5], args[7], args[9], args[11]) else per_device
        return placed(mesh, chosen)(*args)

    return whole


def placed(mesh, chosen):
    return jax.shard_map(
        chosen,
        mesh=mesh,
        in_specs=(
            P(("exp", "fsdp"), None, "ctx", None),
            P(("exp", "fsdp")),
            P(("exp", "fsdp"), None, "ctx", None),
            P(("exp", "fsdp"), "ctx", None),
            P(("ctx", "exp", "fsdp")),
            P(("ctx", "exp", "fsdp"), None),
            P(("ctx", "exp", "fsdp"), None),
            P(("ctx", "exp", "fsdp"), None),
            P(("ctx", "exp", "fsdp")),
            P(("ctx", "exp", "fsdp"), None),
            P(("ctx", "exp", "fsdp"), None),
            P("exp", ("ctx", "fsdp"), None),
            P("exp", ("ctx", "fsdp"), None),
            P(("exp", "fsdp"), None, "ctx", None),
        ),
        out_specs=(
            P(("exp", "fsdp"), None, "ctx", None),
            P(("exp", "fsdp"), None, "ctx", None),
            P(("ctx", "exp", "fsdp")),
            P(("ctx", "exp", "fsdp"), None),
            P(("ctx", "exp", "fsdp"), None),
            P(("ctx", "exp", "fsdp"), None),
            P(("ctx", "exp", "fsdp")),
            P(("ctx", "exp", "fsdp"), None),
            P(("ctx", "exp", "fsdp"), None),
            P("exp", ("ctx", "fsdp"), None),
            P("exp", ("ctx", "fsdp"), None),
        ),
        check_vma=False,
    )
```

```python
import functools
import math

import jax
import jax.numpy as jnp
from jax import lax
from jax.experimental import pallas as pl
from jax.experimental.pallas import tpu as pltpu
from jax.sharding import PartitionSpec as P

HS = 64
CAP = 18


epsilon = 1e-06
masked_out = -1e30
highest = lax.Precision.HIGHEST


def rms_norm(values_in, gain_row):
    return (
        values_in
        * lax.rsqrt(jnp.mean(values_in * values_in, axis=-1, keepdims=True) + epsilon)
        * gain_row
    )


def rope_tables(places):
    half_size = HS // 2
    frequency = 10000.0 ** (-jnp.arange(half_size, dtype=jnp.float32) * 2.0 / HS)
    angles = places.astype(jnp.float32)[:, None] * frequency[None, :]
    return (jnp.cos(angles), jnp.sin(angles))


def rotate(values_in, cosines, sine_rows):
    half_size = values_in.shape[-1] // 2
    leading = values_in[..., :half_size]
    trailing = values_in[..., half_size:]
    cos_rows = cosines[:, None, :]
    sin_rows = sine_rows[:, None, :]
    return jnp.concatenate(
        [leading * cos_rows - trailing * sin_rows, leading * sin_rows + trailing * cos_rows],
        axis=-1,
    )


def swiglu(merged_rows):
    gate_part, up_part = jnp.split(merged_rows, 2, axis=-1)
    return jax.nn.silu(gate_part) * up_part


def first_t(left_side, right_side, precision=None):
    return lax.dot_general(
        left_side,
        right_side,
        (((0,), (0,)), ((), ())),
        precision=precision,
        preferred_element_type=jnp.float32,
    )


def second_t(left_side, right_side, precision=None):
    return lax.dot_general(
        left_side,
        right_side,
        (((1,), (1,)), ((), ())),
        precision=precision,
        preferred_element_type=jnp.float32,
    )


def per_device(
    hidden_in,
    seq_lengths,
    expert_ids,
    route_rank,
    gain_attn,
    w_qkv,
    w_out,
    w_router,
    gain_ffn,
    w_gate_up,
    w_shared_down,
    w_experts_in,
    w_experts_out,
    grad_output,
):
    num_seqs, two_ends, half_len, model_width = hidden_in.shape
    shard_len = 2 * half_len
    tok_count = num_seqs * shard_len
    num_heads = model_width // HS
    score_scale = HS ** (-0.5)
    ctx_size = lax.axis_size("ctx")
    full_len = shard_len * ctx_size
    whole_half = half_len * ctx_size
    gain_one, wqkv_all, wout_all, router_all, gain_two, shared_in, shared_down = (
        lax.all_gather(gain_attn, ("ctx", "exp", "fsdp"), axis=0, tiled=True),
        lax.all_gather(w_qkv, ("ctx", "exp", "fsdp"), axis=0, tiled=True),
        lax.all_gather(w_out, ("ctx", "exp", "fsdp"), axis=0, tiled=True),
        lax.all_gather(w_router, ("ctx", "exp", "fsdp"), axis=0, tiled=True),
        lax.all_gather(gain_ffn, ("ctx", "exp", "fsdp"), axis=0, tiled=True),
        lax.all_gather(w_gate_up, ("ctx", "exp", "fsdp"), axis=0, tiled=True),
        lax.all_gather(w_shared_down, ("ctx", "exp", "fsdp"), axis=0, tiled=True),
    )
    experts_in, experts_out = (
        lax.all_gather(w_experts_in, ("ctx", "fsdp"), axis=1, tiled=True),
        lax.all_gather(w_experts_out, ("ctx", "fsdp"), axis=1, tiled=True),
    )
    lower_places = lax.axis_index("ctx") * half_len + jnp.arange(half_len, dtype=jnp.int32)
    places = jnp.concatenate([lower_places, full_len - 1 - lower_places])
    whole_range = jnp.arange(whole_half, dtype=jnp.int32)
    full_places = jnp.concatenate([whole_range, full_len - 1 - whole_range])
    live_mask = (places[None, :] < seq_lengths[:, None]).astype(jnp.float32)
    live_rows = live_mask.reshape(tok_count, 1)
    inputs_f = hidden_in.astype(jnp.float32).reshape(tok_count, model_width)
    gain_attn_f = gain_one.astype(jnp.float32)
    normed_b = rms_norm(inputs_f, gain_attn_f).astype(jnp.bfloat16)
    qkv_merged = jnp.dot(normed_b, wqkv_all, preferred_element_type=jnp.float32).reshape(
        num_seqs, shard_len, 3, num_heads, HS
    )
    cosines, sine_rows = rope_tables(places)
    queries = rotate(qkv_merged[:, :, 0], cosines, sine_rows).astype(jnp.bfloat16)
    keys_local = rotate(qkv_merged[:, :, 1], cosines, sine_rows).astype(jnp.bfloat16)
    values_local = qkv_merged[:, :, 2].astype(jnp.bfloat16)
    end_shape = (num_seqs, 2, half_len, model_width)
    keys_full, values_full = (
        lax.all_gather(keys_local.reshape(end_shape), "ctx", axis=2, tiled=True),
        lax.all_gather(values_local.reshape(end_shape), "ctx", axis=2, tiled=True),
    )
    keys_full = keys_full.reshape(num_seqs, full_len, num_heads, HS)
    values_full = values_full.reshape(num_seqs, full_len, num_heads, HS)
    stat_shape = (num_seqs, num_heads, shard_len)
    block_range = jnp.arange(ctx_size, dtype=jnp.int32)

    def block_scores(query_rows, query_places, key_rows, key_places):
        scores = (
            jnp.einsum("bqhd,bkhd->bhqk", query_rows, key_rows, preferred_element_type=jnp.float32)
            * score_scale
        )
        allowed = (key_places[None, None, :] <= query_places[None, :, None]) & (
            key_places[None, None, :] < seq_lengths[:, None, None]
        )
        return jnp.where(allowed[:, None], scores, masked_out)

    def key_block(block_idx):
        offset = block_idx * shard_len
        return (
            lax.dynamic_slice_in_dim(keys_full, offset, shard_len, 1),
            lax.dynamic_slice_in_dim(values_full, offset, shard_len, 1),
            lax.dynamic_slice_in_dim(full_places, offset, shard_len, 0),
        )

    def lse_step(state_in, block_idx):
        run_max, run_sum = state_in
        key_rows, value_rows, key_places = key_block(block_idx)
        scores = block_scores(queries, places, key_rows, key_places)
        new_max = jnp.maximum(run_max, jnp.max(scores, axis=-1))
        run_sum = run_sum * jnp.exp(run_max - new_max) + jnp.sum(
            jnp.exp(scores - new_max[..., None]), axis=-1
        )
        return ((new_max, run_sum), None)

    (row_max, row_sum), unused = lax.scan(
        lse_step,
        (jnp.full(stat_shape, masked_out, jnp.float32), jnp.zeros(stat_shape, jnp.float32)),
        block_range,
    )
    log_total = row_max + jnp.log(row_sum)

    def context_step(running, block_idx):
        key_rows, value_rows, key_places = key_block(block_idx)
        prob_rows = jnp.exp(
            block_scores(queries, places, key_rows, key_places) - log_total[..., None]
        ).astype(jnp.bfloat16)
        return (
            running
            + jnp.einsum(
                "bhqk,bkhd->bqhd", prob_rows, value_rows, preferred_element_type=jnp.float32
            ),
            None,
        )

    context, unused = lax.scan(
        context_step, jnp.zeros((num_seqs, shard_len, num_heads, HS), jnp.float32), block_range
    )
    context_b = context.reshape(tok_count, model_width).astype(jnp.bfloat16)
    attended = inputs_f + jnp.dot(context_b, wout_all, preferred_element_type=jnp.float32)
    gain_ffn_f = gain_two.astype(jnp.float32)
    normed_two = rms_norm(attended, gain_ffn_f).astype(jnp.bfloat16)
    logits = jnp.dot(normed_two, router_all, preferred_element_type=jnp.float32)
    num_experts = router_all.shape[1]
    expert_range = jnp.arange(num_experts, dtype=jnp.int32)
    picked_ids = expert_ids.reshape(tok_count, 2)
    pick_hot = (picked_ids[:, :, None] == expert_range).astype(jnp.float32)
    chosen = jnp.sum(pick_hot * logits[:, None, :], axis=-1)
    gate_probs = jax.nn.softmax(chosen, axis=-1)
    expert_load = (jnp.sum(pick_hot, axis=1) * live_rows).astype(jnp.bfloat16)
    rank_rows = route_rank.reshape(tok_count)
    earlier = (rank_rows[None, :] < rank_rows[:, None]).astype(jnp.bfloat16)
    position = jnp.dot(earlier, expert_load, preferred_element_type=jnp.float32)
    chosen_pos = jnp.sum(pick_hot * position[:, None, :], axis=-1)
    kept_mask = live_rows * (chosen_pos < CAP).astype(jnp.float32)
    slot_hot = (chosen_pos[:, :, None] == jnp.arange(CAP, dtype=jnp.float32)).astype(jnp.float32)
    dispatch = (
        (pick_hot[:, :, :, None] * slot_hot[:, :, None, :] * kept_mask[:, :, None, None])
        .reshape(tok_count, 2, num_experts * CAP)
        .astype(jnp.bfloat16)
    )
    dispatch_any = dispatch[:, 0] + dispatch[:, 1]
    exp_size = lax.axis_size("exp")
    per_owner = num_experts // exp_size
    send_rows = (
        first_t(dispatch_any, normed_two)
        .astype(jnp.bfloat16)
        .reshape(exp_size, per_owner, CAP, model_width)
    )
    arrived = lax.all_to_all(send_rows, "exp", split_axis=0, concat_axis=0, tiled=True)
    expert_merged = jnp.einsum(
        "secd,edf->secf", arrived, experts_in, preferred_element_type=jnp.float32
    )
    expert_hidden = swiglu(expert_merged).astype(jnp.bfloat16)
    expert_result = jnp.einsum(
        "secf,efd->secd", expert_hidden, experts_out, preferred_element_type=jnp.float32
    ).astype(jnp.bfloat16)
    returned = lax.all_to_all(
        expert_result, "exp", split_axis=0, concat_axis=0, tiled=True
    ).reshape(num_experts * CAP, model_width)
    routed = jnp.einsum("tks,sd->tkd", dispatch, returned, preferred_element_type=jnp.float32)
    mixture = jnp.sum(gate_probs[:, :, None] * routed, axis=1)
    shared_merged = jnp.dot(normed_two, shared_in, preferred_element_type=jnp.float32)
    shared_hidden = swiglu(shared_merged).astype(jnp.bfloat16)
    shared_result = jnp.dot(shared_hidden, shared_down, preferred_element_type=jnp.float32)
    layer_out = (
        (live_rows * (attended + mixture + shared_result)).reshape(end_shape).astype(jnp.bfloat16)
    )
    upstream = grad_output.astype(jnp.float32).reshape(tok_count, model_width) * live_rows
    upstream_b = upstream.astype(jnp.bfloat16)
    upstream_f = upstream_b.astype(jnp.float32)
    d_shared_down = first_t(shared_hidden, upstream_b)
    d_shared_hidden = second_t(upstream_b, shared_down)
    unused, swiglu_pull = jax.vjp(swiglu, shared_merged)
    d_shared_merged = swiglu_pull(d_shared_hidden)[0].astype(jnp.bfloat16)
    d_shared_in = first_t(normed_two, d_shared_merged)
    d_normed_two = second_t(d_shared_merged, shared_in)
    gate_grads = jnp.sum(routed * upstream_f[:, None, :], axis=-1)
    weighted = (gate_probs[:, :, None] * upstream_f[:, None, :]).astype(jnp.bfloat16)
    d_returned = (
        jnp.einsum("tks,tkd->sd", dispatch, weighted, preferred_element_type=jnp.float32)
        .astype(jnp.bfloat16)
        .reshape(exp_size, per_owner, CAP, model_width)
    )
    d_result = lax.all_to_all(d_returned, "exp", split_axis=0, concat_axis=0, tiled=True)
    d_experts_out = jnp.einsum(
        "secf,secd->efd", expert_hidden, d_result, preferred_element_type=jnp.float32
    )
    d_expert_hidden = jnp.einsum(
        "secd,efd->secf", d_result, experts_out, preferred_element_type=jnp.float32
    )
    unused, expert_pull = jax.vjp(swiglu, expert_merged)
    d_expert_merged = expert_pull(d_expert_hidden)[0].astype(jnp.bfloat16)
    d_experts_in = jnp.einsum(
        "secd,secf->edf", arrived, d_expert_merged, preferred_element_type=jnp.float32
    )
    d_arrived = jnp.einsum(
        "secf,edf->secd", d_expert_merged, experts_in, preferred_element_type=jnp.float32
    ).astype(jnp.bfloat16)
    d_sent = lax.all_to_all(d_arrived, "exp", split_axis=0, concat_axis=0, tiled=True).reshape(
        num_experts * CAP, model_width
    )
    d_normed_two = d_normed_two + jnp.dot(dispatch_any, d_sent, preferred_element_type=jnp.float32)
    unused, gate_pull = jax.vjp(lambda chosen_in: jax.nn.softmax(chosen_in, axis=-1), chosen)
    d_chosen = gate_pull(gate_grads)[0]
    d_logits = jnp.sum(pick_hot * d_chosen[:, :, None], axis=1)
    d_router = first_t(normed_two.astype(jnp.float32), d_logits, highest)
    d_normed_two = d_normed_two + second_t(d_logits, router_all.astype(jnp.float32), highest)
    unused, second_pull = jax.vjp(rms_norm, attended, gain_ffn_f)
    d_attended, d_gain_ffn = second_pull(d_normed_two)
    d_attended = d_attended + upstream
    d_attended_b = d_attended.astype(jnp.bfloat16)
    d_out_proj = first_t(context_b, d_attended_b)
    d_context = (
        second_t(d_attended_b, wout_all)
        .astype(jnp.bfloat16)
        .reshape(num_seqs, shard_len, num_heads, HS)
    )

    def score_grads(
        query_rows, query_places, key_rows, value_rows, key_places, d_rows, lse_rows, delta_rows
    ):
        prob_rows = jnp.exp(
            block_scores(query_rows, query_places, key_rows, key_places) - lse_rows[..., None]
        )
        d_probs = jnp.einsum(
            "bqhd,bkhd->bhqk", d_rows, value_rows, preferred_element_type=jnp.float32
        )
        d_scores = (prob_rows * (d_probs - delta_rows[..., None])).astype(jnp.bfloat16)
        return (prob_rows.astype(jnp.bfloat16), d_scores)

    def delta_step(running, block_idx):
        key_rows, value_rows, key_places = key_block(block_idx)
        prob_rows = jnp.exp(
            block_scores(queries, places, key_rows, key_places) - log_total[..., None]
        )
        d_probs = jnp.einsum(
            "bqhd,bkhd->bhqk", d_context, value_rows, preferred_element_type=jnp.float32
        )
        return (running + jnp.sum(prob_rows * d_probs, axis=-1), None)

    row_delta, unused = lax.scan(delta_step, jnp.zeros(stat_shape, jnp.float32), block_range)
    head_shape = (num_seqs, shard_len, num_heads, HS)

    def query_step(d_query, block_idx):
        key_rows, value_rows, key_places = key_block(block_idx)
        prob_b, d_scores = score_grads(
            queries, places, key_rows, value_rows, key_places, d_context, log_total, row_delta
        )
        return (
            d_query
            + jnp.einsum("bhqk,bkhd->bqhd", d_scores, key_rows, preferred_element_type=jnp.float32)
            * score_scale,
            None,
        )

    d_query, unused = lax.scan(query_step, jnp.zeros(head_shape, jnp.float32), block_range)
    query_all, d_context_all = (
        lax.all_gather(queries.reshape(end_shape), "ctx", axis=2, tiled=True),
        lax.all_gather(d_context.reshape(end_shape), "ctx", axis=2, tiled=True),
    )
    stat_ends = (num_seqs, num_heads, 2, half_len)
    lse_all, delta_all = (
        lax.all_gather(log_total.reshape(stat_ends), "ctx", axis=3, tiled=True),
        lax.all_gather(row_delta.reshape(stat_ends), "ctx", axis=3, tiled=True),
    )
    query_all = query_all.reshape(num_seqs, full_len, num_heads, HS)
    d_context_all = d_context_all.reshape(num_seqs, full_len, num_heads, HS)
    lse_all = lse_all.reshape(num_seqs, num_heads, full_len)
    delta_all = delta_all.reshape(num_seqs, num_heads, full_len)

    def owner_step(state_in, block_idx):
        d_keys, d_values = state_in
        offset = block_idx * shard_len
        query_rows = lax.dynamic_slice_in_dim(query_all, offset, shard_len, 1)
        d_rows = lax.dynamic_slice_in_dim(d_context_all, offset, shard_len, 1)
        lse_rows = lax.dynamic_slice_in_dim(lse_all, offset, shard_len, 2)
        delta_rows = lax.dynamic_slice_in_dim(delta_all, offset, shard_len, 2)
        query_places = lax.dynamic_slice_in_dim(full_places, offset, shard_len, 0)
        prob_b, d_scores = score_grads(
            query_rows, query_places, keys_local, values_local, places, d_rows, lse_rows, delta_rows
        )
        d_keys = (
            d_keys
            + jnp.einsum(
                "bhqk,bqhd->bkhd", d_scores, query_rows, preferred_element_type=jnp.float32
            )
            * score_scale
        )
        d_values = d_values + jnp.einsum(
            "bhqk,bqhd->bkhd", prob_b, d_rows, preferred_element_type=jnp.float32
        )
        return ((d_keys, d_values), None)

    (d_keys_local, d_values_local), unused = lax.scan(
        owner_step,
        (jnp.zeros(head_shape, jnp.float32), jnp.zeros(head_shape, jnp.float32)),
        block_range,
    )
    unused, rope_pull = jax.vjp(
        lambda rows_in: rotate(rows_in, cosines, sine_rows), qkv_merged[:, :, 0]
    )
    d_query_pre = rope_pull(d_query)[0]
    d_key_pre = rope_pull(d_keys_local)[0]
    d_qkv_merged = (
        jnp.stack([d_query_pre, d_key_pre, d_values_local], axis=2)
        .reshape(tok_count, 3 * model_width)
        .astype(jnp.bfloat16)
    )
    d_qkv = first_t(normed_b, d_qkv_merged)
    d_normed = second_t(d_qkv_merged, wqkv_all)
    unused, first_pull = jax.vjp(rms_norm, inputs_f, gain_attn_f)
    d_inputs, d_gain_attn = first_pull(d_normed)
    grad_input = (d_attended + d_inputs).reshape(end_shape)
    dense_sums = (
        lax.psum_scatter(d_gain_attn, ("ctx", "exp", "fsdp"), scatter_dimension=0, tiled=True),
        lax.psum_scatter(d_qkv, ("ctx", "exp", "fsdp"), scatter_dimension=0, tiled=True),
        lax.psum_scatter(d_out_proj, ("ctx", "exp", "fsdp"), scatter_dimension=0, tiled=True),
        lax.psum_scatter(d_router, ("ctx", "exp", "fsdp"), scatter_dimension=0, tiled=True),
        lax.psum_scatter(d_gain_ffn, ("ctx", "exp", "fsdp"), scatter_dimension=0, tiled=True),
        lax.psum_scatter(d_shared_in, ("ctx", "exp", "fsdp"), scatter_dimension=0, tiled=True),
        lax.psum_scatter(d_shared_down, ("ctx", "exp", "fsdp"), scatter_dimension=0, tiled=True),
    )
    expert_sums = (
        lax.psum_scatter(
            d_experts_in.astype(jnp.bfloat16), ("ctx", "fsdp"), scatter_dimension=1, tiled=True
        ).astype(jnp.float32),
        lax.psum_scatter(
            d_experts_out.astype(jnp.bfloat16), ("ctx", "fsdp"), scatter_dimension=1, tiled=True
        ).astype(jnp.float32),
    )
    return (
        layer_out,
        grad_input,
        dense_sums[0],
        dense_sums[1],
        dense_sums[2],
        dense_sums[3],
        dense_sums[4],
        dense_sums[5],
        dense_sums[6],
        expert_sums[0],
        expert_sums[1],
    )


F32 = jnp.float32
BF = jnp.bfloat16
MESH = pl.DeviceIdType.MESH
BOX = 40
SMALL = 64
VMEM_BYTES = 63 * 1024 * 1024
PUMPS = (3, 10, 12, 0, 4, 4)
POSTS = 55
EARLY = 2
LATE = -1
SMALL_AT = 1
WIDEN = 1


def place():
    return lax.axis_index("ctx"), lax.axis_index("exp"), lax.axis_index("fsdp")


def wrap(value, size):
    return lax.rem(value, size)


def mm(left, right):
    return lax.dot_general(
        left, right, (((1,), (0,)), ((), ())), preferred_element_type=F32
    )


def mm_nt(left, right):
    return lax.dot_general(
        left, right, (((1,), (1,)), ((), ())), preferred_element_type=F32
    )


def mm_tn(left, right):
    return lax.dot_general(
        left, right, (((0,), (0,)), ((), ())), preferred_element_type=F32
    )


def greet(peers):
    barrier = pltpu.get_barrier_semaphore()
    for peer in peers:
        pl.semaphore_signal(barrier, inc=1, device_id=peer, device_id_type=MESH)


def met(peers):
    pl.semaphore_wait(pltpu.get_barrier_semaphore(), len(peers))


class Post:
    def __init__(self, send, recv, like, device):
        self.send, self.recv, self.like, self.device = send, recv, like, device

    def add(self, src, dst, device):
        pltpu.make_async_remote_copy(
            src_ref=src,
            dst_ref=dst,
            send_sem=self.send,
            recv_sem=self.recv,
            device_id=device,
            device_id_type=MESH,
        ).start()

    def all_of_it(self, like=None):
        like = self.like if like is None else like
        return pltpu.make_async_remote_copy(
            src_ref=like,
            dst_ref=like,
            send_sem=self.send,
            recv_sem=self.recv,
            device_id=self.device,
            device_id_type=MESH,
        )

    def wait_recv(self, like=None):
        self.all_of_it(like).wait_recv()

    def wait_send(self, like=None):
        self.all_of_it(like).wait_send()


class Courier:
    def __init__(self, send, recv, device):
        self.send, self.recv, self.device, self.count, self.sent = send, recv, device, 0, []

    def open(self, like, keep=True):
        post = Post(self.send.at[self.count], self.recv.at[self.count], like, self.device)
        self.count += 1
        if keep:
            self.sent.append(post)
        return post

    def at(self, index, like):
        return Post(self.send.at[index], self.recv.at[index], like, self.device)

    def post(self, like, moves):
        post = self.open(like)
        for src, dst, device in moves:
            post.add(src, dst, device)
        return post

    def settle(self, posts):
        for post in posts:
            post.wait_send()
        done = {id(post) for post in posts}
        self.sent = [post for post in self.sent if id(post) not in done]

    def finish(self):
        self.settle(list(self.sent))


def swap_halves(rows):
    width = rows.shape[1]
    lane = lax.broadcasted_iota(jnp.int32, rows.shape, 1)
    ahead = pltpu.roll(rows, width - HS // 2, 1)
    behind = pltpu.roll(rows, HS // 2, 1)
    return jnp.where((lane & (HS - 1)) < HS // 2, -ahead, behind)


def wide(table, times):
    return jnp.concatenate([table] * times, axis=1)


def position_of(index, half_len, full_len):
    block = index // (2 * half_len)
    inside = index & (2 * half_len - 1)
    low = block * half_len + (inside & (half_len - 1))
    return jnp.where(inside >= half_len, full_len - 1 - low, low)


def allowed_keys(length, half_len, full_len):
    shape = (full_len, full_len)
    query_at = position_of(lax.broadcasted_iota(jnp.int32, shape, 0), half_len, full_len)
    key_at = position_of(lax.broadcasted_iota(jnp.int32, shape, 1), half_len, full_len)
    return (key_at <= query_at) & (key_at < length)


def head_probs(query, key, allowed):
    scores = jnp.where(allowed, mm_nt(query, key) * (HS**-0.5), masked_out)
    weights = jnp.exp(scores - jnp.max(scores, axis=1, keepdims=True))
    return weights * (1.0 / jnp.sum(weights, axis=1, keepdims=True))


def column_row(tail, lane):
    pick = (lax.broadcasted_iota(jnp.int32, (8, 128), 1) == lane).astype(BF)
    return mm_nt(pick, tail)[0:1]


def split_dot(dot, left, right, left_wide=True):
    whole = left if left_wide else right
    high = whole.astype(BF)
    low = (whole - high.astype(F32)).astype(BF)
    if left_wide:
        return dot(high, right) + dot(low, right)
    return dot(left, high) + dot(left, low)


def inverse_rms(rows):
    return lax.rsqrt(jnp.mean(rows * rows, axis=1, keepdims=True) + epsilon)


def norm_back(rows, inverse, scaled):
    return inverse * scaled - rows * (inverse * inverse * inverse) * jnp.mean(
        rows * scaled, axis=1, keepdims=True
    )


def join(blocks, shape):
    return blocks.astype(F32).reshape(shape).astype(BF)


def ffn_block(j, rows, grads, in_ref, out_ref, hidden_ref, dm_ref, result, back, units, step):
    low = pl.multiple_of(j * step, step) if not isinstance(j, int) else j * step
    high = pl.multiple_of(units + low, step) if not isinstance(j, int) else units + low
    gate_at, up_at = pl.ds(low, step), pl.ds(high, step)
    gate, up = mm(rows, in_ref[:, gate_at]), mm(rows, in_ref[:, up_at])
    down = out_ref[gate_at, :]
    d_hidden = mm_nt(grads, down)
    share = 1.0 / (1.0 + jnp.exp(-gate))
    lit = gate * share
    hidden = (lit * up).astype(BF)
    d_gate = (d_hidden * up * (share * (1.0 + gate * (1.0 - share)))).astype(BF)
    d_up = (d_hidden * lit).astype(BF)
    hidden_ref[:, gate_at] = hidden
    dm_ref[:, gate_at] = d_gate
    dm_ref[:, up_at] = d_up
    result[...] += mm(hidden, down)
    back[...] += mm_nt(d_gate, in_ref[:, gate_at]) + mm_nt(d_up, in_ref[:, up_at])


def box_rows(kept_rows, boxes, shift):
    shape = (boxes * kept_rows, boxes * BOX)
    row = lax.broadcasted_iota(jnp.int32, shape, 0)
    column = lax.broadcasted_iota(jnp.int32, shape, 1)
    box = jnp.floor((column.astype(F32) + 0.5) * (1.0 / BOX)).astype(jnp.int32)
    at = column - box * BOX - shift
    return ((at >= 0) & (at < kept_rows) & (row == box * kept_rows + at)).astype(BF)


def block_kernel(
    nc, nz,
    len_ref, ids_in, rank_in, wqkv_in, router_in, ga_in, gf_in, hid_in, gu_in, wo_in, sd_in, go_in,
    win_ref, wout_ref,
    out_to, gin_to, fq_ref, fgu_ref, fsd_to, fwo_to, ein_ref, eout_ref,
    ids_ref, rank_ref, wqkv_ref, router_ref, ga_ref, gf_ref, hid_ref, gu_ref, wo_ref, sd_ref, go_ref,
    out_ref, gin_ref, fsd_ref, fwo_ref,
    turn_ref, meta_own, meta_all, picks, hot_x, hot_d, dg_send, dg_in, hid_all, up_own, up_all, wq_own, wq_st, wq_buf, w_ref, gu_st, gu_buf, gu_all, wo_st, wo_buf,
    wo_all, sd_all, wie, woe, normed_ref, qkv_ref, probs_all, ctx_all, att_own, nt_all,
    sb, ar, xs, ds, acc_a, acc_b, sh_own, sh_hidden, sh_dm, sh_send, sh_in, sh_mid, sh_end,
    ex_hidden, ex_dm, pin, fb, rb, gsd, da_own, dctx_send, dctx_all, part, part_own, rs_in, rs_mid, rs_end,
    sib_gu, zi_gu, pb_gu, sib_q, zi_q, pb_q, sib_sd, zi_sd, sib_wo, zi_wo, pb_wo, in_wo,
    send, recv, lsem, isem, osem,
):
    c, z, f = place()
    near_x, near_y = c + 1 - 2 * wrap(c, 2), wrap(c + 2, nc)
    far = wrap(near_x + 2, nc)
    to_x, to_y = (near_x, z, f), (near_y, z, f)
    in_plane = [(wrap(c + s, nc), z, f) for s in range(1, nc)]
    in_column = [(c, wrap(z + s, nz), f) for s in range(1, nz)]
    steps_up = list(range(1, nz))
    sibling = (c, z, 1 - f)
    across = [(wrap(c + s, nc), z, 1 - f) for s in range(1, nc)]
    partners = in_plane + in_column + [sibling] + across
    with jax.named_scope("s_greet"):
        greet(partners)

    loads = [
        pltpu.make_async_copy(source, target, isem.at[i])
        for i, (source, target) in enumerate(
            (
                (ids_in, ids_ref), (rank_in, rank_ref), (wqkv_in, wqkv_ref),
                (router_in, router_ref), (ga_in, ga_ref), (gf_in, gf_ref), (hid_in, hid_ref),
                (gu_in, gu_ref), (wo_in, wo_ref), (sd_in, sd_ref), (go_in, go_ref),
            )
        )
    ]
    for load in loads:
        load.start()
    stores = []

    def store(source, target):
        stores.append(pltpu.make_async_copy(source, target, osem.at[len(stores)]))
        stores[-1].start()

    num_seqs, shard_len, width = hid_ref.shape
    full_len = nc * shard_len
    half_len = shard_len // 2
    tok = num_seqs * shard_len
    rows_w = wqkv_ref.shape[0]
    head_width = wqkv_ref.shape[1] // 3 // nc
    heads_here = head_width // HS
    wide_cols = wq_own.shape[2]
    units = gu_ref.shape[1] // 2
    own_units = units // nc
    down_rows = sd_ref.shape[0]
    num_experts = nz * nc
    num_slots = num_experts * CAP
    column_slots = nz * BOX
    block_rows = nz * 2 * rows_w
    mail = Courier(send, recv, sibling)

    for load in loads:
        load.wait()
    small = jnp.concatenate(
        [
            router_ref[...].astype(F32),
            ga_ref[...].astype(F32),
            gf_ref[...].astype(F32),
            jnp.zeros((128 - num_experts - 2, rows_w), F32),
        ],
        axis=0,
    )
    small = jnp.concatenate([small, jnp.zeros((128, 128 - rows_w), F32)], axis=1)
    small = jnp.transpose(small, (1, 0))[:rows_w, :SMALL].astype(BF)
    for owner in range(nc):
        wq_own[owner] = jnp.concatenate(
            [
                wqkv_ref[:, side * width + owner * head_width : side * width + (owner + 1) * head_width]
                for side in range(3)
            ]
            + [small],
            axis=1,
        )
    meta_own[...] = jnp.concatenate(
        [
            jnp.concatenate(
                [ids_ref[q, e, k : k + 1, :] for q in range(num_seqs) for e in range(2)], axis=1
            )
            for k in range(2)
        ]
        + [rank_ref[...], jnp.zeros((5, tok), jnp.int32)],
        axis=0,
    )
    with jax.named_scope("s_met"):
        met(partners)

    others = pl.ds(0, nc - 1)
    staged_wq = mail.post(
        wq_st.at[others],
        [(wq_own.at[wrap(c + s, nc)], wq_st.at[c], in_plane[s - 1]) for s in range(1, nc)],
    )
    arriving = [
        mail.post(
            hid_all.at[q, pl.ds(0, 2)],
            [(hid_ref.at[q], hid_all.at[q, c], peer) for peer in (to_x, to_y)],
        )
        for q in range(num_seqs)
    ]
    meta_copies = mail.post(
        meta_all.at[others], [(meta_own, meta_all.at[c], peer) for peer in in_plane]
    )
    staged_wo = mail.post(wo_st.at[others], [(wo_ref, wo_st.at[c], peer) for peer in in_plane])
    staged_gu = mail.open(gu_st.at[others])
    for s in range(1, nc):
        owner = wrap(c + s, nc)
        for side in range(2):
            at = pl.ds(pl.multiple_of(side * units + owner * own_units, own_units), own_units)
            staged_gu.add(
                gu_ref.at[:, at],
                gu_st.at[c, :, pl.ds(side * own_units, own_units)],
                in_plane[s - 1],
            )

    block = 2 * c + f
    shard_rows = win_ref.shape[1]
    half_units = units // 2
    step = 256
    steps = half_units // step
    lands = pl.ds(pl.multiple_of(block * shard_rows, shard_rows), shard_rows)
    out_rows = wout_ref.shape[1]
    to_core = block // nc
    slot = wrap(block, nc)
    out_lands = pl.ds(pl.multiple_of(slot * out_rows, out_rows), out_rows)
    remote_rows = (2 * nc - 1) * shard_rows
    first_in = mail.count
    expert_in = [
        mail.open(wie.at[pl.ds(0, remote_rows), pl.ds(0, 2 * step)]) for _ in range(steps)
    ]
    expert_out = mail.open(woe, keep=False)
    remote_out = woe.at[pl.ds(0, (nc - 1) * out_rows)]
    own_out = pltpu.make_async_copy(wout_ref.at[c], woe.at[out_lands], lsem.at[0])

    def send_out(s):
        owner = wrap(c + s, nc)
        expert_out.add(wout_ref.at[owner], woe.at[out_lands], (owner, z, to_core))

    def send_out_own():
        @pl.when(to_core == f)
        def _():
            own_out.start()

        @pl.when(to_core != f)
        def _():
            expert_out.add(wout_ref.at[c], woe.at[out_lands], sibling)

    def own_in(j):
        like = wie.at[pl.ds(0, shard_rows), pl.ds(0, 2 * step)]
        return pltpu.make_async_copy(like, like, lsem.at[1 + j])

    def nth_block(j, chip):
        return wrap(2 * j + j // 2 + 2 * wrap(chip, 2), steps)

    def send_in(j, s, g, side):
        owner = wrap(c + s, nc)
        at = nth_block(j, owner) * step
        core = f if g == 0 else 1 - f
        from_lane = pl.multiple_of(side * units + core * half_units + at, step)
        src = win_ref.at[owner, :, pl.ds(from_lane, step)]
        dst = wie.at[lands, pl.ds(pl.multiple_of(side * half_units + at, step), step)]
        if s == 0 and g == 0:
            pltpu.make_async_copy(src, dst, lsem.at[1 + j]).start()
        else:
            expert_in[j].add(src, dst, (owner, z, core))

    bulk = [functools.partial(send_out, s) for s in range(1, nc)] + [send_out_own]
    for j in range(steps):
        for s in range(1, nc + 1):
            for g in range(2):
                for side in range(2):
                    bulk.append(functools.partial(send_in, j, s % nc, g, side))

    def pump(queue, count):
        for _ in range(min(count, len(queue))):
            queue.pop(0)()

    with jax.named_scope("s_turns"):
        row = lax.broadcasted_iota(jnp.int32, (full_len, 128), 0)
        lane = lax.broadcasted_iota(jnp.int32, (full_len, 128), 1) & (HS // 2 - 1)
        frequency = jnp.exp(lane.astype(F32) * (-2.0 * math.log(10000.0) / HS))
        angles = position_of(row, half_len, full_len).astype(F32) * frequency
        turn_ref[:, :128] = jnp.cos(angles)
        turn_ref[:, 128:] = jnp.sin(angles)
    lane = lax.broadcasted_iota(jnp.int32, (tok, 128), 1).astype(F32)

    def live_rows(chip):
        row_at = lax.broadcasted_iota(jnp.int32, (tok, 1), 0)
        inside = row_at & (shard_len - 1)
        low = chip * half_len + (inside & (half_len - 1))
        places = jnp.where(inside >= half_len, full_len - 1 - low, low)
        lengths = jnp.zeros((tok, 1), jnp.int32)
        for q in range(num_seqs):
            lengths = jnp.where(row_at // shard_len == q, len_ref[q], lengths)
        return (places < lengths).astype(F32)

    def turned(rows):
        return jnp.transpose(
            jnp.concatenate([rows, jnp.zeros((128 - rows.shape[0], tok), F32)], axis=0), (1, 0)
        )

    def hot_lanes(columns):
        return [(lane == SMALL + columns[:, k : k + 1]).astype(F32) for k in range(2)]

    def gates_of(hots, logits):
        chosen = [jnp.sum(hot * logits, axis=1, keepdims=True) for hot in hots]
        top = jnp.maximum(chosen[0], chosen[1])
        raised = [jnp.exp(value - top) for value in chosen]
        return [value / (raised[0] + raised[1]) for value in raised]

    def route(chip):
        rows = meta_all[chip].astype(F32)
        columns = turned(rows)
        picks[chip] = columns
        hots = hot_lanes(columns)
        rank_row = jnp.broadcast_to(rows[2:3], (tok, tok))
        earlier = (rank_row < columns[:, 2:3]).astype(BF)
        live = live_rows(chip)
        position = mm(earlier, ((hots[0] + hots[1]) * live).astype(BF))
        slot_lane = lax.broadcasted_iota(jnp.int32, (tok, column_slots), 1).astype(F32)
        for k in range(2):
            at = jnp.sum(hots[k] * position, axis=1, keepdims=True)
            plane = jnp.floor((columns[:, k : k + 1] + 0.5) * (1.0 / nc))
            here = columns[:, k : k + 1] - plane * nc == c.astype(F32)
            slot_at = jnp.where((live > 0) & (at < CAP) & here, plane * BOX + at, -BOX)
            hot_x[chip, k] = (slot_lane == slot_at).astype(BF)
            hot_d[chip, k] = (slot_lane == slot_at + CAP).astype(BF)

    live = live_rows(c)
    upstream = go_ref[...].reshape(tok, width).astype(F32) * live
    up_b = upstream.astype(BF)
    up_own[...] = up_b.reshape(num_seqs, shard_len, width)
    for q in range(num_seqs):
        hid_all[q, c] = hid_ref[q]
        up_all[q, c] = up_own[q]

    def pass_on(post, buffer, q, at):
        post.wait_recv()
        origin, peer = (near_x, to_y) if q == 0 else (near_y, to_x)
        block_at = at(buffer, q, origin)
        return mail.post(block_at, [(block_at, block_at, peer)])

    def by_seq(buffer, q, chip):
        return buffer.at[q, chip]

    def by_chip(buffer, q, chip):
        return buffer.at[chip, q]

    sd_all[z, f] = sd_ref[...]
    planes = pl.ds(0, nz - 1)

    def spread(stage, staged, buffer):
        staged.wait_recv()
        post = mail.post(
            buffer.at[:, planes, 0],
            [(stage, buffer.at[:, z, f], peer) for peer in in_column],
        )
        for i in range(nc):
            buffer[i, z, f] = stage[i]
        return post

    def spread_gate_up(side):
        at = pl.ds(side * own_units, own_units)
        return mail.post(
            gu_buf.at[:, planes, 0, :, at],
            [(gu_st.at[:, :, at], gu_buf.at[:, z, f, :, at], peer) for peer in in_column],
        )

    def forward(posts, buffer):
        for post in posts:
            post.wait_recv()
        both = buffer.at[:, :, f]
        return mail.post(both, [(both, both, sibling)])

    with jax.named_scope("a_stage_wq"):
        wq_st[c] = wq_own[c]
        spread_wq = spread(wq_st, staged_wq, wq_buf)
    with jax.named_scope("a_pass_hidden"):
        passing = [pass_on(arriving[q], hid_all, q, by_seq) for q in range(num_seqs)]
    up_copies = [
        mail.post(
            up_all.at[q, pl.ds(0, 2)],
            [(up_own.at[q], up_all.at[q, c], peer) for peer in (to_x, to_y)],
        )
        for q in range(num_seqs)
    ]
    pump(bulk, PUMPS[3])
    with jax.named_scope("a_route"):
        meta_copies.wait_recv()
        meta_all[c] = meta_own[...]

        def route_one(chip, carry):
            route(chip)
            return carry

        lax.fori_loop(0, nc, route_one, 0)
    wo_st[c] = wo_ref[...]
    for side in range(2):
        at = pl.ds(pl.multiple_of(side * units + c * own_units, own_units), own_units)
        gu_st[c, :, side * own_units : (side + 1) * own_units] = gu_ref[:, at]
    with jax.named_scope("a_forward_wq"):
        passed_wq = forward([spread_wq], wq_buf)
        passed_wq.wait_recv()
        for i in range(nc):
            w_ref[i * block_rows : (i + 1) * block_rows, :] = join(
                wq_buf[i], (block_rows, wide_cols)
            )

    cosines = wide(turn_ref[:, :128], 2 * head_width // 128)
    sines = wide(turn_ref[:, 128:], 2 * head_width // 128)
    tail_at = wide_cols - 128
    attn_gain = column_row(w_ref[:, tail_at:], SMALL + num_experts)
    ctx_copies = []
    for q in range(num_seqs):
        with jax.named_scope("a_wait_hidden"):
            passing[q].wait_recv()
        with jax.named_scope("a_attention"):
            rows = hid_all[q].reshape(full_len, width).astype(F32)
            normed = (rows * inverse_rms(rows) * attn_gain).astype(BF)
            normed_ref[q] = normed
            merged = mm(normed, w_ref[:, : 3 * head_width])
            both = merged[:, : 2 * head_width]
            both = (both * cosines + swap_halves(both) * sines).astype(BF)
            values = merged[:, 2 * head_width :].astype(BF)
            qkv_ref[q, :, : 2 * head_width] = both
            qkv_ref[q, :, 2 * head_width :] = values
            allowed = allowed_keys(len_ref[q], half_len, full_len)
            heads = []
            for h in range(heads_here):
                probs = head_probs(
                    both[:, h * HS : (h + 1) * HS],
                    both[:, head_width + h * HS : head_width + (h + 1) * HS],
                    allowed,
                ).astype(BF)
                heads.append(mm(probs, values[:, h * HS : (h + 1) * HS]))
            context = jnp.concatenate(heads, axis=1).astype(BF)
            ctx_all[c, q] = context.reshape(nc, shard_len, head_width)
        ctx_copies.append(
            mail.post(
                ctx_all.at[pl.ds(0, 2), q],
                [(ctx_all.at[c, q], ctx_all.at[c, q], peer) for peer in (to_x, to_y)],
            )
        )
    spread_wo = spread(wo_st, staged_wo, wo_buf)
    with jax.named_scope("a_pass_upstream"):
        up_passing = [pass_on(up_copies[q], up_all, q, by_seq) for q in range(num_seqs)]
    with jax.named_scope("a_pass_context"):
        ctx_passing = [pass_on(ctx_copies[q], ctx_all, q, by_chip) for q in range(num_seqs)]
    pump(bulk, PUMPS[0])
    with jax.named_scope("a_forward_wo"):
        passed_wo = forward([spread_wo], wo_buf)
        staged_gu.wait_recv()
        for i in range(nc):
            gu_buf[i, z, f] = gu_st[i]
        spread_gu = [spread_gate_up(0)]
        passed_wo.wait_recv()
        for i in range(nc):
            wo_all[i * block_rows : (i + 1) * block_rows, :] = join(
                wo_buf[i], (block_rows, width)
            )
    ffn_gain = column_row(w_ref[:, tail_at:], SMALL + num_experts + 1)
    for q in range(num_seqs):
        with jax.named_scope("a_wait_context"):
            ctx_passing[q].wait_recv()
        with jax.named_scope("a_project"):
            total = hid_all[q].reshape(full_len, width).astype(F32)
            for i in range(nc):
                total = total + mm(
                    ctx_all[i, q].reshape(full_len, head_width),
                    wo_all[i * head_width : (i + 1) * head_width, :],
                )
            acc_a[q * full_len : (q + 1) * full_len] = total
            nt_all[q] = (
                (total * inverse_rms(total) * ffn_gain).astype(BF).reshape(nc, shard_len, width)
            )
    by_block = acc_a.at[pl.ds(0, nc * tok)].reshape(num_seqs, nc, shard_len, width)
    for q in range(num_seqs):
        att_own[q] = by_block[q, c]

    with jax.named_scope("b_wait_upstream"):
        for post in up_passing:
            post.wait_recv()
    with jax.named_scope("b_dispatch"):
        tail = w_ref[:, tail_at:]

        def box_rows_of(chip, carry):
            normed = jnp.concatenate([nt_all[q, chip] for q in range(num_seqs)], axis=0)
            columns = picks[chip]
            gates = gates_of(hot_lanes(columns), mm(normed, tail))
            picks[chip] = jnp.where(lane == 3, gates[0], jnp.where(lane == 4, gates[1], columns))
            up_f = jnp.concatenate([up_all[q, chip] for q in range(num_seqs)], axis=0).astype(F32)
            boxes = mm_tn(hot_x[chip, 0] + hot_x[chip, 1], normed)
            for k in range(2):
                boxes = boxes + mm_tn(hot_d[chip, k], (gates[k] * up_f).astype(BF))
            boxes = boxes.reshape(nz, BOX, width).astype(BF)
            for plane in range(nz):
                sb[plane, chip] = boxes[plane]
            return carry

        lax.fori_loop(0, nc, box_rows_of, 0)
        row_copies = [
            mail.post(ar.at[f, 0], [(sb.at[to[1]], ar.at[f, z], to)]) for to in in_column
        ]
        ar[f, z] = sb[z]
        normed = jnp.concatenate([nt_all[q, c] for q in range(num_seqs)], axis=0)
    pump(bulk, len(bulk))

    with jax.named_scope("b_forward_rows"):
        forwards = mail.open(ar.at[f])
        forwards.add(ar.at[f, z], ar.at[f, z], sibling)
        for s in range(1, nz):
            row_copies[s - 1].wait_recv()
            origin = wrap(z + nz - s, nz)
            forwards.add(ar.at[f, origin], ar.at[f, origin], sibling)
        forwards.wait_recv()
        keep_x, keep_d = (box_rows(CAP, num_experts, shift) for shift in (0, CAP))
        for core in range(2):
            at = slice(core * num_slots, (core + 1) * num_slots)
            boxes = join(ar[core], (num_experts * BOX, width))
            xs[at] = mm(keep_x, boxes).astype(BF)
            ds[at] = mm(keep_d, boxes).astype(BF)
    with jax.named_scope("b_wait_down"):
        @pl.when(to_core == f)
        def _():
            expert_out.wait_recv(remote_out)
            own_out.wait()

        @pl.when(to_core != f)
        def _():
            expert_out.wait_recv()

    gwi, gwo = wie, woe

    def expert_grads(j):
        low = nth_block(j, c) * step
        for side in range(2):
            at = pl.ds(pl.multiple_of(side * half_units + low, step), step)
            gwi[:, at] = mm_tn(xs[...], ex_dm[:, at]).astype(BF)
        at = pl.ds(pl.multiple_of(low, step), step)
        gwo[at, :] = mm_tn(ex_hidden[:, at], ds[...]).astype(BF)

    def homeward(j):
        moves = [
            functools.partial(send_home_in, j, s % nc, g, side)
            for s in range(1, nc + 1)
            for g in range(2)
            for side in range(2)
        ]
        return moves

    home = []
    home_in = mail.open(gwi.at[pl.ds(0, remote_rows)])
    home_out = mail.open(gwo, keep=False)
    remote_home = gwo.at[pl.ds(0, (nc - 1) * out_rows)]
    home_in_own = pltpu.make_async_copy(
        gwi.at[pl.ds(0, shard_rows)], gwi.at[pl.ds(0, shard_rows)], lsem.at[1]
    )

    def send_home_in(j, s, g, side):
        owner = wrap(c + s, nc)
        core = f if g == 0 else 1 - f
        from_rows = pl.ds(
            pl.multiple_of((2 * owner + core) * shard_rows, shard_rows), shard_rows
        )
        low = nth_block(j, c) * step
        to_lane = pl.multiple_of(side * units + f * half_units + low, step)
        src = gwi.at[from_rows, pl.ds(pl.multiple_of(side * half_units + low, step), step)]
        dst = ein_ref.at[c, :, pl.ds(to_lane, step)]
        if s == 0 and g == 0:
            pltpu.make_async_copy(src, dst, lsem.at[1]).start()
        else:
            home_in.add(src, dst, (owner, z, core))

    def home_rows(j):
        return gwo.at[pl.ds(pl.multiple_of(nth_block(j, c) * out_rows, out_rows), out_rows)]

    def home_out_own(j):
        return pltpu.make_async_copy(home_rows(j), eout_ref.at[c], lsem.at[0])

    def send_home_out(j):
        to_block = f * nc + nth_block(j, c)

        @pl.when(to_block == block)
        def _():
            home_out_own(j).start()

        @pl.when(to_block != block)
        def _():
            home_out.add(
                home_rows(j),
                eout_ref.at[c],
                (to_block // 2, z, wrap(to_block, 2)),
            )

    acc_a[...] = jnp.zeros(acc_a.shape, F32)
    acc_b[...] = jnp.zeros(acc_b.shape, F32)
    early = [move for j in range(EARLY) for move in homeward(j)]
    early += [functools.partial(send_home_out, j) for j in range(EARLY)]
    home = [move for j in range(EARLY, steps) for move in homeward(j)]
    home += [functools.partial(send_home_out, j) for j in range(EARLY, steps)]
    late_gate_up = mail.open(gu_buf.at[:, planes, 0, :, pl.ds(0, own_units)])
    spread_sd = mail.open(sd_all.at[planes, 0])
    spread_gu.append(late_gate_up)

    def send_late():
        at = pl.ds(own_units, own_units)
        for peer in in_column:
            late_gate_up.add(gu_st.at[:, :, at], gu_buf.at[:, z, f, :, at], peer)
            spread_sd.add(sd_ref, sd_all.at[z, f], peer)

    if LATE < 0:
        send_late()

    def expert_block(j, carry):
        with jax.named_scope("b_wait_experts"):
            own_in(j).wait()
            mail.at(first_in + j, expert_in[0].like).wait_recv()

        @pl.when(j == steps - 1)
        def _():
            pump(early, len(early))

        with jax.named_scope("b_experts"):
            ffn_block(
                nth_block(j, c), xs[...], ds[...], wie, woe, ex_hidden, ex_dm, acc_a, acc_b,
                half_units, step,
            )

        @pl.when(j < EARLY)
        def _():
            with jax.named_scope("b_early_grads"):
                expert_grads(j)

        @pl.when(j == LATE)
        def _():
            send_late()

        return carry

    lax.fori_loop(0, steps, expert_block, 0)
    mail.settle(row_copies)
    pr = sb
    with jax.named_scope("b_sibling_sum"):

        def boxed(core):
            at = pl.ds(pl.multiple_of(core * num_slots, num_slots), num_slots)
            return (
                mm_tn(keep_x, acc_a[at].astype(BF)) + mm_tn(keep_d, acc_b[at].astype(BF))
            ).reshape(nz, nc, BOX, width)

        pr[...] = boxed(1 - f).astype(BF)
        swap = mail.post(pin, [(pr, pin, sibling)])
        ours = boxed(f)
        swap.wait_recv()
        fb[...] = (ours + pin[...].astype(F32)).astype(BF)
        returns = mail.post(
            rb.at[planes], [(fb.at[to[1]], rb.at[z], to) for to in in_column]
        )
        rb[z] = fb[z]
    with jax.named_scope("b_expert_grads"):

        def late_grads(j, carry):
            expert_grads(j)
            return carry

        lax.fori_loop(EARLY, steps, late_grads, 0)
    pump(home, PUMPS[1])

    with jax.named_scope("b_forward_gu"):
        passed_gu = forward(spread_gu, gu_buf)
        spread_sd.wait_recv()
        passed_sd = mail.post(sd_all.at[:, f], [(sd_all.at[:, f], sd_all.at[:, f], sibling)])
        passed_gu.wait_recv()
        passed_sd.wait_recv()
        for i in range(nc):
            gu_all[i * block_rows : (i + 1) * block_rows, :] = join(
                gu_buf[i], (block_rows, 2 * own_units)
            )
    plane_tok = nc * tok
    shared_rows = nt_all.reshape(plane_tok, width)
    shared_grads = up_all.reshape(plane_tok, width)
    shared_down = sd_all.reshape(own_units, width)
    with jax.named_scope("b_shared"):
        first = pl.ds(0, plane_tok)
        acc_a[...] = jnp.zeros(acc_a.shape, F32)
        acc_b[...] = jnp.zeros(acc_b.shape, F32)

        def shared_block(j, carry):
            ffn_block(
                j, shared_rows[...], shared_grads[...], gu_all, shared_down, sh_hidden, sh_dm,
                acc_a.at[first], acc_b.at[first], own_units, 256,
            )
            return carry

        lax.fori_loop(0, own_units // 256, shared_block, 0)
    mail.settle(spread_gu + [passed_gu])
    ggu = gu_buf
    with jax.named_scope("b_shared_grads"):

        def gate_up_grads(j, carry):
            at = pl.ds(pl.multiple_of(j * 256, 256), 256)
            piece = mm_tn(shared_rows[...], sh_dm[:, at])
            ggu[:, :, :, :, at] = piece.reshape(ggu.shape[:4] + (256,)).astype(BF)
            return carry

        lax.fori_loop(0, 2 * own_units // 256, gate_up_grads, 0)
        gsd[...] = mm_tn(sh_hidden[...], shared_grads[...]).reshape(gsd.shape).astype(BF)
        sibling_gu = mail.post(sib_gu, [(ggu.at[:, :, 1 - f], sib_gu, sibling)])
        sibling_sd = mail.post(sib_sd, [(gsd.at[:, 1 - f], sib_sd, sibling)])

    with jax.named_scope("c_probs"):
        def probs_of(q, carry):
            allowed = allowed_keys(len_ref[q], half_len, full_len)
            merged = qkv_ref[q]
            for h in range(heads_here):
                probs_all[q, h] = head_probs(
                    merged[:, h * HS : (h + 1) * HS],
                    merged[:, head_width + h * HS : head_width + (h + 1) * HS],
                    allowed,
                )
            return carry

        lax.fori_loop(0, num_seqs, probs_of, 0)
    with jax.named_scope("b_reduce_shared"):
        def two_cores(copy, own, inbox):
            copy.wait_recv()
            inbox[...] = (own.astype(F32) + inbox[...].astype(F32)).astype(BF)

        def four_planes(copy, buffer, inbox):
            copy.wait_recv()
            for i in range(nc):
                inbox[i] = (buffer[i, :, f].astype(F32) + inbox[i].astype(F32)).astype(BF)

        four_planes(sibling_gu, ggu, sib_gu)
        two_cores(sibling_sd, gsd[:, f], sib_sd)
    with jax.named_scope("c_wait_returns"):
        returns.wait_recv()
    with jax.named_scope("c_column_mixture"):
        cuts = [
            acc.at[first].reshape(num_seqs, nc, shard_len, width) for acc in (acc_a, acc_b)
        ]

        def add_results(chip, carry):
            results = join(
                jnp.concatenate([rb[plane, chip].astype(F32) for plane in range(nz)], axis=0),
                (column_slots, width),
            )
            up_f = jnp.concatenate([up_all[q, chip] for q in range(num_seqs)], axis=0).astype(F32)
            gates = [picks[chip][:, 3 + k : 4 + k] for k in range(2)]
            routed = [mm(hot_x[chip, k], results) for k in range(2)]
            mixture = gates[0] * routed[0] + gates[1] * routed[1]
            d_rows = mm(hot_d[chip, 0] + hot_d[chip, 1], results)
            for q in range(num_seqs):
                at = slice(q * shard_len, (q + 1) * shard_len)
                cuts[0][q, chip] = cuts[0][q, chip] + mixture[at]
                cuts[1][q, chip] = cuts[1][q, chip] + d_rows[at]
            d_gates = [jnp.sum(routed[k] * up_f, axis=1, keepdims=True) for k in range(2)]
            spread_out = jnp.where(lane == 0, d_gates[0], jnp.where(lane == 1, d_gates[1], 0.0))
            dg_send[chip] = jnp.transpose(spread_out, (1, 0))[:8]
            return carry

        lax.fori_loop(0, nc, add_results, 0)
        for k in range(2):
            for q in range(num_seqs):
                sh_own[k, q, 0] = cuts[k][q, c]
                sh_own[k, q, 1] = cuts[k][q, near_y if q == 0 else near_x]
            sh_send[k] = cuts[k][...].astype(BF)

    def first_leg(inbox, box, lead):
        post = mail.open(inbox)
        for q in range(num_seqs):
            peer = to_x if q == 0 else to_y
            for at, chip in enumerate((near_x if q == 0 else near_y, far)):
                post.add(box.at[lead + (q, chip)], inbox.at[lead + (q, at)], peer)
        return post

    shared_first = first_leg(sh_in, sh_send, (slice(None),))
    dg_copies = mail.post(
        dg_in.at[others],
        [(dg_send.at[wrap(c + s, nc)], dg_in.at[c], in_plane[s - 1]) for s in range(1, nc)],
    )
    dg_in[c] = dg_send[c]
    pump(home, PUMPS[4])

    with jax.named_scope("c_reduce_column"):
        gu_copies = mail.post(
            zi_gu,
            [
                (sib_gu.at[:, to[1]], zi_gu.at[up - 1], to)
                for to, up in zip(in_column, steps_up)
            ],
        )
        sd_copies = mail.post(
            zi_sd,
            [(sib_sd.at[to[1]], zi_sd.at[up - 1], to) for to, up in zip(in_column, steps_up)],
        )
    with jax.named_scope("c_second_sum"):
        shared_first.wait_recv()
        for k in range(2):
            for q in range(num_seqs):
                sh_mid[k, q] = (sh_own[k, q, 1] + sh_in[k, q, 1].astype(F32)).astype(BF)
        shared_second = mail.post(
            sh_end,
            [
                (sh_mid.at[:, q], sh_end.at[:, q], to_y if q == 0 else to_x)
                for q in range(num_seqs)
            ],
        )

    pump(home, PUMPS[5])
    with jax.named_scope("c_wait_shared"):
        dg_copies.wait_recv()
        shared_second.wait_recv()
        added, d_normed = [
            jnp.concatenate(
                [
                    sh_own[k, q, 0] + sh_in[k, q, 0].astype(F32) + sh_end[k, q].astype(F32)
                    for q in range(num_seqs)
                ],
                axis=0,
            )
            for k in range(2)
        ]
    with jax.named_scope("c_combine"):
        attended = att_own[...].reshape(tok, width)
        inverse = inverse_rms(attended)
        out_ref[...] = (live * (attended + added)).astype(BF).reshape(out_ref.shape)
        store(out_ref, out_to)
        hots = hot_lanes(picks[c])
        own_gates = gates_of(hots, mm(normed, tail))
        summed = turned(jnp.sum(dg_in[...], axis=0))
        d_gates = [summed[:, k : k + 1] for k in range(2)]
        mean_gate = own_gates[0] * d_gates[0] + own_gates[1] * d_gates[1]
        d_logits = hots[0] * (own_gates[0] * (d_gates[0] - mean_gate)) + hots[1] * (
            own_gates[1] * (d_gates[1] - mean_gate)
        )
        d_normed = d_normed + split_dot(mm_nt, d_logits, tail)
        d_attended = upstream + norm_back(attended, inverse, d_normed * ffn_gain)
        d_att_b = d_attended.astype(BF)
        d_context = mm_nt(d_att_b, wo_all[...]).astype(BF)
        for i in range(nc):
            dctx_send[i] = d_context[:, i * head_width : (i + 1) * head_width].reshape(
                num_seqs, shard_len, head_width
            )
        for q in range(num_seqs):
            dctx_all[q, c] = dctx_send[c, q]
        dctx_copies = mail.post(
            dctx_all.at[:, others],
            [
                (dctx_send.at[wrap(c + s, nc)], dctx_all.at[:, c], in_plane[s - 1])
                for s in range(1, nc)
            ],
        )
        gin_ref[...] = d_attended.reshape(gin_ref.shape)
    pump(home, PUMPS[2])

    mail.settle([spread_wo, passed_wo])
    gwo_at = wo_buf
    with jax.named_scope("c_reduce"):
        for i in range(nc):
            mine = jnp.concatenate([ctx_all[i, q, c] for q in range(num_seqs)], axis=0)
            gwo_at[i] = mm_tn(mine, d_att_b).reshape(gwo_at.shape[1:]).astype(BF)
        sibling_wo = mail.post(sib_wo, [(gwo_at.at[:, :, 1 - f], sib_wo, sibling)])
        d_router = split_dot(mm_tn, normed, d_logits, left_wide=False)
        d_gain = jnp.sum(d_normed * attended * inverse, axis=0, keepdims=True)
        turned = jnp.transpose(jnp.broadcast_to(d_gain, (128, width)), (1, 0))
        extra_lane = lax.broadcasted_iota(jnp.int32, (width, 128), 1)
        extras = jnp.where(extra_lane == SMALL + num_experts + 1, turned, d_router)
        four_planes(sibling_wo, gwo_at, sib_wo)
        wo_copies = mail.post(
            zi_wo,
            [
                (sib_wo.at[:, wrap(z + s, nz)], zi_wo.at[s - 1], in_column[s - 1])
                for s in range(1, nz)
            ],
        )

    with jax.named_scope("c_wait_dctx"):
        dctx_copies.wait_recv()
    def column_sum(own, copies, inbox):
        copies.wait_recv()
        total = own.astype(F32)
        for s in range(1, nz):
            total = total + inbox[s - 1].astype(F32)
        return total

    def hand_out(box, final):
        store(box.at[c], final.at[c])
        return mail.post(
            final.at[others],
            [(box.at[wrap(c + s, nc)], final.at[c], in_plane[s - 1]) for s in range(1, nc)],
        )

    with jax.named_scope("c_column_gu"):
        pb_gu[...] = column_sum(sib_gu[:, z], gu_copies, zi_gu).astype(BF)
        final_gu = hand_out(pb_gu, fgu_ref)
    grad_qkv = jnp.zeros((width, 3 * head_width), F32)
    merged_grads = []
    for q in range(num_seqs):
        with jax.named_scope("c_attention"):
            d_context = dctx_all[q].reshape(full_len, head_width)
            merged = qkv_ref[q]
            d_query, d_key, d_value = [], [], []
            for h in range(heads_here):
                query = merged[:, h * HS : (h + 1) * HS]
                key = merged[:, head_width + h * HS : head_width + (h + 1) * HS]
                value = merged[:, 2 * head_width + h * HS : 2 * head_width + (h + 1) * HS]
                d_head = d_context[:, h * HS : (h + 1) * HS]
                probs = probs_all[q, h]
                d_probs = mm_nt(d_head, value)
                delta = jnp.sum(probs * d_probs, axis=1, keepdims=True)
                d_scores = (probs * (d_probs - delta)).astype(BF)
                d_query.append(mm(d_scores, key) * (HS**-0.5))
                d_key.append(mm_tn(d_scores, query) * (HS**-0.5))
                d_value.append(mm_tn(probs.astype(BF), d_head))
            both = jnp.concatenate(d_query + d_key, axis=1)
            both = both * cosines - swap_halves(both) * sines
            d_merged = jnp.concatenate([both] + d_value, axis=1).astype(BF)
            merged_grads.append(d_merged)
            grad_qkv = grad_qkv + mm_tn(normed_ref[q], d_merged)
    mail.settle([spread_wq, passed_wq])
    gq = wq_buf
    with jax.named_scope("c_reduce_q"):
        last = jnp.concatenate([grad_qkv[:, tail_at:], extras[:, 3 * head_width - tail_at :]], axis=1)
        gq[...] = (
            jnp.concatenate([grad_qkv[:, :tail_at], last], axis=1).reshape(gq.shape).astype(BF)
        )
        sibling_q = mail.post(sib_q, [(gq.at[:, :, 1 - f], sib_q, sibling)])
    with jax.named_scope("c_d_normed"):
        rs_first = mail.open(rs_in)
        for q in range(num_seqs):
            d_merged = merged_grads[q]
            product = mm_nt(d_merged, w_ref[:, : 3 * head_width]).reshape(nc, shard_len, width)
            part_own[q] = product
            part[q] = product.astype(BF)
            for at, chip in enumerate((near_x if q == 0 else near_y, far)):
                rs_first.add(part.at[q, chip], rs_in.at[q, at], to_x if q == 0 else to_y)
    pump(home, len(home))
    with jax.named_scope("c_reduce_q"):
        four_planes(sibling_q, gq, sib_q)
        q_copies = mail.post(
            zi_q,
            [
                (sib_q.at[:, to[1]], zi_q.at[up - 1], to)
                for to, up in zip(in_column, steps_up)
            ],
        )
    with jax.named_scope("c_second_leg"):
        rs_first.wait_recv()
        for q in range(num_seqs):
            relay = part_own[q, near_y if q == 0 else near_x]
            rs_mid[q] = (relay + rs_in[q, 1].astype(F32)).astype(BF)
        rs_second = mail.post(
            rs_end,
            [(rs_mid.at[q], rs_end.at[q], to_y if q == 0 else to_x) for q in range(num_seqs)],
        )

    with jax.named_scope("c_column_sd"):
        fsd_ref[...] = column_sum(sib_sd[z], sd_copies, zi_sd)
        store(fsd_ref, fsd_to)
    with jax.named_scope("c_column_wo"):
        pb_wo[...] = column_sum(sib_wo[:, z], wo_copies, zi_wo).astype(BF)
        in_wo[c] = pb_wo[c]
        final_wo = mail.post(
            in_wo.at[others],
            [(pb_wo.at[wrap(c + s, nc)], in_wo.at[c], in_plane[s - 1]) for s in range(1, nc)],
        )
    with jax.named_scope("c_column_q"):
        pb_q[...] = column_sum(sib_q[:, z], q_copies, zi_q).astype(BF)
        final_q = hand_out(pb_q, fq_ref)
    with jax.named_scope("c_grad_in"):
        rs_second.wait_recv()
        for q in range(num_seqs):
            d_normed = part_own[q, c] + rs_in[q, 0].astype(F32) + rs_end[q].astype(F32)
            rows = hid_ref[q].astype(F32)
            gin_ref[q] = gin_ref[q] + norm_back(rows, inverse_rms(rows), d_normed * attn_gain)
        store(gin_ref, gin_to)
    with jax.named_scope("c_final"):
        final_wo.wait_recv()
        fwo_ref[...] = jnp.sum(in_wo[...].astype(F32), axis=0)
        store(fwo_ref, fwo_to)
        final_gu.wait_recv()
        final_q.wait_recv()
    with jax.named_scope("c_wait_home"):
        home_in_own.wait()
        home_in.wait_recv()

        @pl.when(to_core == f)
        def _():
            home_out_own(0).wait()
            home_out.wait_recv(remote_home)
            home_out.wait_send(remote_home)
            expert_out.wait_send(remote_out)

        @pl.when(to_core != f)
        def _():
            home_out.wait_recv()
            home_out.wait_send()
            expert_out.wait_send()

    assert mail.count <= POSTS, mail.count
    with jax.named_scope("z_finish"):
        for copy in stores:
            copy.wait()
        mail.finish()


def finish_kernel(
    nc, fq_in, fgu_in, wqkv_in, ga_in, ein_ref, eout_ref, out_in, gin_in, fsd_in, fwo_in,
    gq_to, gr_to, gga_to, ggf_to, ggu_to, oin_ref, oout_ref, out_to, gin_to, fsd_to, fwo_to,
    narrow_in, narrow_out, wide_in, wide_out,
    fq_ref, fgu_ref, wqkv_ref, ga_ref, out_ref, gin_ref, fsd_ref, fwo_ref,
    gq_ref, gr_ref, gga_ref, ggf_ref, ggu_ref, sems, isem, osem,
):
    pieces = []
    for e in range(ein_ref.shape[0]):
        for source, narrow, widened, target in (
            (ein_ref, narrow_in, wide_in, oin_ref),
            (eout_ref, narrow_out, wide_out, oout_ref),
        ):
            rows = source.shape[1] // WIDEN
            for k in range(WIDEN):
                at = (e, pl.ds(k * rows, rows))
                pieces.append((at, source, narrow, widened, target))
    loads = [
        pltpu.make_async_copy(source, target, isem.at[i])
        for i, (source, target) in enumerate(
            (
                (fq_in, fq_ref), (fgu_in, fgu_ref), (wqkv_in, wqkv_ref), (ga_in, ga_ref),
                (out_in, out_ref), (gin_in, gin_ref), (fsd_in, fsd_ref), (fwo_in, fwo_ref),
            )
        )
    ]
    arriving = []
    for i, (at, source, narrow, _, _) in enumerate(pieces):
        arriving.append(pltpu.make_async_copy(source.at[at], narrow.at[at], sems.at[0, i]))
        arriving[-1].start()
        if i == SMALL_AT:
            for load in loads:
                load.start()
    stores = []

    def store(source, target):
        stores.append(pltpu.make_async_copy(source, target, osem.at[len(stores)]))
        stores[-1].start()

    leaving = []

    def widen(i):
        at, _, narrow, widened, target = pieces[i]
        arriving[i].wait()
        widened[at] = narrow[at].astype(F32)
        leaving.append(pltpu.make_async_copy(widened.at[at], target.at[at], sems.at[1, i]))
        leaving[-1].start()

    for i in range(len(pieces) // 2):
        widen(i)
    for load in loads:
        load.wait()
    for source, target in (
        (out_ref, out_to), (gin_ref, gin_to), (fsd_ref, fsd_to), (fwo_ref, fwo_to)
    ):
        store(source, target)
    rows_w = wqkv_ref.shape[0]
    head_width = wqkv_ref.shape[1] // 3 // nc
    grads = jnp.concatenate(
        [
            fq_ref[i, :, side * head_width : (side + 1) * head_width].astype(F32)
            for side in range(3)
            for i in range(nc)
        ],
        axis=1,
    )
    gq_ref[...] = grads
    own_units = fgu_ref.shape[2] // 2
    ggu_ref[...] = jnp.concatenate(
        [
            fgu_ref[i, :, side * own_units : (side + 1) * own_units].astype(F32)
            for side in range(2)
            for i in range(nc)
        ],
        axis=1,
    )
    extras = jnp.sum(fq_ref[:, :, 3 * head_width - SMALL :].astype(F32), axis=0)
    num_experts = gr_ref.shape[0]
    first = jnp.sum(wqkv_ref[...].astype(F32) * grads, axis=1, keepdims=True)
    lane = lax.broadcasted_iota(jnp.int32, (rows_w, 128), 1)
    both = jnp.where(lane == SMALL + num_experts, first, extras)
    turned = jnp.transpose(
        jnp.concatenate([both, jnp.zeros((128 - rows_w, 128), F32)], axis=0), (1, 0)
    )
    gr_ref[...] = turned[SMALL : SMALL + num_experts, :rows_w]
    at = SMALL + num_experts
    gga_ref[...] = turned[at : at + 1, :rows_w] / ga_ref[...].astype(F32)
    ggf_ref[...] = turned[at + 1 : at + 2, :rows_w]

    for source, target in (
        (gq_ref, gq_to), (gr_ref, gr_to), (gga_ref, gga_to), (ggf_ref, ggf_to), (ggu_ref, ggu_to)
    ):
        store(source, target)
    for i in range(len(pieces) // 2, len(pieces)):
        widen(i)
    for copy in leaving + stores:
        copy.wait()


def vmem(*shape, dtype=jnp.bfloat16):
    return pltpu.VMEM(shape, dtype)


def fast_device(
    hidden_in, seq_lengths, expert_ids, route_rank, gain_attn, w_qkv, w_out, w_router, gain_ffn,
    w_gate_up, w_shared_down, w_experts_in, w_experts_out, grad_output,
):
    nc, nz = lax.axis_size("ctx"), lax.axis_size("exp")
    num_seqs, two_ends, half_len, width = hidden_in.shape
    shard_len = 2 * half_len
    full_len = nc * shard_len
    tok = num_seqs * shard_len
    rows_w = w_qkv.shape[0]
    head_width = w_qkv.shape[1] // 3 // nc
    num_experts = w_router.shape[1]
    down_rows = w_shared_down.shape[0]
    own_units = w_gate_up.shape[1] // 2 // nc
    half_units = w_experts_in.shape[2] // 4
    hbm, vm, sm = pl.ANY, pltpu.VMEM, pltpu.SMEM
    dma = pltpu.SemaphoreType.DMA

    seq_shape = (num_seqs, shard_len, width)
    group_shape = (num_seqs, nc, shard_len, width)
    blocks = (nc, nz, 2, rows_w)
    half_blocks = (nc, nz, rows_w)
    wide_cols = 3 * head_width + SMALL
    num_slots = num_experts * CAP
    row_box = (nz, nc, BOX, width)
    plane_tok = nc * tok
    outs = [
        (seq_shape, BF),
        (seq_shape, F32),
        ((nc, rows_w, wide_cols), BF),
        ((nc, rows_w, 2 * own_units), BF),
        ((down_rows, width), F32),
        ((rows_w, width), F32),
        (w_experts_in.shape, BF),
        (w_experts_out.shape, BF),
    ]
    small_ins = [
        expert_ids.transpose(0, 1, 3, 2),
        route_rank.reshape(1, tok),
        w_qkv,
        w_router.T,
        gain_attn.reshape(1, rows_w),
        gain_ffn.reshape(1, rows_w),
        hidden_in.reshape(seq_shape),
        w_gate_up,
        w_out,
        w_shared_down,
        grad_output.reshape(seq_shape),
    ]
    out, gin, fq, fgu, fsd, fwo, ein, eout = pl.pallas_call(
        functools.partial(block_kernel, nc, nz),
        out_shape=[jax.ShapeDtypeStruct(shape, dtype) for shape, dtype in outs],
        in_specs=[
            pl.BlockSpec(memory_space=space) for space in [sm] + [hbm] * 13
        ],
        out_specs=[pl.BlockSpec(memory_space=hbm) for _ in outs],
        scratch_shapes=[
            *[vmem(*x.shape, dtype=x.dtype) for x in small_ins],
            *[vmem(*outs[i][0], dtype=outs[i][1]) for i in (0, 1, 4, 5)],
            vmem(full_len, 256, dtype=F32),
            vmem(8, tok, dtype=jnp.int32),
            vmem(nc, 8, tok, dtype=jnp.int32),
            vmem(nc, tok, 128, dtype=F32),
            vmem(nc, 2, tok, nz * BOX),
            vmem(nc, 2, tok, nz * BOX),
            vmem(nc, 8, tok, dtype=F32),
            vmem(nc, 8, tok, dtype=F32),
            vmem(*group_shape),
            vmem(*seq_shape),
            vmem(*group_shape),
            vmem(nc, rows_w, wide_cols),
            vmem(nc, rows_w, wide_cols),
            vmem(*blocks, wide_cols),
            vmem(width, wide_cols),
            vmem(nc, rows_w, 2 * own_units),
            vmem(*blocks, 2 * own_units),
            vmem(width, 2 * own_units),
            vmem(nc, rows_w, width),
            vmem(*blocks, width),
            vmem(width, width),
            vmem(nz, 2, down_rows, width),
            vmem(width, 2 * half_units),
            vmem(half_units, width),
            vmem(num_seqs, full_len, width),
            vmem(num_seqs, full_len, 3 * head_width),
            vmem(num_seqs, head_width // HS, full_len, full_len, dtype=F32),
            vmem(nc, num_seqs, nc, shard_len, head_width),
            vmem(*seq_shape, dtype=F32),
            vmem(*group_shape),
            vmem(*row_box),
            vmem(2, nz, nc, BOX, width),
            vmem(2 * num_slots, width),
            vmem(2 * num_slots, width),
            vmem(2 * num_slots, width, dtype=F32),
            vmem(2 * num_slots, width, dtype=F32),
            vmem(2, num_seqs, 2, shard_len, width, dtype=F32),
            vmem(plane_tok, own_units),
            vmem(plane_tok, 2 * own_units),
            vmem(2, *group_shape),
            vmem(2, num_seqs, 2, shard_len, width),
            vmem(2, *seq_shape),
            vmem(2, *seq_shape),
            vmem(2 * num_slots, half_units),
            vmem(2 * num_slots, 2 * half_units),
            vmem(*row_box),
            vmem(*row_box),
            vmem(*row_box),
            vmem(nz, 2, down_rows, width),
            vmem(*seq_shape),
            vmem(nc, num_seqs, shard_len, head_width),
            vmem(num_seqs, nc, shard_len, head_width),
            vmem(*group_shape),
            vmem(*group_shape, dtype=F32),
            vmem(num_seqs, 2, shard_len, width),
            vmem(*seq_shape),
            vmem(*seq_shape),
            vmem(*half_blocks, 2 * own_units),
            vmem(nz - 1, nc, rows_w, 2 * own_units),
            vmem(nc, rows_w, 2 * own_units),
            vmem(*half_blocks, wide_cols),
            vmem(nz - 1, nc, rows_w, wide_cols),
            vmem(nc, rows_w, wide_cols),
            vmem(nz, down_rows, width),
            vmem(nz - 1, down_rows, width),
            vmem(*half_blocks, width),
            vmem(nz - 1, nc, rows_w, width),
            vmem(nc, rows_w, width),
            vmem(nc, rows_w, width),
            dma((POSTS,)),
            dma((POSTS,)),
            dma((1 + half_units // 256,)),
            dma((len(small_ins),)),
            dma((6,)),
        ],
        compiler_params=pltpu.CompilerParams(
            collective_id=0, has_side_effects=True, vmem_limit_bytes=VMEM_BYTES
        ),
        cost_estimate=pl.CostEstimate(
            flops=16_000_000_000, bytes_accessed=30_000_000, transcendentals=0
        ),
        name="block_forward_backward",
    )(
        seq_lengths, *small_ins, w_experts_in, w_experts_out
    )

    ins = [fq, fgu, w_qkv, gain_attn.reshape(1, rows_w), ein, eout, out, gin, fsd, fwo]
    results = [
        (w_qkv.shape, F32),
        (w_router.shape[::-1], F32),
        ((1, rows_w), F32),
        ((1, rows_w), F32),
        (w_gate_up.shape, F32),
        (ein.shape, F32),
        (eout.shape, F32),
        (seq_shape, BF),
        (seq_shape, F32),
        (fsd.shape, F32),
        (fwo.shape, F32),
    ]
    grad_qkv, grad_router, grad_ga, grad_gf, grad_gu, grad_in, grad_out, out, gin, fsd, fwo = pl.pallas_call(
        functools.partial(finish_kernel, nc),
        out_shape=[jax.ShapeDtypeStruct(shape, dtype) for shape, dtype in results],
        in_specs=[pl.BlockSpec(memory_space=hbm) for _ in ins],
        out_specs=[pl.BlockSpec(memory_space=hbm) for _ in results],
        scratch_shapes=[
            vmem(*ein.shape),
            vmem(*eout.shape),
            vmem(*ein.shape, dtype=F32),
            vmem(*eout.shape, dtype=F32),
            *[vmem(*ins[i].shape, dtype=ins[i].dtype) for i in (0, 1, 2, 3, 6, 7, 8, 9)],
            *[vmem(*results[i][0], dtype=results[i][1]) for i in range(5)],
            dma((2, 2 * ein.shape[0] * WIDEN)),
            dma((8,)),
            dma((9,)),
        ],
        compiler_params=pltpu.CompilerParams(vmem_limit_bytes=VMEM_BYTES),
        name="widen_gradients",
    )(*ins)
    return (
        out.reshape(hidden_in.shape),
        gin.reshape(hidden_in.shape),
        grad_ga.reshape(rows_w),
        grad_qkv,
        fwo,
        grad_router.T,
        grad_gf.reshape(rows_w),
        grad_gu,
        fsd,
        grad_in,
        grad_out,
    )


def fits(mesh, hidden_in, w_qkv, w_router, w_gate_up, w_experts_in):
    nc, nz, nf = mesh.shape["ctx"], mesh.shape["exp"], mesh.shape["fsdp"]
    heads = w_qkv.shape[1] // 3 // HS
    return (
        nf == 2
        and nc == 4
        and nz == 4
        and heads == 12
        and w_router.shape[1] == nc * nz
        and w_qkv.shape[0] == 768
        and hidden_in.shape[2] == 32 * nc
        and hidden_in.shape[0] == 2 * nz * nf
        and hidden_in.shape[3] == 768
        and w_gate_up.shape[1] == w_experts_in.shape[2] == 4096
        and 2 * CAP <= BOX
    )


def solution(mesh):
    def whole(*args):
        chosen = fast_device if fits(mesh, args[0], args[5], args[7], args[9], args[11]) else per_device
        return placed(mesh, chosen)(*args)

    return whole


def placed(mesh, chosen):
    return jax.shard_map(
        chosen,
        mesh=mesh,
        in_specs=(
            P(("exp", "fsdp"), None, "ctx", None),
            P(("exp", "fsdp")),
            P(("exp", "fsdp"), None, "ctx", None),
            P(("exp", "fsdp"), "ctx", None),
            P(("ctx", "exp", "fsdp")),
            P(("ctx", "exp", "fsdp"), None),
            P(("ctx", "exp", "fsdp"), None),
            P(("ctx", "exp", "fsdp"), None),
            P(("ctx", "exp", "fsdp")),
            P(("ctx", "exp", "fsdp"), None),
            P(("ctx", "exp", "fsdp"), None),
            P("exp", ("ctx", "fsdp"), None),
            P("exp", ("ctx", "fsdp"), None),
            P(("exp", "fsdp"), None, "ctx", None),
        ),
        out_specs=(
            P(("exp", "fsdp"), None, "ctx", None),
            P(("exp", "fsdp"), None, "ctx", None),
            P(("ctx", "exp", "fsdp")),
            P(("ctx", "exp", "fsdp"), None),
            P(("ctx", "exp", "fsdp"), None),
            P(("ctx", "exp", "fsdp"), None),
            P(("ctx", "exp", "fsdp")),
            P(("ctx", "exp", "fsdp"), None),
            P(("ctx", "exp", "fsdp"), None),
            P("exp", ("ctx", "fsdp"), None),
            P("exp", ("ctx", "fsdp"), None),
        ),
        check_vma=False,
    )
```
